32 devices in a mesh: ctx: 8 (over z, core), exp: 4 (over y, x).
Axes of the slice: x: 2, y: 2, z: 4, core: 2. Of those that a mesh axis runs over, the one named last changes fastest.
Arguments:
- tokens: bfloat16 [4, 2048, 1536], P('exp', 'ctx'), may hold values from -6 to 6
- cotangent: bfloat16 [4, 2048, 1536], P('exp', 'ctx'), may hold values from -6 to 6
- routes: int32 [4, 2048, 2], P('exp', 'ctx'), may hold values from 0 to 15, all different within a row; in each aligned block of 256 rows (0 to 255, 256 to 511, ..., all dimensions but the last counted through in order) at most 48 rows name the same one
- lengths: int32 [4, 3], P('exp'), may hold values from 1 to 1024, 2048 in all within a row
- block_order: int32 [4, 16], P('exp'), may hold values from 0 to 15, each once within a row
- gain_attn: float32 [1536], P(('ctx', 'exp')), may hold values from 0.5 to 1.5
- qkv_weight: float32 [1536, 2560], P(('ctx', 'exp')), may hold values from -0.15625 to 0.15625
- out_weight: float32 [1536, 1536], P(('ctx', 'exp')), may hold values from -1.5 to 1.5
- gain_moe: float32 [1536], P(('ctx', 'exp')), may hold values from 0.5 to 1.5
- router_weight: float32 [1536, 16], P(('ctx', 'exp')), may hold values from -0.109375 to 0.109375
- expert_in: float32 [16, 1536, 2048], P('exp', 'ctx'), may hold values from -0.15625 to 0.15625
- expert_out: float32 [16, 1024, 1536], P('exp', 'ctx'), may hold values from -0.375 to 0.375
Outputs:
- block_out: bfloat16 [4, 2048, 1536], P('exp', 'ctx')
- d_tokens: bfloat16 [4, 2048, 1536], P('exp', 'ctx')
- d_gain_attn: float32 [1536], P(('ctx', 'exp'))
- d_qkv_weight: float32 [1536, 2560], P(('ctx', 'exp'))
- d_out_weight: float32 [1536, 1536], P(('ctx', 'exp'))
- d_gain_moe: float32 [1536], P(('ctx', 'exp'))
- d_router_weight: float32 [1536, 16], P(('ctx', 'exp'))
- d_expert_in: float32 [16, 1536, 2048], P('exp', 'ctx')
- d_expert_out: float32 [16, 1024, 1536], P('exp', 'ctx')
The draws below stay inside these ranges and needn't reach their ends.
Inputs may be any that keep to these rules, and one draw needn't show every extreme that they name: `routes`: among the rows of one device no expert is named more than 48 times; the two experts of a row differ. The lengths of a pack sum to 2048; the longest is 1024. `block_order`: each row is a permutation.
All inputs are finite; a program needn't handle non-finite values.
Results may differ from the reference program's by a relative error of at most 0.025.
Values may be sent and summed in bfloat16 or wider, within the bound.
A program may use at most 256 MiB of HBM per device.

```python
import math
import jax
import jax.numpy as jnp
import numpy as np
from jax import lax

D = 1536
HEADS = 24
KV_HEADS = 8
HEAD = 64
FF = 1024
EXPERTS = 16
BLK = 128
NSEQ = 3
TOK_DEV = 256
CAP = 48
PACK = 2048
NBLK = 16
PACKS = 4
LONGEST = 1024
SLOTS = 384
QKV = 2560
GROUP = 3


def steps_of(own_key, shape, pieces, least, high):
    loudness = 1.0
    for axis_at, blocks in pieces:
        heights = jax.random.uniform(jax.random.fold_in(jax.random.fold_in(own_key, 6), axis_at), (blocks,), jnp.float32, least / len(pieces), high / len(pieces))
        loudness = loudness * jnp.repeat(jnp.exp(heights), shape[axis_at] // blocks).reshape((-1,) + (1,) * (len(shape) - 1 - axis_at))
    return loudness


def split_up(count, total, reach, lean):
    weights = [(1 << 20) // math.isqrt(rank ** lean) + 1 for rank in range(2, count + 1)]
    surplus, holding = total - reach - (count - 1), [1] * (count - 1)
    while surplus > 0:
        movable = [i for i in range(count - 1) if holding[i] < reach]
        pool, left = sum([weights[i] for i in movable]), surplus
        for i in movable:
            more = min(reach - holding[i], max(1, left * weights[i] // pool), surplus)
            holding[i] = holding[i] + more
            surplus = surplus - more
    return np.array([reach] + holding)


def uneven_parts(stream_key, count, total, bound, slope):
    if count == 2:
        one = jax.random.randint(stream_key, (), max(1, total - bound), min(bound, total - 1) + 1)
        return jnp.stack([one, total - one])
    sizes = jnp.asarray(split_up(count, total, bound, slope), jnp.int32)
    couples = (count - 1) // 2
    donor, sink = sizes[1:1 + 2 * couples:2], sizes[2:2 + 2 * couples:2]
    slack = jnp.minimum(donor - 1, bound - sink)
    shifted = jax.random.randint(jax.random.fold_in(stream_key, 1), (couples,), 0, 1 << 20) % (slack + 1)
    sizes = sizes.at[1:1 + 2 * couples:2].set(donor - shifted).at[2:2 + 2 * couples:2].set(sink + shifted)
    return sizes[jax.random.permutation(jax.random.fold_in(stream_key, 2), count)]


def shared_out(own_key, own, number, rows, count, top, limit, skew):
    ranking = jax.random.permutation(own_key, count)
    heavy_load, common = portions_of(count, rows * top, limit, skew, True), portions_of(count, rows * top, limit, skew, False)
    places = jnp.arange(count)

    def named(sizes, offset_by):
        used = int((sizes > 0).sum())
        fixed = max(1, used // 4)
        passed = fixed + (places - fixed + offset_by * (used - fixed)) % max(1, count - fixed)
        return jnp.zeros((count,), jnp.int32).at[ranking[jnp.where(places < fixed, places, passed)]].set(jnp.asarray(sizes, jnp.int32))

    sizes = jnp.where(number % 4 == 0, named(heavy_load, number // 4), named(common, number - number // 4 - 1))
    mixed = jax.random.permutation(jax.random.fold_in(own, 3), count)
    donor, taker = mixed[0:count // 2 * 2:2], mixed[1:count // 2 * 2:2]
    margin = jnp.minimum(sizes[donor] - 1, limit - sizes[taker]) // 2
    margin = jnp.where((donor == ranking[0]) | (taker == ranking[0]) | (sizes[taker] == 0), 0, jnp.maximum(margin, 0))
    passed = jax.random.randint(jax.random.fold_in(own, 4), (count // 2,), 0, 1 << 20) % (margin + 1)
    sizes = sizes.at[donor].add(-passed).at[taker].add(passed)
    members = jnp.searchsorted(jnp.cumsum(sizes), jnp.arange(rows * top), side="right").astype(jnp.int32)
    listing = members.reshape(top, rows).T
    listing = listing[jax.random.permutation(jax.random.fold_in(own, 1), rows)]
    offset_by = jax.random.randint(jax.random.fold_in(own, 2), (rows, 1), 0, top)
    return jnp.take_along_axis(listing, (jnp.arange(top)[None, :] + offset_by) % top, axis=1)


def portions_of(number_of, total, limit, skew, full):
    weights = [(1 << 20) // math.isqrt(standing ** skew) + 1 for standing in range(1, number_of + 1)]
    largest = limit if full else min(limit, max(-(-total // number_of), total * weights[0] // sum(weights)))
    least = 1 if total - largest >= number_of - 1 else 0
    counts, spare = [largest] + [least] * (number_of - 1), total - largest - least * (number_of - 1)
    while spare > 0:
        candidates = [i for i in range(1, number_of) if counts[i] < largest] or [i for i in range(1, number_of) if counts[i] < limit]
        whole, left = sum([weights[i] for i in candidates]), spare
        for i in candidates:
            extra = min(limit - counts[i], max(1, left * weights[i] // whole), spare)
            counts[i] = counts[i] + extra
            spare = spare - extra
    return np.array(counts)


def normal_values(stream_key, extent, spread, bound, shards=(), held_as=jnp.bfloat16):
    values = jax.random.normal(stream_key, extent, jnp.float32) * spread
    if len(shards) > 0:
        values = steps_of(stream_key, extent, shards, -0.22, 0.18) * values
    return jnp.clip(values, min=-bound, max=bound).astype(held_as)


def setup_inputs(seed: int = 0) -> dict:
    streams_of = jax.random.split(jax.random.key(seed), 13)
    tokens = normal_values(streams_of[0], (PACKS, PACK, D), 1.0, 6.0, ((0, 4), (1, 8)))
    cotangent = normal_values(streams_of[1], (PACKS, PACK, D), 1.0, 6.0, ((0, 4), (1, 8)))
    routes_keys = jax.random.split(jax.random.fold_in(streams_of[2], 1), PACKS * PACK // TOK_DEV)
    routes_turns = jax.random.permutation(jax.random.fold_in(streams_of[2], 3), PACKS * PACK // TOK_DEV)
    routes = jax.vmap(lambda own, number: shared_out(jax.random.fold_in(streams_of[2], 2), own, number, TOK_DEV, EXPERTS, 2, CAP, 1))(routes_keys, routes_turns).reshape((PACKS, PACK, 2))
    lengths = jax.vmap(lambda own: uneven_parts(own, NSEQ, PACK, LONGEST, 2))(jax.random.split(streams_of[3], PACKS)).reshape((PACKS, NSEQ)).astype(jnp.int32)
    block_order = jax.vmap(lambda own: jax.random.permutation(own, NBLK))(jax.random.split(streams_of[4], PACKS)).reshape((PACKS, NBLK)).astype(jnp.int32)
    gain_attn = jnp.clip(1.0 + 0.1 * jax.random.normal(streams_of[5], (D,), jnp.float32), 0.5, 1.5)
    qkv_weight = normal_values(streams_of[6], (D, QKV), D ** -0.5, 0.15625, ((0, 32),), jnp.float32)
    out_weight = normal_values(streams_of[7], (HEADS * HEAD, D), 16 ** -0.5, 1.5, ((0, 32),), jnp.float32)
    gain_moe = jnp.clip(1.0 + 0.1 * jax.random.normal(streams_of[8], (D,), jnp.float32), 0.5, 1.5)
    router_weight = normal_values(streams_of[9], (D, EXPERTS), (2 * D) ** -0.5, 0.109375, ((0, 32),), jnp.float32)
    expert_in = normal_values(streams_of[10], (EXPERTS, D, 2 * FF), D ** -0.5, 0.15625, ((0, 4), (1, 8)), jnp.float32)
    expert_out = normal_values(streams_of[11], (EXPERTS, FF, D), (FF // 4) ** -0.5, 0.375, ((0, 4), (1, 8)), jnp.float32)
    return dict(tokens=tokens, cotangent=cotangent, routes=routes, lengths=lengths, block_order=block_order, gain_attn=gain_attn, qkv_weight=qkv_weight, out_weight=out_weight, gain_moe=gain_moe, router_weight=router_weight, expert_in=expert_in, expert_out=expert_out)


@jax.custom_vjp
def low(v):
    return lax.optimization_barrier(v.astype(jnp.bfloat16)).astype(jnp.float32)

@jax.custom_vjp
def low_back(v):
    return v

def low_keep(v):
    return (low(v), None)

def low_pass(kept, grad):
    return (grad,)

def back_keep(v):
    return (v, None)

def back_low(kept, grad):
    return (low(grad),)
low.defvjp(low_keep, low_pass)
low_back.defvjp(back_keep, back_low)
highest = lax.Precision.HIGHEST

def norm_scale(values):
    return lax.rsqrt(lax.optimization_barrier(jnp.mean(values * values, axis=-1, keepdims=True)) + 1e-05)

def pack_layout(lengths, block_ids):
    offsets = jnp.arange(BLK, dtype=jnp.int32)
    position = (block_ids.astype(jnp.int32)[:, None] * BLK + offsets[None, :]).reshape(PACK)
    bounds = jnp.cumsum(lengths).astype(jnp.int32)
    document = lax.optimization_barrier(jnp.sum((position[:, None] >= bounds[None, :]).astype(jnp.int32), axis=1))
    return (position, document)

def attend(queries, keys, values, position, document):
    block_rows = min(512, PACK)
    block_count = PACK // block_rows
    scale = HEAD ** (-0.5)

    def one_block(block_item):
        query_block, query_pos, query_doc = block_item
        scores = low_back(jnp.einsum('tkgd,nkd->kgtn', query_block, keys, precision=highest) * scale)
        visible = (query_doc[:, None] == document[None, :]) & (position[None, :] <= query_pos[:, None])
        scores = jnp.where(visible[None, None], scores, -1e+30)
        largest = lax.optimization_barrier(jnp.max(scores, axis=-1, keepdims=True))
        weights = jnp.where(visible[None, None], jnp.exp(scores - largest), 0.0)
        probs = weights / lax.optimization_barrier(jnp.sum(weights, axis=-1, keepdims=True))
        return jnp.einsum('kgtn,nkd->tkgd', low(probs), values, precision=highest)
    outputs = lax.map(jax.checkpoint(one_block), (queries.reshape(block_count, block_rows, KV_HEADS, GROUP, HEAD), position.reshape(block_count, block_rows), document.reshape(block_count, block_rows)))
    return outputs.reshape(PACK, HEADS * HEAD)

def mixture(second, routes, router_weight, expert_in, expert_out):
    route_hot = (routes[:, :, None] == jnp.arange(EXPERTS, dtype=jnp.int32)[None, None, :]).astype(jnp.float32)
    logits = low_back(jnp.dot(second, router_weight, precision=highest))
    chosen = lax.optimization_barrier(jnp.sum(route_hot * logits[:, None, :], axis=-1))
    gates = jax.nn.softmax(chosen, axis=-1)
    flat_hot = route_hot.reshape(PACK * 2, EXPERTS)
    ranks = jnp.cumsum(flat_hot, axis=0) - 1.0
    slot_index = lax.optimization_barrier(jnp.sum(ranks * flat_hot, axis=1)).astype(jnp.int32)
    target = routes.reshape(PACK * 2).astype(jnp.int32) * SLOTS + slot_index
    copies = jnp.repeat(second, 2, axis=0)
    buffer = jnp.zeros((EXPERTS * SLOTS, D), second.dtype).at[target].set(copies)
    buffer = low_back(buffer).reshape(EXPERTS, SLOTS, D)

    def one_expert(expert_item):
        rows_in, weight_in, weight_out = expert_item
        gate_up = low_back(jnp.dot(rows_in, weight_in, precision=highest))
        hidden = low(jax.nn.silu(gate_up[:, :FF]) * gate_up[:, FF:])
        return low_back(low(jnp.dot(hidden, weight_out, precision=highest)))
    expert_rows = lax.map(jax.checkpoint(one_expert), (buffer, expert_in, expert_out))
    picked = expert_rows.reshape(EXPERTS * SLOTS, D)[target].reshape(PACK, 2, D)
    return lax.optimization_barrier(jnp.sum(gates[:, :, None] * picked, axis=1))

def layer(pack_tokens, pack_routes, pack_lengths, pack_order, params):
    gain_attn, qkv_weight, out_weight, gain_moe, router_weight, expert_in, expert_out = params
    position, document = pack_layout(pack_lengths, pack_order)
    first = low(pack_tokens * norm_scale(pack_tokens) * gain_attn)
    projected = low_back(low(jnp.dot(first, qkv_weight, precision=highest)))
    head_width = HEADS * HEAD
    kv_width = KV_HEADS * HEAD
    queries = projected[:, :head_width].reshape(PACK, KV_HEADS, GROUP, HEAD)
    keys = projected[:, head_width:head_width + kv_width].reshape(PACK, KV_HEADS, HEAD)
    values = projected[:, head_width + kv_width:].reshape(PACK, KV_HEADS, HEAD)
    attended = low_back(low(attend(queries, keys, values, position, document)))
    middle = pack_tokens + low_back(jnp.dot(attended, out_weight, precision=highest))
    second = low(middle * norm_scale(middle) * gain_moe)
    return middle + mixture(second, pack_routes, router_weight, expert_in, expert_out)

def reference(tokens, cotangent, routes, lengths, block_order, gain_attn, qkv_weight, out_weight, gain_moe, router_weight, expert_in, expert_out):

    def forward(inputs, gain_a, weight_qkv, weight_attn_out, gain_m, weight_router, weight_in, weight_down):
        params = (low(gain_a), low(weight_qkv), low(weight_attn_out), low(gain_m), low(weight_router), low(weight_in), low(weight_down))
        checked = jax.checkpoint(layer)

        def step(running, pack_item):
            pack_tokens, pack_routes, pack_lengths, pack_order = pack_item
            return (running, checked(pack_tokens, pack_routes, pack_lengths, pack_order, params))
        _, outputs = lax.scan(step, jnp.zeros((), jnp.float32), (inputs, routes, lengths, block_order))
        return outputs
    primal, pullback = jax.vjp(forward, tokens.astype(jnp.float32), gain_attn, qkv_weight, out_weight, gain_moe, router_weight, expert_in, expert_out)
    grads = pullback(cotangent.astype(jnp.float32))
    return (primal.astype(jnp.bfloat16), grads[0].astype(jnp.bfloat16), grads[1], grads[2], grads[3], grads[4], grads[5], grads[6], grads[7])
```

```python
import functools

import jax
import jax.numpy as jnp
from jax import lax
from jax.experimental import pallas as pl
from jax.experimental.pallas import tpu as pltpu
from jax.sharding import Mesh
from jax.sharding import PartitionSpec as P

D = 1536
HEADS = 24
KV_HEADS = 8
HEAD = 64
GROUP = HEADS // KV_HEADS
FF = 1024
EXPERTS = 16
BLK = 128
CAP = 48
AUX = 128

epsilon = 1e-05
far_negative = -1e30
start_max = -1e29
F32 = jnp.float32
BF16 = jnp.bfloat16


def norm_scale(values):
    return lax.rsqrt(jnp.mean(values * values, axis=-1, keepdims=True) + epsilon)


def dot(a, b, dims=((1,), (0,))):
    return lax.dot_general(a, b, (dims, ((), ())), preferred_element_type=F32)


def lane_half(shape, half):
    lane = lax.broadcasted_iota(jnp.int32, shape, 1)
    return (lane >= HEAD) if half else (lane < HEAD)


def head_tiles(ref, rows, group, scale):
    tiles = []
    for i in range(GROUP):
        head = group * GROUP + i
        tile = ref[rows, (head // 2) * 128 : (head // 2 + 1) * 128].astype(F32)
        if head % 2 != group % 2:
            tile = pltpu.roll(tile, HEAD, 1)
        tile = jnp.where(lane_half(tile.shape, group % 2), tile * scale, 0.0)
        tiles.append(tile.astype(BF16))
    return jnp.concatenate(tiles, axis=0)


def block_visibility(lengths_ref, query_block, key_block, parts):
    lanes = lax.broadcasted_iota(jnp.int32, (1, BLK), 1)
    query_pos = query_block * BLK + lanes
    start = jnp.zeros((1, BLK), jnp.int32)
    bound = jnp.int32(0)
    for s in range(parts - 1):
        bound = bound + lengths_ref[0, s]
        start = jnp.where(query_pos >= bound, bound, start)
    key_pos = key_block * BLK + lax.broadcasted_iota(jnp.int32, (BLK, BLK), 0)
    one = ((key_pos >= start) & (key_pos <= query_pos)).astype(jnp.int32)
    return jnp.concatenate([one] * GROUP, axis=1) > 0


def first_row_start(lengths_ref, query_block, parts):
    start = jnp.int32(0)
    bound = jnp.int32(0)
    for s in range(parts - 1):
        bound = bound + lengths_ref[0, s]
        start = jnp.where(query_block * BLK >= bound, bound, start)
    return start


def attend_kernel(
    parts, lengths_ref, order_ref, mine_ref, q_ref, kv_ref, exact_ref, out_ref, lse_ref, q_s, m_s, acc_s
):
    width = KV_HEADS * HEAD
    for qb in range(q_ref.shape[0] // BLK):
        rows = pl.ds(qb * BLK, BLK)
        for g in range(KV_HEADS):
            q_s[g] = head_tiles(q_ref, rows, g, HEAD**-0.5)
            m_s[g] = jnp.full((8, GROUP * BLK), start_max, F32)
            acc_s[g] = jnp.zeros((BLK, GROUP * BLK), F32)
        query_block = order_ref[0, mine_ref[0] + qb]
        first = first_row_start(lengths_ref, query_block, parts)

        @pl.loop(0, order_ref.shape[1])
        def _(kb):
            key_block = order_ref[0, kb]

            @pl.when((key_block <= query_block) & (key_block * BLK + BLK > first))
            def _():
                seen = block_visibility(lengths_ref, query_block, key_block, parts)
                key_rows = pl.ds(kb * BLK, BLK)
                for g in range(KV_HEADS):
                    lanes = pl.ds((g // 2) * 128, 128)
                    keys = kv_ref[key_rows, lanes]
                    values = kv_ref[key_rows, pl.ds(width + (g // 2) * 128, 128)]
                    values = jnp.where(lane_half(values.shape, g % 2), values, jnp.ones_like(values))
                    scores = dot(keys, q_s[g], ((1,), (1,)))
                    scores = jnp.where(seen, scores, far_negative)
                    old = m_s[g, 0:1, :]
                    new = jnp.maximum(old, jnp.max(scores, axis=0, keepdims=True))
                    weights = jnp.exp(scores - new)
                    acc_s[g] = acc_s[g] * jnp.exp(old - new) + dot(
                        values, weights.astype(BF16), ((0,), (0,))
                    )
                    m_s[g, 0:1, :] = new

        tiles = []
        for g in range(KV_HEADS):
            acc = acc_s[g]
            at = (1 - g % 2) * HEAD
            total = acc[at : at + 1, :]
            lse_ref[qb, g : g + 1, :] = m_s[g, 0:1, :] + jnp.log(total)
            acc = acc / total
            for i in range(GROUP):
                head = g * GROUP + i
                tile = jnp.transpose(acc[:, i * BLK : (i + 1) * BLK])
                if head % 2 != g % 2:
                    tile = pltpu.roll(tile, HEAD, 1)
                tiles.append(tile)
                if head % 2 == 1:
                    both = jnp.where(lane_half(tile.shape, 0), tiles[head - 1], tile)
                    lanes = pl.ds((head // 2) * 128, 128)
                    exact_ref[rows, lanes] = both
                    out_ref[rows, lanes] = both.astype(BF16)


def attend(lengths, order, mine, projected, kv):
    rows = projected.shape[0]
    smem = pl.BlockSpec(memory_space=pltpu.SMEM)
    vmem = pl.BlockSpec(memory_space=pltpu.VMEM)
    wide = GROUP * BLK
    return pl.pallas_call(
        functools.partial(attend_kernel, lengths.shape[1]),
        out_shape=(
            jax.ShapeDtypeStruct((rows, HEADS * HEAD), F32),
            jax.ShapeDtypeStruct((rows, HEADS * HEAD), BF16),
            jax.ShapeDtypeStruct((rows // BLK, KV_HEADS, wide), F32),
        ),
        in_specs=[smem, smem, smem, vmem, vmem],
        out_specs=(vmem, vmem, vmem),
        scratch_shapes=[
            pltpu.VMEM((KV_HEADS, wide, 128), BF16),
            pltpu.VMEM((KV_HEADS, 8, wide), F32),
            pltpu.VMEM((KV_HEADS, BLK, wide), F32),
        ],
        compiler_params=pltpu.CompilerParams(vmem_limit_bytes=48 * 2**20),
        cost_estimate=pl.CostEstimate(flops=10**10, bytes_accessed=10**7, transcendentals=10**7),
        name="attend",
    )(lengths, order, mine, projected, kv)


def attend_back_kernel(
    parts,
    lengths_ref,
    order_ref,
    mine_ref,
    q_ref,
    kv_ref,
    grad_ref,
    lse_ref,
    delta_ref,
    dq_ref,
    dkv_ref,
    q_s,
    g_s,
    dq_s,
    dkv_s,
):
    width = KV_HEADS * HEAD

    @pl.loop(0, order_ref.shape[1])
    def _(kb):
        dkv_s[pl.ds(kb * BLK, BLK), :] = jnp.zeros((BLK, 2 * width), F32)

    for qb in range(q_ref.shape[0] // BLK):
        rows = pl.ds(qb * BLK, BLK)
        for g in range(KV_HEADS):
            q_s[g] = head_tiles(q_ref, rows, g, HEAD**-0.5)
            g_s[g] = head_tiles(grad_ref, rows, g, 1.0)
            dq_s[g] = jnp.zeros((GROUP * BLK, 128), F32)
        query_block = order_ref[0, mine_ref[0] + qb]
        first = first_row_start(lengths_ref, query_block, parts)

        @pl.loop(0, order_ref.shape[1])
        def _(kb):
            key_block = order_ref[0, kb]

            @pl.when((key_block <= query_block) & (key_block * BLK + BLK > first))
            def _():
                seen = block_visibility(lengths_ref, query_block, key_block, parts)
                key_rows = pl.ds(kb * BLK, BLK)
                for pair in range(KV_HEADS // 2):
                    key_lanes = pl.ds(pair * 128, 128)
                    value_lanes = pl.ds(width + pair * 128, 128)
                    keys = kv_ref[key_rows, key_lanes]
                    values = kv_ref[key_rows, value_lanes]
                    grad_keys = dkv_s[key_rows, key_lanes]
                    grad_values = dkv_s[key_rows, value_lanes]
                    for g in (2 * pair, 2 * pair + 1):
                        scores = dot(keys, q_s[g], ((1,), (1,)))
                        scores = jnp.where(seen, scores, far_negative)
                        probs = jnp.exp(scores - lse_ref[qb, g : g + 1, :])
                        grad_probs = dot(values, g_s[g], ((1,), (1,)))
                        grad_scores = (probs * (grad_probs - delta_ref[qb, g : g + 1, :])).astype(BF16)
                        grad_values = grad_values + dot(probs.astype(BF16), g_s[g])
                        grad_keys = grad_keys + dot(grad_scores, q_s[g])
                        dq_s[g] += dot(grad_scores, keys, ((0,), (0,)))
                    dkv_s[key_rows, key_lanes] = grad_keys
                    dkv_s[key_rows, value_lanes] = grad_values

        tiles = []
        for g in range(KV_HEADS):
            for i in range(GROUP):
                head = g * GROUP + i
                tile = dq_s[g, i * BLK : (i + 1) * BLK, :] * HEAD**-0.5
                if head % 2 != g % 2:
                    tile = pltpu.roll(tile, HEAD, 1)
                tiles.append(tile)
                if head % 2 == 1:
                    both = jnp.where(lane_half(tile.shape, 0), tiles[head - 1], tile)
                    dq_ref[rows, (head // 2) * 128 : (head // 2 + 1) * 128] = both.astype(BF16)

    @pl.loop(0, order_ref.shape[1])
    def _(kb):
        key_rows = pl.ds(kb * BLK, BLK)
        dkv_ref[key_rows, :] = dkv_s[key_rows, :].astype(BF16)


def attend_back(lengths, order, mine, projected, kv, grad_attended, lse, delta):
    rows = projected.shape[0]
    smem = pl.BlockSpec(memory_space=pltpu.SMEM)
    vmem = pl.BlockSpec(memory_space=pltpu.VMEM)
    wide = GROUP * BLK
    return pl.pallas_call(
        functools.partial(attend_back_kernel, lengths.shape[1]),
        out_shape=(
            jax.ShapeDtypeStruct((rows, HEADS * HEAD), BF16),
            jax.ShapeDtypeStruct(kv.shape, BF16),
        ),
        in_specs=[smem, smem, smem, vmem, vmem, vmem, vmem, vmem],
        out_specs=(vmem, vmem),
        scratch_shapes=[
            pltpu.VMEM((KV_HEADS, wide, 128), BF16),
            pltpu.VMEM((KV_HEADS, wide, 128), BF16),
            pltpu.VMEM((KV_HEADS, wide, 128), F32),
            pltpu.VMEM(kv.shape, F32),
        ],
        compiler_params=pltpu.CompilerParams(vmem_limit_bytes=56 * 2**20),
        cost_estimate=pl.CostEstimate(flops=3 * 10**10, bytes_accessed=10**7, transcendentals=10**7),
        name="attend_back",
    )(lengths, order, mine, projected, kv, grad_attended, lse, delta)


CTX = ("le", "rep", "core")
ALL = ("le", "rep", "core", "exp")
OWNERS = ("exp", "le")


def on_device(
    tokens,
    cotangent,
    routes,
    lengths,
    block_order,
    gain_attn,
    qkv_weight,
    out_weight,
    gain_moe,
    router_weight,
    expert_in,
    expert_out,
):
    tok_rows = tokens.shape[1]
    head_width = HEADS * HEAD
    exp_local = expert_in.shape[0]
    n_ctx = D // expert_in.shape[1]
    copies = n_ctx // exp_local
    in_rows, out_rows = expert_in.shape[1], expert_out.shape[1]

    aux = jnp.concatenate([gain_attn[:, None], gain_moe[:, None], router_weight], axis=1)
    aux = jnp.pad(aux, ((0, 0), (0, AUX - aux.shape[1]))).astype(BF16)
    w_first = lax.all_gather(
        jnp.concatenate([qkv_weight.astype(BF16), aux], axis=1), ALL, axis=0, tiled=True
    )
    w_qkv = w_first[:, : qkv_weight.shape[1]]
    aux_all = w_first[:, qkv_weight.shape[1] :]
    gain_first = aux_all[:, 0].astype(F32)
    gain_second = aux_all[:, 1].astype(F32)
    w_router = aux_all[:, 2 : 2 + EXPERTS]
    w_attn_out = lax.all_gather(out_weight.astype(BF16), ALL, axis=0, tiled=True)

    def to_owner(weight):
        rows, cols = weight.shape[1:]
        halves = weight.astype(BF16).reshape(exp_local, rows, 2, cols // 2).transpose(0, 2, 1, 3)
        halves = jnp.broadcast_to(
            halves[:, None], (exp_local, copies // 2, 2, rows, cols // 2)
        ).reshape(n_ctx, rows, cols // 2)
        mine = lax.all_to_all(halves, CTX, split_axis=0, concat_axis=0, tiled=True)
        return lax.all_gather(mine.reshape(n_ctx * rows, cols // 2), "core", axis=0)

    w_in = to_owner(expert_in)
    w_down = to_owner(expert_out)

    route_hot = (
        routes[0][:, :, None] == jnp.arange(EXPERTS, dtype=jnp.int32)[None, None, :]
    ).astype(F32)
    flat_hot = route_hot.reshape(tok_rows * 2, EXPERTS).astype(BF16)
    order = jnp.arange(tok_rows * 2, dtype=jnp.int32)
    earlier = (order[:, None] > order[None, :]).astype(BF16)
    ranks = dot(earlier, flat_hot)
    slot_index = jnp.sum(ranks * flat_hot.astype(F32), axis=1).astype(jnp.int32)
    target = (routes[0].reshape(tok_rows * 2) * CAP + slot_index).reshape(tok_rows, 2)
    slots = jnp.arange(EXPERTS * CAP, dtype=jnp.int32)
    picks = [(target[:, k : k + 1] == slots[None, :]) for k in range(2)]
    sends = [(target[:, k][None, :] == slots[:, None]) for k in range(2)]
    send_hot = (sends[0] | sends[1]).astype(BF16)

    def to_experts(rows):
        return lax.all_to_all(
            rows.reshape((EXPERTS, CAP) + rows.shape[1:]),
            OWNERS,
            split_axis=0,
            concat_axis=0,
            tiled=True,
        ).reshape(rows.shape)

    grad_y_rows = to_experts(dot(send_hot, cotangent[0]).astype(BF16)).astype(F32)

    inputs = tokens[0].astype(F32)
    scale_first = norm_scale(inputs)
    norm_first = inputs * scale_first
    first = (norm_first * gain_first).astype(BF16)
    projected = dot(first, w_qkv).astype(BF16)
    kv = lax.all_gather(projected[:, head_width:], CTX, axis=0, tiled=True)
    mine = (lax.axis_index(CTX) * (tok_rows // BLK)).astype(jnp.int32).reshape(1)
    exact, attended, lse = attend(lengths, block_order, mine, projected, kv)
    middle = inputs + dot(attended, w_attn_out)
    scale_second = norm_scale(middle)
    norm_second = middle * scale_second
    second = (norm_second * gain_second).astype(BF16)
    logits = dot(second, w_router)
    chosen = jnp.sum(route_hot * logits[:, None, :], axis=-1)
    gates = jax.nn.softmax(chosen, axis=-1)

    gate_rows = jnp.sum(
        jnp.where(sends[0], gates[:, 0][None, :], 0.0) + jnp.where(sends[1], gates[:, 1][None, :], 0.0),
        axis=1,
        keepdims=True,
    )
    high = lax.reduce_precision(gate_rows, 8, 7)
    rest = gate_rows - high
    mid = lax.reduce_precision(rest, 8, 7)
    low = rest - mid
    gate_parts = jnp.pad(
        jnp.concatenate([high, mid, low], axis=1).astype(BF16), ((0, 0), (0, AUX - 3))
    )
    payload = to_experts(
        jnp.concatenate([dot(send_hot, second).astype(BF16), gate_parts], axis=1)
    )
    received = payload[:, :D]
    gate_got = jnp.sum(payload[:, D : D + 3].astype(F32), axis=1, keepdims=True)

    gate_part = dot(received, w_in[0])
    up_part = dot(received, w_in[1])
    sigmoid_gate = jax.nn.sigmoid(gate_part)
    silu_gate = gate_part * sigmoid_gate
    hidden = (silu_gate * up_part).astype(BF16)
    expert_rows = jnp.concatenate([dot(hidden, w_down[0]), dot(hidden, w_down[1])], axis=1)
    returned = to_experts(expert_rows.astype(BF16))

    grad_rows = (gate_got * grad_y_rows).astype(BF16)
    half_d = D // 2
    grad_hidden = dot(grad_rows[:, :half_d], w_down[0], ((1,), (1,))) + dot(
        grad_rows[:, half_d:], w_down[1], ((1,), (1,))
    )
    grad_gate = (
        grad_hidden * up_part * sigmoid_gate * (1.0 + gate_part * (1.0 - sigmoid_gate))
    ).astype(BF16)
    grad_up = (grad_hidden * silu_gate).astype(BF16)
    grad_back = dot(grad_gate, w_in[0], ((1,), (1,))) + dot(grad_up, w_in[1], ((1,), (1,)))
    grad_returned = to_experts(grad_back.astype(BF16))

    grad_in = jnp.stack(
        [dot(received, grad_gate, ((0,), (0,))), dot(received, grad_up, ((0,), (0,)))]
    ).astype(BF16)
    grad_down = jnp.stack(
        [
            dot(hidden, grad_rows[:, :half_d], ((0,), (0,))),
            dot(hidden, grad_rows[:, half_d:], ((0,), (0,))),
        ]
    ).astype(BF16)

    def to_rows(grad, rows):
        cols = grad.shape[2]
        half = lax.psum_scatter(grad, "core", scatter_dimension=0, tiled=True)
        got = lax.all_to_all(
            half.reshape(n_ctx, rows, cols), CTX, split_axis=0, concat_axis=0, tiled=True
        ).astype(F32)
        got = got.reshape(exp_local, copies // 2, 2, rows, cols).sum(axis=1)
        return got.transpose(0, 2, 1, 3).reshape(exp_local, rows, 2 * cols)

    sum_in = to_rows(grad_in, in_rows)
    sum_down = to_rows(grad_down, out_rows)

    grad_y = cotangent[0].astype(F32)
    pick_hot = [p.astype(BF16) for p in picks]
    picked = [dot(p, returned) for p in pick_hot]
    block_out = (middle + gates[:, 0:1] * picked[0] + gates[:, 1:2] * picked[1]).astype(BF16)
    grad_gates = jnp.stack([jnp.sum(grad_y * p, axis=-1) for p in picked], axis=1)
    grad_chosen = gates * (grad_gates - jnp.sum(gates * grad_gates, axis=-1, keepdims=True))
    grad_logits = jnp.sum(grad_chosen[:, :, None] * route_hot, axis=1).astype(BF16)
    grad_router = dot(second, grad_logits, ((0,), (0,)))
    grad_second = dot(pick_hot[0] + pick_hot[1], grad_returned) + dot(
        grad_logits, w_router, ((1,), (1,))
    )
    grad_gain_second = jnp.sum(grad_second * norm_second, axis=0)
    grad_norm_second = grad_second * gain_second
    grad_middle = grad_y + scale_second * (
        grad_norm_second
        - norm_second * jnp.mean(grad_norm_second * norm_second, axis=-1, keepdims=True)
    )
    grad_branch = grad_middle.astype(BF16)
    grad_attn_out = dot(attended, grad_branch, ((0,), (0,)))
    late = jnp.concatenate([grad_gain_second[:, None], grad_router], axis=1)
    late = jnp.pad(late, ((0, 0), (0, AUX - late.shape[1])))
    sum_second = lax.psum_scatter(
        jnp.concatenate([grad_attn_out, late], axis=1).astype(BF16),
        ALL,
        scatter_dimension=0,
        tiled=True,
    ).astype(F32)

    grad_attended = dot(grad_branch, w_attn_out, ((1,), (1,))).astype(BF16)
    delta = jnp.sum(
        (grad_attended.astype(F32) * exact).reshape(tok_rows, HEADS, HEAD), axis=-1
    )
    delta = (
        delta.reshape(tok_rows // BLK, BLK, KV_HEADS, GROUP)
        .transpose(0, 2, 3, 1)
        .reshape(lse.shape)
    )
    grad_queries, grad_kv = attend_back(
        lengths, block_order, mine, projected, kv, grad_attended, lse, delta
    )
    grad_kv = lax.psum_scatter(grad_kv, CTX, scatter_dimension=0, tiled=True)
    grad_projected = jnp.concatenate([grad_queries, grad_kv], axis=1)
    grad_qkv = dot(first, grad_projected, ((0,), (0,)))
    grad_first = dot(grad_projected, w_qkv, ((1,), (1,)))
    grad_gain_first = jnp.sum(grad_first * norm_first, axis=0)
    grad_norm_first = grad_first * gain_first
    grad_inputs = grad_middle + scale_first * (
        grad_norm_first
        - norm_first * jnp.mean(grad_norm_first * norm_first, axis=-1, keepdims=True)
    )
    last = jnp.pad(grad_gain_first[:, None], ((0, 0), (0, AUX - 1)))
    sum_first = lax.psum_scatter(
        jnp.concatenate([grad_qkv, last], axis=1).astype(BF16),
        ALL,
        scatter_dimension=0,
        tiled=True,
    ).astype(F32)
    cols = qkv_weight.shape[1]
    return (
        block_out[None],
        grad_inputs.astype(BF16)[None],
        sum_first[:, cols],
        sum_first[:, :cols],
        sum_second[:, :D],
        sum_second[:, D],
        sum_second[:, D + 1 : D + 1 + EXPERTS],
        sum_in,
        sum_down,
    )


def solution(mesh):
    n_ctx, n_exp = mesh.shape["ctx"], mesh.shape["exp"]
    exp_local = EXPERTS // n_exp
    copies = n_ctx // exp_local
    inner = Mesh(mesh.devices.reshape(exp_local, copies // 2, 2, n_exp), ALL)
    by_token = P("exp", CTX, None)
    by_row = P(ALL, None)
    by_expert = P("exp", CTX, None)
    return jax.shard_map(
        on_device,
        mesh=inner,
        in_specs=(
            by_token,
            by_token,
            by_token,
            P("exp", None),
            P("exp", None),
            P(ALL),
            by_row,
            by_row,
            P(ALL),
            by_row,
            by_expert,
            by_expert,
        ),
        out_specs=(
            by_token,
            by_token,
            P(ALL),
            by_row,
            by_row,
            P(ALL),
            by_row,
            by_expert,
            by_expert,
        ),
        check_vma=False,
    )
```

```python
import functools

import jax
import jax.numpy as jnp
from jax import lax
from jax.experimental import pallas as pl
from jax.experimental.pallas import tpu as pltpu
from jax.sharding import Mesh
from jax.sharding import PartitionSpec as P

D = 1536
HEADS = 24
KV_HEADS = 8
HEAD = 64
GROUP = HEADS // KV_HEADS
FF = 1024
EXPERTS = 16
BLK = 128
CAP = 48
AUX = 128

epsilon = 1e-05
far_negative = -1e30
start_max = -1e29
F32 = jnp.float32
BF16 = jnp.bfloat16


def norm_scale(values):
    return lax.rsqrt(jnp.mean(values * values, axis=-1, keepdims=True) + epsilon)


def dot(a, b, dims=((1,), (0,))):
    return lax.dot_general(a, b, (dims, ((), ())), preferred_element_type=F32)


def lane_half(shape, half):
    lane = lax.broadcasted_iota(jnp.int32, shape, 1)
    return (lane >= HEAD) if half else (lane < HEAD)


def head_tiles(ref, rows, group, scale):
    tiles = []
    for i in range(GROUP):
        head = group * GROUP + i
        tile = ref[rows, (head // 2) * 128 : (head // 2 + 1) * 128].astype(F32)
        if head % 2 != group % 2:
            tile = pltpu.roll(tile, HEAD, 1)
        tile = jnp.where(lane_half(tile.shape, group % 2), tile * scale, 0.0)
        tiles.append(tile.astype(BF16))
    return jnp.concatenate(tiles, axis=0)


def block_visibility(lengths_ref, query_block, key_block, parts):
    lanes = lax.broadcasted_iota(jnp.int32, (1, BLK), 1)
    query_pos = query_block * BLK + lanes
    start = jnp.zeros((1, BLK), jnp.int32)
    bound = jnp.int32(0)
    for s in range(parts - 1):
        bound = bound + lengths_ref[0, s]
        start = jnp.where(query_pos >= bound, bound, start)
    key_pos = key_block * BLK + lax.broadcasted_iota(jnp.int32, (BLK, BLK), 0)
    one = ((key_pos >= start) & (key_pos <= query_pos)).astype(jnp.int32)
    return jnp.concatenate([one] * GROUP, axis=1) > 0


def first_row_start(lengths_ref, query_block, parts):
    start = jnp.int32(0)
    bound = jnp.int32(0)
    for s in range(parts - 1):
        bound = bound + lengths_ref[0, s]
        start = jnp.where(query_block * BLK >= bound, bound, start)
    return start


def attend_kernel(
    parts, lengths_ref, order_ref, mine_ref, q_ref, kv_ref, exact_ref, out_ref, lse_ref, q_s, m_s, acc_s
):
    width = KV_HEADS * HEAD
    for qb in range(q_ref.shape[0] // BLK):
        rows = pl.ds(qb * BLK, BLK)
        for g in range(KV_HEADS):
            q_s[g] = head_tiles(q_ref, rows, g, HEAD**-0.5)
            m_s[g] = jnp.full((8, GROUP * BLK), start_max, F32)
            acc_s[g] = jnp.zeros((BLK, GROUP * BLK), F32)
        query_block = order_ref[0, mine_ref[0] + qb]
        first = first_row_start(lengths_ref, query_block, parts)

        @pl.loop(0, order_ref.shape[1])
        def _(kb):
            key_block = order_ref[0, kb]

            @pl.when((key_block <= query_block) & (key_block * BLK + BLK > first))
            def _():
                seen = block_visibility(lengths_ref, query_block, key_block, parts)
                key_rows = pl.ds(kb * BLK, BLK)
                for g in range(KV_HEADS):
                    lanes = pl.ds((g // 2) * 128, 128)
                    keys = kv_ref[key_rows, lanes]
                    values = kv_ref[key_rows, pl.ds(width + (g // 2) * 128, 128)]
                    values = jnp.where(lane_half(values.shape, g % 2), values, jnp.ones_like(values))
                    scores = dot(keys, q_s[g], ((1,), (1,)))
                    scores = jnp.where(seen, scores, far_negative)
                    old = m_s[g, 0:1, :]
                    new = jnp.maximum(old, jnp.max(scores, axis=0, keepdims=True))
                    weights = jnp.exp(scores - new)
                    acc_s[g] = acc_s[g] * jnp.exp(old - new) + dot(
                        values, weights.astype(BF16), ((0,), (0,))
                    )
                    m_s[g, 0:1, :] = new

        tiles = []
        for g in range(KV_HEADS):
            acc = acc_s[g]
            at = (1 - g % 2) * HEAD
            total = acc[at : at + 1, :]
            lse_ref[qb, g : g + 1, :] = m_s[g, 0:1, :] + jnp.log(total)
            acc = acc / total
            for i in range(GROUP):
                head = g * GROUP + i
                tile = jnp.transpose(acc[:, i * BLK : (i + 1) * BLK])
                if head % 2 != g % 2:
                    tile = pltpu.roll(tile, HEAD, 1)
                tiles.append(tile)
                if head % 2 == 1:
                    both = jnp.where(lane_half(tile.shape, 0), tiles[head - 1], tile)
                    lanes = pl.ds((head // 2) * 128, 128)
                    exact_ref[rows, lanes] = both
                    out_ref[rows, lanes] = both.astype(BF16)


def attend(lengths, order, mine, projected, kv):
    rows = projected.shape[0]
    smem = pl.BlockSpec(memory_space=pltpu.SMEM)
    vmem = pl.BlockSpec(memory_space=pltpu.VMEM)
    wide = GROUP * BLK
    return pl.pallas_call(
        functools.partial(attend_kernel, lengths.shape[1]),
        out_shape=(
            jax.ShapeDtypeStruct((rows, HEADS * HEAD), F32),
            jax.ShapeDtypeStruct((rows, HEADS * HEAD), BF16),
            jax.ShapeDtypeStruct((rows // BLK, KV_HEADS, wide), F32),
        ),
        in_specs=[smem, smem, smem, vmem, vmem],
        out_specs=(vmem, vmem, vmem),
        scratch_shapes=[
            pltpu.VMEM((KV_HEADS, wide, 128), BF16),
            pltpu.VMEM((KV_HEADS, 8, wide), F32),
            pltpu.VMEM((KV_HEADS, BLK, wide), F32),
        ],
        compiler_params=pltpu.CompilerParams(vmem_limit_bytes=48 * 2**20),
        cost_estimate=pl.CostEstimate(flops=10**10, bytes_accessed=10**7, transcendentals=10**7),
        name="attend",
    )(lengths, order, mine, projected, kv)


def attend_back_kernel(
    parts,
    lengths_ref,
    order_ref,
    mine_ref,
    q_ref,
    kv_ref,
    grad_ref,
    lse_ref,
    delta_ref,
    dq_ref,
    dkv_ref,
    q_s,
    g_s,
    dq_s,
    dkv_s,
):
    width = KV_HEADS * HEAD

    @pl.loop(0, order_ref.shape[1])
    def _(kb):
        dkv_s[pl.ds(kb * BLK, BLK), :] = jnp.zeros((BLK, 2 * width), F32)

    for qb in range(q_ref.shape[0] // BLK):
        rows = pl.ds(qb * BLK, BLK)
        for g in range(KV_HEADS):
            q_s[g] = head_tiles(q_ref, rows, g, HEAD**-0.5)
            g_s[g] = head_tiles(grad_ref, rows, g, 1.0)
            dq_s[g] = jnp.zeros((GROUP * BLK, 128), F32)
        query_block = order_ref[0, mine_ref[0] + qb]
        first = first_row_start(lengths_ref, query_block, parts)

        @pl.loop(0, order_ref.shape[1])
        def _(kb):
            key_block = order_ref[0, kb]

            @pl.when((key_block <= query_block) & (key_block * BLK + BLK > first))
            def _():
                seen = block_visibility(lengths_ref, query_block, key_block, parts)
                key_rows = pl.ds(kb * BLK, BLK)
                for pair in range(KV_HEADS // 2):
                    key_lanes = pl.ds(pair * 128, 128)
                    value_lanes = pl.ds(width + pair * 128, 128)
                    keys = kv_ref[key_rows, key_lanes]
                    values = kv_ref[key_rows, value_lanes]
                    grad_keys = dkv_s[key_rows, key_lanes]
                    grad_values = dkv_s[key_rows, value_lanes]
                    for g in (2 * pair, 2 * pair + 1):
                        scores = dot(keys, q_s[g], ((1,), (1,)))
                        scores = jnp.where(seen, scores, far_negative)
                        probs = jnp.exp(scores - lse_ref[qb, g : g + 1, :])
                        grad_probs = dot(values, g_s[g], ((1,), (1,)))
                        grad_scores = (probs * (grad_probs - delta_ref[qb, g : g + 1, :])).astype(BF16)
                        grad_values = grad_values + dot(probs.astype(BF16), g_s[g])
                        grad_keys = grad_keys + dot(grad_scores, q_s[g])
                        dq_s[g] += dot(grad_scores, keys, ((0,), (0,)))
                    dkv_s[key_rows, key_lanes] = grad_keys
                    dkv_s[key_rows, value_lanes] = grad_values

        tiles = []
        for g in range(KV_HEADS):
            for i in range(GROUP):
                head = g * GROUP + i
                tile = dq_s[g, i * BLK : (i + 1) * BLK, :] * HEAD**-0.5
                if head % 2 != g % 2:
                    tile = pltpu.roll(tile, HEAD, 1)
                tiles.append(tile)
                if head % 2 == 1:
                    both = jnp.where(lane_half(tile.shape, 0), tiles[head - 1], tile)
                    dq_ref[rows, (head // 2) * 128 : (head // 2 + 1) * 128] = both.astype(BF16)

    @pl.loop(0, order_ref.shape[1])
    def _(kb):
        key_rows = pl.ds(kb * BLK, BLK)
        dkv_ref[key_rows, :] = dkv_s[key_rows, :].astype(BF16)


def attend_back(lengths, order, mine, projected, kv, grad_attended, lse, delta):
    rows = projected.shape[0]
    smem = pl.BlockSpec(memory_space=pltpu.SMEM)
    vmem = pl.BlockSpec(memory_space=pltpu.VMEM)
    wide = GROUP * BLK
    return pl.pallas_call(
        functools.partial(attend_back_kernel, lengths.shape[1]),
        out_shape=(
            jax.ShapeDtypeStruct((rows, HEADS * HEAD), BF16),
            jax.ShapeDtypeStruct(kv.shape, BF16),
        ),
        in_specs=[smem, smem, smem, vmem, vmem, vmem, vmem, vmem],
        out_specs=(vmem, vmem),
        scratch_shapes=[
            pltpu.VMEM((KV_HEADS, wide, 128), BF16),
            pltpu.VMEM((KV_HEADS, wide, 128), BF16),
            pltpu.VMEM((KV_HEADS, wide, 128), F32),
            pltpu.VMEM(kv.shape, F32),
        ],
        compiler_params=pltpu.CompilerParams(vmem_limit_bytes=56 * 2**20),
        cost_estimate=pl.CostEstimate(flops=3 * 10**10, bytes_accessed=10**7, transcendentals=10**7),
        name="attend_back",
    )(lengths, order, mine, projected, kv, grad_attended, lse, delta)


MESH = pl.DeviceIdType.MESH


def place(z, core, exp):
    return {"le": z, "rep": 0, "core": core, "exp": exp}


def x_of(exp):
    return (exp // 2) * 2 + 1 - exp % 2


def y_of(exp):
    return (1 - exp // 2) * 2 + exp % 2


def remote(src, dst, send_sem, recv_sem, device):
    return pltpu.make_async_remote_copy(
        src_ref=src,
        dst_ref=dst,
        send_sem=send_sem,
        recv_sem=recv_sem,
        device_id=device,
        device_id_type=MESH,
    )


def meet(devices):
    barrier = pltpu.get_barrier_semaphore()
    for device in devices:
        pl.semaphore_signal(barrier, inc=1, device_id=device, device_id_type=MESH)
    pl.semaphore_wait(barrier, len(devices))


def spread_kernel(
    layers,
    shard_ref,
    in_ref,
    down_ref,
    all_ref,
    w_in_ref,
    w_down_ref,
    unit_sem,
    line_sem,
    x_sem,
    y_sem,
    far_sem,
    core_sem,
    half_sem,
    half_send,
    over_sem,
    over_send,
    own_sem,
):
    z, core, exp = lax.axis_index("le"), lax.axis_index("core"), lax.axis_index("exp")
    other = 1 - core
    column = [((z + s) % layers, p) for s in range(layers) for p in range(2)]
    x, y = x_of(exp), y_of(exp)
    meet(
        [place(zz, (core + p) % 2, exp) for zz, p in column if not (zz is column[0][0] and p == 0)]
        + [place(z, core, x), place(z, core, y)]
    )
    rows = shard_ref.shape[0]

    def number(zz, cc, ee):
        return (zz * 2 + cc) * 4 + ee

    def unit(zz, cc, ee):
        return all_ref.at[pl.ds(number(zz, cc, ee) * rows, rows), :]

    def send(src, who, sem, device):
        return remote(src, unit(*who), sem, unit_sem.at[number(*who)], device)

    def arrive(who):
        send(unit(*who), who, line_sem.at[0], place(z, other, exp)).wait_recv()

    started = []

    def go(copy, condition=None):
        if condition is None:
            copy.start()
        else:
            pl.when(condition)(copy.start)
        started.append((copy, condition))

    me = (z, core, exp)
    keep = pltpu.make_async_copy(shard_ref, unit(*me), own_sem.at[0])
    keep.start()
    go(send(shard_ref, me, line_sem.at[layers], place(z + 1, core, exp)), z < layers - 1)
    go(send(shard_ref, me, line_sem.at[layers + 1], place(z - 1, core, exp)), z > 0)

    ctx = z * 2 + core
    arrays = ((in_ref, w_in_ref), (down_ref, w_down_ref))

    def half(a, source, p):
        src, dst = arrays[a]
        n, cols = src.shape[1], src.shape[2] // 2
        return dst.at[pl.ds(source * n, n), pl.ds(pl.multiple_of(p * cols, 128), cols)]

    def mine(a, zz, p):
        src = arrays[a][0]
        cols = src.shape[2] // 2
        return src.at[zz, :, pl.ds(pl.multiple_of(p * cols, 128), cols)]

    for a in range(2):
        pltpu.make_async_copy(mine(a, z, core), half(a, ctx, core), own_sem.at[1 + a]).start()

    def own_sends(k, src):
        go(send(src, me, x_sem.at[k], place(z, core, x)))
        go(send(src, me, y_sem.at[k], place(z, core, y)))
        go(send(src, me, core_sem.at[k], place(z, other, exp)))

    own_sends(layers, shard_ref)
    def layer(k):
        return jnp.where(z < layers // 2, k, layers - 1 - k)

    for k in range(layers):
        zz = layer(k)
        who = (zz, core, exp)

        @pl.when(zz != z)
        def _(zz=zz, who=who, k=k):
            arrive(who)

        go(send(unit(*who), who, line_sem.at[k], place(z + 1, core, exp)), (zz < z) & (z < layers - 1))
        go(send(unit(*who), who, line_sem.at[k], place(z - 1, core, exp)), (zz > z) & (z > 0))
        go(send(unit(*who), who, x_sem.at[k], place(z, core, x)), zz != z)
        go(send(unit(*who), who, y_sem.at[k], place(z, core, y)), zz != z)
        go(send(unit(*who), who, core_sem.at[k], place(z, other, exp)), zz != z)

    for s in range(layers):
        zz = (z + s) % layers
        for p in range(2):
            if s == 0 and p == 0:
                continue
            pp = (core + p) % 2
            for a in range(2):
                go(
                    remote(
                        mine(a, zz, pp),
                        half(a, ctx, pp),
                        half_send.at[a, s * 2 + p],
                        half_sem.at[a, ctx],
                        place(zz, pp, exp),
                    )
                )
    for a in range(2):
        go(
            remote(
                mine(a, z, core),
                half(a, ctx, core),
                over_send.at[a, 2 * layers],
                over_sem.at[a, ctx],
                place(z, other, exp),
            )
        )

    for k in range(layers):
        zz = layer(k)
        from_x, from_y = (zz, core, x), (zz, core, y)
        arrive(from_x)
        go(send(unit(*from_x), from_x, core_sem.at[layers + 1 + k], place(z, other, exp)))
        if k % 2 == 0:
            go(send(unit(*from_x), from_x, far_sem.at[k], place(z, core, y)))
        arrive(from_y)
        go(send(unit(*from_y), from_y, core_sem.at[2 * layers + 1 + k], place(z, other, exp)))
        if k % 2 == 1:
            go(send(unit(*from_y), from_y, far_sem.at[k], place(z, core, x)))
    for k in range(layers):
        far = (layer(k), core, y_of(x))
        arrive(far)
        go(send(unit(*far), far, core_sem.at[3 * layers + 1 + k], place(z, other, exp)))

    for s in range(layers):
        for p in range(2):
            if s == 0 and p == 0:
                continue
            source = ((z + s) % layers) * 2 + (core + p) % 2
            for a in range(2):
                copy = remote(
                    half(a, source, core),
                    half(a, source, core),
                    over_send.at[a, s * 2 + p],
                    over_sem.at[a, source],
                    place(z, other, exp),
                )
                remote(
                    half(a, source, core),
                    half(a, source, core),
                    half_send.at[a, 0],
                    half_sem.at[a, source],
                    place(z, other, exp),
                ).wait_recv()
                go(copy)

    for ee in range(4):
        for zz in range(layers):
            arrive((zz, other, ee))
    for source in range(2 * layers):
        for a in range(2):
            remote(
                half(a, source, other),
                half(a, source, other),
                half_send.at[a, 0],
                over_sem.at[a, source],
                place(z, other, exp),
            ).wait_recv()
    keep.wait()
    for a in range(2):
        pltpu.make_async_copy(mine(a, z, core), half(a, ctx, core), own_sem.at[1 + a]).wait()
    for copy, condition in started:
        if condition is None:
            copy.wait_send()
        else:
            pl.when(condition)(copy.wait_send)


def spread(shard, expert_in, expert_out):
    layers = expert_in.shape[0]
    rows_in, rows_out = expert_in.shape[1], expert_out.shape[1]
    any_space = pl.BlockSpec(memory_space=pl.ANY)
    dma = pltpu.SemaphoreType.DMA
    return pl.pallas_call(
        functools.partial(spread_kernel, layers),
        out_shape=(
            jax.ShapeDtypeStruct((shard.shape[0] * 8 * layers, shard.shape[1]), BF16),
            jax.ShapeDtypeStruct((rows_in * 2 * layers, expert_in.shape[2]), BF16),
            jax.ShapeDtypeStruct((rows_out * 2 * layers, expert_out.shape[2]), BF16),
        ),
        in_specs=[any_space] * 3,
        out_specs=(any_space,) * 3,
        scratch_shapes=[
            dma((8 * layers,)),
            dma((layers + 2,)),
            dma((layers + 1,)),
            dma((layers + 1,)),
            dma((layers,)),
            dma((4 * layers + 1,)),
            dma((2, 2 * layers)),
            dma((2, 2 * layers)),
            dma((2, 2 * layers)),
            dma((2, 2 * layers + 1)),
            dma((3,)),
        ],
        compiler_params=pltpu.CompilerParams(collective_id=0, has_side_effects=True),
        name="spread",
    )(shard, expert_in, expert_out)


def collect_kernel(
    layers,
    part_ref,
    in_ref,
    down_ref,
    out_ref,
    got_in_ref,
    got_down_ref,
    own,
    pair,
    near,
    line,
    half_sem,
    half_send,
    load_sem,
    pair_sem,
    pair_send,
    near_sem,
    near_send,
    line_sem,
    line_send,
):
    z, core, exp = lax.axis_index("le"), lax.axis_index("core"), lax.axis_index("exp")
    other = 1 - core
    x, y = x_of(exp), y_of(exp)
    layer_mates = (x, y, y_of(x))
    meet(
        [
            place((z + s) % layers, (core + p) % 2, exp)
            for s in range(layers)
            for p in range(2)
            if s + p > 0
        ]
        + [place(z, core, mate) for mate in layer_mates]
    )
    rows = out_ref.shape[0]
    ctx = z * 2 + core
    started = []

    def go(copy):
        copy.start()
        started.append(copy)

    order = [(z + s) % layers for s in (2, 1, 3, 0)] if layers == 4 else [(z + s) % layers for s in range(layers)]
    loads = []
    for k, zz in enumerate(order):
        go(
            remote(
                part_ref.at[pl.ds((zz * 2 + other) * 4 * rows, 4 * rows), :],
                pair.at[zz],
                pair_send.at[k],
                pair_sem.at[zz],
                place(z, other, exp),
            )
        )
        load = pltpu.make_async_copy(
            part_ref.at[pl.ds((zz * 2 + core) * 4 * rows, 4 * rows), :], own.at[zz], load_sem.at[k]
        )
        load.start()
        loads.append(load)

    arrays = ((in_ref, got_in_ref), (down_ref, got_down_ref))

    def mine(a, owner):
        n = arrays[a][1].shape[1]
        return arrays[a][0].at[pl.ds(owner * n, n), :]

    def half(a, expert, p):
        cols = arrays[a][0].shape[1]
        return arrays[a][1].at[expert, :, pl.ds(pl.multiple_of(p * cols, 128), cols)]

    keeps = []
    for a in range(2):
        keep = pltpu.make_async_copy(mine(a, ctx), half(a, z, core), load_sem.at[layers + a])
        keep.start()
        keeps.append(keep)
    for s in range(layers):
        for p in range(2):
            if s + p == 0:
                continue
            zz, pp = (z + s) % layers, (core + p) % 2
            for a in range(2):
                go(
                    remote(
                        mine(a, zz * 2 + pp),
                        half(a, z, core),
                        half_send.at[a, s * 2 + p],
                        half_sem.at[a, ctx],
                        place(zz, pp, exp),
                    )
                )

    slab = 16
    for k, zz in enumerate(order):
        loads[k].wait()
        remote(pair.at[zz], pair.at[zz], pair_send.at[k], pair_sem.at[zz], place(z, other, exp)).wait_recv()

        @pl.loop(0, 4 * rows // slab)
        def _(i, zz=zz):
            at = pl.ds(pl.multiple_of(i * slab, slab), slab)
            own[zz, at, :] = (own[zz, at, :].astype(F32) + pair[zz, at, :].astype(F32)).astype(BF16)

        for m, mate in enumerate(layer_mates):
            go(
                remote(
                    own.at[zz, pl.ds(pl.multiple_of(mate * rows, slab), rows), :],
                    near.at[m, zz],
                    near_send.at[m, k],
                    near_sem.at[m, zz],
                    place(z, core, mate),
                )
            )

    for k, zz in enumerate(order):
        for m, mate in enumerate(layer_mates):
            remote(
                near.at[m, zz], near.at[m, zz], near_send.at[m, k], near_sem.at[m, zz], place(z, core, mate)
            ).wait_recv()

        @pl.loop(0, rows // slab)
        def _(i, zz=zz):
            at = pl.ds(pl.multiple_of(exp * rows + i * slab, slab), slab)
            here = pl.ds(pl.multiple_of(i * slab, slab), slab)
            total = own[zz, at, :].astype(F32)
            for m in range(3):
                total = total + near[m, zz, here, :].astype(F32)
            own[zz, at, :] = total.astype(BF16)

        if k < layers - 1:
            go(
                remote(
                    own.at[zz, pl.ds(pl.multiple_of(exp * rows, slab), rows), :],
                    line.at[z],
                    line_send.at[k],
                    line_sem.at[z],
                    place(zz, core, exp),
                )
            )

    for zz in order[:-1]:
        remote(line.at[zz], line.at[zz], line_send.at[0], line_sem.at[zz], place(zz, core, exp)).wait_recv()

    @pl.loop(0, rows // slab)
    def _(i):
        at = pl.ds(pl.multiple_of(exp * rows + i * slab, slab), slab)
        here = pl.ds(pl.multiple_of(i * slab, slab), slab)
        total = own[z, at, :].astype(F32)
        for zz in order[:-1]:
            total = total + line[zz, here, :].astype(F32)
        out_ref[here, :] = total

    for source in range(2 * layers):
        for a in range(2):

            @pl.when(source != ctx)
            def _(source=source, a=a):
                remote(
                    half(a, source // 2, source % 2),
                    half(a, source // 2, source % 2),
                    half_send.at[a, 0],
                    half_sem.at[a, source],
                    place(z, other, exp),
                ).wait_recv()

    for keep in keeps:
        keep.wait()
    for copy in started:
        copy.wait_send()


def collect(part, grad_in, grad_down, layers):
    rows, cols = part.shape[0] // (8 * layers), part.shape[1]
    n_in, n_down = grad_in.shape[0] // (2 * layers), grad_down.shape[0] // (2 * layers)
    any_space = pl.BlockSpec(memory_space=pl.ANY)
    dma = pltpu.SemaphoreType.DMA
    return pl.pallas_call(
        functools.partial(collect_kernel, layers),
        out_shape=(
            jax.ShapeDtypeStruct((rows, cols), F32),
            jax.ShapeDtypeStruct((layers, n_in, 2 * grad_in.shape[1]), BF16),
            jax.ShapeDtypeStruct((layers, n_down, 2 * grad_down.shape[1]), BF16),
        ),
        in_specs=[any_space] * 3,
        out_specs=(pl.BlockSpec(memory_space=pltpu.VMEM), any_space, any_space),
        scratch_shapes=[
            pltpu.VMEM((layers, 4 * rows, cols), BF16),
            pltpu.VMEM((layers, 4 * rows, cols), BF16),
            pltpu.VMEM((3, layers, rows, cols), BF16),
            pltpu.VMEM((layers, rows, cols), BF16),
            dma((2, 2 * layers)),
            dma((2, 2 * layers)),
            dma((layers + 2,)),
            dma((layers,)),
            dma((layers,)),
            dma((3, layers)),
            dma((3, layers)),
            dma((layers,)),
            dma((layers,)),
        ],
        compiler_params=pltpu.CompilerParams(
            collective_id=1, has_side_effects=True, vmem_limit_bytes=40 * 2**20
        ),
        name="collect",
    )(part, grad_in, grad_down)


CTX = ("le", "rep", "core")
ALL = ("le", "rep", "core", "exp")
OWNERS = ("exp", "le")


def on_device(
    tokens,
    cotangent,
    routes,
    lengths,
    block_order,
    gain_attn,
    qkv_weight,
    out_weight,
    gain_moe,
    router_weight,
    expert_in,
    expert_out,
):
    tok_rows = tokens.shape[1]
    head_width = HEADS * HEAD
    exp_local = expert_in.shape[0]
    n_ctx = D // expert_in.shape[1]
    copies = n_ctx // exp_local
    n_exp = EXPERTS // exp_local
    in_rows, out_rows = expert_in.shape[1], expert_out.shape[1]

    cols = qkv_weight.shape[1]
    aux = jnp.concatenate([gain_attn[:, None], gain_moe[:, None], router_weight], axis=1)
    aux = jnp.pad(aux, ((0, 0), (0, AUX - aux.shape[1])))
    shard = jnp.concatenate([qkv_weight, aux, out_weight], axis=1).astype(BF16)
    if (copies, exp_local, n_exp) == (2, 4, 4):
        w_all, w_in, w_down = spread(shard, expert_in.astype(BF16), expert_out.astype(BF16))
    else:
        w_all = lax.all_gather(shard, ALL, axis=0, tiled=True)

        def to_owner(weight):
            rows, width = weight.shape[1:]
            halves = weight.astype(BF16).reshape(exp_local, rows, 2, width // 2).transpose(0, 2, 1, 3)
            halves = jnp.broadcast_to(
                halves[:, None], (exp_local, copies // 2, 2, rows, width // 2)
            ).reshape(n_ctx, rows, width // 2)
            mine = lax.all_to_all(halves, CTX, split_axis=0, concat_axis=0, tiled=True)
            return lax.all_gather(mine.reshape(n_ctx * rows, width // 2), "core", axis=1, tiled=True)

        w_in = to_owner(expert_in)
        w_down = to_owner(expert_out)
    w_qkv = w_all[:, :cols]
    aux_all = w_all[:, cols : cols + AUX]
    w_attn_out = w_all[:, cols + AUX :]
    gain_first = aux_all[:, 0].astype(F32)
    gain_second = aux_all[:, 1].astype(F32)
    w_router = aux_all[:, 2 : 2 + EXPERTS]

    route_hot = (
        routes[0][:, :, None] == jnp.arange(EXPERTS, dtype=jnp.int32)[None, None, :]
    ).astype(F32)
    flat_hot = route_hot.reshape(tok_rows * 2, EXPERTS).astype(BF16)
    order = jnp.arange(tok_rows * 2, dtype=jnp.int32)
    earlier = (order[:, None] > order[None, :]).astype(BF16)
    ranks = dot(earlier, flat_hot)
    slot_index = jnp.sum(ranks * flat_hot.astype(F32), axis=1).astype(jnp.int32)
    target = (routes[0].reshape(tok_rows * 2) * CAP + slot_index).reshape(tok_rows, 2)
    slots = jnp.arange(EXPERTS * CAP, dtype=jnp.int32)
    picks = [(target[:, k : k + 1] == slots[None, :]) for k in range(2)]
    sends = [(target[:, k][None, :] == slots[:, None]) for k in range(2)]
    send_hot = (sends[0] | sends[1]).astype(BF16)

    def to_experts(rows):
        return lax.all_to_all(
            rows.reshape((EXPERTS, CAP) + rows.shape[1:]),
            OWNERS,
            split_axis=0,
            concat_axis=0,
            tiled=True,
        ).reshape(rows.shape)

    inputs = tokens[0].astype(F32)
    scale_first = norm_scale(inputs)
    norm_first = inputs * scale_first
    first = (norm_first * gain_first).astype(BF16)
    projected = dot(first, w_qkv).astype(BF16)
    kv = lax.all_gather(projected[:, head_width:], CTX, axis=0, tiled=True)
    kv, grad_y_send = lax.optimization_barrier((kv, dot(send_hot, cotangent[0]).astype(BF16)))
    grad_y_rows = to_experts(grad_y_send)
    mine = (lax.axis_index(CTX) * (tok_rows // BLK)).astype(jnp.int32).reshape(1)
    exact, attended, lse = attend(lengths, block_order, mine, projected, kv)
    attended, grad_y_rows = lax.optimization_barrier((attended, grad_y_rows))
    middle = inputs + dot(attended, w_attn_out)
    scale_second = norm_scale(middle)
    norm_second = middle * scale_second
    second = (norm_second * gain_second).astype(BF16)
    logits = dot(second, w_router)
    chosen = jnp.sum(route_hot * logits[:, None, :], axis=-1)
    gates = jax.nn.softmax(chosen, axis=-1)

    gate_rows = jnp.sum(
        jnp.where(sends[0], gates[:, 0][None, :], 0.0) + jnp.where(sends[1], gates[:, 1][None, :], 0.0),
        axis=1,
        keepdims=True,
    )

    def in_parts(column):
        high = lax.reduce_precision(column, 8, 7)
        rest = column - high
        mid = lax.reduce_precision(rest, 8, 7)
        parts = jnp.concatenate([high, mid, rest - mid], axis=1).astype(BF16)
        return jnp.pad(parts, ((0, 0), (0, AUX - 3)))

    gate_parts = in_parts(gate_rows)
    payload = to_experts(
        jnp.concatenate([dot(send_hot, second).astype(BF16), gate_parts], axis=1)
    )
    received = payload[:, :D]
    gate_got = jnp.sum(payload[:, D : D + 3].astype(F32), axis=1, keepdims=True)

    gate_up = dot(received, w_in)
    gate_part = gate_up[:, :FF]
    up_part = gate_up[:, FF:]
    sigmoid_gate = jax.nn.sigmoid(gate_part)
    silu_gate = gate_part * sigmoid_gate
    hidden = (silu_gate * up_part).astype(BF16)
    expert_rows = dot(hidden, w_down)
    expert_rows = expert_rows.astype(BF16)
    grad_y_rows = grad_y_rows.astype(F32)
    returned = to_experts(expert_rows)

    grad_rows = (gate_got * grad_y_rows).astype(BF16)
    gate_grad_parts = in_parts(
        jnp.sum(grad_y_rows * expert_rows.astype(F32), axis=1, keepdims=True)
    )
    half_d = D // 2
    grad_hidden = dot(grad_rows, w_down, ((1,), (1,)))
    grad_gate = (
        grad_hidden * up_part * sigmoid_gate * (1.0 + gate_part * (1.0 - sigmoid_gate))
    ).astype(BF16)
    grad_up = (grad_hidden * silu_gate).astype(BF16)
    grad_gate_up = jnp.concatenate([grad_gate, grad_up], axis=1)
    grad_back = dot(grad_gate_up, w_in, ((1,), (1,)))
    grad_returned = to_experts(jnp.concatenate([grad_back.astype(BF16), gate_grad_parts], axis=1))

    grad_in = jnp.stack(
        [dot(received, grad_gate, ((0,), (0,))), dot(received, grad_up, ((0,), (0,)))]
    ).astype(BF16)
    grad_down = jnp.stack(
        [
            dot(hidden, grad_rows[:, :half_d], ((0,), (0,))),
            dot(hidden, grad_rows[:, half_d:], ((0,), (0,))),
        ]
    ).astype(BF16)

    grad_in = lax.psum_scatter(grad_in, "core", scatter_dimension=0, tiled=True)[0]
    grad_down = lax.psum_scatter(grad_down, "core", scatter_dimension=0, tiled=True)[0]
    grad_returned, grad_in, grad_down = lax.optimization_barrier((grad_returned, grad_in, grad_down))

    grad_y = cotangent[0].astype(F32)
    pick_hot = [p.astype(BF16) for p in picks]
    grad_gates = jnp.concatenate(
        [jnp.sum(dot(p, grad_returned[:, D:]), axis=1, keepdims=True) for p in pick_hot], axis=1
    )
    grad_chosen = gates * (grad_gates - jnp.sum(gates * grad_gates, axis=-1, keepdims=True))
    grad_logits = jnp.sum(grad_chosen[:, :, None] * route_hot, axis=1).astype(BF16)
    grad_router = dot(second, grad_logits, ((0,), (0,)))
    grad_second = dot(pick_hot[0] + pick_hot[1], grad_returned[:, :D]) + dot(
        grad_logits, w_router, ((1,), (1,))
    )
    grad_gain_second = jnp.sum(grad_second * norm_second, axis=0)
    grad_norm_second = grad_second * gain_second
    grad_middle = grad_y + scale_second * (
        grad_norm_second
        - norm_second * jnp.mean(grad_norm_second * norm_second, axis=-1, keepdims=True)
    )
    grad_branch = grad_middle.astype(BF16)
    grad_attn_out = dot(attended, grad_branch, ((0,), (0,)))
    late = jnp.concatenate([grad_gain_second[:, None], grad_router], axis=1)
    late = jnp.pad(late, ((0, 0), (0, AUX - late.shape[1])))
    grad_attended = dot(grad_branch, w_attn_out, ((1,), (1,))).astype(BF16)
    delta = jnp.sum(
        (grad_attended.astype(F32) * exact).reshape(tok_rows, HEADS, HEAD), axis=-1
    )
    delta = (
        delta.reshape(tok_rows // BLK, BLK, KV_HEADS, GROUP)
        .transpose(0, 2, 3, 1)
        .reshape(lse.shape)
    )
    grad_queries, grad_kv = attend_back(
        lengths, block_order, mine, projected, kv, grad_attended, lse, delta
    )
    grad_queries, grad_kv, returned = lax.optimization_barrier((grad_queries, grad_kv, returned))
    picked = [dot(p, returned) for p in pick_hot]
    block_out = (middle + gates[:, 0:1] * picked[0] + gates[:, 1:2] * picked[1]).astype(BF16)
    grad_kv = lax.psum_scatter(grad_kv, CTX, scatter_dimension=0, tiled=True)
    grad_projected = jnp.concatenate([grad_queries, grad_kv], axis=1)
    grad_qkv = dot(first, grad_projected, ((0,), (0,)))
    grad_first = dot(grad_projected, w_qkv, ((1,), (1,)))
    grad_gain_first = jnp.sum(grad_first * norm_first, axis=0)
    grad_norm_first = grad_first * gain_first
    grad_inputs = grad_middle + scale_first * (
        grad_norm_first
        - norm_first * jnp.mean(grad_norm_first * norm_first, axis=-1, keepdims=True)
    )
    last = jnp.pad(grad_gain_first[:, None], ((0, 0), (0, AUX - 1)))
    part = jnp.concatenate(
        [grad_qkv.astype(BF16), last.astype(BF16), grad_attn_out.astype(BF16), late.astype(BF16)], axis=1
    )
    if (copies, exp_local, n_exp) == (2, 4, 4):
        total, sum_in, sum_down = collect(part, grad_in, grad_down, exp_local)
    else:
        total = lax.psum_scatter(part, ALL, scatter_dimension=0, tiled=True).astype(F32)

        def to_rows(half, rows):
            width = half.shape[1]
            got = lax.all_to_all(
                half.reshape(n_ctx, rows, width), CTX, split_axis=0, concat_axis=0, tiled=True
            ).astype(F32)
            got = got.reshape(exp_local, copies // 2, 2, rows, width).sum(axis=1)
            return got.transpose(0, 2, 1, 3).reshape(exp_local, rows, 2 * width)

        sum_in = to_rows(grad_in, in_rows)
        sum_down = to_rows(grad_down, out_rows)
    sum_second = total[:, cols + AUX :]
    return (
        block_out[None],
        grad_inputs.astype(BF16)[None],
        total[:, cols],
        total[:, :cols],
        sum_second[:, :D],
        sum_second[:, D],
        sum_second[:, D + 1 : D + 1 + EXPERTS],
        sum_in.astype(F32),
        sum_down.astype(F32),
    )


def solution(mesh):
    n_ctx, n_exp = mesh.shape["ctx"], mesh.shape["exp"]
    exp_local = EXPERTS // n_exp
    copies = n_ctx // exp_local
    inner = Mesh(mesh.devices.reshape(exp_local, copies // 2, 2, n_exp), ALL)
    by_token = P("exp", CTX, None)
    by_row = P(ALL, None)
    by_expert = P("exp", CTX, None)
    return jax.shard_map(
        on_device,
        mesh=inner,
        in_specs=(
            by_token,
            by_token,
            by_token,
            P("exp", None),
            P("exp", None),
            P(ALL),
            by_row,
            by_row,
            P(ALL),
            by_row,
            by_expert,
            by_expert,
        ),
        out_specs=(
            by_token,
            by_token,
            P(ALL),
            by_row,
            by_row,
            P(ALL),
            by_row,
            by_expert,
            by_expert,
        ),
        check_vma=False,
    )
```

```python
import functools

import jax
import jax.numpy as jnp
from jax import lax
from jax.experimental import pallas as pl
from jax.experimental.pallas import tpu as pltpu
from jax.sharding import Mesh
from jax.sharding import PartitionSpec as P

D = 1536
HEADS = 24
KV_HEADS = 8
HEAD = 64
GROUP = HEADS // KV_HEADS
FF = 1024
EXPERTS = 16
BLK = 128
CAP = 48
AUX = 128

epsilon = 1e-05
far_negative = -1e30
start_max = -1e29
F32 = jnp.float32
BF16 = jnp.bfloat16


def norm_scale(values):
    return lax.rsqrt(jnp.mean(values * values, axis=-1, keepdims=True) + epsilon)


def dot(a, b, dims=((1,), (0,))):
    return lax.dot_general(a, b, (dims, ((), ())), preferred_element_type=F32)


def lane_half(shape, half):
    lane = lax.broadcasted_iota(jnp.int32, shape, 1)
    return (lane >= HEAD) if half else (lane < HEAD)


def head_tiles(ref, rows, group, scale):
    tiles = []
    for i in range(GROUP):
        head = group * GROUP + i
        tile = ref[rows, (head // 2) * 128 : (head // 2 + 1) * 128].astype(F32)
        if head % 2 != group % 2:
            tile = pltpu.roll(tile, HEAD, 1)
        tile = jnp.where(lane_half(tile.shape, group % 2), tile * scale, 0.0)
        tiles.append(tile.astype(BF16))
    return jnp.concatenate(tiles, axis=0)


def block_visibility(lengths_ref, query_block, key_block, parts):
    lanes = lax.broadcasted_iota(jnp.int32, (1, BLK), 1)
    query_pos = query_block * BLK + lanes
    start = jnp.zeros((1, BLK), jnp.int32)
    bound = jnp.int32(0)
    for s in range(parts - 1):
        bound = bound + lengths_ref[0, s]
        start = jnp.where(query_pos >= bound, bound, start)
    key_pos = key_block * BLK + lax.broadcasted_iota(jnp.int32, (BLK, BLK), 0)
    one = ((key_pos >= start) & (key_pos <= query_pos)).astype(jnp.int32)
    return jnp.concatenate([one] * GROUP, axis=1) > 0


def first_row_start(lengths_ref, query_block, parts):
    start = jnp.int32(0)
    bound = jnp.int32(0)
    for s in range(parts - 1):
        bound = bound + lengths_ref[0, s]
        start = jnp.where(query_block * BLK >= bound, bound, start)
    return start


def attend_kernel(
    parts, lengths_ref, order_ref, mine_ref, q_ref, kv_ref, exact_ref, out_ref, lse_ref, q_s, m_s, acc_s
):
    width = KV_HEADS * HEAD
    for qb in range(q_ref.shape[0] // BLK):
        rows = pl.ds(qb * BLK, BLK)
        for g in range(KV_HEADS):
            q_s[g] = head_tiles(q_ref, rows, g, HEAD**-0.5)
            m_s[g] = jnp.full((8, GROUP * BLK), start_max, F32)
            acc_s[g] = jnp.zeros((BLK, GROUP * BLK), F32)
        query_block = order_ref[0, mine_ref[0] + qb]
        first = first_row_start(lengths_ref, query_block, parts)

        @pl.loop(0, order_ref.shape[1])
        def _(kb):
            key_block = order_ref[0, kb]

            @pl.when((key_block <= query_block) & (key_block * BLK + BLK > first))
            def _():
                seen = block_visibility(lengths_ref, query_block, key_block, parts)
                key_rows = pl.ds(kb * BLK, BLK)
                for g in range(KV_HEADS):
                    lanes = pl.ds((g // 2) * 128, 128)
                    keys = kv_ref[key_rows, lanes]
                    values = kv_ref[key_rows, pl.ds(width + (g // 2) * 128, 128)]
                    values = jnp.where(lane_half(values.shape, g % 2), values, jnp.ones_like(values))
                    scores = dot(keys, q_s[g], ((1,), (1,)))
                    scores = jnp.where(seen, scores, far_negative)
                    old = m_s[g, 0:1, :]
                    new = jnp.maximum(old, jnp.max(scores, axis=0, keepdims=True))
                    weights = jnp.exp(scores - new)
                    acc_s[g] = acc_s[g] * jnp.exp(old - new) + dot(
                        values, weights.astype(BF16), ((0,), (0,))
                    )
                    m_s[g, 0:1, :] = new

        tiles = []
        for g in range(KV_HEADS):
            acc = acc_s[g]
            at = (1 - g % 2) * HEAD
            total = acc[at : at + 1, :]
            lse_ref[qb, g : g + 1, :] = m_s[g, 0:1, :] + jnp.log(total)
            acc = acc / total
            for i in range(GROUP):
                head = g * GROUP + i
                tile = jnp.transpose(acc[:, i * BLK : (i + 1) * BLK])
                if head % 2 != g % 2:
                    tile = pltpu.roll(tile, HEAD, 1)
                tiles.append(tile)
                if head % 2 == 1:
                    both = jnp.where(lane_half(tile.shape, 0), tiles[head - 1], tile)
                    lanes = pl.ds((head // 2) * 128, 128)
                    exact_ref[rows, lanes] = both
                    out_ref[rows, lanes] = both.astype(BF16)


def attend(lengths, order, mine, projected, kv):
    rows = projected.shape[0]
    smem = pl.BlockSpec(memory_space=pltpu.SMEM)
    vmem = pl.BlockSpec(memory_space=pltpu.VMEM)
    wide = GROUP * BLK
    return pl.pallas_call(
        functools.partial(attend_kernel, lengths.shape[1]),
        out_shape=(
            jax.ShapeDtypeStruct((rows, HEADS * HEAD), F32),
            jax.ShapeDtypeStruct((rows, HEADS * HEAD), BF16),
            jax.ShapeDtypeStruct((rows // BLK, KV_HEADS, wide), F32),
        ),
        in_specs=[smem, smem, smem, vmem, vmem],
        out_specs=(vmem, vmem, vmem),
        scratch_shapes=[
            pltpu.VMEM((KV_HEADS, wide, 128), BF16),
            pltpu.VMEM((KV_HEADS, 8, wide), F32),
            pltpu.VMEM((KV_HEADS, BLK, wide), F32),
        ],
        compiler_params=pltpu.CompilerParams(vmem_limit_bytes=48 * 2**20),
        cost_estimate=pl.CostEstimate(flops=10**10, bytes_accessed=10**7, transcendentals=10**7),
        name="attend",
    )(lengths, order, mine, projected, kv)


def attend_back_kernel(
    parts,
    lengths_ref,
    order_ref,
    mine_ref,
    q_ref,
    kv_ref,
    grad_ref,
    lse_ref,
    delta_ref,
    dq_ref,
    dkv_ref,
    q_s,
    g_s,
    dq_s,
    dkv_s,
):
    width = KV_HEADS * HEAD

    @pl.loop(0, order_ref.shape[1])
    def _(kb):
        dkv_s[pl.ds(kb * BLK, BLK), :] = jnp.zeros((BLK, 2 * width), F32)

    for qb in range(q_ref.shape[0] // BLK):
        rows = pl.ds(qb * BLK, BLK)
        for g in range(KV_HEADS):
            q_s[g] = head_tiles(q_ref, rows, g, HEAD**-0.5)
            g_s[g] = head_tiles(grad_ref, rows, g, 1.0)
            dq_s[g] = jnp.zeros((GROUP * BLK, 128), F32)
        query_block = order_ref[0, mine_ref[0] + qb]
        first = first_row_start(lengths_ref, query_block, parts)

        @pl.loop(0, order_ref.shape[1])
        def _(kb):
            key_block = order_ref[0, kb]

            @pl.when((key_block <= query_block) & (key_block * BLK + BLK > first))
            def _():
                seen = block_visibility(lengths_ref, query_block, key_block, parts)
                key_rows = pl.ds(kb * BLK, BLK)
                for pair in range(KV_HEADS // 2):
                    key_lanes = pl.ds(pair * 128, 128)
                    value_lanes = pl.ds(width + pair * 128, 128)
                    keys = kv_ref[key_rows, key_lanes]
                    values = kv_ref[key_rows, value_lanes]
                    grad_keys = dkv_s[key_rows, key_lanes]
                    grad_values = dkv_s[key_rows, value_lanes]
                    for g in (2 * pair, 2 * pair + 1):
                        scores = dot(keys, q_s[g], ((1,), (1,)))
                        scores = jnp.where(seen, scores, far_negative)
                        probs = jnp.exp(scores - lse_ref[qb, g : g + 1, :])
                        grad_probs = dot(values, g_s[g], ((1,), (1,)))
                        grad_scores = (probs * (grad_probs - delta_ref[qb, g : g + 1, :])).astype(BF16)
                        grad_values = grad_values + dot(probs.astype(BF16), g_s[g])
                        grad_keys = grad_keys + dot(grad_scores, q_s[g])
                        dq_s[g] += dot(grad_scores, keys, ((0,), (0,)))
                    dkv_s[key_rows, key_lanes] = grad_keys
                    dkv_s[key_rows, value_lanes] = grad_values

        tiles = []
        for g in range(KV_HEADS):
            for i in range(GROUP):
                head = g * GROUP + i
                tile = dq_s[g, i * BLK : (i + 1) * BLK, :] * HEAD**-0.5
                if head % 2 != g % 2:
                    tile = pltpu.roll(tile, HEAD, 1)
                tiles.append(tile)
                if head % 2 == 1:
                    both = jnp.where(lane_half(tile.shape, 0), tiles[head - 1], tile)
                    dq_ref[rows, (head // 2) * 128 : (head // 2 + 1) * 128] = both.astype(BF16)

    @pl.loop(0, order_ref.shape[1])
    def _(kb):
        key_rows = pl.ds(kb * BLK, BLK)
        dkv_ref[key_rows, :] = dkv_s[key_rows, :].astype(BF16)


def attend_back(lengths, order, mine, projected, kv, grad_attended, lse, delta):
    rows = projected.shape[0]
    smem = pl.BlockSpec(memory_space=pltpu.SMEM)
    vmem = pl.BlockSpec(memory_space=pltpu.VMEM)
    wide = GROUP * BLK
    return pl.pallas_call(
        functools.partial(attend_back_kernel, lengths.shape[1]),
        out_shape=(
            jax.ShapeDtypeStruct((rows, HEADS * HEAD), BF16),
            jax.ShapeDtypeStruct(kv.shape, BF16),
        ),
        in_specs=[smem, smem, smem, vmem, vmem, vmem, vmem, vmem],
        out_specs=(vmem, vmem),
        scratch_shapes=[
            pltpu.VMEM((KV_HEADS, wide, 128), BF16),
            pltpu.VMEM((KV_HEADS, wide, 128), BF16),
            pltpu.VMEM((KV_HEADS, wide, 128), F32),
            pltpu.VMEM(kv.shape, F32),
        ],
        compiler_params=pltpu.CompilerParams(vmem_limit_bytes=56 * 2**20),
        cost_estimate=pl.CostEstimate(flops=3 * 10**10, bytes_accessed=10**7, transcendentals=10**7),
        name="attend_back",
    )(lengths, order, mine, projected, kv, grad_attended, lse, delta)


MESH = pl.DeviceIdType.MESH


def place(z, core, exp):
    return {"le": z, "rep": 0, "core": core, "exp": exp}


def x_of(exp):
    return (exp // 2) * 2 + 1 - exp % 2


def y_of(exp):
    return (1 - exp // 2) * 2 + exp % 2


def remote(src, dst, send_sem, recv_sem, device):
    return pltpu.make_async_remote_copy(
        src_ref=src,
        dst_ref=dst,
        send_sem=send_sem,
        recv_sem=recv_sem,
        device_id=device,
        device_id_type=MESH,
    )


def meet(devices):
    barrier = pltpu.get_barrier_semaphore()
    for device in devices:
        pl.semaphore_signal(barrier, inc=1, device_id=device, device_id_type=MESH)
    pl.semaphore_wait(barrier, len(devices))


def front_kernel(
    layers,
    shard_ref,
    in_ref,
    down_ref,
    tokens_ref,
    w_all_ref,
    w_in_ref,
    w_down_ref,
    first_ref,
    projected_ref,
    kv_ref,
    weights,
    in_wide,
    down_wide,
    in_half,
    down_half,
    unit_sem,
    line_sem,
    x_sem,
    y_sem,
    far_sem,
    core_sem,
    half_sem,
    half_send,
    over_sem,
    over_send,
    kv_sem,
    kv_send,
    own_sem,
    wide_sem,
):
    z, core, exp = lax.axis_index("le"), lax.axis_index("core"), lax.axis_index("exp")
    other = 1 - core
    x, y = x_of(exp), y_of(exp)
    ctx = z * 2 + core
    rows = shard_ref.shape[0]
    order = [(z + s) % layers for s in ((2, 1, 3, 0) if layers == 4 else range(layers))]
    wides = ((in_ref, in_wide), (down_ref, down_wide))
    halves = ((in_half, w_in_ref), (down_half, w_down_ref))

    loads = []
    for k, zz in enumerate(order):
        for a in range(2):
            load = pltpu.make_async_copy(wides[a][0].at[zz], wides[a][1].at[zz], wide_sem.at[a, k])
            load.start()
            loads.append(load)
    meet(
        [
            place((z + s) % layers, (core + p) % 2, exp)
            for s in range(layers)
            for p in range(2)
            if s + p > 0
        ]
        + [place(z, core, x), place(z, core, y)]
    )

    def number(zz, cc, ee):
        return (zz * 2 + cc) * 4 + ee

    def unit(zz, cc, ee):
        return weights.at[pl.ds(pl.multiple_of(number(zz, cc, ee) * rows, 16), rows), :]

    def send(src, who, sem, device):
        return remote(src, unit(*who), sem, unit_sem.at[number(*who)], device)

    def arrive(who):
        send(unit(*who), who, line_sem.at[0], place(z, other, exp)).wait_recv()

    started = []

    def go(copy, condition=None):
        if condition is None:
            copy.start()
        else:
            pl.when(condition)(copy.start)
        started.append((copy, condition))

    me = (z, core, exp)
    keep = pltpu.make_async_copy(shard_ref, unit(*me), own_sem.at[0])
    keep.start()
    go(send(shard_ref, me, line_sem.at[layers], place(z + 1, core, exp)), z < layers - 1)
    go(send(shard_ref, me, line_sem.at[layers + 1], place(z - 1, core, exp)), z > 0)
    go(send(shard_ref, me, x_sem.at[layers], place(z, core, x)))
    go(send(shard_ref, me, y_sem.at[layers], place(z, core, y)))
    go(send(shard_ref, me, core_sem.at[layers], place(z, other, exp)))

    slab = 16
    for k, zz in enumerate(order):
        for a in range(2):
            loads[2 * k + a].wait()
            src, dst = wides[a][1], halves[a][0]

            @pl.loop(0, src.shape[1] // slab)
            def _(i, zz=zz, src=src, dst=dst):
                at = pl.ds(pl.multiple_of(i * slab, slab), slab)
                dst[zz, at, :] = src[zz, at, :].astype(BF16)

    def half(a, source, p):
        src, dst = halves[a]
        n, cols = src.shape[1], src.shape[2] // 2
        return dst.at[pl.ds(source * n, n), pl.ds(pl.multiple_of(p * cols, 128), cols)]

    def mine(a, zz, p):
        src = halves[a][0]
        cols = src.shape[2] // 2
        return src.at[zz, :, pl.ds(pl.multiple_of(p * cols, 128), cols)]

    def layer(k):
        return jnp.where(z < layers // 2, k, layers - 1 - k)

    for k in range(layers):
        zz = layer(k)
        who = (zz, core, exp)

        @pl.when(zz != z)
        def _(who=who):
            arrive(who)

        go(send(unit(*who), who, line_sem.at[k], place(z + 1, core, exp)), (zz < z) & (z < layers - 1))
        go(send(unit(*who), who, line_sem.at[k], place(z - 1, core, exp)), (zz > z) & (z > 0))
        go(send(unit(*who), who, x_sem.at[k], place(z, core, x)), zz != z)
        go(send(unit(*who), who, y_sem.at[k], place(z, core, y)), zz != z)
        go(send(unit(*who), who, core_sem.at[k], place(z, other, exp)), zz != z)

    for a in range(2):
        pltpu.make_async_copy(mine(a, z, core), half(a, ctx, core), own_sem.at[1 + a]).start()

    def hand_out(a):
        for s, zz in enumerate(order):
            for p in range(2):
                if s == layers - 1 and p == 0:
                    continue
                pp = (core + p) % 2
                go(
                    remote(
                        mine(a, zz, pp),
                        half(a, ctx, pp),
                        half_send.at[a, s * 2 + p],
                        half_sem.at[a, ctx],
                        place(zz, pp, exp),
                    )
                )
        go(
            remote(
                mine(a, z, core),
                half(a, ctx, core),
                over_send.at[a, 2 * layers],
                over_sem.at[a, ctx],
                place(z, other, exp),
            )
        )

    hand_out(0)

    for k in range(layers):
        zz = layer(k)
        from_x, from_y = (zz, core, x), (zz, core, y)
        arrive(from_x)
        go(send(unit(*from_x), from_x, core_sem.at[layers + 1 + k], place(z, other, exp)))
        if k % 2 == 0:
            go(send(unit(*from_x), from_x, far_sem.at[k], place(z, core, y)))
        arrive(from_y)
        go(send(unit(*from_y), from_y, core_sem.at[2 * layers + 1 + k], place(z, other, exp)))
        if k % 2 == 1:
            go(send(unit(*from_y), from_y, far_sem.at[k], place(z, core, x)))
    for k in range(layers):
        far = (layer(k), core, y_of(x))
        arrive(far)
        go(send(unit(*far), far, core_sem.at[3 * layers + 1 + k], place(z, other, exp)))
    for ee in range(4):
        for zz in range(layers):
            arrive((zz, other, ee))
    keep.wait()
    save = pltpu.make_async_copy(weights, w_all_ref, own_sem.at[3])
    save.start()

    depth, count = tokens_ref.shape[1], tokens_ref.shape[0]
    qkv_cols, head_cols = projected_ref.shape[1], HEADS * HEAD
    inputs = tokens_ref[...].astype(F32)
    gain = jnp.concatenate(
        [
            jnp.transpose(weights[i * 128 : (i + 1) * 128, qkv_cols : qkv_cols + AUX].astype(F32))[0:1, :]
            for i in range(depth // 128)
        ],
        axis=1,
    )
    first_ref[...] = (inputs * norm_scale(inputs) * gain).astype(BF16)
    tile = 512

    @pl.loop(0, (qkv_cols - head_cols) // tile)
    def _(i):
        at = pl.ds(pl.multiple_of(head_cols + i * tile, tile), tile)
        projected_ref[:, at] = dot(first_ref[...], weights[:, at]).astype(BF16)

    def block(source):
        return kv_ref.at[pl.ds(pl.multiple_of(source * count, 16), count), :]

    def share(src, source, sem, device):
        return remote(src, block(source), sem, kv_sem.at[source], device)

    own = projected_ref.at[:, pl.ds(head_cols, qkv_cols - head_cols)]
    keep_kv = pltpu.make_async_copy(own, block(ctx), own_sem.at[0])
    keep_kv.start()
    go(share(own, ctx, kv_send.at[2 * layers], place(z + 1, core, exp)), z < layers - 1)
    go(share(own, ctx, kv_send.at[2 * layers + 1], place(z - 1, core, exp)), z > 0)
    go(share(own, ctx, kv_send.at[2 * layers + 2], place(z, other, exp)))

    @pl.loop(0, head_cols // tile)
    def _(i):
        at = pl.ds(pl.multiple_of(i * tile, tile), tile)
        projected_ref[:, at] = dot(first_ref[...], weights[:, at]).astype(BF16)

    for k in range(layers):
        zz = layer(k)
        source = zz * 2 + core

        @pl.when(zz != z)
        def _(source=source):
            share(block(source), source, kv_send.at[0], place(z, other, exp)).wait_recv()

        go(share(block(source), source, kv_send.at[k], place(z + 1, core, exp)), (zz < z) & (z < layers - 1))
        go(share(block(source), source, kv_send.at[k], place(z - 1, core, exp)), (zz > z) & (z > 0))
        go(share(block(source), source, kv_send.at[layers + k], place(z, other, exp)), zz != z)
        if k == layers // 2:
            hand_out(1)

    for s, zz in enumerate(order[::-1]):
        for p in range(2):
            if s == 0 and p == 0:
                continue
            source = zz * 2 + (core + p) % 2
            for a in range(2):
                remote(
                    half(a, source, core),
                    half(a, source, core),
                    half_send.at[a, 0],
                    half_sem.at[a, source],
                    place(z, other, exp),
                ).wait_recv()
                go(
                    remote(
                        half(a, source, core),
                        half(a, source, core),
                        over_send.at[a, s * 2 + p],
                        over_sem.at[a, source],
                        place(z, other, exp),
                    )
                )

    for zz in range(layers):
        source = zz * 2 + other
        share(block(source), source, kv_send.at[0], place(z, other, exp)).wait_recv()
    for source in range(2 * layers):
        for a in range(2):
            remote(
                half(a, source, other),
                half(a, source, other),
                half_send.at[a, 0],
                over_sem.at[a, source],
                place(z, other, exp),
            ).wait_recv()
    keep_kv.wait()
    save.wait()
    for a in range(2):
        pltpu.make_async_copy(mine(a, z, core), half(a, ctx, core), own_sem.at[1 + a]).wait()
    for copy, condition in started:
        if condition is None:
            copy.wait_send()
        else:
            pl.when(condition)(copy.wait_send)


def front(shard, expert_in, expert_out, tokens, qkv_cols):
    layers = expert_in.shape[0]
    rows_in, rows_out = expert_in.shape[1], expert_out.shape[1]
    depth, cols = shard.shape[0] * 8 * layers, shard.shape[1]
    count = tokens.shape[0]
    any_space = pl.BlockSpec(memory_space=pl.ANY)
    vmem = pl.BlockSpec(memory_space=pltpu.VMEM)
    dma = pltpu.SemaphoreType.DMA
    return pl.pallas_call(
        functools.partial(front_kernel, layers),
        out_shape=(
            jax.ShapeDtypeStruct((depth, cols), BF16),
            jax.ShapeDtypeStruct((rows_in * 2 * layers, expert_in.shape[2]), BF16),
            jax.ShapeDtypeStruct((rows_out * 2 * layers, expert_out.shape[2]), BF16),
            jax.ShapeDtypeStruct((count, depth), BF16),
            jax.ShapeDtypeStruct((count, qkv_cols), BF16),
            jax.ShapeDtypeStruct((count * 2 * layers, qkv_cols - HEADS * HEAD), BF16),
        ),
        in_specs=[any_space] * 3 + [vmem],
        out_specs=(any_space,) * 3 + (vmem, vmem, any_space),
        scratch_shapes=[
            pltpu.VMEM((depth, cols), BF16),
            pltpu.VMEM(expert_in.shape, F32),
            pltpu.VMEM(expert_out.shape, F32),
            pltpu.VMEM(expert_in.shape, BF16),
            pltpu.VMEM(expert_out.shape, BF16),
            dma((8 * layers,)),
            dma((layers + 2,)),
            dma((layers + 1,)),
            dma((layers + 1,)),
            dma((layers,)),
            dma((4 * layers + 1,)),
            dma((2, 2 * layers)),
            dma((2, 2 * layers)),
            dma((2, 2 * layers)),
            dma((2, 2 * layers + 1)),
            dma((2 * layers,)),
            dma((2 * layers + 3,)),
            dma((4,)),
            dma((2, layers)),
        ],
        compiler_params=pltpu.CompilerParams(
            collective_id=0, has_side_effects=True, vmem_limit_bytes=48 * 2**20
        ),
        name="front",
    )(shard, expert_in, expert_out, tokens)


def experts_kernel(
    layers,
    rows_ref,
    gates_ref,
    grads_ref,
    w_in_ref,
    w_down_ref,
    out_ref,
    back_ref,
    back_gates_ref,
    d_in_ref,
    d_down_ref,
    w_in,
    w_down,
    got,
    got_gates,
    x_s,
    grad_s,
    hidden_s,
    inner_s,
    back_s,
    back_gates_s,
    other_in,
    other_down,
    pair_in,
    pair_down,
    row_sem,
    row_send,
    gate_sem,
    gate_send,
    back_sem,
    back_send,
    back_gate_sem,
    back_gate_send,
    pair_sem,
    pair_send,
    load_sem,
):
    z, core, exp = lax.axis_index("le"), lax.axis_index("core"), lax.axis_index("exp")
    other = 1 - core
    columns = rows_ref.shape[0] // layers
    me = exp * layers + z
    cap, depth = rows_ref.shape[1], rows_ref.shape[2]
    chunk = columns * cap
    loads = [
        pltpu.make_async_copy(w_in_ref, w_in, load_sem.at[0]),
        pltpu.make_async_copy(w_down_ref, w_down, load_sem.at[1]),
    ]
    for load in loads:
        load.start()
    order = [(z + s) % layers for s in ((2, 1, 3, 0) if layers == 4 else range(layers))]
    peers = [
        (zz, (exp + t) % columns)
        for s, zz in enumerate(order)
        for t in range(columns)
        if not (s == layers - 1 and t == 0)
    ]
    meet([place(zz, core, ee) for zz, ee in peers] + [place(z, other, exp)])

    started = []

    def go(copy):
        copy.start()
        started.append(copy)

    keeps = [
        pltpu.make_async_copy(rows_ref.at[me], got.at[me], load_sem.at[2]),
        pltpu.make_async_copy(gates_ref.at[me], got_gates.at[me], load_sem.at[3]),
    ]
    for keep in keeps:
        keep.start()
    for k, (zz, ee) in enumerate(peers):
        there = ee * layers + zz
        go(remote(gates_ref.at[there], got_gates.at[me], gate_send.at[k], gate_sem.at[me], place(zz, core, ee)))
        go(remote(rows_ref.at[there], got.at[me], row_send.at[k], row_sem.at[me], place(zz, core, ee)))
    for load in loads + keeps:
        load.wait()

    eye = lax.broadcasted_iota(jnp.int32, (cap, 128), 0) == lax.broadcasted_iota(jnp.int32, (cap, 128), 1)
    tile = 256

    def tiles(i):
        return pl.ds(pl.multiple_of(i * tile, tile), tile)

    for k, zz in enumerate(order[::-1]):
        rows = pl.ds(k * chunk, chunk)
        for ee in range(columns):
            source = ee * layers + zz

            @pl.when(source != me)
            def _(source=source):
                here = place(z, other, exp)
                remote(got.at[source], got.at[source], row_send.at[0], row_sem.at[source], here).wait_recv()
                remote(
                    got_gates.at[source], got_gates.at[source], gate_send.at[0], gate_sem.at[source], here
                ).wait_recv()

            at = pl.ds(k * chunk + ee * cap, cap)
            x_s[at, :] = got[source]
            gate = jnp.sum(jnp.where(eye, got_gates[source, 0:1, :], 0.0), axis=1, keepdims=True)
            grad_s[at, :] = (gate * grads_ref[source].astype(F32)).astype(BF16)

        @pl.loop(0, FF // tile)
        def _(i, rows=rows):
            up_at = pl.ds(pl.multiple_of(FF + i * tile, tile), tile)
            gate = dot(x_s[rows, :], w_in[:, tiles(i)])
            up = dot(x_s[rows, :], w_in[:, up_at])
            grad_hidden = dot(grad_s[rows, :], w_down[tiles(i), :], ((1,), (1,)))
            sigmoid = jax.nn.sigmoid(gate)
            silu = gate * sigmoid
            hidden_s[rows, tiles(i)] = (silu * up).astype(BF16)
            inner_s[rows, tiles(i)] = (grad_hidden * up * sigmoid * (1.0 + gate * (1.0 - sigmoid))).astype(BF16)
            inner_s[rows, up_at] = (grad_hidden * silu).astype(BF16)

        @pl.loop(0, depth // tile)
        def _(i, rows=rows, zz=zz):
            back = dot(inner_s[rows, :], w_in[tiles(i), :], ((1,), (1,))).astype(BF16)
            for ee in range(columns):
                back_s[ee * layers + zz, :, tiles(i)] = back[ee * cap : (ee + 1) * cap]

        @pl.loop(0, depth // tile, init_carry=jnp.zeros((chunk, 128), F32))
        def gate_grads(i, sums, rows=rows, zz=zz):
            result = dot(hidden_s[rows, :], w_down[:, tiles(i)]).astype(BF16)
            parts = []
            for ee in range(columns):
                part = result[ee * cap : (ee + 1) * cap]
                out_ref[ee * layers + zz, :, tiles(i)] = part
                parts.append(part.astype(F32) * grads_ref[ee * layers + zz, :, tiles(i)].astype(F32))
            product = jnp.concatenate(parts, axis=0)
            return sums + product[:, :128] + product[:, 128:]

        gate_grads = jnp.sum(gate_grads, axis=1, keepdims=True)
        for ee in range(columns):
            there = ee * layers + zz
            column = gate_grads[ee * cap : (ee + 1) * cap]
            line = jnp.sum(jnp.where(eye, column, 0.0), axis=0, keepdims=True)
            back_gates_s[there] = jnp.broadcast_to(line, (8, 128))
            row_copy = remote(
                back_s.at[there],
                back_ref.at[me],
                back_send.at[there],
                back_sem.at[me],
                place(zz, core, ee),
            )
            gate_copy = remote(
                back_gates_s.at[there],
                back_gates_ref.at[me],
                back_gate_send.at[there],
                back_gate_sem.at[me],
                place(zz, core, ee),
            )

            @pl.when(there != me)
            def _(row_copy=row_copy, gate_copy=gate_copy):
                row_copy.start()
                gate_copy.start()

    own = [
        pltpu.make_async_copy(back_s.at[me], back_ref.at[me], load_sem.at[2]),
        pltpu.make_async_copy(back_gates_s.at[me], back_gates_ref.at[me], load_sem.at[3]),
    ]
    for copy in own:
        copy.start()

    half_in, half_down = d_in_ref.shape[1], d_down_ref.shape[1]

    def in_part(i, p):
        cols = pl.ds(pl.multiple_of(p * half_in, 128), half_in)
        return dot(x_s[:, tiles(i)], inner_s[:, cols], ((0,), (0,)))

    def down_part(i, p):
        cols = pl.ds(pl.multiple_of(p * half_down, 128), half_down)
        return dot(hidden_s[:, tiles(i)], grad_s[:, cols], ((0,), (0,)))

    @pl.loop(0, depth // tile)
    def _(i):
        other_in[tiles(i), :] = in_part(i, other).astype(BF16)

    go(remote(other_in, pair_in, pair_send.at[0], pair_sem.at[0], place(z, other, exp)))

    @pl.loop(0, FF // tile)
    def _(i):
        other_down[tiles(i), :] = down_part(i, other).astype(BF16)

    go(remote(other_down, pair_down, pair_send.at[1], pair_sem.at[1], place(z, other, exp)))
    remote(other_in, pair_in, pair_send.at[0], pair_sem.at[0], place(z, other, exp)).wait_recv()

    @pl.loop(0, depth // tile)
    def _(i):
        d_in_ref[tiles(i), :] = (in_part(i, core) + pair_in[tiles(i), :].astype(F32)).astype(BF16)

    remote(other_down, pair_down, pair_send.at[1], pair_sem.at[1], place(z, other, exp)).wait_recv()

    @pl.loop(0, FF // tile)
    def _(i):
        d_down_ref[tiles(i), :] = (down_part(i, core) + pair_down[tiles(i), :].astype(F32)).astype(BF16)

    for copy in own:
        copy.wait()
    for k, (zz, ee) in enumerate(peers):
        there = ee * layers + zz
        row_copy = remote(
            back_s.at[there], back_ref.at[there], back_send.at[there], back_sem.at[there], place(zz, core, ee)
        )
        gate_copy = remote(
            back_gates_s.at[there],
            back_gates_ref.at[there],
            back_gate_send.at[there],
            back_gate_sem.at[there],
            place(zz, core, ee),
        )
        row_copy.wait()
        gate_copy.wait()
    for copy in started:
        copy.wait_send()


def experts(rows, gates, grads, w_in, w_down, layers):
    count, cap, depth = rows.shape
    any_space = pl.BlockSpec(memory_space=pl.ANY)
    vmem = pl.BlockSpec(memory_space=pltpu.VMEM)
    dma = pltpu.SemaphoreType.DMA
    half_in = jax.ShapeDtypeStruct((depth, FF), BF16)
    half_down = jax.ShapeDtypeStruct((FF, depth // 2), BF16)
    return pl.pallas_call(
        functools.partial(experts_kernel, layers),
        out_shape=(
            jax.ShapeDtypeStruct(rows.shape, BF16),
            jax.ShapeDtypeStruct(rows.shape, BF16),
            jax.ShapeDtypeStruct(gates.shape, F32),
            half_in,
            half_down,
        ),
        in_specs=[any_space, any_space, vmem, any_space, any_space],
        out_specs=(vmem, any_space, any_space, vmem, vmem),
        scratch_shapes=[
            pltpu.VMEM(w_in.shape, BF16),
            pltpu.VMEM(w_down.shape, BF16),
            pltpu.VMEM(rows.shape, BF16),
            pltpu.VMEM(gates.shape, F32),
            pltpu.VMEM((count * cap, depth), BF16),
            pltpu.VMEM((count * cap, depth), BF16),
            pltpu.VMEM((count * cap, FF), BF16),
            pltpu.VMEM((count * cap, 2 * FF), BF16),
            pltpu.VMEM(rows.shape, BF16),
            pltpu.VMEM(gates.shape, F32),
            pltpu.VMEM(half_in.shape, BF16),
            pltpu.VMEM(half_down.shape, BF16),
            pltpu.VMEM(half_in.shape, BF16),
            pltpu.VMEM(half_down.shape, BF16),
        ]
        + [dma((count,))] * 8
        + [dma((2,)), dma((2,)), dma((4,))],
        compiler_params=pltpu.CompilerParams(
            collective_id=2, has_side_effects=True, vmem_limit_bytes=60 * 2**20
        ),
        name="experts",
    )(rows, gates, grads, w_in, w_down)


def collect_kernel(
    layers,
    part_ref,
    in_ref,
    down_ref,
    out_ref,
    got_in_ref,
    got_down_ref,
    own,
    pair,
    near,
    line,
    half_sem,
    half_send,
    load_sem,
    pair_sem,
    pair_send,
    near_sem,
    near_send,
    line_sem,
    line_send,
):
    z, core, exp = lax.axis_index("le"), lax.axis_index("core"), lax.axis_index("exp")
    other = 1 - core
    x, y = x_of(exp), y_of(exp)
    layer_mates = (x, y, y_of(x))
    meet(
        [
            place((z + s) % layers, (core + p) % 2, exp)
            for s in range(layers)
            for p in range(2)
            if s + p > 0
        ]
        + [place(z, core, mate) for mate in layer_mates]
    )
    rows = out_ref.shape[0]
    ctx = z * 2 + core
    started = []

    def go(copy):
        copy.start()
        started.append(copy)

    order = [(z + s) % layers for s in (2, 1, 3, 0)] if layers == 4 else [(z + s) % layers for s in range(layers)]
    loads = []
    for k, zz in enumerate(order):
        go(
            remote(
                part_ref.at[pl.ds((zz * 2 + other) * 4 * rows, 4 * rows), :],
                pair.at[zz],
                pair_send.at[k],
                pair_sem.at[zz],
                place(z, other, exp),
            )
        )
        load = pltpu.make_async_copy(
            part_ref.at[pl.ds((zz * 2 + core) * 4 * rows, 4 * rows), :], own.at[zz], load_sem.at[k]
        )
        load.start()
        loads.append(load)

    arrays = ((in_ref, got_in_ref), (down_ref, got_down_ref))

    def mine(a, owner):
        n = arrays[a][1].shape[1]
        return arrays[a][0].at[pl.ds(owner * n, n), :]

    def half(a, expert, p):
        cols = arrays[a][0].shape[1]
        return arrays[a][1].at[expert, :, pl.ds(pl.multiple_of(p * cols, 128), cols)]

    keeps = []
    for a in range(2):
        keep = pltpu.make_async_copy(mine(a, ctx), half(a, z, core), load_sem.at[layers + a])
        keep.start()
        keeps.append(keep)
    for s in range(layers):
        for p in range(2):
            if s + p == 0:
                continue
            zz, pp = (z + s) % layers, (core + p) % 2
            for a in range(2):
                go(
                    remote(
                        mine(a, zz * 2 + pp),
                        half(a, z, core),
                        half_send.at[a, s * 2 + p],
                        half_sem.at[a, ctx],
                        place(zz, pp, exp),
                    )
                )

    slab = 16
    for k, zz in enumerate(order):
        loads[k].wait()
        remote(pair.at[zz], pair.at[zz], pair_send.at[k], pair_sem.at[zz], place(z, other, exp)).wait_recv()

        @pl.loop(0, 4 * rows // slab)
        def _(i, zz=zz):
            at = pl.ds(pl.multiple_of(i * slab, slab), slab)
            own[zz, at, :] = (own[zz, at, :].astype(F32) + pair[zz, at, :].astype(F32)).astype(BF16)

        for m, mate in enumerate(layer_mates):
            go(
                remote(
                    own.at[zz, pl.ds(pl.multiple_of(mate * rows, slab), rows), :],
                    near.at[m, zz],
                    near_send.at[m, k],
                    near_sem.at[m, zz],
                    place(z, core, mate),
                )
            )

    for k, zz in enumerate(order):
        for m, mate in enumerate(layer_mates):
            remote(
                near.at[m, zz], near.at[m, zz], near_send.at[m, k], near_sem.at[m, zz], place(z, core, mate)
            ).wait_recv()

        @pl.loop(0, rows // slab)
        def _(i, zz=zz):
            at = pl.ds(pl.multiple_of(exp * rows + i * slab, slab), slab)
            here = pl.ds(pl.multiple_of(i * slab, slab), slab)
            total = own[zz, at, :].astype(F32)
            for m in range(3):
                total = total + near[m, zz, here, :].astype(F32)
            own[zz, at, :] = total.astype(BF16)

        if k < layers - 1:
            go(
                remote(
                    own.at[zz, pl.ds(pl.multiple_of(exp * rows, slab), rows), :],
                    line.at[z],
                    line_send.at[k],
                    line_sem.at[z],
                    place(zz, core, exp),
                )
            )

    for zz in order[:-1]:
        remote(line.at[zz], line.at[zz], line_send.at[0], line_sem.at[zz], place(zz, core, exp)).wait_recv()

    @pl.loop(0, rows // slab)
    def _(i):
        at = pl.ds(pl.multiple_of(exp * rows + i * slab, slab), slab)
        here = pl.ds(pl.multiple_of(i * slab, slab), slab)
        total = own[z, at, :].astype(F32)
        for zz in order[:-1]:
            total = total + line[zz, here, :].astype(F32)
        out_ref[here, :] = total

    for source in range(2 * layers):
        for a in range(2):

            @pl.when(source != ctx)
            def _(source=source, a=a):
                remote(
                    half(a, source // 2, source % 2),
                    half(a, source // 2, source % 2),
                    half_send.at[a, 0],
                    half_sem.at[a, source],
                    place(z, other, exp),
                ).wait_recv()

    for keep in keeps:
        keep.wait()
    for copy in started:
        copy.wait_send()


def collect(part, grad_in, grad_down, layers):
    rows, cols = part.shape[0] // (8 * layers), part.shape[1]
    n_in, n_down = grad_in.shape[0] // (2 * layers), grad_down.shape[0] // (2 * layers)
    any_space = pl.BlockSpec(memory_space=pl.ANY)
    dma = pltpu.SemaphoreType.DMA
    return pl.pallas_call(
        functools.partial(collect_kernel, layers),
        out_shape=(
            jax.ShapeDtypeStruct((rows, cols), F32),
            jax.ShapeDtypeStruct((layers, n_in, 2 * grad_in.shape[1]), BF16),
            jax.ShapeDtypeStruct((layers, n_down, 2 * grad_down.shape[1]), BF16),
        ),
        in_specs=[any_space] * 3,
        out_specs=(pl.BlockSpec(memory_space=pltpu.VMEM), any_space, any_space),
        scratch_shapes=[
            pltpu.VMEM((layers, 4 * rows, cols), BF16),
            pltpu.VMEM((layers, 4 * rows, cols), BF16),
            pltpu.VMEM((3, layers, rows, cols), BF16),
            pltpu.VMEM((layers, rows, cols), BF16),
            dma((2, 2 * layers)),
            dma((2, 2 * layers)),
            dma((layers + 2,)),
            dma((layers,)),
            dma((layers,)),
            dma((3, layers)),
            dma((3, layers)),
            dma((layers,)),
            dma((layers,)),
        ],
        compiler_params=pltpu.CompilerParams(
            collective_id=1, has_side_effects=True, vmem_limit_bytes=40 * 2**20
        ),
        name="collect",
    )(part, grad_in, grad_down)


CTX = ("le", "rep", "core")
ALL = ("le", "rep", "core", "exp")
OWNERS = ("exp", "le")


def on_device(
    tokens,
    cotangent,
    routes,
    lengths,
    block_order,
    gain_attn,
    qkv_weight,
    out_weight,
    gain_moe,
    router_weight,
    expert_in,
    expert_out,
):
    tok_rows = tokens.shape[1]
    head_width = HEADS * HEAD
    exp_local = expert_in.shape[0]
    n_ctx = D // expert_in.shape[1]
    copies = n_ctx // exp_local
    n_exp = EXPERTS // exp_local
    in_rows, out_rows = expert_in.shape[1], expert_out.shape[1]

    cols = qkv_weight.shape[1]
    aux = jnp.concatenate([gain_attn[:, None], gain_moe[:, None], router_weight], axis=1)
    aux = jnp.pad(aux, ((0, 0), (0, AUX - aux.shape[1])))
    shard = jnp.concatenate([qkv_weight, aux, out_weight], axis=1).astype(BF16)
    special = (copies, exp_local, n_exp) == (2, 4, 4)
    if special:
        w_all, w_in, w_down, first, projected, kv = front(shard, expert_in, expert_out, tokens[0], cols)
    else:
        w_all = lax.all_gather(shard, ALL, axis=0, tiled=True)

        def to_owner(weight):
            rows, width = weight.shape[1:]
            halves = weight.astype(BF16).reshape(exp_local, rows, 2, width // 2).transpose(0, 2, 1, 3)
            halves = jnp.broadcast_to(
                halves[:, None], (exp_local, copies // 2, 2, rows, width // 2)
            ).reshape(n_ctx, rows, width // 2)
            mine = lax.all_to_all(halves, CTX, split_axis=0, concat_axis=0, tiled=True)
            return lax.all_gather(mine.reshape(n_ctx * rows, width // 2), "core", axis=1, tiled=True)

        w_in = to_owner(expert_in)
        w_down = to_owner(expert_out)
    w_qkv = w_all[:, :cols]
    aux_all = w_all[:, cols : cols + AUX]
    w_attn_out = w_all[:, cols + AUX :]
    gain_first = aux_all[:, 0].astype(F32)
    gain_second = aux_all[:, 1].astype(F32)
    w_router = aux_all[:, 2 : 2 + EXPERTS]

    route_hot = (
        routes[0][:, :, None] == jnp.arange(EXPERTS, dtype=jnp.int32)[None, None, :]
    ).astype(F32)
    flat_hot = route_hot.reshape(tok_rows * 2, EXPERTS).astype(BF16)
    order = jnp.arange(tok_rows * 2, dtype=jnp.int32)
    earlier = (order[:, None] > order[None, :]).astype(BF16)
    ranks = dot(earlier, flat_hot)
    slot_index = jnp.sum(ranks * flat_hot.astype(F32), axis=1).astype(jnp.int32)
    target = (routes[0].reshape(tok_rows * 2) * CAP + slot_index).reshape(tok_rows, 2)
    slots = jnp.arange(EXPERTS * CAP, dtype=jnp.int32)
    picks = [(target[:, k : k + 1] == slots[None, :]) for k in range(2)]
    sends = [(target[:, k][None, :] == slots[:, None]) for k in range(2)]
    send_hot = (sends[0] | sends[1]).astype(BF16)

    def to_experts(rows):
        return lax.all_to_all(
            rows.reshape((EXPERTS, CAP) + rows.shape[1:]),
            OWNERS,
            split_axis=0,
            concat_axis=0,
            tiled=True,
        ).reshape(rows.shape)

    inputs = tokens[0].astype(F32)
    scale_first = norm_scale(inputs)
    norm_first = inputs * scale_first
    if not special:
        first = (norm_first * gain_first).astype(BF16)
        projected = dot(first, w_qkv).astype(BF16)
        kv = lax.all_gather(projected[:, head_width:], CTX, axis=0, tiled=True)
    kv, grad_y_send = lax.optimization_barrier((kv, dot(send_hot, cotangent[0]).astype(BF16)))
    grad_y_rows = to_experts(grad_y_send)
    mine = (lax.axis_index(CTX) * (tok_rows // BLK)).astype(jnp.int32).reshape(1)
    exact, attended, lse = attend(lengths, block_order, mine, projected, kv)
    attended, grad_y_rows = lax.optimization_barrier((attended, grad_y_rows))
    middle = inputs + dot(attended, w_attn_out)
    scale_second = norm_scale(middle)
    norm_second = middle * scale_second
    second = (norm_second * gain_second).astype(BF16)
    logits = dot(second, w_router)
    chosen = jnp.sum(route_hot * logits[:, None, :], axis=-1)
    gates = jax.nn.softmax(chosen, axis=-1)

    gate_rows = jnp.sum(
        jnp.where(sends[0], gates[:, 0][None, :], 0.0) + jnp.where(sends[1], gates[:, 1][None, :], 0.0),
        axis=1,
        keepdims=True,
    )
    if special:
        slot_gates = jnp.broadcast_to(
            jnp.pad(gate_rows.reshape(EXPERTS, 1, CAP), ((0, 0), (0, 0), (0, 128 - CAP))), (EXPERTS, 8, 128)
        )
        expert_rows, grad_returned, gate_grads, grad_in, grad_down = experts(
            dot(send_hot, second).astype(BF16).reshape(EXPERTS, CAP, D),
            slot_gates,
            grad_y_rows.reshape(EXPERTS, CAP, D),
            w_in,
            w_down,
            exp_local,
        )
        returned = to_experts(expert_rows.reshape(EXPERTS * CAP, D))
        grad_returned = grad_returned.reshape(EXPERTS * CAP, D)
        gate_grads = gate_grads[:, 0, :CAP].reshape(1, EXPERTS * CAP)
    else:
        def in_parts(column):
            high = lax.reduce_precision(column, 8, 7)
            rest = column - high
            mid = lax.reduce_precision(rest, 8, 7)
            parts = jnp.concatenate([high, mid, rest - mid], axis=1).astype(BF16)
            return jnp.pad(parts, ((0, 0), (0, AUX - 3)))

        gate_parts = in_parts(gate_rows)
        payload = to_experts(
            jnp.concatenate([dot(send_hot, second).astype(BF16), gate_parts], axis=1)
        )
        received = payload[:, :D]
        gate_got = jnp.sum(payload[:, D : D + 3].astype(F32), axis=1, keepdims=True)

        gate_up = dot(received, w_in)
        gate_part = gate_up[:, :FF]
        up_part = gate_up[:, FF:]
        sigmoid_gate = jax.nn.sigmoid(gate_part)
        silu_gate = gate_part * sigmoid_gate
        hidden = (silu_gate * up_part).astype(BF16)
        expert_rows = dot(hidden, w_down)
        expert_rows = expert_rows.astype(BF16)
        grad_y_rows = grad_y_rows.astype(F32)
        returned = to_experts(expert_rows)

        grad_rows = (gate_got * grad_y_rows).astype(BF16)
        gate_grad_parts = in_parts(
            jnp.sum(grad_y_rows * expert_rows.astype(F32), axis=1, keepdims=True)
        )
        half_d = D // 2
        grad_hidden = dot(grad_rows, w_down, ((1,), (1,)))
        grad_gate = (
            grad_hidden * up_part * sigmoid_gate * (1.0 + gate_part * (1.0 - sigmoid_gate))
        ).astype(BF16)
        grad_up = (grad_hidden * silu_gate).astype(BF16)
        grad_gate_up = jnp.concatenate([grad_gate, grad_up], axis=1)
        grad_back = dot(grad_gate_up, w_in, ((1,), (1,)))
        grad_returned = to_experts(jnp.concatenate([grad_back.astype(BF16), gate_grad_parts], axis=1))

        grad_in = jnp.stack(
            [dot(received, grad_gate, ((0,), (0,))), dot(received, grad_up, ((0,), (0,)))]
        ).astype(BF16)
        grad_down = jnp.stack(
            [
                dot(hidden, grad_rows[:, :half_d], ((0,), (0,))),
                dot(hidden, grad_rows[:, half_d:], ((0,), (0,))),
            ]
        ).astype(BF16)

        grad_in = lax.psum_scatter(grad_in, "core", scatter_dimension=0, tiled=True)[0]
        grad_down = lax.psum_scatter(grad_down, "core", scatter_dimension=0, tiled=True)[0]
        grad_returned, grad_in, grad_down = lax.optimization_barrier((grad_returned, grad_in, grad_down))
        gate_grads = jnp.sum(grad_returned[:, D:].astype(F32), axis=1).reshape(1, EXPERTS * CAP)
        grad_returned = grad_returned[:, :D]

    grad_y = cotangent[0].astype(F32)
    pick_hot = [p.astype(BF16) for p in picks]
    grad_gates = jnp.concatenate(
        [jnp.sum(jnp.where(p, gate_grads, 0.0), axis=1, keepdims=True) for p in picks], axis=1
    )
    grad_chosen = gates * (grad_gates - jnp.sum(gates * grad_gates, axis=-1, keepdims=True))
    grad_logits = jnp.sum(grad_chosen[:, :, None] * route_hot, axis=1).astype(BF16)
    grad_router = dot(second, grad_logits, ((0,), (0,)))
    grad_second = dot(pick_hot[0] + pick_hot[1], grad_returned) + dot(
        grad_logits, w_router, ((1,), (1,))
    )
    grad_gain_second = jnp.sum(grad_second * norm_second, axis=0)
    grad_norm_second = grad_second * gain_second
    grad_middle = grad_y + scale_second * (
        grad_norm_second
        - norm_second * jnp.mean(grad_norm_second * norm_second, axis=-1, keepdims=True)
    )
    grad_branch = grad_middle.astype(BF16)
    grad_attn_out = dot(attended, grad_branch, ((0,), (0,)))
    late = jnp.concatenate([grad_gain_second[:, None], grad_router], axis=1)
    late = jnp.pad(late, ((0, 0), (0, AUX - late.shape[1])))
    grad_attended = dot(grad_branch, w_attn_out, ((1,), (1,))).astype(BF16)
    delta = jnp.sum(
        (grad_attended.astype(F32) * exact).reshape(tok_rows, HEADS, HEAD), axis=-1
    )
    delta = (
        delta.reshape(tok_rows // BLK, BLK, KV_HEADS, GROUP)
        .transpose(0, 2, 3, 1)
        .reshape(lse.shape)
    )
    grad_queries, grad_kv = attend_back(
        lengths, block_order, mine, projected, kv, grad_attended, lse, delta
    )
    grad_queries, grad_kv, returned = lax.optimization_barrier((grad_queries, grad_kv, returned))
    picked = [dot(p, returned) for p in pick_hot]
    block_out = (middle + gates[:, 0:1] * picked[0] + gates[:, 1:2] * picked[1]).astype(BF16)
    grad_kv = lax.psum_scatter(grad_kv, CTX, scatter_dimension=0, tiled=True)
    grad_projected = jnp.concatenate([grad_queries, grad_kv], axis=1)
    grad_qkv = dot(first, grad_projected, ((0,), (0,)))
    grad_first = dot(grad_projected, w_qkv, ((1,), (1,)))
    grad_gain_first = jnp.sum(grad_first * norm_first, axis=0)
    grad_norm_first = grad_first * gain_first
    grad_inputs = grad_middle + scale_first * (
        grad_norm_first
        - norm_first * jnp.mean(grad_norm_first * norm_first, axis=-1, keepdims=True)
    )
    last = jnp.pad(grad_gain_first[:, None], ((0, 0), (0, AUX - 1)))
    part = jnp.concatenate(
        [grad_qkv.astype(BF16), last.astype(BF16), grad_attn_out.astype(BF16), late.astype(BF16)], axis=1
    )
    if special:
        total, sum_in, sum_down = collect(part, grad_in, grad_down, exp_local)
    else:
        total = lax.psum_scatter(part, ALL, scatter_dimension=0, tiled=True).astype(F32)

        def to_rows(half, rows):
            width = half.shape[1]
            got = lax.all_to_all(
                half.reshape(n_ctx, rows, width), CTX, split_axis=0, concat_axis=0, tiled=True
            ).astype(F32)
            got = got.reshape(exp_local, copies // 2, 2, rows, width).sum(axis=1)
            return got.transpose(0, 2, 1, 3).reshape(exp_local, rows, 2 * width)

        sum_in = to_rows(grad_in, in_rows)
        sum_down = to_rows(grad_down, out_rows)
    sum_second = total[:, cols + AUX :]
    return (
        block_out[None],
        grad_inputs.astype(BF16)[None],
        total[:, cols],
        total[:, :cols],
        sum_second[:, :D],
        sum_second[:, D],
        sum_second[:, D + 1 : D + 1 + EXPERTS],
        sum_in.astype(F32),
        sum_down.astype(F32),
    )


def solution(mesh):
    n_ctx, n_exp = mesh.shape["ctx"], mesh.shape["exp"]
    exp_local = EXPERTS // n_exp
    copies = n_ctx // exp_local
    inner = Mesh(mesh.devices.reshape(exp_local, copies // 2, 2, n_exp), ALL)
    by_token = P("exp", CTX, None)
    by_row = P(ALL, None)
    by_expert = P("exp", CTX, None)
    return jax.shard_map(
        on_device,
        mesh=inner,
        in_specs=(
            by_token,
            by_token,
            by_token,
            P("exp", None),
            P("exp", None),
            P(ALL),
            by_row,
            by_row,
            P(ALL),
            by_row,
            by_expert,
            by_expert,
        ),
        out_specs=(
            by_token,
            by_token,
            P(ALL),
            by_row,
            by_row,
            P(ALL),
            by_row,
            by_expert,
            by_expert,
        ),
        check_vma=False,
    )
```

```python
import functools

import jax
import jax.numpy as jnp
from jax import lax
from jax.experimental import pallas as pl
from jax.experimental.pallas import tpu as pltpu
from jax.sharding import Mesh
from jax.sharding import PartitionSpec as P

D = 1536
HEADS = 24
KV_HEADS = 8
HEAD = 64
GROUP = HEADS // KV_HEADS
FF = 1024
EXPERTS = 16
BLK = 128
CAP = 48
AUX = 128

epsilon = 1e-05
far_negative = -1e30
start_max = -1e29
F32 = jnp.float32
BF16 = jnp.bfloat16


def norm_scale(values):
    return lax.rsqrt(jnp.mean(values * values, axis=-1, keepdims=True) + epsilon)


def dot(a, b, dims=((1,), (0,))):
    return lax.dot_general(a, b, (dims, ((), ())), preferred_element_type=F32)


def lane_half(shape, half):
    lane = lax.broadcasted_iota(jnp.int32, shape, 1)
    return (lane >= HEAD) if half else (lane < HEAD)


def head_tiles(ref, rows, group, scale):
    tiles = []
    for i in range(GROUP):
        head = group * GROUP + i
        tile = ref[rows, (head // 2) * 128 : (head // 2 + 1) * 128].astype(F32)
        if head % 2 != group % 2:
            tile = pltpu.roll(tile, HEAD, 1)
        tile = jnp.where(lane_half(tile.shape, group % 2), tile * scale, 0.0)
        tiles.append(tile.astype(BF16))
    return jnp.concatenate(tiles, axis=0)


def block_visibility(lengths_ref, query_block, key_block, parts):
    lanes = lax.broadcasted_iota(jnp.int32, (1, BLK), 1)
    query_pos = query_block * BLK + lanes
    start = jnp.zeros((1, BLK), jnp.int32)
    bound = jnp.int32(0)
    for s in range(parts - 1):
        bound = bound + lengths_ref[0, s]
        start = jnp.where(query_pos >= bound, bound, start)
    key_pos = key_block * BLK + lax.broadcasted_iota(jnp.int32, (BLK, BLK), 0)
    one = ((key_pos >= start) & (key_pos <= query_pos)).astype(jnp.int32)
    return jnp.concatenate([one] * GROUP, axis=1) > 0


def first_row_start(lengths_ref, query_block, parts):
    start = jnp.int32(0)
    bound = jnp.int32(0)
    for s in range(parts - 1):
        bound = bound + lengths_ref[0, s]
        start = jnp.where(query_block * BLK >= bound, bound, start)
    return start


def attend_kernel(
    parts, lengths_ref, order_ref, mine_ref, q_ref, kv_ref, exact_ref, out_ref, lse_ref, q_s, m_s, acc_s
):
    width = KV_HEADS * HEAD
    for qb in range(q_ref.shape[0] // BLK):
        rows = pl.ds(qb * BLK, BLK)
        for g in range(KV_HEADS):
            q_s[g] = head_tiles(q_ref, rows, g, HEAD**-0.5)
            m_s[g] = jnp.full((8, GROUP * BLK), start_max, F32)
            acc_s[g] = jnp.zeros((BLK, GROUP * BLK), F32)
        query_block = order_ref[0, mine_ref[0] + qb]
        first = first_row_start(lengths_ref, query_block, parts)

        @pl.loop(0, order_ref.shape[1])
        def _(kb):
            key_block = order_ref[0, kb]

            @pl.when((key_block <= query_block) & (key_block * BLK + BLK > first))
            def _():
                seen = block_visibility(lengths_ref, query_block, key_block, parts)
                key_rows = pl.ds(kb * BLK, BLK)
                for g in range(KV_HEADS):
                    lanes = pl.ds((g // 2) * 128, 128)
                    keys = kv_ref[key_rows, lanes]
                    values = kv_ref[key_rows, pl.ds(width + (g // 2) * 128, 128)]
                    values = jnp.where(lane_half(values.shape, g % 2), values, jnp.ones_like(values))
                    scores = dot(keys, q_s[g], ((1,), (1,)))
                    scores = jnp.where(seen, scores, far_negative)
                    old = m_s[g, 0:1, :]
                    new = jnp.maximum(old, jnp.max(scores, axis=0, keepdims=True))
                    weights = jnp.exp(scores - new)
                    acc_s[g] = acc_s[g] * jnp.exp(old - new) + dot(
                        values, weights.astype(BF16), ((0,), (0,))
                    )
                    m_s[g, 0:1, :] = new

        tiles = []
        for g in range(KV_HEADS):
            acc = acc_s[g]
            at = (1 - g % 2) * HEAD
            total = acc[at : at + 1, :]
            lse_ref[qb, g : g + 1, :] = m_s[g, 0:1, :] + jnp.log(total)
            acc = acc / total
            for i in range(GROUP):
                head = g * GROUP + i
                tile = jnp.transpose(acc[:, i * BLK : (i + 1) * BLK])
                if head % 2 != g % 2:
                    tile = pltpu.roll(tile, HEAD, 1)
                tiles.append(tile)
                if head % 2 == 1:
                    both = jnp.where(lane_half(tile.shape, 0), tiles[head - 1], tile)
                    lanes = pl.ds((head // 2) * 128, 128)
                    exact_ref[rows, lanes] = both
                    out_ref[rows, lanes] = both.astype(BF16)


def attend(lengths, order, mine, projected, kv):
    rows = projected.shape[0]
    smem = pl.BlockSpec(memory_space=pltpu.SMEM)
    vmem = pl.BlockSpec(memory_space=pltpu.VMEM)
    wide = GROUP * BLK
    return pl.pallas_call(
        functools.partial(attend_kernel, lengths.shape[1]),
        out_shape=(
            jax.ShapeDtypeStruct((rows, HEADS * HEAD), F32),
            jax.ShapeDtypeStruct((rows, HEADS * HEAD), BF16),
            jax.ShapeDtypeStruct((rows // BLK, KV_HEADS, wide), F32),
        ),
        in_specs=[smem, smem, smem, vmem, vmem],
        out_specs=(vmem, vmem, vmem),
        scratch_shapes=[
            pltpu.VMEM((KV_HEADS, wide, 128), BF16),
            pltpu.VMEM((KV_HEADS, 8, wide), F32),
            pltpu.VMEM((KV_HEADS, BLK, wide), F32),
        ],
        compiler_params=pltpu.CompilerParams(vmem_limit_bytes=48 * 2**20),
        cost_estimate=pl.CostEstimate(flops=10**10, bytes_accessed=10**7, transcendentals=10**7),
        name="attend",
    )(lengths, order, mine, projected, kv)


def attend_back_kernel(
    parts,
    lengths_ref,
    order_ref,
    mine_ref,
    q_ref,
    kv_ref,
    grad_ref,
    lse_ref,
    exact_ref,
    dq_ref,
    dkv_ref,
    q_s,
    g_s,
    delta_s,
    dq_s,
    dkv_s,
):
    width = KV_HEADS * HEAD

    @pl.loop(0, order_ref.shape[1])
    def _(kb):
        dkv_s[pl.ds(kb * BLK, BLK), :] = jnp.zeros((BLK, 2 * width), F32)

    for qb in range(q_ref.shape[0] // BLK):
        rows = pl.ds(qb * BLK, BLK)
        for g in range(KV_HEADS):
            q_s[g] = head_tiles(q_ref, rows, g, HEAD**-0.5)
            g_s[g] = head_tiles(grad_ref, rows, g, 1.0)
            dq_s[g] = jnp.zeros((GROUP * BLK, 128), F32)
            for i in range(GROUP):
                head = g * GROUP + i
                exact = exact_ref[rows, (head // 2) * 128 : (head // 2 + 1) * 128]
                if head % 2 != g % 2:
                    exact = pltpu.roll(exact, HEAD, 1)
                product = exact * g_s[g, i * BLK : (i + 1) * BLK, :].astype(F32)
                delta_s[g : g + 1, i * BLK : (i + 1) * BLK] = jnp.sum(
                    jnp.transpose(product), axis=0, keepdims=True
                )
        query_block = order_ref[0, mine_ref[0] + qb]
        first = first_row_start(lengths_ref, query_block, parts)

        @pl.loop(0, order_ref.shape[1])
        def _(kb):
            key_block = order_ref[0, kb]

            @pl.when((key_block <= query_block) & (key_block * BLK + BLK > first))
            def _():
                seen = block_visibility(lengths_ref, query_block, key_block, parts)
                key_rows = pl.ds(kb * BLK, BLK)
                for pair in range(KV_HEADS // 2):
                    key_lanes = pl.ds(pair * 128, 128)
                    value_lanes = pl.ds(width + pair * 128, 128)
                    keys = kv_ref[key_rows, key_lanes]
                    values = kv_ref[key_rows, value_lanes]
                    grad_keys = dkv_s[key_rows, key_lanes]
                    grad_values = dkv_s[key_rows, value_lanes]
                    for g in (2 * pair, 2 * pair + 1):
                        scores = dot(keys, q_s[g], ((1,), (1,)))
                        scores = jnp.where(seen, scores, far_negative)
                        probs = jnp.exp(scores - lse_ref[qb, g : g + 1, :])
                        grad_probs = dot(values, g_s[g], ((1,), (1,)))
                        grad_scores = (probs * (grad_probs - delta_s[g : g + 1, :])).astype(BF16)
                        grad_values = grad_values + dot(probs.astype(BF16), g_s[g])
                        grad_keys = grad_keys + dot(grad_scores, q_s[g])
                        dq_s[g] += dot(grad_scores, keys, ((0,), (0,)))
                    dkv_s[key_rows, key_lanes] = grad_keys
                    dkv_s[key_rows, value_lanes] = grad_values

        tiles = []
        for g in range(KV_HEADS):
            for i in range(GROUP):
                head = g * GROUP + i
                tile = dq_s[g, i * BLK : (i + 1) * BLK, :] * HEAD**-0.5
                if head % 2 != g % 2:
                    tile = pltpu.roll(tile, HEAD, 1)
                tiles.append(tile)
                if head % 2 == 1:
                    both = jnp.where(lane_half(tile.shape, 0), tiles[head - 1], tile)
                    dq_ref[rows, (head // 2) * 128 : (head // 2 + 1) * 128] = both.astype(BF16)

    @pl.loop(0, order_ref.shape[1])
    def _(kb):
        key_rows = pl.ds(kb * BLK, BLK)
        dkv_ref[key_rows, :] = dkv_s[key_rows, :].astype(BF16)


def attend_back(lengths, order, mine, projected, kv, grad_attended, lse, exact):
    rows = projected.shape[0]
    smem = pl.BlockSpec(memory_space=pltpu.SMEM)
    vmem = pl.BlockSpec(memory_space=pltpu.VMEM)
    wide = GROUP * BLK
    return pl.pallas_call(
        functools.partial(attend_back_kernel, lengths.shape[1]),
        out_shape=(
            jax.ShapeDtypeStruct((rows, HEADS * HEAD), BF16),
            jax.ShapeDtypeStruct(kv.shape, BF16),
        ),
        in_specs=[smem, smem, smem, vmem, vmem, vmem, vmem, vmem],
        out_specs=(vmem, vmem),
        scratch_shapes=[
            pltpu.VMEM((KV_HEADS, wide, 128), BF16),
            pltpu.VMEM((KV_HEADS, wide, 128), BF16),
            pltpu.VMEM((KV_HEADS, wide), F32),
            pltpu.VMEM((KV_HEADS, wide, 128), F32),
            pltpu.VMEM(kv.shape, F32),
        ],
        compiler_params=pltpu.CompilerParams(vmem_limit_bytes=56 * 2**20),
        cost_estimate=pl.CostEstimate(flops=10**9, bytes_accessed=10**6, transcendentals=10**5),
        name="attend_back",
    )(lengths, order, mine, projected, kv, grad_attended, lse, exact)


MESH = pl.DeviceIdType.MESH


def place(z, core, exp):
    return {"le": z, "rep": 0, "core": core, "exp": exp}


def x_of(exp):
    return (exp // 2) * 2 + 1 - exp % 2


def y_of(exp):
    return (1 - exp // 2) * 2 + exp % 2


def remote(src, dst, send_sem, recv_sem, device):
    return pltpu.make_async_remote_copy(
        src_ref=src,
        dst_ref=dst,
        send_sem=send_sem,
        recv_sem=recv_sem,
        device_id=device,
        device_id_type=MESH,
    )


def meet(devices):
    barrier = pltpu.get_barrier_semaphore()
    for device in devices:
        pl.semaphore_signal(barrier, inc=1, device_id=device, device_id_type=MESH)
    pl.semaphore_wait(barrier, len(devices))


def front_kernel(
    layers,
    shard_ref,
    in_ref,
    down_ref,
    tokens_ref,
    w_all_ref,
    w_in_ref,
    w_down_ref,
    first_ref,
    projected_ref,
    kv_ref,
    weights,
    in_wide,
    down_wide,
    in_half,
    down_half,
    unit_sem,
    line_sem,
    x_sem,
    y_sem,
    far_sem,
    core_sem,
    half_sem,
    half_send,
    over_sem,
    over_send,
    kv_sem,
    kv_send,
    own_sem,
    wide_sem,
):
    z, core, exp = lax.axis_index("le"), lax.axis_index("core"), lax.axis_index("exp")
    other = 1 - core
    x, y = x_of(exp), y_of(exp)
    ctx = z * 2 + core
    rows = shard_ref.shape[0]
    order = [(z + s) % layers for s in ((2, 1, 3, 0) if layers == 4 else range(layers))]
    wides = ((in_ref, in_wide), (down_ref, down_wide))
    halves = ((in_half, w_in_ref), (down_half, w_down_ref))

    loads = []
    for k, zz in enumerate(order):
        for a in range(2):
            load = pltpu.make_async_copy(wides[a][0].at[zz], wides[a][1].at[zz], wide_sem.at[a, k])
            load.start()
            loads.append(load)
    meet(
        [
            place((z + s) % layers, (core + p) % 2, exp)
            for s in range(layers)
            for p in range(2)
            if s + p > 0
        ]
        + [place(z, core, x), place(z, core, y)]
    )

    def number(zz, cc, ee):
        return (zz * 2 + cc) * 4 + ee

    def unit(zz, cc, ee):
        return weights.at[pl.ds(pl.multiple_of(number(zz, cc, ee) * rows, 16), rows), :]

    def send(src, who, sem, device):
        return remote(src, unit(*who), sem, unit_sem.at[number(*who)], device)

    def arrive(who):
        send(unit(*who), who, line_sem.at[0], place(z, other, exp)).wait_recv()

    started = []

    def go(copy, condition=None):
        if condition is None:
            copy.start()
        else:
            pl.when(condition)(copy.start)
        started.append((copy, condition))

    me = (z, core, exp)
    keep = pltpu.make_async_copy(shard_ref, unit(*me), own_sem.at[0])
    keep.start()
    go(send(shard_ref, me, line_sem.at[layers], place(z + 1, core, exp)), z < layers - 1)
    go(send(shard_ref, me, line_sem.at[layers + 1], place(z - 1, core, exp)), z > 0)
    go(send(shard_ref, me, x_sem.at[layers], place(z, core, x)))
    go(send(shard_ref, me, y_sem.at[layers], place(z, core, y)))
    go(send(shard_ref, me, core_sem.at[layers], place(z, other, exp)))

    slab = 16
    for k, zz in enumerate(order):
        for a in range(2):
            loads[2 * k + a].wait()
            src, dst = wides[a][1], halves[a][0]

            @pl.loop(0, src.shape[1] // slab)
            def _(i, zz=zz, src=src, dst=dst):
                at = pl.ds(pl.multiple_of(i * slab, slab), slab)
                dst[zz, at, :] = src[zz, at, :].astype(BF16)

    def half(a, source, p):
        src, dst = halves[a]
        n, cols = src.shape[1], src.shape[2] // 2
        return dst.at[pl.ds(source * n, n), pl.ds(pl.multiple_of(p * cols, 128), cols)]

    def mine(a, zz, p):
        src = halves[a][0]
        cols = src.shape[2] // 2
        return src.at[zz, :, pl.ds(pl.multiple_of(p * cols, 128), cols)]

    def layer(k):
        return jnp.where(z < layers // 2, k, layers - 1 - k)

    for k in range(layers):
        zz = layer(k)
        who = (zz, core, exp)

        @pl.when(zz != z)
        def _(who=who):
            arrive(who)

        go(send(unit(*who), who, line_sem.at[k], place(z + 1, core, exp)), (zz < z) & (z < layers - 1))
        go(send(unit(*who), who, line_sem.at[k], place(z - 1, core, exp)), (zz > z) & (z > 0))
        go(send(unit(*who), who, x_sem.at[k], place(z, core, x)), zz != z)
        go(send(unit(*who), who, y_sem.at[k], place(z, core, y)), zz != z)
        go(send(unit(*who), who, core_sem.at[k], place(z, other, exp)), zz != z)

    for a in range(2):
        pltpu.make_async_copy(mine(a, z, core), half(a, ctx, core), own_sem.at[1 + a]).start()

    def hand_out(a):
        for s, zz in enumerate(order):
            for p in range(2):
                if s == layers - 1 and p == 0:
                    continue
                pp = (core + p) % 2
                go(
                    remote(
                        mine(a, zz, pp),
                        half(a, ctx, pp),
                        half_send.at[a, s * 2 + p],
                        half_sem.at[a, ctx],
                        place(zz, pp, exp),
                    )
                )
        go(
            remote(
                mine(a, z, core),
                half(a, ctx, core),
                over_send.at[a, 2 * layers],
                over_sem.at[a, ctx],
                place(z, other, exp),
            )
        )

    hand_out(0)

    for k in range(layers):
        zz = layer(k)
        from_x, from_y = (zz, core, x), (zz, core, y)
        arrive(from_x)
        go(send(unit(*from_x), from_x, core_sem.at[layers + 1 + k], place(z, other, exp)))
        if k % 2 == 0:
            go(send(unit(*from_x), from_x, far_sem.at[k], place(z, core, y)))
        arrive(from_y)
        go(send(unit(*from_y), from_y, core_sem.at[2 * layers + 1 + k], place(z, other, exp)))
        if k % 2 == 1:
            go(send(unit(*from_y), from_y, far_sem.at[k], place(z, core, x)))
    for k in range(layers):
        far = (layer(k), core, y_of(x))
        arrive(far)
        go(send(unit(*far), far, core_sem.at[3 * layers + 1 + k], place(z, other, exp)))
    for ee in range(4):
        for zz in range(layers):
            arrive((zz, other, ee))
    keep.wait()
    save = pltpu.make_async_copy(weights, w_all_ref, own_sem.at[3])
    save.start()

    depth, count = tokens_ref.shape[1], tokens_ref.shape[0]
    qkv_cols, head_cols = projected_ref.shape[1], HEADS * HEAD
    inputs = tokens_ref[...].astype(F32)
    gain = jnp.concatenate(
        [
            jnp.transpose(weights[i * 128 : (i + 1) * 128, qkv_cols : qkv_cols + AUX].astype(F32))[0:1, :]
            for i in range(depth // 128)
        ],
        axis=1,
    )
    first_ref[...] = (inputs * norm_scale(inputs) * gain).astype(BF16)
    tile = 512

    @pl.loop(0, (qkv_cols - head_cols) // tile)
    def _(i):
        at = pl.ds(pl.multiple_of(head_cols + i * tile, tile), tile)
        projected_ref[:, at] = dot(first_ref[...], weights[:, at]).astype(BF16)

    def block(source):
        return kv_ref.at[pl.ds(pl.multiple_of(source * count, 16), count), :]

    def share(src, source, sem, device):
        return remote(src, block(source), sem, kv_sem.at[source], device)

    own = projected_ref.at[:, pl.ds(head_cols, qkv_cols - head_cols)]
    keep_kv = pltpu.make_async_copy(own, block(ctx), own_sem.at[0])
    keep_kv.start()
    go(share(own, ctx, kv_send.at[2 * layers], place(z + 1, core, exp)), z < layers - 1)
    go(share(own, ctx, kv_send.at[2 * layers + 1], place(z - 1, core, exp)), z > 0)
    go(share(own, ctx, kv_send.at[2 * layers + 2], place(z, other, exp)))

    @pl.loop(0, head_cols // tile)
    def _(i):
        at = pl.ds(pl.multiple_of(i * tile, tile), tile)
        projected_ref[:, at] = dot(first_ref[...], weights[:, at]).astype(BF16)

    for k in range(layers):
        zz = layer(k)
        source = zz * 2 + core

        @pl.when(zz != z)
        def _(source=source):
            share(block(source), source, kv_send.at[0], place(z, other, exp)).wait_recv()

        go(share(block(source), source, kv_send.at[k], place(z + 1, core, exp)), (zz < z) & (z < layers - 1))
        go(share(block(source), source, kv_send.at[k], place(z - 1, core, exp)), (zz > z) & (z > 0))
        go(share(block(source), source, kv_send.at[layers + k], place(z, other, exp)), zz != z)
        if k == layers // 2:
            hand_out(1)

    for s, zz in enumerate(order[::-1]):
        for p in range(2):
            if s == 0 and p == 0:
                continue
            source = zz * 2 + (core + p) % 2
            for a in range(2):
                remote(
                    half(a, source, core),
                    half(a, source, core),
                    half_send.at[a, 0],
                    half_sem.at[a, source],
                    place(z, other, exp),
                ).wait_recv()
                go(
                    remote(
                        half(a, source, core),
                        half(a, source, core),
                        over_send.at[a, s * 2 + p],
                        over_sem.at[a, source],
                        place(z, other, exp),
                    )
                )

    for zz in range(layers):
        source = zz * 2 + other
        share(block(source), source, kv_send.at[0], place(z, other, exp)).wait_recv()
    for source in range(2 * layers):
        for a in range(2):
            remote(
                half(a, source, other),
                half(a, source, other),
                half_send.at[a, 0],
                over_sem.at[a, source],
                place(z, other, exp),
            ).wait_recv()
    keep_kv.wait()
    save.wait()
    for a in range(2):
        pltpu.make_async_copy(mine(a, z, core), half(a, ctx, core), own_sem.at[1 + a]).wait()
    for copy, condition in started:
        if condition is None:
            copy.wait_send()
        else:
            pl.when(condition)(copy.wait_send)


def front(shard, expert_in, expert_out, tokens, qkv_cols):
    layers = expert_in.shape[0]
    rows_in, rows_out = expert_in.shape[1], expert_out.shape[1]
    depth, cols = shard.shape[0] * 8 * layers, shard.shape[1]
    count = tokens.shape[0]
    any_space = pl.BlockSpec(memory_space=pl.ANY)
    vmem = pl.BlockSpec(memory_space=pltpu.VMEM)
    dma = pltpu.SemaphoreType.DMA
    return pl.pallas_call(
        functools.partial(front_kernel, layers),
        out_shape=(
            jax.ShapeDtypeStruct((depth, cols), BF16),
            jax.ShapeDtypeStruct((rows_in * 2 * layers, expert_in.shape[2]), BF16),
            jax.ShapeDtypeStruct((rows_out * 2 * layers, expert_out.shape[2]), BF16),
            jax.ShapeDtypeStruct((count, depth), BF16),
            jax.ShapeDtypeStruct((count, qkv_cols), BF16),
            jax.ShapeDtypeStruct((count * 2 * layers, qkv_cols - HEADS * HEAD), BF16),
        ),
        in_specs=[any_space] * 3 + [vmem],
        out_specs=(any_space,) * 3 + (vmem, vmem, any_space),
        scratch_shapes=[
            pltpu.VMEM((depth, cols), BF16),
            pltpu.VMEM(expert_in.shape, F32),
            pltpu.VMEM(expert_out.shape, F32),
            pltpu.VMEM(expert_in.shape, BF16),
            pltpu.VMEM(expert_out.shape, BF16),
            dma((8 * layers,)),
            dma((layers + 2,)),
            dma((layers + 1,)),
            dma((layers + 1,)),
            dma((layers,)),
            dma((4 * layers + 1,)),
            dma((2, 2 * layers)),
            dma((2, 2 * layers)),
            dma((2, 2 * layers)),
            dma((2, 2 * layers + 1)),
            dma((2 * layers,)),
            dma((2 * layers + 3,)),
            dma((4,)),
            dma((2, layers)),
        ],
        compiler_params=pltpu.CompilerParams(
            collective_id=0, has_side_effects=True, vmem_limit_bytes=48 * 2**20
        ),
        name="front",
    )(shard, expert_in, expert_out, tokens)


def experts_kernel(
    layers,
    rows_ref,
    gates_ref,
    grads_ref,
    w_in_ref,
    w_down_ref,
    out_ref,
    back_ref,
    back_gates_ref,
    d_in_ref,
    d_down_ref,
    w_in,
    w_down,
    got,
    got_gates,
    x_s,
    grad_s,
    hidden_s,
    inner_s,
    back_s,
    back_gates_s,
    other_in,
    other_down,
    pair_in,
    pair_down,
    row_sem,
    row_send,
    gate_sem,
    gate_send,
    back_sem,
    back_send,
    back_gate_sem,
    back_gate_send,
    pair_sem,
    pair_send,
    load_sem,
):
    z, core, exp = lax.axis_index("le"), lax.axis_index("core"), lax.axis_index("exp")
    other = 1 - core
    columns = rows_ref.shape[0] // layers
    me = exp * layers + z
    cap, depth = rows_ref.shape[1], rows_ref.shape[2]
    chunk = columns * cap
    loads = [
        pltpu.make_async_copy(w_in_ref, w_in, load_sem.at[0]),
        pltpu.make_async_copy(w_down_ref, w_down, load_sem.at[1]),
    ]
    for load in loads:
        load.start()
    order = [(z + s) % layers for s in ((2, 1, 3, 0) if layers == 4 else range(layers))]
    peers = [
        (zz, (exp + t) % columns)
        for s, zz in enumerate(order)
        for t in range(columns)
        if not (s == layers - 1 and t == 0)
    ]
    meet([place(zz, core, ee) for zz, ee in peers] + [place(z, other, exp)])

    started = []

    def go(copy):
        copy.start()
        started.append(copy)

    keeps = [
        pltpu.make_async_copy(rows_ref.at[me], got.at[me], load_sem.at[2]),
        pltpu.make_async_copy(gates_ref.at[me], got_gates.at[me], load_sem.at[3]),
    ]
    for keep in keeps:
        keep.start()
    for k, (zz, ee) in enumerate(peers):
        there = ee * layers + zz
        go(remote(gates_ref.at[there], got_gates.at[me], gate_send.at[k], gate_sem.at[me], place(zz, core, ee)))
        go(remote(rows_ref.at[there], got.at[me], row_send.at[k], row_sem.at[me], place(zz, core, ee)))
    for load in loads + keeps:
        load.wait()

    eye = lax.broadcasted_iota(jnp.int32, (cap, 128), 0) == lax.broadcasted_iota(jnp.int32, (cap, 128), 1)
    tile = 256

    def tiles(i):
        return pl.ds(pl.multiple_of(i * tile, tile), tile)

    for k, zz in enumerate(order[::-1]):
        rows = pl.ds(k * chunk, chunk)
        for ee in range(columns):
            source = ee * layers + zz

            @pl.when(source != me)
            def _(source=source):
                here = place(z, other, exp)
                remote(got.at[source], got.at[source], row_send.at[0], row_sem.at[source], here).wait_recv()
                remote(
                    got_gates.at[source], got_gates.at[source], gate_send.at[0], gate_sem.at[source], here
                ).wait_recv()

            at = pl.ds(k * chunk + ee * cap, cap)
            x_s[at, :] = got[source]
            gate = jnp.sum(jnp.where(eye, got_gates[source, 0:1, :], 0.0), axis=1, keepdims=True)
            grad_s[at, :] = (gate * grads_ref[source].astype(F32)).astype(BF16)

        @pl.loop(0, FF // tile)
        def _(i, rows=rows):
            up_at = pl.ds(pl.multiple_of(FF + i * tile, tile), tile)
            gate = dot(x_s[rows, :], w_in[:, tiles(i)])
            up = dot(x_s[rows, :], w_in[:, up_at])
            grad_hidden = dot(grad_s[rows, :], w_down[tiles(i), :], ((1,), (1,)))
            sigmoid = jax.nn.sigmoid(gate)
            silu = gate * sigmoid
            hidden_s[rows, tiles(i)] = (silu * up).astype(BF16)
            inner_s[rows, tiles(i)] = (grad_hidden * up * sigmoid * (1.0 + gate * (1.0 - sigmoid))).astype(BF16)
            inner_s[rows, up_at] = (grad_hidden * silu).astype(BF16)

        @pl.loop(0, depth // tile)
        def _(i, rows=rows, zz=zz):
            back = dot(inner_s[rows, :], w_in[tiles(i), :], ((1,), (1,))).astype(BF16)
            for ee in range(columns):
                back_s[ee * layers + zz, :, tiles(i)] = back[ee * cap : (ee + 1) * cap]

        @pl.loop(0, depth // tile, init_carry=jnp.zeros((chunk, 128), F32))
        def gate_grads(i, sums, rows=rows, zz=zz):
            result = dot(hidden_s[rows, :], w_down[:, tiles(i)]).astype(BF16)
            parts = []
            for ee in range(columns):
                part = result[ee * cap : (ee + 1) * cap]
                out_ref[ee * layers + zz, :, tiles(i)] = part
                parts.append(part.astype(F32) * grads_ref[ee * layers + zz, :, tiles(i)].astype(F32))
            product = jnp.concatenate(parts, axis=0)
            return sums + product[:, :128] + product[:, 128:]

        gate_grads = jnp.sum(gate_grads, axis=1, keepdims=True)
        for ee in range(columns):
            there = ee * layers + zz
            column = gate_grads[ee * cap : (ee + 1) * cap]
            line = jnp.sum(jnp.where(eye, column, 0.0), axis=0, keepdims=True)
            back_gates_s[there] = jnp.broadcast_to(line, (8, 128))
            row_copy = remote(
                back_s.at[there],
                back_ref.at[me],
                back_send.at[there],
                back_sem.at[me],
                place(zz, core, ee),
            )
            gate_copy = remote(
                back_gates_s.at[there],
                back_gates_ref.at[me],
                back_gate_send.at[there],
                back_gate_sem.at[me],
                place(zz, core, ee),
            )

            @pl.when(there != me)
            def _(row_copy=row_copy, gate_copy=gate_copy):
                row_copy.start()
                gate_copy.start()

    own = [
        pltpu.make_async_copy(back_s.at[me], back_ref.at[me], load_sem.at[2]),
        pltpu.make_async_copy(back_gates_s.at[me], back_gates_ref.at[me], load_sem.at[3]),
    ]
    for copy in own:
        copy.start()

    half_in, half_down = d_in_ref.shape[1], d_down_ref.shape[1]

    def in_part(i, p):
        cols = pl.ds(pl.multiple_of(p * half_in, 128), half_in)
        return dot(x_s[:, tiles(i)], inner_s[:, cols], ((0,), (0,)))

    def down_part(i, p):
        cols = pl.ds(pl.multiple_of(p * half_down, 128), half_down)
        return dot(hidden_s[:, tiles(i)], grad_s[:, cols], ((0,), (0,)))

    @pl.loop(0, depth // tile)
    def _(i):
        other_in[tiles(i), :] = in_part(i, other).astype(BF16)

    go(remote(other_in, pair_in, pair_send.at[0], pair_sem.at[0], place(z, other, exp)))

    @pl.loop(0, FF // tile)
    def _(i):
        other_down[tiles(i), :] = down_part(i, other).astype(BF16)

    go(remote(other_down, pair_down, pair_send.at[1], pair_sem.at[1], place(z, other, exp)))
    remote(other_in, pair_in, pair_send.at[0], pair_sem.at[0], place(z, other, exp)).wait_recv()

    @pl.loop(0, depth // tile)
    def _(i):
        d_in_ref[tiles(i), :] = (in_part(i, core) + pair_in[tiles(i), :].astype(F32)).astype(BF16)

    remote(other_down, pair_down, pair_send.at[1], pair_sem.at[1], place(z, other, exp)).wait_recv()

    @pl.loop(0, FF // tile)
    def _(i):
        d_down_ref[tiles(i), :] = (down_part(i, core) + pair_down[tiles(i), :].astype(F32)).astype(BF16)

    for copy in own:
        copy.wait()
    for k, (zz, ee) in enumerate(peers):
        there = ee * layers + zz
        row_copy = remote(
            back_s.at[there], back_ref.at[there], back_send.at[there], back_sem.at[there], place(zz, core, ee)
        )
        gate_copy = remote(
            back_gates_s.at[there],
            back_gates_ref.at[there],
            back_gate_send.at[there],
            back_gate_sem.at[there],
            place(zz, core, ee),
        )
        row_copy.wait()
        gate_copy.wait()
    for copy in started:
        copy.wait_send()


def experts(rows, gates, grads, w_in, w_down, layers):
    count, cap, depth = rows.shape
    any_space = pl.BlockSpec(memory_space=pl.ANY)
    vmem = pl.BlockSpec(memory_space=pltpu.VMEM)
    dma = pltpu.SemaphoreType.DMA
    half_in = jax.ShapeDtypeStruct((depth, FF), BF16)
    half_down = jax.ShapeDtypeStruct((FF, depth // 2), BF16)
    return pl.pallas_call(
        functools.partial(experts_kernel, layers),
        out_shape=(
            jax.ShapeDtypeStruct(rows.shape, BF16),
            jax.ShapeDtypeStruct(rows.shape, BF16),
            jax.ShapeDtypeStruct(gates.shape, F32),
            half_in,
            half_down,
        ),
        in_specs=[any_space, any_space, vmem, any_space, any_space],
        out_specs=(vmem, any_space, any_space, vmem, vmem),
        scratch_shapes=[
            pltpu.VMEM(w_in.shape, BF16),
            pltpu.VMEM(w_down.shape, BF16),
            pltpu.VMEM(rows.shape, BF16),
            pltpu.VMEM(gates.shape, F32),
            pltpu.VMEM((count * cap, depth), BF16),
            pltpu.VMEM((count * cap, depth), BF16),
            pltpu.VMEM((count * cap, FF), BF16),
            pltpu.VMEM((count * cap, 2 * FF), BF16),
            pltpu.VMEM(rows.shape, BF16),
            pltpu.VMEM(gates.shape, F32),
            pltpu.VMEM(half_in.shape, BF16),
            pltpu.VMEM(half_down.shape, BF16),
            pltpu.VMEM(half_in.shape, BF16),
            pltpu.VMEM(half_down.shape, BF16),
        ]
        + [dma((count,))] * 8
        + [dma((2,)), dma((2,)), dma((4,))],
        compiler_params=pltpu.CompilerParams(
            collective_id=2, has_side_effects=True, vmem_limit_bytes=60 * 2**20
        ),
        name="experts",
    )(rows, gates, grads, w_in, w_down)


def add_rows(total, part, rows):
    slab = 16

    @pl.loop(0, rows // slab)
    def _(i):
        at = pl.ds(pl.multiple_of(i * slab, slab), slab)
        total[at, :] = (total[at, :].astype(F32) + part[at, :].astype(F32)).astype(BF16)


class Chain:
    def __init__(self, layers, z, above, below, own, rows, up, down, sems, sends):
        self.layers, self.z, self.above, self.below = layers, z, above, below
        self.own, self.rows, self.up, self.down = own, rows, up, down
        self.sems, self.sends = sems, sends

    def rise(self, d):
        return remote(self.own(d), self.up.at[d], self.sends.at[0, d], self.sems.at[0, d], self.above)

    def fall(self, d):
        return remote(self.own(d), self.down.at[d], self.sends.at[1, d], self.sems.at[1, d], self.below)

    def ends(self):
        for step in range(self.layers - 1):
            pl.when(self.z == 0)(self.rise(self.layers - 1 - step).start)
            pl.when(self.z == self.layers - 1)(self.fall(step).start)

    def middle(self):
        z, last = self.z, self.layers - 1

        def pass_on(copy, d, buffer):
            copy.wait_recv()
            add_rows(self.own(d), buffer.at[d], self.rows)
            copy.start()

        def both(first_half):
            for step in range(last):
                high, low = last - step, step

                def upward(high=high):
                    pl.when((z > 0) & (z < high))(lambda: pass_on(self.rise(high), high, self.up))

                def downward(low=low):
                    pl.when((z < last) & (z > low))(lambda: pass_on(self.fall(low), low, self.down))

                for turn in (upward, downward) if first_half else (downward, upward):
                    turn()

        pl.when(z <= last // 2)(lambda: both(True))
        pl.when(z > last // 2)(lambda: both(False))

    def finish(self):
        z, last = self.z, self.layers - 1

        @pl.when(z > 0)
        def _():
            self.rise(z).wait_recv()
            add_rows(self.own(z), self.up.at[z], self.rows)

        @pl.when(z < last)
        def _():
            self.fall(z).wait_recv()
            add_rows(self.own(z), self.down.at[z], self.rows)

    def wait_sends(self):
        for d in range(self.layers):
            pl.when(self.z < d)(self.rise(d).wait_send)
            pl.when(self.z > d)(self.fall(d).wait_send)


def finish_kernel(
    layers,
    grad_kv_ref,
    grad_q_ref,
    first_ref,
    tokens_ref,
    gain_ref,
    middle_ref,
    w_all_ref,
    attended_ref,
    second_ref,
    logits_ref,
    gain_moe_ref,
    in_ref,
    down_ref,
    d_tokens_ref,
    d_qkv_ref,
    d_late_ref,
    d_aux_ref,
    got_in_ref,
    got_down_ref,
    weights,
    projected,
    grad_first,
    kv_own,
    kv_pair,
    kv_up,
    kv_down,
    late_both,
    late_pair,
    late_near,
    late_up,
    late_down,
    q_both,
    q_pair,
    q_near,
    q_up,
    q_down,
    k_both,
    k_pair,
    k_near,
    k_up,
    k_down,
    load_sem,
    kv_sem,
    kv_send,
    half_sem,
    half_send,
    pair_sem,
    pair_send,
    near_sem,
    near_send,
    line_sem,
    line_send,
):
    z, core, exp = lax.axis_index("le"), lax.axis_index("core"), lax.axis_index("exp")
    other = 1 - core
    partner = place(z, other, exp)
    above, below = place(z + 1, core, exp), place(z - 1, core, exp)
    x, y = x_of(exp), y_of(exp)
    mates = (x, y, y_of(x))
    ctx = z * 2 + core
    rows = d_qkv_ref.shape[0]
    count = tokens_ref.shape[0]
    head_cols = HEADS * HEAD
    qkv_cols = d_qkv_ref.shape[1]
    kv_cols = qkv_cols - head_cols

    loads = []

    def load(src, dst):
        copy = pltpu.make_async_copy(src, dst, load_sem.at[len(loads)])
        copy.start()
        loads.append(copy)
        return copy

    kv_loads = [
        load(grad_kv_ref.at[pl.ds(pl.multiple_of((d * 2 + core) * count, 16), count), :], kv_own.at[d])
        for d in range(layers)
    ]
    depth = w_all_ref.shape[0]

    def weights_part(i):
        part = w_all_ref.at[pl.ds(i * depth // 2, depth // 2), pl.ds(0, qkv_cols)]
        return pltpu.make_async_copy(part, weights, load_sem.at[2 * layers + 2])

    weights_part(0).start()
    meet(
        [
            place((z + s) % layers, (core + p) % 2, exp)
            for s in range(layers)
            for p in range(2)
            if s + p > 0
        ]
        + [place(z, core, mate) for mate in mates]
    )
    started = []

    def go(copy):
        copy.start()
        started.append(copy)

    for d in range(layers):
        go(
            remote(
                grad_kv_ref.at[pl.ds(pl.multiple_of((d * 2 + other) * count, 16), count), :],
                kv_pair.at[d],
                kv_send.at[2, d],
                kv_sem.at[2, d],
                partner,
            )
        )
    for d in range(layers):
        kv_loads[d].wait()
        remote(kv_pair.at[d], kv_pair.at[d], kv_send.at[2, d], kv_sem.at[2, d], partner).wait_recv()
        add_rows(kv_own.at[d], kv_pair.at[d], count)
    kv_line = Chain(
        layers, z, above, below, lambda d: kv_own.at[d], count, kv_up, kv_down, kv_sem, kv_send
    )
    kv_line.ends()

    def near_copy(i, near, own, d, m, target):
        return remote(
            own.at[d, pl.ds(pl.multiple_of(target * rows, 16), rows), :],
            near.at[m, d],
            near_send.at[i, m, d],
            near_sem.at[i, m, d],
            place(z, core, mates[m]),
        )

    def pair_sums(i, own, pair, near):
        for d in range(layers):
            remote(pair.at[d], pair.at[d], pair_send.at[i, d], pair_sem.at[i, d], partner).wait_recv()
            add_rows(own.at[d], pair.at[d], 4 * rows)
            for m in range(3):
                go(near_copy(i, near, own, d, m, mates[m]))

    def near_sums(i, own, near):
        for d in range(layers):
            for m in range(3):
                near_copy(i, near, own, d, m, exp).wait_recv()
            mine = own.at[d, pl.ds(pl.multiple_of(exp * rows, 16), rows), :]

            @pl.loop(0, rows // 16)
            def _(r, mine=mine, d=d):
                at = pl.ds(pl.multiple_of(r * 16, 16), 16)
                total = mine[at, :].astype(F32)
                for m in range(3):
                    total = total + near[m, d, at, :].astype(F32)
                mine[at, :] = total.astype(BF16)

    def line_of(i, own, up, down):
        return Chain(
            layers,
            z,
            above,
            below,
            lambda d: own.at[d, pl.ds(pl.multiple_of(exp * rows, 16), rows), :],
            rows,
            up,
            down,
            line_sem.at[i],
            line_send.at[i],
        )

    def outer_product(both, cols, left, right, gains=None):
        for d in range(layers):
            block = left[:, d * 8 * rows : (d + 1) * 8 * rows]
            part = dot(block, right, ((0,), (0,)))
            if gains is not None:
                turned = [
                    jnp.transpose(jnp.broadcast_to(gains[:, at : at + 128], (128, 128)))
                    for at in range(d * 8 * rows, (d + 1) * 8 * rows, 128)
                ]
                lane = lax.broadcasted_iota(jnp.int32, part.shape, 1)
                part = jnp.where(lane == 0, jnp.concatenate(turned, axis=0), part)
            part = part.astype(BF16)
            both[0, d, :, cols] = part[: 4 * rows]
            both[1, d, :, cols] = part[4 * rows :]

    def pair_up(i, both, pair):
        for d in range(layers):
            go(remote(both.at[other, d], pair.at[d], pair_send.at[i, d], pair_sem.at[i, d], partner))

    arrays = ((in_ref, got_in_ref), (down_ref, got_down_ref))

    def mine(a, owner):
        n = arrays[a][1].shape[1]
        return arrays[a][0].at[pl.ds(owner * n, n), :]

    def half(a, expert, p):
        cols = arrays[a][0].shape[1]
        return arrays[a][1].at[expert, :, pl.ds(pl.multiple_of(p * cols, 128), cols)]

    for a in range(2):
        load(mine(a, ctx), half(a, z, core))

    def hand_back(p):
        for s in (2, 1, 3, 0) if layers == 4 else range(layers):
            if s + p == 0:
                continue
            zz, pp = (z + s) % layers, (core + p) % 2
            for a in range(2):
                go(
                    remote(
                        mine(a, zz * 2 + pp),
                        half(a, z, core),
                        half_send.at[a, s * 2 + p],
                        half_sem.at[a, ctx],
                        place(zz, pp, exp),
                    )
                )

    outer_product(q_both, slice(0, head_cols), first_ref, grad_q_ref[...])
    pair_up(1, q_both, q_pair)
    width = middle_ref.shape[1]
    outer_product(late_both, slice(0, width), attended_ref, middle_ref[...].astype(BF16))
    outer_product(late_both, slice(width, width + AUX), second_ref, logits_ref[...], gain_moe_ref[...])
    pair_up(0, late_both, late_pair)
    late_own = late_both.at[core]
    q_own = q_both.at[core]
    pair_sums(1, q_own, q_pair, q_near)
    pair_sums(0, late_own, late_pair, late_near)
    kv_line.middle()
    kv_line.finish()

    hand_back(0)

    projected[:, :head_cols] = grad_q_ref[...]
    projected[:, head_cols:] = kv_own[z]
    outer_product(k_both, slice(0, kv_cols), first_ref, projected[:, head_cols:])
    tile = 256
    for i in range(2):
        weights_part(i).wait()

        @pl.loop(0, depth // 2 // tile)
        def _(j, i=i):
            at = pl.ds(pl.multiple_of(j * tile, tile), tile)
            to = pl.ds(pl.multiple_of(i * depth // 2 + j * tile, tile), tile)
            grad_first[:, to] = dot(projected[...], weights[at, :], ((1,), (1,)))

        if i == 0:
            weights_part(1).start()

    inputs = tokens_ref[...].astype(F32)
    scale = norm_scale(inputs)
    norm = inputs * scale
    grad = grad_first[...]
    grad_gain = jnp.sum(grad * norm, axis=0, keepdims=True)
    for d in range(layers):
        block = jnp.concatenate(
            [
                jnp.transpose(jnp.broadcast_to(grad_gain[:, at : at + 128], (128, 128)))
                for at in range(d * 8 * rows, (d + 1) * 8 * rows, 128)
            ],
            axis=0,
        ).astype(BF16)
        k_both[0, d, :, kv_cols:] = block[: 4 * rows]
        k_both[1, d, :, kv_cols:] = block[4 * rows :]
    pair_up(2, k_both, k_pair)
    grad = grad * gain_ref[...]
    d_tokens_ref[...] = (
        middle_ref[...] + scale * (grad - norm * jnp.mean(grad * norm, axis=-1, keepdims=True))
    ).astype(BF16)
    k_own = k_both.at[core]
    pair_sums(2, k_own, k_pair, k_near)

    late_line = line_of(0, late_own, late_up, late_down)
    q_line = line_of(1, q_own, q_up, q_down)
    k_line = line_of(2, k_own, k_up, k_down)
    near_sums(1, q_own, q_near)
    q_line.ends()
    near_sums(0, late_own, late_near)
    late_line.ends()
    q_line.middle()
    near_sums(2, k_own, k_near)
    k_line.ends()
    late_line.middle()
    k_line.middle()
    mine_rows = pl.ds(pl.multiple_of(exp * rows, 16), rows)
    q_line.finish()
    d_qkv_ref[:, :head_cols] = q_both[core, z, mine_rows, :].astype(F32)
    late_line.finish()
    d_late_ref[...] = late_both[core, z, mine_rows, :].astype(F32)
    k_line.finish()
    hand_back(1)
    last = k_both[core, z, mine_rows, :].astype(F32)
    d_qkv_ref[:, head_cols:] = last[:, :kv_cols]
    d_aux_ref[...] = last[:, kv_cols:]

    for source in range(2 * layers):
        for a in range(2):

            @pl.when(source != ctx)
            def _(source=source, a=a):
                remote(
                    half(a, source // 2, source % 2),
                    half(a, source // 2, source % 2),
                    half_send.at[a, 0],
                    half_sem.at[a, source],
                    partner,
                ).wait_recv()

    for copy in loads[-2:]:
        copy.wait()
    for line in (kv_line, late_line, q_line, k_line):
        line.wait_sends()
    for copy in started:
        copy.wait_send()


def finish(
    grad_kv,
    grad_q,
    first,
    tokens,
    gain,
    middle,
    w_all,
    attended,
    second,
    grad_logits,
    gain_moe,
    grad_in,
    grad_down,
    layers,
):
    depth, count = first.shape[1], first.shape[0]
    rows = depth // (8 * layers)
    qkv_cols = grad_q.shape[1] + grad_kv.shape[1]
    n_in, n_down = grad_in.shape[0] // (2 * layers), grad_down.shape[0] // (2 * layers)
    any_space = pl.BlockSpec(memory_space=pl.ANY)
    vmem = pl.BlockSpec(memory_space=pltpu.VMEM)
    dma = pltpu.SemaphoreType.DMA

    def sums(cols):
        return [
            pltpu.VMEM((2, layers, 4 * rows, cols), BF16),
            pltpu.VMEM((layers, 4 * rows, cols), BF16),
            pltpu.VMEM((3, layers, rows, cols), BF16),
            pltpu.VMEM((layers, rows, cols), BF16),
            pltpu.VMEM((layers, rows, cols), BF16),
        ]

    return pl.pallas_call(
        functools.partial(finish_kernel, layers),
        out_shape=(
            jax.ShapeDtypeStruct((count, depth), BF16),
            jax.ShapeDtypeStruct((rows, qkv_cols), F32),
            jax.ShapeDtypeStruct((rows, depth + AUX), F32),
            jax.ShapeDtypeStruct((rows, AUX), F32),
            jax.ShapeDtypeStruct((layers, n_in, 2 * grad_in.shape[1]), BF16),
            jax.ShapeDtypeStruct((layers, n_down, 2 * grad_down.shape[1]), BF16),
        ),
        in_specs=[any_space] + [vmem] * 5 + [any_space] + [vmem] * 4 + [any_space] * 2,
        out_specs=(vmem,) * 4 + (any_space,) * 2,
        scratch_shapes=[
            pltpu.VMEM((depth // 2, qkv_cols), BF16),
            pltpu.VMEM((count, qkv_cols), BF16),
            pltpu.VMEM((count, depth), F32),
        ]
        + [pltpu.VMEM((layers, count, grad_kv.shape[1]), BF16)] * 4
        + sums(depth + AUX)
        + sums(grad_q.shape[1])
        + sums(grad_kv.shape[1] + AUX)
        + [
            dma((2 * layers + 3,)),
            dma((3, layers)),
            dma((3, layers)),
            dma((2, 2 * layers)),
            dma((2, 2 * layers)),
            dma((3, layers)),
            dma((3, layers)),
            dma((3, 3, layers)),
            dma((3, 3, layers)),
            dma((3, 2, layers)),
            dma((3, 2, layers)),
        ],
        compiler_params=pltpu.CompilerParams(
            collective_id=1, has_side_effects=True, vmem_limit_bytes=60 * 2**20
        ),
        name="finish",
    )(
        grad_kv,
        grad_q,
        first,
        tokens,
        gain,
        middle,
        w_all,
        attended,
        second,
        grad_logits,
        gain_moe,
        grad_in,
        grad_down,
    )


CTX = ("le", "rep", "core")
ALL = ("le", "rep", "core", "exp")
OWNERS = ("exp", "le")


def on_device(
    tokens,
    cotangent,
    routes,
    lengths,
    block_order,
    gain_attn,
    qkv_weight,
    out_weight,
    gain_moe,
    router_weight,
    expert_in,
    expert_out,
):
    tok_rows = tokens.shape[1]
    head_width = HEADS * HEAD
    exp_local = expert_in.shape[0]
    n_ctx = D // expert_in.shape[1]
    copies = n_ctx // exp_local
    n_exp = EXPERTS // exp_local
    in_rows, out_rows = expert_in.shape[1], expert_out.shape[1]

    cols = qkv_weight.shape[1]
    aux = jnp.concatenate([gain_attn[:, None], gain_moe[:, None], router_weight], axis=1)
    aux = jnp.pad(aux, ((0, 0), (0, AUX - aux.shape[1])))
    shard = jnp.concatenate([qkv_weight, aux, out_weight], axis=1).astype(BF16)
    special = (copies, exp_local, n_exp) == (2, 4, 4)
    if special:
        w_all, w_in, w_down, first, projected, kv = front(shard, expert_in, expert_out, tokens[0], cols)
    else:
        w_all = lax.all_gather(shard, ALL, axis=0, tiled=True)

        def to_owner(weight):
            rows, width = weight.shape[1:]
            halves = weight.astype(BF16).reshape(exp_local, rows, 2, width // 2).transpose(0, 2, 1, 3)
            halves = jnp.broadcast_to(
                halves[:, None], (exp_local, copies // 2, 2, rows, width // 2)
            ).reshape(n_ctx, rows, width // 2)
            mine = lax.all_to_all(halves, CTX, split_axis=0, concat_axis=0, tiled=True)
            return lax.all_gather(mine.reshape(n_ctx * rows, width // 2), "core", axis=1, tiled=True)

        w_in = to_owner(expert_in)
        w_down = to_owner(expert_out)
    w_qkv = w_all[:, :cols]
    aux_all = w_all[:, cols : cols + AUX]
    w_attn_out = w_all[:, cols + AUX :]
    gain_first = aux_all[:, 0].astype(F32)
    gain_second = aux_all[:, 1].astype(F32)
    w_router = aux_all[:, 2 : 2 + EXPERTS]

    route_hot = (
        routes[0][:, :, None] == jnp.arange(EXPERTS, dtype=jnp.int32)[None, None, :]
    ).astype(F32)
    flat_hot = route_hot.reshape(tok_rows * 2, EXPERTS).astype(BF16)
    order = jnp.arange(tok_rows * 2, dtype=jnp.int32)
    earlier = (order[:, None] > order[None, :]).astype(BF16)
    ranks = dot(earlier, flat_hot)
    slot_index = jnp.sum(ranks * flat_hot.astype(F32), axis=1).astype(jnp.int32)
    target = (routes[0].reshape(tok_rows * 2) * CAP + slot_index).reshape(tok_rows, 2)
    slots = jnp.arange(EXPERTS * CAP, dtype=jnp.int32)
    picks = [(target[:, k : k + 1] == slots[None, :]) for k in range(2)]
    sends = [(target[:, k][None, :] == slots[:, None]) for k in range(2)]
    send_hot = (sends[0] | sends[1]).astype(BF16)

    def to_experts(rows):
        return lax.all_to_all(
            rows.reshape((EXPERTS, CAP) + rows.shape[1:]),
            OWNERS,
            split_axis=0,
            concat_axis=0,
            tiled=True,
        ).reshape(rows.shape)

    inputs = tokens[0].astype(F32)
    scale_first = norm_scale(inputs)
    norm_first = inputs * scale_first
    if not special:
        first = (norm_first * gain_first).astype(BF16)
        projected = dot(first, w_qkv).astype(BF16)
        kv = lax.all_gather(projected[:, head_width:], CTX, axis=0, tiled=True)
    kv, grad_y_send = lax.optimization_barrier((kv, dot(send_hot, cotangent[0]).astype(BF16)))
    grad_y_rows = to_experts(grad_y_send)
    mine = (lax.axis_index(CTX) * (tok_rows // BLK)).astype(jnp.int32).reshape(1)
    exact, attended, lse = attend(lengths, block_order, mine, projected, kv)
    middle = inputs + dot(attended, w_attn_out)
    scale_second = norm_scale(middle)
    norm_second = middle * scale_second
    second = (norm_second * gain_second).astype(BF16)
    logits = dot(second, w_router)
    chosen = jnp.sum(route_hot * logits[:, None, :], axis=-1)
    gates = jax.nn.softmax(chosen, axis=-1)

    gate_rows = jnp.sum(
        jnp.where(sends[0], gates[:, 0][None, :], 0.0) + jnp.where(sends[1], gates[:, 1][None, :], 0.0),
        axis=1,
        keepdims=True,
    )
    if special:
        slot_gates = jnp.broadcast_to(
            jnp.pad(gate_rows.reshape(EXPERTS, 1, CAP), ((0, 0), (0, 0), (0, 128 - CAP))), (EXPERTS, 8, 128)
        )
        expert_rows, grad_returned, gate_grads, grad_in, grad_down = experts(
            dot(send_hot, second).astype(BF16).reshape(EXPERTS, CAP, D),
            slot_gates,
            grad_y_rows.reshape(EXPERTS, CAP, D),
            w_in,
            w_down,
            exp_local,
        )
        returned = to_experts(expert_rows.reshape(EXPERTS * CAP, D))
        grad_returned = grad_returned.reshape(EXPERTS * CAP, D)
        gate_grads = gate_grads[:, 0, :CAP].reshape(1, EXPERTS * CAP)
    else:
        def in_parts(column):
            high = lax.reduce_precision(column, 8, 7)
            rest = column - high
            mid = lax.reduce_precision(rest, 8, 7)
            parts = jnp.concatenate([high, mid, rest - mid], axis=1).astype(BF16)
            return jnp.pad(parts, ((0, 0), (0, AUX - 3)))

        gate_parts = in_parts(gate_rows)
        payload = to_experts(
            jnp.concatenate([dot(send_hot, second).astype(BF16), gate_parts], axis=1)
        )
        received = payload[:, :D]
        gate_got = jnp.sum(payload[:, D : D + 3].astype(F32), axis=1, keepdims=True)

        gate_up = dot(received, w_in)
        gate_part = gate_up[:, :FF]
        up_part = gate_up[:, FF:]
        sigmoid_gate = jax.nn.sigmoid(gate_part)
        silu_gate = gate_part * sigmoid_gate
        hidden = (silu_gate * up_part).astype(BF16)
        expert_rows = dot(hidden, w_down)
        expert_rows = expert_rows.astype(BF16)
        grad_y_rows = grad_y_rows.astype(F32)
        returned = to_experts(expert_rows)

        grad_rows = (gate_got * grad_y_rows).astype(BF16)
        gate_grad_parts = in_parts(
            jnp.sum(grad_y_rows * expert_rows.astype(F32), axis=1, keepdims=True)
        )
        half_d = D // 2
        grad_hidden = dot(grad_rows, w_down, ((1,), (1,)))
        grad_gate = (
            grad_hidden * up_part * sigmoid_gate * (1.0 + gate_part * (1.0 - sigmoid_gate))
        ).astype(BF16)
        grad_up = (grad_hidden * silu_gate).astype(BF16)
        grad_gate_up = jnp.concatenate([grad_gate, grad_up], axis=1)
        grad_back = dot(grad_gate_up, w_in, ((1,), (1,)))
        grad_returned = to_experts(jnp.concatenate([grad_back.astype(BF16), gate_grad_parts], axis=1))

        grad_in = jnp.stack(
            [dot(received, grad_gate, ((0,), (0,))), dot(received, grad_up, ((0,), (0,)))]
        ).astype(BF16)
        grad_down = jnp.stack(
            [
                dot(hidden, grad_rows[:, :half_d], ((0,), (0,))),
                dot(hidden, grad_rows[:, half_d:], ((0,), (0,))),
            ]
        ).astype(BF16)

        grad_in = lax.psum_scatter(grad_in, "core", scatter_dimension=0, tiled=True)[0]
        grad_down = lax.psum_scatter(grad_down, "core", scatter_dimension=0, tiled=True)[0]
        grad_returned, grad_in, grad_down = lax.optimization_barrier((grad_returned, grad_in, grad_down))
        gate_grads = jnp.sum(grad_returned[:, D:].astype(F32), axis=1).reshape(1, EXPERTS * CAP)
        grad_returned = grad_returned[:, :D]

    grad_y = cotangent[0].astype(F32)
    pick_hot = [p.astype(BF16) for p in picks]
    grad_gates = jnp.concatenate(
        [jnp.sum(jnp.where(p, gate_grads, 0.0), axis=1, keepdims=True) for p in picks], axis=1
    )
    grad_chosen = gates * (grad_gates - jnp.sum(gates * grad_gates, axis=-1, keepdims=True))
    grad_logits = jnp.sum(grad_chosen[:, :, None] * route_hot, axis=1).astype(BF16)
    grad_second = dot(pick_hot[0] + pick_hot[1], grad_returned) + dot(
        grad_logits, w_router, ((1,), (1,))
    )
    grad_gain_second = jnp.sum(grad_second * norm_second, axis=0)
    grad_norm_second = grad_second * gain_second
    grad_middle = grad_y + scale_second * (
        grad_norm_second
        - norm_second * jnp.mean(grad_norm_second * norm_second, axis=-1, keepdims=True)
    )
    grad_branch = grad_middle.astype(BF16)
    grad_attended = dot(grad_branch, w_attn_out, ((1,), (1,))).astype(BF16)
    grad_queries, grad_kv = attend_back(
        lengths, block_order, mine, projected, kv, grad_attended, lse, exact
    )
    grad_queries, grad_kv, returned = lax.optimization_barrier((grad_queries, grad_kv, returned))
    picked = [dot(p, returned) for p in pick_hot]
    block_out = (middle + gates[:, 0:1] * picked[0] + gates[:, 1:2] * picked[1]).astype(BF16)
    if special:
        grad_inputs, sum_qkv, sum_late, sum_aux, sum_in, sum_down = finish(
            grad_kv,
            grad_queries,
            first,
            tokens[0],
            gain_first[None, :],
            grad_middle,
            w_all,
            attended,
            second,
            jnp.pad(grad_logits, ((0, 0), (1, AUX - 1 - EXPERTS))),
            grad_gain_second[None, :],
            grad_in,
            grad_down,
            exp_local,
        )
    else:
        grad_router = dot(second, grad_logits, ((0,), (0,)))
        grad_attn_out = dot(attended, grad_branch, ((0,), (0,)))
        late = jnp.concatenate([grad_gain_second[:, None], grad_router], axis=1)
        late = jnp.pad(late, ((0, 0), (0, AUX - late.shape[1])))
        late = jnp.concatenate([grad_attn_out.astype(BF16), late.astype(BF16)], axis=1)
        grad_kv = lax.psum_scatter(grad_kv, CTX, scatter_dimension=0, tiled=True)
        grad_projected = jnp.concatenate([grad_queries, grad_kv], axis=1)
        grad_qkv = dot(first, grad_projected, ((0,), (0,)))
        grad_first = dot(grad_projected, w_qkv, ((1,), (1,)))
        grad_gain_first = jnp.sum(grad_first * norm_first, axis=0)
        grad_norm_first = grad_first * gain_first
        grad_inputs = grad_middle + scale_first * (
            grad_norm_first
            - norm_first * jnp.mean(grad_norm_first * norm_first, axis=-1, keepdims=True)
        )
        grad_inputs = grad_inputs.astype(BF16)
        last = jnp.pad(grad_gain_first[:, None], ((0, 0), (0, AUX - 1)))
        part = jnp.concatenate([grad_qkv.astype(BF16), last.astype(BF16), late], axis=1)
        total = lax.psum_scatter(part, ALL, scatter_dimension=0, tiled=True).astype(F32)
        sum_qkv, sum_aux, sum_late = total[:, :cols], total[:, cols : cols + AUX], total[:, cols + AUX :]

        def to_rows(half, rows):
            width = half.shape[1]
            got = lax.all_to_all(
                half.reshape(n_ctx, rows, width), CTX, split_axis=0, concat_axis=0, tiled=True
            ).astype(F32)
            got = got.reshape(exp_local, copies // 2, 2, rows, width).sum(axis=1)
            return got.transpose(0, 2, 1, 3).reshape(exp_local, rows, 2 * width)

        sum_in = to_rows(grad_in, in_rows)
        sum_down = to_rows(grad_down, out_rows)
    return (
        block_out[None],
        grad_inputs[None],
        sum_aux[:, 0],
        sum_qkv,
        sum_late[:, :D],
        sum_late[:, D],
        sum_late[:, D + 1 : D + 1 + EXPERTS],
        sum_in.astype(F32),
        sum_down.astype(F32),
    )


def solution(mesh):
    n_ctx, n_exp = mesh.shape["ctx"], mesh.shape["exp"]
    exp_local = EXPERTS // n_exp
    copies = n_ctx // exp_local
    inner = Mesh(mesh.devices.reshape(exp_local, copies // 2, 2, n_exp), ALL)
    by_token = P("exp", CTX, None)
    by_row = P(ALL, None)
    by_expert = P("exp", CTX, None)
    return jax.shard_map(
        on_device,
        mesh=inner,
        in_specs=(
            by_token,
            by_token,
            by_token,
            P("exp", None),
            P("exp", None),
            P(ALL),
            by_row,
            by_row,
            P(ALL),
            by_row,
            by_expert,
            by_expert,
        ),
        out_specs=(
            by_token,
            by_token,
            P(ALL),
            by_row,
            by_row,
            P(ALL),
            by_row,
            by_expert,
            by_expert,
        ),
        check_vma=False,
    )
```

```python
import functools

import jax
import jax.numpy as jnp
from jax import lax
from jax.experimental import pallas as pl
from jax.experimental.pallas import tpu as pltpu
from jax.sharding import Mesh
from jax.sharding import PartitionSpec as P

D = 1536
HEADS = 24
KV_HEADS = 8
HEAD = 64
GROUP = HEADS // KV_HEADS
FF = 1024
EXPERTS = 16
BLK = 128
CAP = 48
AUX = 128

epsilon = 1e-05
far_negative = -1e30
start_max = -1e29
F32 = jnp.float32
BF16 = jnp.bfloat16


def norm_scale(values):
    return lax.rsqrt(jnp.mean(values * values, axis=-1, keepdims=True) + epsilon)


def dot(a, b, dims=((1,), (0,))):
    return lax.dot_general(a, b, (dims, ((), ())), preferred_element_type=F32)


def lane_half(shape, half):
    lane = lax.broadcasted_iota(jnp.int32, shape, 1)
    return (lane >= HEAD) if half else (lane < HEAD)


def head_tiles(ref, rows, group, scale):
    tiles = []
    for i in range(GROUP):
        head = group * GROUP + i
        tile = ref[rows, (head // 2) * 128 : (head // 2 + 1) * 128].astype(F32)
        if head % 2 != group % 2:
            tile = pltpu.roll(tile, HEAD, 1)
        tile = jnp.where(lane_half(tile.shape, group % 2), tile * scale, 0.0)
        tiles.append(tile.astype(BF16))
    return jnp.concatenate(tiles, axis=0)


def block_visibility(lengths_ref, query_block, key_block, parts):
    lanes = lax.broadcasted_iota(jnp.int32, (1, BLK), 1)
    query_pos = query_block * BLK + lanes
    start = jnp.zeros((1, BLK), jnp.int32)
    bound = jnp.int32(0)
    for s in range(parts - 1):
        bound = bound + lengths_ref[0, s]
        start = jnp.where(query_pos >= bound, bound, start)
    key_pos = key_block * BLK + lax.broadcasted_iota(jnp.int32, (BLK, BLK), 0)
    one = ((key_pos >= start) & (key_pos <= query_pos)).astype(jnp.int32)
    return jnp.concatenate([one] * GROUP, axis=1) > 0


def first_row_start(lengths_ref, query_block, parts):
    start = jnp.int32(0)
    bound = jnp.int32(0)
    for s in range(parts - 1):
        bound = bound + lengths_ref[0, s]
        start = jnp.where(query_block * BLK >= bound, bound, start)
    return start


def attend_kernel(
    parts, lengths_ref, order_ref, mine_ref, q_ref, kv_ref, exact_ref, out_ref, lse_ref, q_s, m_s, acc_s
):
    width = KV_HEADS * HEAD
    for qb in range(q_ref.shape[0] // BLK):
        rows = pl.ds(qb * BLK, BLK)
        for g in range(KV_HEADS):
            q_s[g] = head_tiles(q_ref, rows, g, HEAD**-0.5)
            m_s[g] = jnp.full((8, GROUP * BLK), start_max, F32)
            acc_s[g] = jnp.zeros((BLK, GROUP * BLK), F32)
        query_block = order_ref[0, mine_ref[0] + qb]
        first = first_row_start(lengths_ref, query_block, parts)

        @pl.loop(0, order_ref.shape[1])
        def _(kb):
            key_block = order_ref[0, kb]

            @pl.when((key_block <= query_block) & (key_block * BLK + BLK > first))
            def _():
                seen = block_visibility(lengths_ref, query_block, key_block, parts)
                key_rows = pl.ds(kb * BLK, BLK)
                for g in range(KV_HEADS):
                    lanes = pl.ds((g // 2) * 128, 128)
                    keys = kv_ref[key_rows, lanes]
                    values = kv_ref[key_rows, pl.ds(width + (g // 2) * 128, 128)]
                    values = jnp.where(lane_half(values.shape, g % 2), values, jnp.ones_like(values))
                    scores = dot(keys, q_s[g], ((1,), (1,)))
                    scores = jnp.where(seen, scores, far_negative)
                    old = m_s[g, 0:1, :]
                    new = jnp.maximum(old, jnp.max(scores, axis=0, keepdims=True))
                    weights = jnp.exp(scores - new)
                    acc_s[g] = acc_s[g] * jnp.exp(old - new) + dot(
                        values, weights.astype(BF16), ((0,), (0,))
                    )
                    m_s[g, 0:1, :] = new

        tiles = []
        for g in range(KV_HEADS):
            acc = acc_s[g]
            at = (1 - g % 2) * HEAD
            total = acc[at : at + 1, :]
            lse_ref[qb, g : g + 1, :] = m_s[g, 0:1, :] + jnp.log(total)
            acc = acc / total
            for i in range(GROUP):
                head = g * GROUP + i
                tile = jnp.transpose(acc[:, i * BLK : (i + 1) * BLK])
                if head % 2 != g % 2:
                    tile = pltpu.roll(tile, HEAD, 1)
                tiles.append(tile)
                if head % 2 == 1:
                    both = jnp.where(lane_half(tile.shape, 0), tiles[head - 1], tile)
                    lanes = pl.ds((head // 2) * 128, 128)
                    exact_ref[rows, lanes] = both
                    out_ref[rows, lanes] = both.astype(BF16)


def attend(lengths, order, mine, projected, kv):
    rows = projected.shape[0]
    smem = pl.BlockSpec(memory_space=pltpu.SMEM)
    vmem = pl.BlockSpec(memory_space=pltpu.VMEM)
    wide = GROUP * BLK
    return pl.pallas_call(
        functools.partial(attend_kernel, lengths.shape[1]),
        out_shape=(
            jax.ShapeDtypeStruct((rows, HEADS * HEAD), F32),
            jax.ShapeDtypeStruct((rows, HEADS * HEAD), BF16),
            jax.ShapeDtypeStruct((rows // BLK, KV_HEADS, wide), F32),
        ),
        in_specs=[smem, smem, smem, vmem, vmem],
        out_specs=(vmem, vmem, vmem),
        scratch_shapes=[
            pltpu.VMEM((KV_HEADS, wide, 128), BF16),
            pltpu.VMEM((KV_HEADS, 8, wide), F32),
            pltpu.VMEM((KV_HEADS, BLK, wide), F32),
        ],
        compiler_params=pltpu.CompilerParams(vmem_limit_bytes=48 * 2**20),
        cost_estimate=pl.CostEstimate(flops=10**10, bytes_accessed=10**7, transcendentals=10**7),
        name="attend",
    )(lengths, order, mine, projected, kv)


def attend_back_kernel(
    parts,
    lengths_ref,
    order_ref,
    mine_ref,
    q_ref,
    kv_ref,
    grad_ref,
    lse_ref,
    exact_ref,
    dq_ref,
    dkv_ref,
    q_s,
    g_s,
    delta_s,
    dq_s,
    dkv_s,
):
    width = KV_HEADS * HEAD

    @pl.loop(0, order_ref.shape[1])
    def _(kb):
        dkv_s[pl.ds(kb * BLK, BLK), :] = jnp.zeros((BLK, 2 * width), F32)

    for qb in range(q_ref.shape[0] // BLK):
        rows = pl.ds(qb * BLK, BLK)
        for g in range(KV_HEADS):
            q_s[g] = head_tiles(q_ref, rows, g, HEAD**-0.5)
            g_s[g] = head_tiles(grad_ref, rows, g, 1.0)
            dq_s[g] = jnp.zeros((GROUP * BLK, 128), F32)
            for i in range(GROUP):
                head = g * GROUP + i
                exact = exact_ref[rows, (head // 2) * 128 : (head // 2 + 1) * 128]
                if head % 2 != g % 2:
                    exact = pltpu.roll(exact, HEAD, 1)
                product = exact * g_s[g, i * BLK : (i + 1) * BLK, :].astype(F32)
                delta_s[g : g + 1, i * BLK : (i + 1) * BLK] = jnp.sum(
                    jnp.transpose(product), axis=0, keepdims=True
                )
        query_block = order_ref[0, mine_ref[0] + qb]
        first = first_row_start(lengths_ref, query_block, parts)

        @pl.loop(0, order_ref.shape[1])
        def _(kb):
            key_block = order_ref[0, kb]

            @pl.when((key_block <= query_block) & (key_block * BLK + BLK > first))
            def _():
                seen = block_visibility(lengths_ref, query_block, key_block, parts)
                key_rows = pl.ds(kb * BLK, BLK)
                for pair in range(KV_HEADS // 2):
                    key_lanes = pl.ds(pair * 128, 128)
                    value_lanes = pl.ds(width + pair * 128, 128)
                    keys = kv_ref[key_rows, key_lanes]
                    values = kv_ref[key_rows, value_lanes]
                    grad_keys = dkv_s[key_rows, key_lanes]
                    grad_values = dkv_s[key_rows, value_lanes]
                    for g in (2 * pair, 2 * pair + 1):
                        scores = dot(keys, q_s[g], ((1,), (1,)))
                        scores = jnp.where(seen, scores, far_negative)
                        probs = jnp.exp(scores - lse_ref[qb, g : g + 1, :])
                        grad_probs = dot(values, g_s[g], ((1,), (1,)))
                        grad_scores = (probs * (grad_probs - delta_s[g : g + 1, :])).astype(BF16)
                        grad_values = grad_values + dot(probs.astype(BF16), g_s[g])
                        grad_keys = grad_keys + dot(grad_scores, q_s[g])
                        dq_s[g] += dot(grad_scores, keys, ((0,), (0,)))
                    dkv_s[key_rows, key_lanes] = grad_keys
                    dkv_s[key_rows, value_lanes] = grad_values

        tiles = []
        for g in range(KV_HEADS):
            for i in range(GROUP):
                head = g * GROUP + i
                tile = dq_s[g, i * BLK : (i + 1) * BLK, :] * HEAD**-0.5
                if head % 2 != g % 2:
                    tile = pltpu.roll(tile, HEAD, 1)
                tiles.append(tile)
                if head % 2 == 1:
                    both = jnp.where(lane_half(tile.shape, 0), tiles[head - 1], tile)
                    dq_ref[rows, (head // 2) * 128 : (head // 2 + 1) * 128] = both.astype(BF16)

    @pl.loop(0, order_ref.shape[1])
    def _(kb):
        key_rows = pl.ds(kb * BLK, BLK)
        dkv_ref[key_rows, :] = dkv_s[key_rows, :].astype(BF16)


def attend_back(lengths, order, mine, projected, kv, grad_attended, lse, exact):
    rows = projected.shape[0]
    smem = pl.BlockSpec(memory_space=pltpu.SMEM)
    vmem = pl.BlockSpec(memory_space=pltpu.VMEM)
    wide = GROUP * BLK
    return pl.pallas_call(
        functools.partial(attend_back_kernel, lengths.shape[1]),
        out_shape=(
            jax.ShapeDtypeStruct((rows, HEADS * HEAD), BF16),
            jax.ShapeDtypeStruct(kv.shape, BF16),
        ),
        in_specs=[smem, smem, smem, vmem, vmem, vmem, vmem, vmem],
        out_specs=(vmem, vmem),
        scratch_shapes=[
            pltpu.VMEM((KV_HEADS, wide, 128), BF16),
            pltpu.VMEM((KV_HEADS, wide, 128), BF16),
            pltpu.VMEM((KV_HEADS, wide), F32),
            pltpu.VMEM((KV_HEADS, wide, 128), F32),
            pltpu.VMEM(kv.shape, F32),
        ],
        compiler_params=pltpu.CompilerParams(vmem_limit_bytes=56 * 2**20),
        cost_estimate=pl.CostEstimate(flops=10**9, bytes_accessed=10**6, transcendentals=10**5),
        name="attend_back",
    )(lengths, order, mine, projected, kv, grad_attended, lse, exact)


MESH = pl.DeviceIdType.MESH


def place(z, core, exp):
    return {"le": z, "rep": 0, "core": core, "exp": exp}


def x_of(exp):
    return (exp // 2) * 2 + 1 - exp % 2


def y_of(exp):
    return (1 - exp // 2) * 2 + exp % 2


def remote(src, dst, send_sem, recv_sem, device):
    return pltpu.make_async_remote_copy(
        src_ref=src,
        dst_ref=dst,
        send_sem=send_sem,
        recv_sem=recv_sem,
        device_id=device,
        device_id_type=MESH,
    )


def between(z, layers, offset):
    low = layers // 2 - 1
    return ((z == low) & (offset == 1)) | ((z == low + 1) & (offset == layers - 1))


def meet(devices):
    barrier = pltpu.get_barrier_semaphore()
    for device in devices:
        pl.semaphore_signal(barrier, inc=1, device_id=device, device_id_type=MESH)
    pl.semaphore_wait(barrier, len(devices))


def front_kernel(
    layers,
    shard_ref,
    in_ref,
    down_ref,
    tokens_ref,
    w_all_ref,
    w_in_ref,
    w_down_ref,
    first_ref,
    projected_ref,
    kv_ref,
    weights,
    in_wide,
    down_wide,
    in_half,
    down_half,
    unit_sem,
    line_sem,
    x_sem,
    y_sem,
    far_sem,
    core_sem,
    half_sem,
    half_send,
    over_sem,
    over_send,
    kv_sem,
    kv_send,
    own_sem,
    wide_sem,
):
    z, core, exp = lax.axis_index("le"), lax.axis_index("core"), lax.axis_index("exp")
    other = 1 - core
    x, y = x_of(exp), y_of(exp)
    ctx = z * 2 + core
    rows = shard_ref.shape[0]
    offsets = (2, 1, 3, 0)
    order = [(z + s) % layers for s in offsets]
    wides = ((in_ref, in_wide), (down_ref, down_wide))
    halves = ((in_half, w_in_ref), (down_half, w_down_ref))

    loads = []
    for k, zz in enumerate(order):
        for a in range(2):
            load = pltpu.make_async_copy(wides[a][0].at[zz], wides[a][1].at[zz], wide_sem.at[a, k])
            load.start()
            loads.append(load)
    meet(
        [
            place((z + s) % layers, (core + p) % 2, exp)
            for s in range(layers)
            for p in range(2)
            if s + p > 0
        ]
        + [place(z, core, x), place(z, core, y)]
    )

    def number(zz, cc, ee):
        return (zz * 2 + cc) * 4 + ee

    def unit(zz, cc, ee):
        return weights.at[pl.ds(pl.multiple_of(number(zz, cc, ee) * rows, 16), rows), :]

    def send(src, who, sem, device):
        return remote(src, unit(*who), sem, unit_sem.at[number(*who)], device)

    def arrive(who):
        send(unit(*who), who, line_sem.at[0], place(z, other, exp)).wait_recv()

    started = []

    def go(copy, condition=None):
        if condition is None:
            copy.start()
        else:
            pl.when(condition)(copy.start)
        started.append((copy, condition))

    me = (z, core, exp)
    keep = pltpu.make_async_copy(shard_ref, unit(*me), own_sem.at[0])
    keep.start()
    go(send(shard_ref, me, line_sem.at[layers], place(z + 1, core, exp)), z < layers - 1)
    go(send(shard_ref, me, line_sem.at[layers + 1], place(z - 1, core, exp)), z > 0)
    go(send(shard_ref, me, x_sem.at[layers], place(z, core, x)))
    go(send(shard_ref, me, y_sem.at[layers], place(z, core, y)))
    go(send(shard_ref, me, core_sem.at[layers], place(z, other, exp)))

    slab = 16
    for k, zz in enumerate(order):
        for a in range(2):
            loads[2 * k + a].wait()
            src, dst = wides[a][1], halves[a][0]

            @pl.loop(0, src.shape[1] // slab)
            def _(i, zz=zz, src=src, dst=dst):
                at = pl.ds(pl.multiple_of(i * slab, slab), slab)
                dst[zz, at, :] = src[zz, at, :].astype(BF16)

    def half(a, source, p):
        src, dst = halves[a]
        n, cols = src.shape[1], src.shape[2] // 2
        return dst.at[pl.ds(source * n, n), pl.ds(pl.multiple_of(p * cols, 128), cols)]

    def mine(a, zz, p):
        src = halves[a][0]
        cols = src.shape[2] // 2
        return src.at[zz, :, pl.ds(pl.multiple_of(p * cols, 128), cols)]

    def layer(k):
        return jnp.where(z < layers // 2, k, layers - 1 - k)

    def hand_out(a, early):
        for s, zz in enumerate(order):
            across = between(z, layers, offsets[s])
            for p in range(2):
                if offsets[s] + p == 0:
                    continue
                pp = (core + p) % 2
                copy = remote(
                    mine(a, zz, pp),
                    half(a, ctx, pp),
                    half_send.at[a, s * 2 + p],
                    half_sem.at[a, ctx],
                    place(zz, pp, exp),
                )
                if early:
                    pl.when(across)(copy.start)
                else:
                    pl.when(~across)(copy.start)
                    started.append((copy, None))
        if not early:
            go(
                remote(
                    mine(a, z, core),
                    half(a, ctx, core),
                    over_send.at[a, 2 * layers],
                    over_sem.at[a, ctx],
                    place(z, other, exp),
                )
            )

    for k in range(layers):
        zz = layer(k)
        who = (zz, core, exp)

        @pl.when(zz != z)
        def _(who=who):
            arrive(who)

        go(send(unit(*who), who, line_sem.at[k], place(z + 1, core, exp)), (zz < z) & (z < layers - 1))
        go(send(unit(*who), who, line_sem.at[k], place(z - 1, core, exp)), (zz > z) & (z > 0))
        go(send(unit(*who), who, x_sem.at[k], place(z, core, x)), zz != z)
        go(send(unit(*who), who, y_sem.at[k], place(z, core, y)), zz != z)
        go(send(unit(*who), who, core_sem.at[k], place(z, other, exp)), zz != z)
        if k == 0:
            hand_out(0, True)

    for a in range(2):
        pltpu.make_async_copy(mine(a, z, core), half(a, ctx, core), own_sem.at[1 + a]).start()

    hand_out(0, False)

    for k in range(layers):
        zz = layer(k)
        from_x, from_y = (zz, core, x), (zz, core, y)
        arrive(from_x)
        go(send(unit(*from_x), from_x, core_sem.at[layers + 1 + k], place(z, other, exp)))
        if k % 2 == 0:
            go(send(unit(*from_x), from_x, far_sem.at[k], place(z, core, y)))
        arrive(from_y)
        go(send(unit(*from_y), from_y, core_sem.at[2 * layers + 1 + k], place(z, other, exp)))
        if k % 2 == 1:
            go(send(unit(*from_y), from_y, far_sem.at[k], place(z, core, x)))
    for k in range(layers):
        far = (layer(k), core, y_of(x))
        arrive(far)
        go(send(unit(*far), far, core_sem.at[3 * layers + 1 + k], place(z, other, exp)))
    for ee in range(4):
        for zz in range(layers):
            arrive((zz, other, ee))
    keep.wait()
    save = pltpu.make_async_copy(weights, w_all_ref, own_sem.at[3])
    save.start()

    depth, count = tokens_ref.shape[1], tokens_ref.shape[0]
    qkv_cols, head_cols = projected_ref.shape[1], HEADS * HEAD
    inputs = tokens_ref[...].astype(F32)
    gain = jnp.concatenate(
        [
            jnp.transpose(weights[i * 128 : (i + 1) * 128, qkv_cols : qkv_cols + AUX].astype(F32))[0:1, :]
            for i in range(depth // 128)
        ],
        axis=1,
    )
    first_ref[...] = (inputs * norm_scale(inputs) * gain).astype(BF16)
    tile = 512

    @pl.loop(0, (qkv_cols - head_cols) // tile)
    def _(i):
        at = pl.ds(pl.multiple_of(head_cols + i * tile, tile), tile)
        projected_ref[:, at] = dot(first_ref[...], weights[:, at]).astype(BF16)

    def block(source):
        return kv_ref.at[pl.ds(pl.multiple_of(source * count, 16), count), :]

    def share(src, source, sem, device):
        return remote(src, block(source), sem, kv_sem.at[source], device)

    own = projected_ref.at[:, pl.ds(head_cols, qkv_cols - head_cols)]
    keep_kv = pltpu.make_async_copy(own, block(ctx), own_sem.at[0])
    keep_kv.start()
    go(share(own, ctx, kv_send.at[2 * layers], place(z + 1, core, exp)), z < layers - 1)
    go(share(own, ctx, kv_send.at[2 * layers + 1], place(z - 1, core, exp)), z > 0)
    go(share(own, ctx, kv_send.at[2 * layers + 2], place(z, other, exp)))

    @pl.loop(0, head_cols // tile)
    def _(i):
        at = pl.ds(pl.multiple_of(i * tile, tile), tile)
        projected_ref[:, at] = dot(first_ref[...], weights[:, at]).astype(BF16)

    for k in range(layers):
        zz = layer(k)
        source = zz * 2 + core

        @pl.when(zz != z)
        def _(source=source):
            share(block(source), source, kv_send.at[0], place(z, other, exp)).wait_recv()

        go(share(block(source), source, kv_send.at[k], place(z + 1, core, exp)), (zz < z) & (z < layers - 1))
        go(share(block(source), source, kv_send.at[k], place(z - 1, core, exp)), (zz > z) & (z > 0))
        go(share(block(source), source, kv_send.at[layers + k], place(z, other, exp)), zz != z)
        if k == layers // 2:
            hand_out(1, True)
            hand_out(1, False)

    for s, zz in enumerate(order[::-1]):
        for p in range(2):
            if s == 0 and p == 0:
                continue
            source = zz * 2 + (core + p) % 2
            for a in range(2):
                remote(
                    half(a, source, core),
                    half(a, source, core),
                    half_send.at[a, 0],
                    half_sem.at[a, source],
                    place(z, other, exp),
                ).wait_recv()
                go(
                    remote(
                        half(a, source, core),
                        half(a, source, core),
                        over_send.at[a, s * 2 + p],
                        over_sem.at[a, source],
                        place(z, other, exp),
                    )
                )

    for zz in range(layers):
        source = zz * 2 + other
        share(block(source), source, kv_send.at[0], place(z, other, exp)).wait_recv()
    for source in range(2 * layers):
        for a in range(2):
            remote(
                half(a, source, other),
                half(a, source, other),
                half_send.at[a, 0],
                over_sem.at[a, source],
                place(z, other, exp),
            ).wait_recv()
    keep_kv.wait()
    save.wait()
    for a in range(2):
        pltpu.make_async_copy(mine(a, z, core), half(a, ctx, core), own_sem.at[1 + a]).wait()
    for copy, condition in started:
        if condition is None:
            copy.wait_send()
        else:
            pl.when(condition)(copy.wait_send)


def front(shard, expert_in, expert_out, tokens, qkv_cols):
    layers = expert_in.shape[0]
    rows_in, rows_out = expert_in.shape[1], expert_out.shape[1]
    depth, cols = shard.shape[0] * 8 * layers, shard.shape[1]
    count = tokens.shape[0]
    any_space = pl.BlockSpec(memory_space=pl.ANY)
    vmem = pl.BlockSpec(memory_space=pltpu.VMEM)
    dma = pltpu.SemaphoreType.DMA
    return pl.pallas_call(
        functools.partial(front_kernel, layers),
        out_shape=(
            jax.ShapeDtypeStruct((depth, cols), BF16),
            jax.ShapeDtypeStruct((rows_in * 2 * layers, expert_in.shape[2]), BF16),
            jax.ShapeDtypeStruct((rows_out * 2 * layers, expert_out.shape[2]), BF16),
            jax.ShapeDtypeStruct((count, depth), BF16),
            jax.ShapeDtypeStruct((count, qkv_cols), BF16),
            jax.ShapeDtypeStruct((count * 2 * layers, qkv_cols - HEADS * HEAD), BF16),
        ),
        in_specs=[any_space] * 3 + [vmem],
        out_specs=(any_space,) * 3 + (vmem, vmem, any_space),
        scratch_shapes=[
            pltpu.VMEM((depth, cols), BF16),
            pltpu.VMEM(expert_in.shape, F32),
            pltpu.VMEM(expert_out.shape, F32),
            pltpu.VMEM(expert_in.shape, BF16),
            pltpu.VMEM(expert_out.shape, BF16),
            dma((8 * layers,)),
            dma((layers + 2,)),
            dma((layers + 1,)),
            dma((layers + 1,)),
            dma((layers,)),
            dma((4 * layers + 1,)),
            dma((2, 2 * layers)),
            dma((2, 2 * layers)),
            dma((2, 2 * layers)),
            dma((2, 2 * layers + 1)),
            dma((2 * layers,)),
            dma((2 * layers + 3,)),
            dma((4,)),
            dma((2, layers)),
        ],
        compiler_params=pltpu.CompilerParams(
            collective_id=0, has_side_effects=True, vmem_limit_bytes=48 * 2**20
        ),
        name="front",
    )(shard, expert_in, expert_out, tokens)


def experts_kernel(
    layers,
    rows_ref,
    gates_ref,
    grads_ref,
    w_in_ref,
    w_down_ref,
    out_ref,
    back_ref,
    back_gates_ref,
    d_in_ref,
    d_down_ref,
    w_in,
    w_down,
    got,
    got_gates,
    x_s,
    grad_s,
    hidden_s,
    inner_s,
    back_s,
    back_gates_s,
    other_in,
    other_down,
    pair_in,
    pair_down,
    row_sem,
    row_send,
    gate_sem,
    gate_send,
    back_sem,
    back_send,
    back_gate_sem,
    back_gate_send,
    pair_sem,
    pair_send,
    load_sem,
):
    z, core, exp = lax.axis_index("le"), lax.axis_index("core"), lax.axis_index("exp")
    other = 1 - core
    columns = rows_ref.shape[0] // layers
    me = exp * layers + z
    cap, depth = rows_ref.shape[1], rows_ref.shape[2]
    chunk = columns * cap
    loads = [
        pltpu.make_async_copy(w_in_ref, w_in, load_sem.at[0]),
        pltpu.make_async_copy(w_down_ref, w_down, load_sem.at[1]),
    ]
    for load in loads:
        load.start()
    first_half = z < layers // 2
    by_distance = [
        z,
        z + 1 - 2 * (z % 2),
        jnp.where(first_half, 2, 1),
        jnp.where(first_half, 3, 0),
    ]
    peers = [
        (zz, (exp + t) % columns)
        for s, zz in enumerate(by_distance[::-1])
        for t in range(columns)
        if not (s == layers - 1 and t == 0)
    ]
    meet([place(zz, core, ee) for zz, ee in peers] + [place(z, other, exp)])

    started = []

    def go(copy):
        copy.start()
        started.append(copy)

    keeps = [
        pltpu.make_async_copy(rows_ref.at[me], got.at[me], load_sem.at[2]),
        pltpu.make_async_copy(gates_ref.at[me], got_gates.at[me], load_sem.at[3]),
    ]
    for keep in keeps:
        keep.start()
    for k, (zz, ee) in enumerate(peers):
        there = ee * layers + zz
        go(remote(gates_ref.at[there], got_gates.at[me], gate_send.at[k], gate_sem.at[me], place(zz, core, ee)))
        go(remote(rows_ref.at[there], got.at[me], row_send.at[k], row_sem.at[me], place(zz, core, ee)))
    for load in loads + keeps:
        load.wait()

    eye = lax.broadcasted_iota(jnp.int32, (cap, 128), 0) == lax.broadcasted_iota(jnp.int32, (cap, 128), 1)
    tile = 256

    def tiles(i):
        return pl.ds(pl.multiple_of(i * tile, tile), tile)

    for k, zz in enumerate(by_distance):
        rows = pl.ds(k * chunk, chunk)
        for ee in range(columns):
            source = ee * layers + zz

            @pl.when(source != me)
            def _(source=source):
                here = place(z, other, exp)
                remote(got.at[source], got.at[source], row_send.at[0], row_sem.at[source], here).wait_recv()
                remote(
                    got_gates.at[source], got_gates.at[source], gate_send.at[0], gate_sem.at[source], here
                ).wait_recv()

            at = pl.ds(k * chunk + ee * cap, cap)
            x_s[at, :] = got[source]
            gate = jnp.sum(jnp.where(eye, got_gates[source, 0:1, :], 0.0), axis=1, keepdims=True)
            grad_s[at, :] = (gate * grads_ref[source].astype(F32)).astype(BF16)

        @pl.loop(0, FF // tile)
        def _(i, rows=rows):
            up_at = pl.ds(pl.multiple_of(FF + i * tile, tile), tile)
            gate = dot(x_s[rows, :], w_in[:, tiles(i)])
            up = dot(x_s[rows, :], w_in[:, up_at])
            grad_hidden = dot(grad_s[rows, :], w_down[tiles(i), :], ((1,), (1,)))
            sigmoid = jax.nn.sigmoid(gate)
            silu = gate * sigmoid
            hidden_s[rows, tiles(i)] = (silu * up).astype(BF16)
            inner_s[rows, tiles(i)] = (grad_hidden * up * sigmoid * (1.0 + gate * (1.0 - sigmoid))).astype(BF16)
            inner_s[rows, up_at] = (grad_hidden * silu).astype(BF16)

        @pl.loop(0, depth // tile)
        def _(i, rows=rows, zz=zz):
            back = dot(inner_s[rows, :], w_in[tiles(i), :], ((1,), (1,))).astype(BF16)
            for ee in range(columns):
                back_s[ee * layers + zz, :, tiles(i)] = back[ee * cap : (ee + 1) * cap]

        @pl.loop(0, depth // tile, init_carry=jnp.zeros((chunk, 128), F32))
        def gate_grads(i, sums, rows=rows, zz=zz):
            result = dot(hidden_s[rows, :], w_down[:, tiles(i)]).astype(BF16)
            parts = []
            for ee in range(columns):
                part = result[ee * cap : (ee + 1) * cap]
                out_ref[ee * layers + zz, :, tiles(i)] = part
                parts.append(part.astype(F32) * grads_ref[ee * layers + zz, :, tiles(i)].astype(F32))
            product = jnp.concatenate(parts, axis=0)
            return sums + product[:, :128] + product[:, 128:]

        gate_grads = jnp.sum(gate_grads, axis=1, keepdims=True)
        for ee in range(columns):
            there = ee * layers + zz
            column = gate_grads[ee * cap : (ee + 1) * cap]
            line = jnp.sum(jnp.where(eye, column, 0.0), axis=0, keepdims=True)
            back_gates_s[there] = jnp.broadcast_to(line, (8, 128))
            row_copy = remote(
                back_s.at[there],
                back_ref.at[me],
                back_send.at[there],
                back_sem.at[me],
                place(zz, core, ee),
            )
            gate_copy = remote(
                back_gates_s.at[there],
                back_gates_ref.at[me],
                back_gate_send.at[there],
                back_gate_sem.at[me],
                place(zz, core, ee),
            )

            @pl.when(there != me)
            def _(row_copy=row_copy, gate_copy=gate_copy):
                row_copy.start()
                gate_copy.start()

    own = [
        pltpu.make_async_copy(back_s.at[me], back_ref.at[me], load_sem.at[2]),
        pltpu.make_async_copy(back_gates_s.at[me], back_gates_ref.at[me], load_sem.at[3]),
    ]
    for copy in own:
        copy.start()

    half_in, half_down = d_in_ref.shape[1], d_down_ref.shape[1]

    def in_part(i, p):
        cols = pl.ds(pl.multiple_of(p * half_in, 128), half_in)
        return dot(x_s[:, tiles(i)], inner_s[:, cols], ((0,), (0,)))

    def down_part(i, p):
        cols = pl.ds(pl.multiple_of(p * half_down, 128), half_down)
        return dot(hidden_s[:, tiles(i)], grad_s[:, cols], ((0,), (0,)))

    @pl.loop(0, depth // tile)
    def _(i):
        other_in[tiles(i), :] = in_part(i, other).astype(BF16)

    go(remote(other_in, pair_in, pair_send.at[0], pair_sem.at[0], place(z, other, exp)))

    @pl.loop(0, FF // tile)
    def _(i):
        other_down[tiles(i), :] = down_part(i, other).astype(BF16)

    go(remote(other_down, pair_down, pair_send.at[1], pair_sem.at[1], place(z, other, exp)))
    remote(other_in, pair_in, pair_send.at[0], pair_sem.at[0], place(z, other, exp)).wait_recv()

    @pl.loop(0, depth // tile)
    def _(i):
        d_in_ref[tiles(i), :] = (in_part(i, core) + pair_in[tiles(i), :].astype(F32)).astype(BF16)

    remote(other_down, pair_down, pair_send.at[1], pair_sem.at[1], place(z, other, exp)).wait_recv()

    @pl.loop(0, FF // tile)
    def _(i):
        d_down_ref[tiles(i), :] = (down_part(i, core) + pair_down[tiles(i), :].astype(F32)).astype(BF16)

    for copy in own:
        copy.wait()
    for k, (zz, ee) in enumerate(peers):
        there = ee * layers + zz
        row_copy = remote(
            back_s.at[there], back_ref.at[there], back_send.at[there], back_sem.at[there], place(zz, core, ee)
        )
        gate_copy = remote(
            back_gates_s.at[there],
            back_gates_ref.at[there],
            back_gate_send.at[there],
            back_gate_sem.at[there],
            place(zz, core, ee),
        )
        row_copy.wait()
        gate_copy.wait()
    for copy in started:
        copy.wait_send()


def experts(rows, gates, grads, w_in, w_down, layers):
    count, cap, depth = rows.shape
    any_space = pl.BlockSpec(memory_space=pl.ANY)
    vmem = pl.BlockSpec(memory_space=pltpu.VMEM)
    dma = pltpu.SemaphoreType.DMA
    half_in = jax.ShapeDtypeStruct((depth, FF), BF16)
    half_down = jax.ShapeDtypeStruct((FF, depth // 2), BF16)
    return pl.pallas_call(
        functools.partial(experts_kernel, layers),
        out_shape=(
            jax.ShapeDtypeStruct(rows.shape, BF16),
            jax.ShapeDtypeStruct(rows.shape, BF16),
            jax.ShapeDtypeStruct(gates.shape, F32),
            half_in,
            half_down,
        ),
        in_specs=[any_space, any_space, vmem, any_space, any_space],
        out_specs=(vmem, any_space, any_space, vmem, vmem),
        scratch_shapes=[
            pltpu.VMEM(w_in.shape, BF16),
            pltpu.VMEM(w_down.shape, BF16),
            pltpu.VMEM(rows.shape, BF16),
            pltpu.VMEM(gates.shape, F32),
            pltpu.VMEM((count * cap, depth), BF16),
            pltpu.VMEM((count * cap, depth), BF16),
            pltpu.VMEM((count * cap, FF), BF16),
            pltpu.VMEM((count * cap, 2 * FF), BF16),
            pltpu.VMEM(rows.shape, BF16),
            pltpu.VMEM(gates.shape, F32),
            pltpu.VMEM(half_in.shape, BF16),
            pltpu.VMEM(half_down.shape, BF16),
            pltpu.VMEM(half_in.shape, BF16),
            pltpu.VMEM(half_down.shape, BF16),
        ]
        + [dma((count,))] * 8
        + [dma((2,)), dma((2,)), dma((4,))],
        compiler_params=pltpu.CompilerParams(
            collective_id=2, has_side_effects=True, vmem_limit_bytes=60 * 2**20
        ),
        name="experts",
    )(rows, gates, grads, w_in, w_down)


def add_rows(total, part, rows):
    slab = 16

    @pl.loop(0, rows // slab)
    def _(i):
        at = pl.ds(pl.multiple_of(i * slab, slab), slab)
        total[at, :] = (total[at, :].astype(F32) + part[at, :].astype(F32)).astype(BF16)


class Chain:
    def __init__(self, layers, z, above, below, own, rows, up, down, sems, sends):
        self.layers, self.z, self.above, self.below = layers, z, above, below
        self.own, self.rows, self.up, self.down = own, rows, up, down
        self.sems, self.sends = sems, sends
        self.parts = sems.shape[2]
        self.width = up.shape[2] // self.parts

    def columns(self, ref, h):
        return ref.at[:, pl.ds(h * self.width, self.width)]

    def rise(self, d, h):
        return remote(
            self.columns(self.own(d), h),
            self.columns(self.up.at[d], h),
            self.sends.at[0, d, h],
            self.sems.at[0, d, h],
            self.above,
        )

    def fall(self, d, h):
        return remote(
            self.columns(self.own(d), h),
            self.columns(self.down.at[d], h),
            self.sends.at[1, d, h],
            self.sems.at[1, d, h],
            self.below,
        )

    def end(self, step):
        for h in range(self.parts):
            pl.when(self.z == 0)(self.rise(self.layers - 1 - step, h).start)
            pl.when(self.z == self.layers - 1)(self.fall(step, h).start)

    def ends(self):
        for step in range(self.layers - 1):
            self.end(step)

    def add(self, d, h, buffer):
        add_rows(self.columns(self.own(d), h), self.columns(buffer.at[d], h), self.rows)

    def middle(self):
        z, last = self.z, self.layers - 1

        def pass_on(make, d, buffer):
            for h in range(self.parts):
                copy = make(d, h)
                copy.wait_recv()
                self.add(d, h, buffer)
                copy.start()

        def both(first_half):
            for step in range(last):
                high, low = last - step, step

                def upward(high=high):
                    pl.when((z > 0) & (z < high))(lambda: pass_on(self.rise, high, self.up))

                def downward(low=low):
                    pl.when((z < last) & (z > low))(lambda: pass_on(self.fall, low, self.down))

                for turn in (upward, downward) if first_half else (downward, upward):
                    turn()

        pl.when(z <= last // 2)(lambda: both(True))
        pl.when(z > last // 2)(lambda: both(False))

    def finish(self):
        z, last = self.z, self.layers - 1

        def take(make, buffer):
            for h in range(self.parts):
                make(z, h).wait_recv()
                self.add(z, h, buffer)

        pl.when(z > 0)(lambda: take(self.rise, self.up))
        pl.when(z < last)(lambda: take(self.fall, self.down))

    def wait_sends(self):
        for d in range(self.layers):
            for h in range(self.parts):
                pl.when(self.z < d)(self.rise(d, h).wait_send)
                pl.when(self.z > d)(self.fall(d, h).wait_send)


def finish_kernel(
    layers,
    grad_kv_ref,
    grad_q_ref,
    first_ref,
    tokens_ref,
    gain_ref,
    middle_ref,
    w_all_ref,
    attended_ref,
    second_ref,
    logits_ref,
    gain_moe_ref,
    base_ref,
    returned_ref,
    picks_ref,
    gates_ref,
    in_ref,
    down_ref,
    block_ref,
    d_tokens_ref,
    d_qkv_ref,
    d_out_ref,
    d_aux_ref,
    got_in_ref,
    got_down_ref,
    weights,
    projected,
    grad_first,
    kv_own,
    kv_pair,
    kv_up,
    kv_down,
    late_both,
    late_pair,
    late_near,
    late_up,
    late_down,
    q_both,
    q_pair,
    q_near,
    q_up,
    q_down,
    k_both,
    k_pair,
    k_near,
    k_up,
    k_down,
    load_sem,
    kv_pair_sem,
    kv_pair_send,
    kv_sem,
    kv_send,
    half_sem,
    half_send,
    pair_sem,
    pair_send,
    near_sem,
    near_send,
    line_sem,
    line_send,
):
    z, core, exp = lax.axis_index("le"), lax.axis_index("core"), lax.axis_index("exp")
    other = 1 - core
    partner = place(z, other, exp)
    above, below = place(z + 1, core, exp), place(z - 1, core, exp)
    x, y = x_of(exp), y_of(exp)
    mates = (x, y, y_of(x))
    ctx = z * 2 + core
    rows = d_qkv_ref.shape[0]
    count = tokens_ref.shape[0]
    head_cols = HEADS * HEAD
    qkv_cols = d_qkv_ref.shape[1]
    kv_cols = qkv_cols - head_cols

    loads = []

    def load(src, dst):
        copy = pltpu.make_async_copy(src, dst, load_sem.at[len(loads)])
        copy.start()
        loads.append(copy)
        return copy

    kv_loads = [
        load(grad_kv_ref.at[pl.ds(pl.multiple_of((d * 2 + core) * count, 16), count), :], kv_own.at[d])
        for d in range(layers)
    ]
    depth = w_all_ref.shape[0]

    def weights_part(i):
        part = w_all_ref.at[pl.ds(i * depth // 2, depth // 2), pl.ds(0, qkv_cols)]
        return pltpu.make_async_copy(part, weights, load_sem.at[2 * layers + 2])

    weights_part(0).start()
    meet(
        [
            place((z + s) % layers, (core + p) % 2, exp)
            for s in range(layers)
            for p in range(2)
            if s + p > 0
        ]
        + [place(z, core, mate) for mate in mates]
    )
    started = []

    def go(copy):
        copy.start()
        started.append(copy)

    arrays = ((in_ref, got_in_ref), (down_ref, got_down_ref))

    def mine(a, owner):
        n = arrays[a][1].shape[1]
        return arrays[a][0].at[pl.ds(owner * n, n), :]

    def half(a, expert, p):
        cols = arrays[a][0].shape[1]
        return arrays[a][1].at[expert, :, pl.ds(pl.multiple_of(p * cols, 128), cols)]

    for a in range(2):
        load(mine(a, ctx), half(a, z, core))

    def hand_back(a, early):
        for s in (2, 1, 3, 0):
            across = between(z, layers, s)
            for p in range(2):
                if s + p == 0:
                    continue
                zz, pp = (z + s) % layers, (core + p) % 2
                copy = remote(
                    mine(a, zz * 2 + pp),
                    half(a, z, core),
                    half_send.at[a, s * 2 + p],
                    half_sem.at[a, ctx],
                    place(zz, pp, exp),
                )
                if early:
                    pl.when(across)(copy.start)
                else:
                    pl.when(~across)(copy.start)
                    started.append(copy)

    hand_back(0, True)

    for d in range(layers):
        go(
            remote(
                grad_kv_ref.at[pl.ds(pl.multiple_of((d * 2 + other) * count, 16), count), :],
                kv_pair.at[d],
                kv_pair_send.at[d],
                kv_pair_sem.at[d],
                partner,
            )
        )
    kv_line = Chain(
        layers, z, above, below, lambda d: kv_own.at[d], count, kv_up, kv_down, kv_sem, kv_send
    )
    for copy in kv_loads:
        copy.wait()
    for k in range(layers):
        d = jnp.where(z < layers // 2, layers - 1 - k, k)
        remote(kv_pair.at[d], kv_pair.at[d], kv_pair_send.at[d], kv_pair_sem.at[d], partner).wait_recv()
        add_rows(kv_own.at[d], kv_pair.at[d], count)
        if k < layers - 1:
            kv_line.end(k)

    def near_copy(i, near, own, d, m, target):
        return remote(
            own.at[d, pl.ds(pl.multiple_of(target * rows, 16), rows), :],
            near.at[m, d],
            near_send.at[i, m, d],
            near_sem.at[i, m, d],
            place(z, core, mates[m]),
        )

    def pair_sums(i, own, pair, near):
        for d in range(layers):
            remote(pair.at[d], pair.at[d], pair_send.at[i, d], pair_sem.at[i, d], partner).wait_recv()
            add_rows(own.at[d], pair.at[d], 4 * rows)
            for m in range(3):
                go(near_copy(i, near, own, d, m, mates[m]))

    def near_sums(i, own, near):
        for d in range(layers):
            for m in range(3):
                near_copy(i, near, own, d, m, exp).wait_recv()
            mine = own.at[d, pl.ds(pl.multiple_of(exp * rows, 16), rows), :]

            @pl.loop(0, rows // 16)
            def _(r, mine=mine, d=d):
                at = pl.ds(pl.multiple_of(r * 16, 16), 16)
                total = mine[at, :].astype(F32)
                for m in range(3):
                    total = total + near[m, d, at, :].astype(F32)
                mine[at, :] = total.astype(BF16)

    def line_of(i, own, up, down):
        return Chain(
            layers,
            z,
            above,
            below,
            lambda d: own.at[d, pl.ds(pl.multiple_of(exp * rows, 16), rows), :],
            rows,
            up,
            down,
            line_sem.at[i],
            line_send.at[i],
        )

    def outer_product(both, cols, left, right, gains=None):
        for d in range(layers):
            block = left[:, d * 8 * rows : (d + 1) * 8 * rows]
            part = dot(block, right, ((0,), (0,)))
            if gains is not None:
                turned = [
                    jnp.transpose(jnp.broadcast_to(gains[:, at : at + 128], (128, 128)))
                    for at in range(d * 8 * rows, (d + 1) * 8 * rows, 128)
                ]
                lane = lax.broadcasted_iota(jnp.int32, part.shape, 1)
                part = jnp.where(lane == 0, jnp.concatenate(turned, axis=0), part)
            part = part.astype(BF16)
            both[0, d, :, cols] = part[: 4 * rows]
            both[1, d, :, cols] = part[4 * rows :]

    def pair_up(i, both, pair):
        for d in range(layers):
            go(remote(both.at[other, d], pair.at[d], pair_send.at[i, d], pair_sem.at[i, d], partner))

    outer_product(q_both, slice(0, head_cols), first_ref, grad_q_ref[...])
    pair_up(1, q_both, q_pair)
    width = middle_ref.shape[1]
    outer_product(late_both, slice(0, width), attended_ref, middle_ref[...].astype(BF16))
    outer_product(late_both, slice(width, width + AUX), second_ref, logits_ref[...], gain_moe_ref[...])
    pair_up(0, late_both, late_pair)
    late_own = late_both.at[core]
    q_own = q_both.at[core]
    pair_sums(1, q_own, q_pair, q_near)
    pair_sums(0, late_own, late_pair, late_near)
    kv_line.middle()
    hand_back(0, False)
    hand_back(1, True)
    hand_back(1, False)
    kv_line.finish()

    projected[:, :head_cols] = grad_q_ref[...]
    projected[:, head_cols:] = kv_own[z]
    outer_product(k_both, slice(0, kv_cols), first_ref, projected[:, head_cols:])
    tile = 256
    for i in range(2):
        weights_part(i).wait()

        @pl.loop(0, depth // 2 // tile)
        def _(j, i=i):
            at = pl.ds(pl.multiple_of(j * tile, tile), tile)
            to = pl.ds(pl.multiple_of(i * depth // 2 + j * tile, tile), tile)
            grad_first[:, to] = dot(projected[...], weights[at, :], ((1,), (1,)))

        if i == 0:
            weights_part(1).start()

    inputs = tokens_ref[...].astype(F32)
    scale = norm_scale(inputs)
    norm = inputs * scale
    grad = grad_first[...]
    grad_gain = jnp.sum(grad * norm, axis=0, keepdims=True)
    for d in range(layers):
        block = jnp.concatenate(
            [
                jnp.transpose(jnp.broadcast_to(grad_gain[:, at : at + 128], (128, 128)))
                for at in range(d * 8 * rows, (d + 1) * 8 * rows, 128)
            ],
            axis=0,
        ).astype(BF16)
        k_both[0, d, :, kv_cols:] = block[: 4 * rows]
        k_both[1, d, :, kv_cols:] = block[4 * rows :]
    pair_up(2, k_both, k_pair)
    grad = grad * gain_ref[...]
    d_tokens_ref[...] = (
        middle_ref[...] + scale * (grad - norm * jnp.mean(grad * norm, axis=-1, keepdims=True))
    ).astype(BF16)
    k_own = k_both.at[core]
    pair_sums(2, k_own, k_pair, k_near)

    @pl.loop(0, depth // tile)
    def _(i):
        at = pl.ds(pl.multiple_of(i * tile, tile), tile)
        total = base_ref[:, at]
        for k in range(2):
            total = total + gates_ref[:, k : k + 1] * dot(picks_ref[k], returned_ref[:, at])
        block_ref[:, at] = total.astype(BF16)

    late_line = line_of(0, late_own, late_up, late_down)
    q_line = line_of(1, q_own, q_up, q_down)
    k_line = line_of(2, k_own, k_up, k_down)
    near_sums(1, q_own, q_near)
    q_line.ends()
    near_sums(0, late_own, late_near)
    late_line.ends()
    q_line.middle()
    near_sums(2, k_own, k_near)
    k_line.ends()
    late_line.middle()
    k_line.middle()
    mine_rows = pl.ds(pl.multiple_of(exp * rows, 16), rows)
    q_line.finish()
    d_qkv_ref[:, :head_cols] = q_both[core, z, mine_rows, :].astype(F32)
    late_line.finish()
    last = late_both[core, z, mine_rows, :].astype(F32)
    d_out_ref[...] = last[:, :width]
    d_aux_ref[:, AUX:] = last[:, width:]
    k_line.finish()
    last = k_both[core, z, mine_rows, :].astype(F32)
    d_qkv_ref[:, head_cols:] = last[:, :kv_cols]
    d_aux_ref[:, :AUX] = last[:, kv_cols:]

    for source in range(2 * layers):
        for a in range(2):

            @pl.when(source != ctx)
            def _(source=source, a=a):
                remote(
                    half(a, source // 2, source % 2),
                    half(a, source // 2, source % 2),
                    half_send.at[a, 0],
                    half_sem.at[a, source],
                    partner,
                ).wait_recv()

    for copy in loads[-2:]:
        copy.wait()
    for line in (kv_line, late_line, q_line, k_line):
        line.wait_sends()
    for copy in started:
        copy.wait_send()


def finish(
    grad_kv,
    grad_q,
    first,
    tokens,
    gain,
    middle,
    w_all,
    attended,
    second,
    grad_logits,
    gain_moe,
    base,
    returned,
    picks,
    gates,
    grad_in,
    grad_down,
    layers,
):
    depth, count = first.shape[1], first.shape[0]
    rows = depth // (8 * layers)
    qkv_cols = grad_q.shape[1] + grad_kv.shape[1]
    n_in, n_down = grad_in.shape[0] // (2 * layers), grad_down.shape[0] // (2 * layers)
    any_space = pl.BlockSpec(memory_space=pl.ANY)
    vmem = pl.BlockSpec(memory_space=pltpu.VMEM)
    dma = pltpu.SemaphoreType.DMA

    def sums(cols):
        return [
            pltpu.VMEM((2, layers, 4 * rows, cols), BF16),
            pltpu.VMEM((layers, 4 * rows, cols), BF16),
            pltpu.VMEM((3, layers, rows, cols), BF16),
            pltpu.VMEM((layers, rows, cols), BF16),
            pltpu.VMEM((layers, rows, cols), BF16),
        ]

    return pl.pallas_call(
        functools.partial(finish_kernel, layers),
        out_shape=(
            jax.ShapeDtypeStruct((count, depth), BF16),
            jax.ShapeDtypeStruct((count, depth), BF16),
            jax.ShapeDtypeStruct((rows, qkv_cols), F32),
            jax.ShapeDtypeStruct((rows, depth), F32),
            jax.ShapeDtypeStruct((rows, 2 * AUX), F32),
            jax.ShapeDtypeStruct((layers, n_in, 2 * grad_in.shape[1]), BF16),
            jax.ShapeDtypeStruct((layers, n_down, 2 * grad_down.shape[1]), BF16),
        ),
        in_specs=[any_space] + [vmem] * 5 + [any_space] + [vmem] * 8 + [any_space] * 2,
        out_specs=(vmem,) * 5 + (any_space,) * 2,
        scratch_shapes=[
            pltpu.VMEM((depth // 2, qkv_cols), BF16),
            pltpu.VMEM((count, qkv_cols), BF16),
            pltpu.VMEM((count, depth), F32),
        ]
        + [pltpu.VMEM((layers, count, grad_kv.shape[1]), BF16)] * 4
        + sums(depth + AUX)
        + sums(grad_q.shape[1])
        + sums(grad_kv.shape[1] + AUX)
        + [
            dma((2 * layers + 3,)),
            dma((layers,)),
            dma((layers,)),
            dma((2, layers, 2)),
            dma((2, layers, 2)),
            dma((2, 2 * layers)),
            dma((2, 2 * layers)),
            dma((3, layers)),
            dma((3, layers)),
            dma((3, 3, layers)),
            dma((3, 3, layers)),
            dma((3, 2, layers, 1)),
            dma((3, 2, layers, 1)),
        ],
        compiler_params=pltpu.CompilerParams(
            collective_id=1, has_side_effects=True, vmem_limit_bytes=60 * 2**20
        ),
        name="finish",
    )(
        grad_kv,
        grad_q,
        first,
        tokens,
        gain,
        middle,
        w_all,
        attended,
        second,
        grad_logits,
        gain_moe,
        base,
        returned,
        picks,
        gates,
        grad_in,
        grad_down,
    )


def settle_kernel(*refs):
    count = len(refs) // 2
    for src, dst in zip(refs[:count], refs[count:]):
        dst[...] = src[...].astype(dst.dtype)


def settle(arrays, steps):
    def spec(array):
        if array.ndim == 2 and array.shape[0] % (16 * steps) == 0:
            return pl.BlockSpec((array.shape[0] // steps, array.shape[1]), lambda i: (i, 0))
        if array.ndim == 3 and array.shape[1] % (16 * steps) == 0:
            return pl.BlockSpec(
                (array.shape[0], array.shape[1] // steps, array.shape[2]), lambda i: (0, i, 0)
            )
        return pl.BlockSpec(array.shape, lambda i: (0,) * array.ndim)

    specs = [spec(array) for array, _ in arrays]
    return pl.pallas_call(
        settle_kernel,
        grid=(steps,),
        out_shape=[jax.ShapeDtypeStruct(array.shape, dtype) for array, dtype in arrays],
        in_specs=specs,
        out_specs=specs,
        compiler_params=pltpu.CompilerParams(vmem_limit_bytes=60 * 2**20),
        name="settle",
    )(*[array for array, _ in arrays])


CTX = ("le", "rep", "core")
ALL = ("le", "rep", "core", "exp")
OWNERS = ("exp", "le")


def on_device(
    tokens,
    cotangent,
    routes,
    lengths,
    block_order,
    gain_attn,
    qkv_weight,
    out_weight,
    gain_moe,
    router_weight,
    expert_in,
    expert_out,
):
    tok_rows = tokens.shape[1]
    head_width = HEADS * HEAD
    exp_local = expert_in.shape[0]
    n_ctx = D // expert_in.shape[1]
    copies = n_ctx // exp_local
    n_exp = EXPERTS // exp_local
    in_rows, out_rows = expert_in.shape[1], expert_out.shape[1]

    cols = qkv_weight.shape[1]
    aux = jnp.concatenate([gain_attn[:, None], gain_moe[:, None], router_weight], axis=1)
    aux = jnp.pad(aux, ((0, 0), (0, AUX - aux.shape[1])))
    shard = jnp.concatenate([qkv_weight, aux, out_weight], axis=1).astype(BF16)
    special = (copies, exp_local, n_exp) == (2, 4, 4)
    if special:
        w_all, w_in, w_down, first, projected, kv = front(shard, expert_in, expert_out, tokens[0], cols)
    else:
        w_all = lax.all_gather(shard, ALL, axis=0, tiled=True)

        def to_owner(weight):
            rows, width = weight.shape[1:]
            halves = weight.astype(BF16).reshape(exp_local, rows, 2, width // 2).transpose(0, 2, 1, 3)
            halves = jnp.broadcast_to(
                halves[:, None], (exp_local, copies // 2, 2, rows, width // 2)
            ).reshape(n_ctx, rows, width // 2)
            mine = lax.all_to_all(halves, CTX, split_axis=0, concat_axis=0, tiled=True)
            return lax.all_gather(mine.reshape(n_ctx * rows, width // 2), "core", axis=1, tiled=True)

        w_in = to_owner(expert_in)
        w_down = to_owner(expert_out)
    w_qkv = w_all[:, :cols]
    aux_all = w_all[:, cols : cols + AUX]
    w_attn_out = w_all[:, cols + AUX :]
    gain_first = aux_all[:, 0].astype(F32)
    gain_second = aux_all[:, 1].astype(F32)
    w_router = aux_all[:, 2 : 2 + EXPERTS]

    route_hot = (
        routes[0][:, :, None] == jnp.arange(EXPERTS, dtype=jnp.int32)[None, None, :]
    ).astype(F32)
    flat_hot = route_hot.reshape(tok_rows * 2, EXPERTS).astype(BF16)
    order = jnp.arange(tok_rows * 2, dtype=jnp.int32)
    earlier = (order[:, None] > order[None, :]).astype(BF16)
    ranks = dot(earlier, flat_hot)
    slot_index = jnp.sum(ranks * flat_hot.astype(F32), axis=1).astype(jnp.int32)
    target = (routes[0].reshape(tok_rows * 2) * CAP + slot_index).reshape(tok_rows, 2)
    slots = jnp.arange(EXPERTS * CAP, dtype=jnp.int32)
    picks = [(target[:, k : k + 1] == slots[None, :]) for k in range(2)]
    sends = [(target[:, k][None, :] == slots[:, None]) for k in range(2)]
    send_hot = (sends[0] | sends[1]).astype(BF16)

    def to_experts(rows):
        return lax.all_to_all(
            rows.reshape((EXPERTS, CAP) + rows.shape[1:]),
            OWNERS,
            split_axis=0,
            concat_axis=0,
            tiled=True,
        ).reshape(rows.shape)

    inputs = tokens[0].astype(F32)
    scale_first = norm_scale(inputs)
    norm_first = inputs * scale_first
    if not special:
        first = (norm_first * gain_first).astype(BF16)
        projected = dot(first, w_qkv).astype(BF16)
        kv = lax.all_gather(projected[:, head_width:], CTX, axis=0, tiled=True)
    kv, grad_y_send = lax.optimization_barrier((kv, dot(send_hot, cotangent[0]).astype(BF16)))
    grad_y_rows = to_experts(grad_y_send)
    mine = (lax.axis_index(CTX) * (tok_rows // BLK)).astype(jnp.int32).reshape(1)
    exact, attended, lse = attend(lengths, block_order, mine, projected, kv)
    middle = inputs + dot(attended, w_attn_out)
    scale_second = norm_scale(middle)
    norm_second = middle * scale_second
    second = (norm_second * gain_second).astype(BF16)
    logits = dot(second, w_router)
    chosen = jnp.sum(route_hot * logits[:, None, :], axis=-1)
    gates = jax.nn.softmax(chosen, axis=-1)

    gate_rows = jnp.sum(
        jnp.where(sends[0], gates[:, 0][None, :], 0.0) + jnp.where(sends[1], gates[:, 1][None, :], 0.0),
        axis=1,
        keepdims=True,
    )
    if special:
        slot_gates = jnp.broadcast_to(
            jnp.pad(gate_rows.reshape(EXPERTS, 1, CAP), ((0, 0), (0, 0), (0, 128 - CAP))), (EXPERTS, 8, 128)
        )
        expert_rows, grad_returned, gate_grads, grad_in, grad_down = experts(
            dot(send_hot, second).astype(BF16).reshape(EXPERTS, CAP, D),
            slot_gates,
            grad_y_rows.reshape(EXPERTS, CAP, D),
            w_in,
            w_down,
            exp_local,
        )
        returned = to_experts(expert_rows.reshape(EXPERTS * CAP, D))
        grad_returned = grad_returned.reshape(EXPERTS * CAP, D)
        gate_grads = gate_grads[:, 0, :CAP].reshape(1, EXPERTS * CAP)
    else:
        def in_parts(column):
            high = lax.reduce_precision(column, 8, 7)
            rest = column - high
            mid = lax.reduce_precision(rest, 8, 7)
            parts = jnp.concatenate([high, mid, rest - mid], axis=1).astype(BF16)
            return jnp.pad(parts, ((0, 0), (0, AUX - 3)))

        gate_parts = in_parts(gate_rows)
        payload = to_experts(
            jnp.concatenate([dot(send_hot, second).astype(BF16), gate_parts], axis=1)
        )
        received = payload[:, :D]
        gate_got = jnp.sum(payload[:, D : D + 3].astype(F32), axis=1, keepdims=True)

        gate_up = dot(received, w_in)
        gate_part = gate_up[:, :FF]
        up_part = gate_up[:, FF:]
        sigmoid_gate = jax.nn.sigmoid(gate_part)
        silu_gate = gate_part * sigmoid_gate
        hidden = (silu_gate * up_part).astype(BF16)
        expert_rows = dot(hidden, w_down)
        expert_rows = expert_rows.astype(BF16)
        grad_y_rows = grad_y_rows.astype(F32)
        returned = to_experts(expert_rows)

        grad_rows = (gate_got * grad_y_rows).astype(BF16)
        gate_grad_parts = in_parts(
            jnp.sum(grad_y_rows * expert_rows.astype(F32), axis=1, keepdims=True)
        )
        half_d = D // 2
        grad_hidden = dot(grad_rows, w_down, ((1,), (1,)))
        grad_gate = (
            grad_hidden * up_part * sigmoid_gate * (1.0 + gate_part * (1.0 - sigmoid_gate))
        ).astype(BF16)
        grad_up = (grad_hidden * silu_gate).astype(BF16)
        grad_gate_up = jnp.concatenate([grad_gate, grad_up], axis=1)
        grad_back = dot(grad_gate_up, w_in, ((1,), (1,)))
        grad_returned = to_experts(jnp.concatenate([grad_back.astype(BF16), gate_grad_parts], axis=1))

        grad_in = jnp.stack(
            [dot(received, grad_gate, ((0,), (0,))), dot(received, grad_up, ((0,), (0,)))]
        ).astype(BF16)
        grad_down = jnp.stack(
            [
                dot(hidden, grad_rows[:, :half_d], ((0,), (0,))),
                dot(hidden, grad_rows[:, half_d:], ((0,), (0,))),
            ]
        ).astype(BF16)

        grad_in = lax.psum_scatter(grad_in, "core", scatter_dimension=0, tiled=True)[0]
        grad_down = lax.psum_scatter(grad_down, "core", scatter_dimension=0, tiled=True)[0]
        grad_returned, grad_in, grad_down = lax.optimization_barrier((grad_returned, grad_in, grad_down))
        gate_grads = jnp.sum(grad_returned[:, D:].astype(F32), axis=1).reshape(1, EXPERTS * CAP)
        grad_returned = grad_returned[:, :D]

    grad_y = cotangent[0].astype(F32)
    pick_hot = [p.astype(BF16) for p in picks]
    grad_gates = jnp.concatenate(
        [jnp.sum(jnp.where(p, gate_grads, 0.0), axis=1, keepdims=True) for p in picks], axis=1
    )
    grad_chosen = gates * (grad_gates - jnp.sum(gates * grad_gates, axis=-1, keepdims=True))
    grad_logits = jnp.sum(grad_chosen[:, :, None] * route_hot, axis=1).astype(BF16)
    grad_second = dot(pick_hot[0] + pick_hot[1], grad_returned) + dot(
        grad_logits, w_router, ((1,), (1,))
    )
    grad_gain_second = jnp.sum(grad_second * norm_second, axis=0)
    grad_norm_second = grad_second * gain_second
    grad_middle = grad_y + scale_second * (
        grad_norm_second
        - norm_second * jnp.mean(grad_norm_second * norm_second, axis=-1, keepdims=True)
    )
    grad_branch = grad_middle.astype(BF16)
    grad_attended = dot(grad_branch, w_attn_out, ((1,), (1,))).astype(BF16)
    grad_queries, grad_kv = attend_back(
        lengths, block_order, mine, projected, kv, grad_attended, lse, exact
    )
    grad_queries, grad_kv, returned = lax.optimization_barrier((grad_queries, grad_kv, returned))
    if special:
        block_out, grad_inputs, sum_qkv, sum_out, sum_aux, sum_in, sum_down = finish(
            grad_kv,
            grad_queries,
            first,
            tokens[0],
            gain_first[None, :],
            grad_middle,
            w_all,
            attended,
            second,
            jnp.pad(grad_logits, ((0, 0), (1, AUX - 1 - EXPERTS))),
            grad_gain_second[None, :],
            middle,
            returned,
            jnp.stack(pick_hot),
            gates,
            grad_in,
            grad_down,
            exp_local,
        )
        block_out, grad_inputs, sum_qkv, sum_out, sum_in, sum_down = settle(
            (
                (block_out, BF16),
                (grad_inputs, BF16),
                (sum_qkv, F32),
                (sum_out, F32),
                (sum_in, F32),
                (sum_down, F32),
            ),
            4,
        )
    else:
        grad_router = dot(second, grad_logits, ((0,), (0,)))
        grad_attn_out = dot(attended, grad_branch, ((0,), (0,)))
        late = jnp.concatenate([grad_gain_second[:, None], grad_router], axis=1)
        late = jnp.pad(late, ((0, 0), (0, AUX - late.shape[1])))
        late = jnp.concatenate([grad_attn_out.astype(BF16), late.astype(BF16)], axis=1)
        grad_kv = lax.psum_scatter(grad_kv, CTX, scatter_dimension=0, tiled=True)
        grad_projected = jnp.concatenate([grad_queries, grad_kv], axis=1)
        grad_qkv = dot(first, grad_projected, ((0,), (0,)))
        grad_first = dot(grad_projected, w_qkv, ((1,), (1,)))
        grad_gain_first = jnp.sum(grad_first * norm_first, axis=0)
        grad_norm_first = grad_first * gain_first
        grad_inputs = grad_middle + scale_first * (
            grad_norm_first
            - norm_first * jnp.mean(grad_norm_first * norm_first, axis=-1, keepdims=True)
        )
        grad_inputs = grad_inputs.astype(BF16)
        last = jnp.pad(grad_gain_first[:, None], ((0, 0), (0, AUX - 1)))
        part = jnp.concatenate([grad_qkv.astype(BF16), last.astype(BF16), late], axis=1)
        total = lax.psum_scatter(part, ALL, scatter_dimension=0, tiled=True).astype(F32)
        sum_qkv, sum_out = total[:, :cols], total[:, cols + AUX : cols + AUX + D]
        sum_aux = jnp.concatenate([total[:, cols : cols + AUX], total[:, cols + AUX + D :]], axis=1)
        picked = [dot(p, returned) for p in pick_hot]
        block_out = (middle + gates[:, 0:1] * picked[0] + gates[:, 1:2] * picked[1]).astype(BF16)

        def to_rows(half, rows):
            width = half.shape[1]
            got = lax.all_to_all(
                half.reshape(n_ctx, rows, width), CTX, split_axis=0, concat_axis=0, tiled=True
            ).astype(F32)
            got = got.reshape(exp_local, copies // 2, 2, rows, width).sum(axis=1)
            return got.transpose(0, 2, 1, 3).reshape(exp_local, rows, 2 * width)

        sum_in = to_rows(grad_in, in_rows)
        sum_down = to_rows(grad_down, out_rows)
    return (
        block_out[None],
        grad_inputs[None],
        sum_aux[:, 0],
        sum_qkv,
        sum_out,
        sum_aux[:, AUX],
        sum_aux[:, AUX + 1 : AUX + 1 + EXPERTS],
        sum_in.astype(F32),
        sum_down.astype(F32),
    )


def solution(mesh):
    n_ctx, n_exp = mesh.shape["ctx"], mesh.shape["exp"]
    exp_local = EXPERTS // n_exp
    copies = n_ctx // exp_local
    inner = Mesh(mesh.devices.reshape(exp_local, copies // 2, 2, n_exp), ALL)
    by_token = P("exp", CTX, None)
    by_row = P(ALL, None)
    by_expert = P("exp", CTX, None)
    return jax.shard_map(
        on_device,
        mesh=inner,
        in_specs=(
            by_token,
            by_token,
            by_token,
            P("exp", None),
            P("exp", None),
            P(ALL),
            by_row,
            by_row,
            P(ALL),
            by_row,
            by_expert,
            by_expert,
        ),
        out_specs=(
            by_token,
            by_token,
            P(ALL),
            by_row,
            by_row,
            P(ALL),
            by_row,
            by_expert,
            by_expert,
        ),
        check_vma=False,
    )
```

```python
import functools

import jax
import jax.numpy as jnp
from jax import lax
from jax.experimental import pallas as pl
from jax.experimental.pallas import tpu as pltpu
from jax.sharding import Mesh
from jax.sharding import PartitionSpec as P

D = 1536
HEADS = 24
KV_HEADS = 8
HEAD = 64
GROUP = HEADS // KV_HEADS
FF = 1024
EXPERTS = 16
BLK = 128
CAP = 48
AUX = 128

epsilon = 1e-05
far_negative = -1e30
start_max = -1e29
F32 = jnp.float32
BF16 = jnp.bfloat16


def norm_scale(values):
    return lax.rsqrt(jnp.mean(values * values, axis=-1, keepdims=True) + epsilon)


def dot(a, b, dims=((1,), (0,))):
    return lax.dot_general(a, b, (dims, ((), ())), preferred_element_type=F32)


def lane_half(shape, half):
    lane = lax.broadcasted_iota(jnp.int32, shape, 1)
    return (lane >= HEAD) if half else (lane < HEAD)


def head_tiles(ref, rows, pair, scale):
    tiles = []
    for i in range(2 * GROUP):
        head = pair * 2 * GROUP + i
        group = head // GROUP
        tile = ref[rows, (head // 2) * 128 : (head // 2 + 1) * 128].astype(F32)
        if head % 2 != group % 2:
            tile = pltpu.roll(tile, HEAD, 1)
        tile = jnp.where(lane_half(tile.shape, group % 2), tile * scale, 0.0)
        tiles.append(tile.astype(BF16))
    return jnp.concatenate(tiles, axis=0)


def block_visibility(lengths_ref, query_block, key_block, parts):
    lanes = lax.broadcasted_iota(jnp.int32, (1, BLK), 1)
    query_pos = query_block * BLK + lanes
    start = jnp.zeros((1, BLK), jnp.int32)
    bound = jnp.int32(0)
    for s in range(parts - 1):
        bound = bound + lengths_ref[0, s]
        start = jnp.where(query_pos >= bound, bound, start)
    key_pos = key_block * BLK + lax.broadcasted_iota(jnp.int32, (BLK, BLK), 0)
    one = ((key_pos >= start) & (key_pos <= query_pos)).astype(jnp.int32)
    return jnp.concatenate([one] * (2 * GROUP), axis=1) > 0


def first_row_start(lengths_ref, query_block, parts):
    start = jnp.int32(0)
    bound = jnp.int32(0)
    for s in range(parts - 1):
        bound = bound + lengths_ref[0, s]
        start = jnp.where(query_block * BLK >= bound, bound, start)
    return start


def attend_kernel(
    parts, lengths_ref, order_ref, mine_ref, q_ref, kv_ref, exact_ref, out_ref, lse_ref, q_s, m_s, sum_s, acc_s
):
    width = KV_HEADS * HEAD
    wide = 2 * GROUP * BLK
    for qb in range(q_ref.shape[0] // BLK):
        rows = pl.ds(qb * BLK, BLK)
        for pair in range(KV_HEADS // 2):
            q_s[pair] = head_tiles(q_ref, rows, pair, HEAD**-0.5)
            m_s[pair] = jnp.full((8, wide), start_max, F32)
            sum_s[pair] = jnp.zeros((8, wide), F32)
            acc_s[pair] = jnp.zeros((BLK, wide), F32)
        query_block = order_ref[0, mine_ref[0] + qb]
        first = first_row_start(lengths_ref, query_block, parts)

        @pl.loop(0, order_ref.shape[1])
        def _(kb):
            key_block = order_ref[0, kb]

            @pl.when((key_block <= query_block) & (key_block * BLK + BLK > first))
            def _():
                seen = block_visibility(lengths_ref, query_block, key_block, parts)
                key_rows = pl.ds(kb * BLK, BLK)
                for pair in range(KV_HEADS // 2):
                    keys = kv_ref[key_rows, pl.ds(pair * 128, 128)]
                    values = kv_ref[key_rows, pl.ds(width + pair * 128, 128)]
                    scores = dot(keys, q_s[pair], ((1,), (1,)))
                    scores = jnp.where(seen, scores, far_negative)
                    old = m_s[pair, 0:1, :]
                    new = jnp.maximum(old, jnp.max(scores, axis=0, keepdims=True))
                    weights = jnp.exp(scores - new)
                    factor = jnp.exp(old - new)
                    sum_s[pair, 0:1, :] = sum_s[pair, 0:1, :] * factor + jnp.sum(
                        weights, axis=0, keepdims=True
                    )
                    acc_s[pair] = acc_s[pair] * factor + dot(values, weights.astype(BF16), ((0,), (0,)))
                    m_s[pair, 0:1, :] = new

        tiles = []
        for pair in range(KV_HEADS // 2):
            total = sum_s[pair, 0:1, :]
            lse_ref[qb, pair : pair + 1, :] = m_s[pair, 0:1, :] + jnp.log(total)
            acc = acc_s[pair] / total
            for i in range(2 * GROUP):
                head = pair * 2 * GROUP + i
                tile = jnp.transpose(acc[:, i * BLK : (i + 1) * BLK])
                if head % 2 != (head // GROUP) % 2:
                    tile = pltpu.roll(tile, HEAD, 1)
                tiles.append(tile)
                if head % 2 == 1:
                    both = jnp.where(lane_half(tile.shape, 0), tiles[head - 1], tile)
                    lanes = pl.ds((head // 2) * 128, 128)
                    exact_ref[rows, lanes] = both
                    out_ref[rows, lanes] = both.astype(BF16)


def attend(lengths, order, mine, projected, kv):
    rows = projected.shape[0]
    smem = pl.BlockSpec(memory_space=pltpu.SMEM)
    vmem = pl.BlockSpec(memory_space=pltpu.VMEM)
    wide = 2 * GROUP * BLK
    pairs = KV_HEADS // 2
    return pl.pallas_call(
        functools.partial(attend_kernel, lengths.shape[1]),
        out_shape=(
            jax.ShapeDtypeStruct((rows, HEADS * HEAD), F32),
            jax.ShapeDtypeStruct((rows, HEADS * HEAD), BF16),
            jax.ShapeDtypeStruct((rows // BLK, pairs, wide), F32),
        ),
        in_specs=[smem, smem, smem, vmem, vmem],
        out_specs=(vmem, vmem, vmem),
        scratch_shapes=[
            pltpu.VMEM((pairs, wide, 128), BF16),
            pltpu.VMEM((pairs, 8, wide), F32),
            pltpu.VMEM((pairs, 8, wide), F32),
            pltpu.VMEM((pairs, BLK, wide), F32),
        ],
        compiler_params=pltpu.CompilerParams(vmem_limit_bytes=48 * 2**20),
        cost_estimate=pl.CostEstimate(flops=10**10, bytes_accessed=10**7, transcendentals=10**7),
        name="attend",
    )(lengths, order, mine, projected, kv)


def attend_back_kernel(
    parts,
    lengths_ref,
    order_ref,
    mine_ref,
    q_ref,
    kv_ref,
    grad_ref,
    lse_ref,
    exact_ref,
    dq_ref,
    dkv_ref,
    q_s,
    g_s,
    delta_s,
    dq_s,
    dkv_s,
):
    width = KV_HEADS * HEAD

    @pl.loop(0, order_ref.shape[1])
    def _(kb):
        dkv_s[pl.ds(kb * BLK, BLK), :] = jnp.zeros((BLK, 2 * width), F32)

    for qb in range(q_ref.shape[0] // BLK):
        rows = pl.ds(qb * BLK, BLK)
        for pair in range(KV_HEADS // 2):
            q_s[pair] = head_tiles(q_ref, rows, pair, HEAD**-0.5)
            g_s[pair] = head_tiles(grad_ref, rows, pair, 1.0)
            dq_s[pair] = jnp.zeros((2 * GROUP * BLK, 128), F32)
            for i in range(2 * GROUP):
                head = pair * 2 * GROUP + i
                exact = exact_ref[rows, (head // 2) * 128 : (head // 2 + 1) * 128]
                if head % 2 != (head // GROUP) % 2:
                    exact = pltpu.roll(exact, HEAD, 1)
                product = exact * g_s[pair, i * BLK : (i + 1) * BLK, :].astype(F32)
                delta_s[pair : pair + 1, i * BLK : (i + 1) * BLK] = jnp.sum(
                    jnp.transpose(product), axis=0, keepdims=True
                )
        query_block = order_ref[0, mine_ref[0] + qb]
        first = first_row_start(lengths_ref, query_block, parts)

        @pl.loop(0, order_ref.shape[1])
        def _(kb):
            key_block = order_ref[0, kb]

            @pl.when((key_block <= query_block) & (key_block * BLK + BLK > first))
            def _():
                seen = block_visibility(lengths_ref, query_block, key_block, parts)
                key_rows = pl.ds(kb * BLK, BLK)
                for pair in range(KV_HEADS // 2):
                    key_lanes = pl.ds(pair * 128, 128)
                    value_lanes = pl.ds(width + pair * 128, 128)
                    keys = kv_ref[key_rows, key_lanes]
                    values = kv_ref[key_rows, value_lanes]
                    scores = dot(keys, q_s[pair], ((1,), (1,)))
                    scores = jnp.where(seen, scores, far_negative)
                    probs = jnp.exp(scores - lse_ref[qb, pair : pair + 1, :])
                    grad_probs = dot(values, g_s[pair], ((1,), (1,)))
                    grad_scores = (probs * (grad_probs - delta_s[pair : pair + 1, :])).astype(BF16)
                    dkv_s[key_rows, value_lanes] += dot(probs.astype(BF16), g_s[pair])
                    dkv_s[key_rows, key_lanes] += dot(grad_scores, q_s[pair])
                    dq_s[pair] += dot(grad_scores, keys, ((0,), (0,)))

        tiles = []
        for pair in range(KV_HEADS // 2):
            for i in range(2 * GROUP):
                head = pair * 2 * GROUP + i
                tile = dq_s[pair, i * BLK : (i + 1) * BLK, :] * HEAD**-0.5
                if head % 2 != (head // GROUP) % 2:
                    tile = pltpu.roll(tile, HEAD, 1)
                tiles.append(tile)
                if head % 2 == 1:
                    both = jnp.where(lane_half(tile.shape, 0), tiles[head - 1], tile)
                    dq_ref[rows, (head // 2) * 128 : (head // 2 + 1) * 128] = both.astype(BF16)

    @pl.loop(0, order_ref.shape[1])
    def _(kb):
        key_rows = pl.ds(kb * BLK, BLK)
        dkv_ref[key_rows, :] = dkv_s[key_rows, :].astype(BF16)


def attend_back(lengths, order, mine, projected, kv, grad_attended, lse, exact):
    rows = projected.shape[0]
    smem = pl.BlockSpec(memory_space=pltpu.SMEM)
    vmem = pl.BlockSpec(memory_space=pltpu.VMEM)
    wide = 2 * GROUP * BLK
    pairs = KV_HEADS // 2
    return pl.pallas_call(
        functools.partial(attend_back_kernel, lengths.shape[1]),
        out_shape=(
            jax.ShapeDtypeStruct((rows, HEADS * HEAD), BF16),
            jax.ShapeDtypeStruct(kv.shape, BF16),
        ),
        in_specs=[smem, smem, smem, vmem, vmem, vmem, vmem, vmem],
        out_specs=(vmem, vmem),
        scratch_shapes=[
            pltpu.VMEM((pairs, wide, 128), BF16),
            pltpu.VMEM((pairs, wide, 128), BF16),
            pltpu.VMEM((pairs, wide), F32),
            pltpu.VMEM((pairs, wide, 128), F32),
            pltpu.VMEM(kv.shape, F32),
        ],
        compiler_params=pltpu.CompilerParams(vmem_limit_bytes=56 * 2**20),
        cost_estimate=pl.CostEstimate(flops=10**9, bytes_accessed=10**6, transcendentals=10**5),
        name="attend_back",
    )(lengths, order, mine, projected, kv, grad_attended, lse, exact)


MESH = pl.DeviceIdType.MESH


def place(z, core, exp):
    return {"le": z, "rep": 0, "core": core, "exp": exp}


def x_of(exp):
    return (exp // 2) * 2 + 1 - exp % 2


def y_of(exp):
    return (1 - exp // 2) * 2 + exp % 2


def remote(src, dst, send_sem, recv_sem, device):
    return pltpu.make_async_remote_copy(
        src_ref=src,
        dst_ref=dst,
        send_sem=send_sem,
        recv_sem=recv_sem,
        device_id=device,
        device_id_type=MESH,
    )


def near_to_far(z):
    first_half = z < 2
    return [z, z + 1 - 2 * (z % 2), jnp.where(first_half, 3, 0), jnp.where(first_half, 2, 1)]


def between(z, zz):
    return ((z == 1) & (zz == 2)) | ((z == 2) & (zz == 1))


def meet(devices):
    barrier = pltpu.get_barrier_semaphore()
    for device in devices:
        pl.semaphore_signal(barrier, inc=1, device_id=device, device_id_type=MESH)
    pl.semaphore_wait(barrier, len(devices))


def front_kernel(
    layers,
    shard_ref,
    in_ref,
    down_ref,
    tokens_ref,
    w_all_ref,
    w_in_ref,
    w_down_ref,
    first_ref,
    projected_ref,
    kv_ref,
    weights,
    in_wide,
    down_wide,
    in_half,
    down_half,
    unit_sem,
    line_sem,
    x_sem,
    y_sem,
    far_sem,
    core_sem,
    half_sem,
    half_send,
    over_sem,
    over_send,
    kv_sem,
    kv_send,
    own_sem,
    wide_sem,
):
    z, core, exp = lax.axis_index("le"), lax.axis_index("core"), lax.axis_index("exp")
    other = 1 - core
    x, y = x_of(exp), y_of(exp)
    ctx = z * 2 + core
    rows = shard_ref.shape[0]
    own_layer, mate, farthest, middle = near_to_far(z)
    order = [mate, farthest, middle, own_layer]
    wides = ((in_ref, in_wide), (down_ref, down_wide))
    halves = ((in_half, w_in_ref), (down_half, w_down_ref))

    loads = []
    for k, zz in enumerate(order):
        for a in range(2):
            load = pltpu.make_async_copy(wides[a][0].at[zz], wides[a][1].at[zz], wide_sem.at[a, k])
            load.start()
            loads.append(load)
    meet(
        [
            place((z + s) % layers, (core + p) % 2, exp)
            for s in range(layers)
            for p in range(2)
            if s + p > 0
        ]
        + [place(z, core, x), place(z, core, y)]
    )

    def number(zz, cc, ee):
        return (zz * 2 + cc) * 4 + ee

    def unit(zz, cc, ee):
        return weights.at[pl.ds(pl.multiple_of(number(zz, cc, ee) * rows, 16), rows), :]

    def send(src, who, sem, device):
        return remote(src, unit(*who), sem, unit_sem.at[number(*who)], device)

    def arrive(who):
        send(unit(*who), who, line_sem.at[0], place(z, other, exp)).wait_recv()

    started = []

    def go(copy, condition=None):
        if condition is None:
            copy.start()
        else:
            pl.when(condition)(copy.start)
        started.append((copy, condition))

    me = (z, core, exp)
    keep = pltpu.make_async_copy(shard_ref, unit(*me), own_sem.at[0])
    keep.start()
    go(send(shard_ref, me, line_sem.at[layers], place(z + 1, core, exp)), z < layers - 1)
    go(send(shard_ref, me, line_sem.at[layers + 1], place(z - 1, core, exp)), z > 0)
    go(send(shard_ref, me, x_sem.at[layers], place(z, core, x)))
    go(send(shard_ref, me, y_sem.at[layers], place(z, core, y)))
    go(send(shard_ref, me, core_sem.at[layers], place(z, other, exp)))

    slab = 16
    for k, zz in enumerate(order):
        for a in range(2):
            loads[2 * k + a].wait()
            src, dst = wides[a][1], halves[a][0]

            @pl.loop(0, src.shape[1] // slab)
            def _(i, zz=zz, src=src, dst=dst):
                at = pl.ds(pl.multiple_of(i * slab, slab), slab)
                dst[zz, at, :] = src[zz, at, :].astype(BF16)

    def half(a, source, p):
        src, dst = halves[a]
        n, cols = src.shape[1], src.shape[2] // 2
        return dst.at[pl.ds(source * n, n), pl.ds(pl.multiple_of(p * cols, 128), cols)]

    def mine(a, zz, p):
        src = halves[a][0]
        cols = src.shape[2] // 2
        return src.at[zz, :, pl.ds(pl.multiple_of(p * cols, 128), cols)]

    def layer(k):
        return jnp.where(z < layers // 2, k, layers - 1 - k)

    def ahead(zz):
        return between(z, zz)

    def hand_out(a, early):
        for s, zz in enumerate(order):
            across = ahead(zz)
            for p in range(2):
                if s == layers - 1 and p == 0:
                    continue
                pp = (core + p) % 2
                copy = remote(
                    mine(a, zz, pp),
                    half(a, ctx, pp),
                    half_send.at[a, s * 2 + p],
                    half_sem.at[a, ctx],
                    place(zz, pp, exp),
                )
                if early:
                    pl.when(across)(copy.start)
                else:
                    pl.when(~across)(copy.start)
                    started.append((copy, None))
        if not early:
            go(
                remote(
                    mine(a, z, core),
                    half(a, ctx, core),
                    over_send.at[a, 2 * layers],
                    over_sem.at[a, ctx],
                    place(z, other, exp),
                )
            )

    for k in range(layers):
        zz = layer(k)
        who = (zz, core, exp)

        @pl.when(zz != z)
        def _(who=who):
            arrive(who)

        go(send(unit(*who), who, line_sem.at[k], place(z + 1, core, exp)), (zz < z) & (z < layers - 1))
        go(send(unit(*who), who, line_sem.at[k], place(z - 1, core, exp)), (zz > z) & (z > 0))
        go(send(unit(*who), who, x_sem.at[k], place(z, core, x)), zz != z)
        go(send(unit(*who), who, y_sem.at[k], place(z, core, y)), zz != z)
        go(send(unit(*who), who, core_sem.at[k], place(z, other, exp)), zz != z)
        if k == 0:
            hand_out(0, True)

    for a in range(2):
        pltpu.make_async_copy(mine(a, z, core), half(a, ctx, core), own_sem.at[1 + a]).start()

    hand_out(0, False)

    for k in range(layers):
        zz = layer(k)
        from_x, from_y = (zz, core, x), (zz, core, y)
        arrive(from_x)
        go(send(unit(*from_x), from_x, core_sem.at[layers + 1 + k], place(z, other, exp)))
        if k % 2 == 0:
            go(send(unit(*from_x), from_x, far_sem.at[k], place(z, core, y)))
        arrive(from_y)
        go(send(unit(*from_y), from_y, core_sem.at[2 * layers + 1 + k], place(z, other, exp)))
        if k % 2 == 1:
            go(send(unit(*from_y), from_y, far_sem.at[k], place(z, core, x)))
    for k in range(layers):
        far = (layer(k), core, y_of(x))
        arrive(far)
        go(send(unit(*far), far, core_sem.at[3 * layers + 1 + k], place(z, other, exp)))
    for ee in range(4):
        for zz in range(layers):
            arrive((zz, other, ee))
    keep.wait()
    save = pltpu.make_async_copy(weights, w_all_ref, own_sem.at[3])
    save.start()

    depth, count = tokens_ref.shape[1], tokens_ref.shape[0]
    qkv_cols, head_cols = projected_ref.shape[1], HEADS * HEAD
    inputs = tokens_ref[...].astype(F32)
    gain = jnp.concatenate(
        [
            jnp.transpose(weights[i * 128 : (i + 1) * 128, qkv_cols : qkv_cols + AUX].astype(F32))[0:1, :]
            for i in range(depth // 128)
        ],
        axis=1,
    )
    first_ref[...] = (inputs * norm_scale(inputs) * gain).astype(BF16)
    tile = 512

    @pl.loop(0, (qkv_cols - head_cols) // tile)
    def _(i):
        at = pl.ds(pl.multiple_of(head_cols + i * tile, tile), tile)
        projected_ref[:, at] = dot(first_ref[...], weights[:, at]).astype(BF16)

    def block(source):
        return kv_ref.at[pl.ds(pl.multiple_of(source * count, 16), count), :]

    def share(src, source, sem, device):
        return remote(src, block(source), sem, kv_sem.at[source], device)

    own = projected_ref.at[:, pl.ds(head_cols, qkv_cols - head_cols)]
    keep_kv = pltpu.make_async_copy(own, block(ctx), own_sem.at[0])
    keep_kv.start()
    go(share(own, ctx, kv_send.at[2 * layers], place(z + 1, core, exp)), z < layers - 1)
    go(share(own, ctx, kv_send.at[2 * layers + 1], place(z - 1, core, exp)), z > 0)
    go(share(own, ctx, kv_send.at[2 * layers + 2], place(z, other, exp)))

    @pl.loop(0, head_cols // tile)
    def _(i):
        at = pl.ds(pl.multiple_of(i * tile, tile), tile)
        projected_ref[:, at] = dot(first_ref[...], weights[:, at]).astype(BF16)

    for k in range(layers):
        zz = layer(k)
        source = zz * 2 + core

        @pl.when(zz != z)
        def _(source=source):
            share(block(source), source, kv_send.at[0], place(z, other, exp)).wait_recv()

        go(share(block(source), source, kv_send.at[k], place(z + 1, core, exp)), (zz < z) & (z < layers - 1))
        go(share(block(source), source, kv_send.at[k], place(z - 1, core, exp)), (zz > z) & (z > 0))
        go(share(block(source), source, kv_send.at[layers + k], place(z, other, exp)), zz != z)
        if k == layers // 2:
            hand_out(1, True)
            hand_out(1, False)

    for s, zz in enumerate(order[::-1]):
        for p in range(2):
            if s == 0 and p == 0:
                continue
            source = zz * 2 + (core + p) % 2
            for a in range(2):
                remote(
                    half(a, source, core),
                    half(a, source, core),
                    half_send.at[a, 0],
                    half_sem.at[a, source],
                    place(z, other, exp),
                ).wait_recv()
                go(
                    remote(
                        half(a, source, core),
                        half(a, source, core),
                        over_send.at[a, s * 2 + p],
                        over_sem.at[a, source],
                        place(z, other, exp),
                    )
                )

    for zz in range(layers):
        source = zz * 2 + other
        share(block(source), source, kv_send.at[0], place(z, other, exp)).wait_recv()
    for source in range(2 * layers):
        for a in range(2):
            remote(
                half(a, source, other),
                half(a, source, other),
                half_send.at[a, 0],
                over_sem.at[a, source],
                place(z, other, exp),
            ).wait_recv()
    keep_kv.wait()
    save.wait()
    for a in range(2):
        pltpu.make_async_copy(mine(a, z, core), half(a, ctx, core), own_sem.at[1 + a]).wait()
    for copy, condition in started:
        if condition is None:
            copy.wait_send()
        else:
            pl.when(condition)(copy.wait_send)


def front(shard, expert_in, expert_out, tokens, qkv_cols):
    layers = expert_in.shape[0]
    rows_in, rows_out = expert_in.shape[1], expert_out.shape[1]
    depth, cols = shard.shape[0] * 8 * layers, shard.shape[1]
    count = tokens.shape[0]
    any_space = pl.BlockSpec(memory_space=pl.ANY)
    vmem = pl.BlockSpec(memory_space=pltpu.VMEM)
    dma = pltpu.SemaphoreType.DMA
    return pl.pallas_call(
        functools.partial(front_kernel, layers),
        out_shape=(
            jax.ShapeDtypeStruct((depth, cols), BF16),
            jax.ShapeDtypeStruct((rows_in * 2 * layers, expert_in.shape[2]), BF16),
            jax.ShapeDtypeStruct((rows_out * 2 * layers, expert_out.shape[2]), BF16),
            jax.ShapeDtypeStruct((count, depth), BF16),
            jax.ShapeDtypeStruct((count, qkv_cols), BF16),
            jax.ShapeDtypeStruct((count * 2 * layers, qkv_cols - HEADS * HEAD), BF16),
        ),
        in_specs=[any_space] * 3 + [vmem],
        out_specs=(any_space,) * 3 + (vmem, vmem, any_space),
        scratch_shapes=[
            pltpu.VMEM((depth, cols), BF16),
            pltpu.VMEM(expert_in.shape, F32),
            pltpu.VMEM(expert_out.shape, F32),
            pltpu.VMEM(expert_in.shape, BF16),
            pltpu.VMEM(expert_out.shape, BF16),
            dma((8 * layers,)),
            dma((layers + 2,)),
            dma((layers + 1,)),
            dma((layers + 1,)),
            dma((layers,)),
            dma((4 * layers + 1,)),
            dma((2, 2 * layers)),
            dma((2, 2 * layers)),
            dma((2, 2 * layers)),
            dma((2, 2 * layers + 1)),
            dma((2 * layers,)),
            dma((2 * layers + 3,)),
            dma((4,)),
            dma((2, layers)),
        ],
        compiler_params=pltpu.CompilerParams(
            collective_id=0, has_side_effects=True, vmem_limit_bytes=48 * 2**20
        ),
        name="front",
    )(shard, expert_in, expert_out, tokens)


def experts_kernel(
    layers,
    rows_ref,
    gates_ref,
    grads_ref,
    w_in_ref,
    w_down_ref,
    out_ref,
    back_ref,
    back_gates_ref,
    d_in_ref,
    d_down_ref,
    w_in,
    w_down,
    got,
    got_gates,
    x_s,
    grad_s,
    hidden_s,
    inner_s,
    back_s,
    back_gates_s,
    other_in,
    other_down,
    pair_in,
    pair_down,
    row_sem,
    row_send,
    gate_sem,
    gate_send,
    back_sem,
    back_send,
    back_gate_sem,
    back_gate_send,
    pair_sem,
    pair_send,
    load_sem,
):
    z, core, exp = lax.axis_index("le"), lax.axis_index("core"), lax.axis_index("exp")
    other = 1 - core
    columns = rows_ref.shape[0] // layers
    me = exp * layers + z
    cap, depth = rows_ref.shape[1], rows_ref.shape[2]
    chunk = columns * cap
    loads = [
        pltpu.make_async_copy(w_in_ref, w_in, load_sem.at[0]),
        pltpu.make_async_copy(w_down_ref, w_down, load_sem.at[1]),
    ]
    for load in loads:
        load.start()
    own_layer, mate, farthest, middle = near_to_far(z)
    peers = [
        (zz, (exp + t) % columns)
        for s, zz in enumerate([mate, farthest, middle, own_layer])
        for t in range(columns)
        if not (s == layers - 1 and t == 0)
    ]
    meet([place(zz, core, ee) for zz, ee in peers] + [place(z, other, exp)])

    started = []

    def go(copy):
        copy.start()
        started.append(copy)

    keeps = [
        pltpu.make_async_copy(rows_ref.at[me], got.at[me], load_sem.at[2]),
        pltpu.make_async_copy(gates_ref.at[me], got_gates.at[me], load_sem.at[3]),
    ]
    for keep in keeps:
        keep.start()
    for k, (zz, ee) in enumerate(peers):
        there = ee * layers + zz
        go(remote(gates_ref.at[there], got_gates.at[me], gate_send.at[k], gate_sem.at[me], place(zz, core, ee)))
        go(remote(rows_ref.at[there], got.at[me], row_send.at[k], row_sem.at[me], place(zz, core, ee)))
    for load in loads + keeps:
        load.wait()

    eye = lax.broadcasted_iota(jnp.int32, (cap, 128), 0) == lax.broadcasted_iota(jnp.int32, (cap, 128), 1)
    tile = 256

    def tiles(i):
        return pl.ds(pl.multiple_of(i * tile, tile), tile)

    for k, zz in enumerate([own_layer, mate, farthest, middle]):
        rows = pl.ds(k * chunk, chunk)
        for ee in range(columns):
            source = ee * layers + zz

            @pl.when(source != me)
            def _(source=source):
                here = place(z, other, exp)
                remote(got.at[source], got.at[source], row_send.at[0], row_sem.at[source], here).wait_recv()
                remote(
                    got_gates.at[source], got_gates.at[source], gate_send.at[0], gate_sem.at[source], here
                ).wait_recv()

            at = pl.ds(k * chunk + ee * cap, cap)
            x_s[at, :] = got[source]
            gate = jnp.sum(jnp.where(eye, got_gates[source, 0:1, :], 0.0), axis=1, keepdims=True)
            grad_s[at, :] = (gate * grads_ref[source].astype(F32)).astype(BF16)

        @pl.loop(0, FF // tile)
        def _(i, rows=rows):
            up_at = pl.ds(pl.multiple_of(FF + i * tile, tile), tile)
            gate = dot(x_s[rows, :], w_in[:, tiles(i)])
            up = dot(x_s[rows, :], w_in[:, up_at])
            grad_hidden = dot(grad_s[rows, :], w_down[tiles(i), :], ((1,), (1,)))
            sigmoid = jax.nn.sigmoid(gate)
            silu = gate * sigmoid
            hidden_s[rows, tiles(i)] = (silu * up).astype(BF16)
            inner_s[rows, tiles(i)] = (grad_hidden * up * sigmoid * (1.0 + gate * (1.0 - sigmoid))).astype(BF16)
            inner_s[rows, up_at] = (grad_hidden * silu).astype(BF16)

        @pl.loop(0, depth // tile)
        def _(i, rows=rows, zz=zz):
            back = dot(inner_s[rows, :], w_in[tiles(i), :], ((1,), (1,))).astype(BF16)
            for ee in range(columns):
                back_s[ee * layers + zz, :, tiles(i)] = back[ee * cap : (ee + 1) * cap]

        @pl.loop(0, depth // tile, init_carry=jnp.zeros((chunk, 128), F32))
        def gate_grads(i, sums, rows=rows, zz=zz):
            result = dot(hidden_s[rows, :], w_down[:, tiles(i)]).astype(BF16)
            parts = []
            for ee in range(columns):
                part = result[ee * cap : (ee + 1) * cap]
                out_ref[ee * layers + zz, :, tiles(i)] = part
                parts.append(part.astype(F32) * grads_ref[ee * layers + zz, :, tiles(i)].astype(F32))
            product = jnp.concatenate(parts, axis=0)
            return sums + product[:, :128] + product[:, 128:]

        gate_grads = jnp.sum(gate_grads, axis=1, keepdims=True)
        for ee in range(columns):
            there = ee * layers + zz
            column = gate_grads[ee * cap : (ee + 1) * cap]
            line = jnp.sum(jnp.where(eye, column, 0.0), axis=0, keepdims=True)
            back_gates_s[there] = jnp.broadcast_to(line, (8, 128))
            row_copy = remote(
                back_s.at[there],
                back_ref.at[me],
                back_send.at[there],
                back_sem.at[me],
                place(zz, core, ee),
            )
            gate_copy = remote(
                back_gates_s.at[there],
                back_gates_ref.at[me],
                back_gate_send.at[there],
                back_gate_sem.at[me],
                place(zz, core, ee),
            )

            @pl.when(there != me)
            def _(row_copy=row_copy, gate_copy=gate_copy):
                row_copy.start()
                gate_copy.start()

    own = [
        pltpu.make_async_copy(back_s.at[me], back_ref.at[me], load_sem.at[2]),
        pltpu.make_async_copy(back_gates_s.at[me], back_gates_ref.at[me], load_sem.at[3]),
    ]
    for copy in own:
        copy.start()

    half_in, half_down = d_in_ref.shape[1], d_down_ref.shape[1]

    def in_part(i, p):
        cols = pl.ds(pl.multiple_of(p * half_in, 128), half_in)
        return dot(x_s[:, tiles(i)], inner_s[:, cols], ((0,), (0,)))

    def down_part(i, p):
        cols = pl.ds(pl.multiple_of(p * half_down, 128), half_down)
        return dot(hidden_s[:, tiles(i)], grad_s[:, cols], ((0,), (0,)))

    @pl.loop(0, depth // tile)
    def _(i):
        other_in[tiles(i), :] = in_part(i, other).astype(BF16)

    go(remote(other_in, pair_in, pair_send.at[0], pair_sem.at[0], place(z, other, exp)))

    @pl.loop(0, FF // tile)
    def _(i):
        other_down[tiles(i), :] = down_part(i, other).astype(BF16)

    go(remote(other_down, pair_down, pair_send.at[1], pair_sem.at[1], place(z, other, exp)))
    remote(other_in, pair_in, pair_send.at[0], pair_sem.at[0], place(z, other, exp)).wait_recv()

    @pl.loop(0, depth // tile)
    def _(i):
        d_in_ref[tiles(i), :] = (in_part(i, core) + pair_in[tiles(i), :].astype(F32)).astype(BF16)

    remote(other_down, pair_down, pair_send.at[1], pair_sem.at[1], place(z, other, exp)).wait_recv()

    @pl.loop(0, FF // tile)
    def _(i):
        d_down_ref[tiles(i), :] = (down_part(i, core) + pair_down[tiles(i), :].astype(F32)).astype(BF16)

    for copy in own:
        copy.wait()
    for k, (zz, ee) in enumerate(peers):
        there = ee * layers + zz
        row_copy = remote(
            back_s.at[there], back_ref.at[there], back_send.at[there], back_sem.at[there], place(zz, core, ee)
        )
        gate_copy = remote(
            back_gates_s.at[there],
            back_gates_ref.at[there],
            back_gate_send.at[there],
            back_gate_sem.at[there],
            place(zz, core, ee),
        )
        row_copy.wait()
        gate_copy.wait()
    for copy in started:
        copy.wait_send()


def experts(rows, gates, grads, w_in, w_down, layers):
    count, cap, depth = rows.shape
    any_space = pl.BlockSpec(memory_space=pl.ANY)
    vmem = pl.BlockSpec(memory_space=pltpu.VMEM)
    dma = pltpu.SemaphoreType.DMA
    half_in = jax.ShapeDtypeStruct((depth, FF), BF16)
    half_down = jax.ShapeDtypeStruct((FF, depth // 2), BF16)
    return pl.pallas_call(
        functools.partial(experts_kernel, layers),
        out_shape=(
            jax.ShapeDtypeStruct(rows.shape, BF16),
            jax.ShapeDtypeStruct(rows.shape, BF16),
            jax.ShapeDtypeStruct(gates.shape, F32),
            half_in,
            half_down,
        ),
        in_specs=[any_space, any_space, vmem, any_space, any_space],
        out_specs=(vmem, any_space, any_space, vmem, vmem),
        scratch_shapes=[
            pltpu.VMEM(w_in.shape, BF16),
            pltpu.VMEM(w_down.shape, BF16),
            pltpu.VMEM(rows.shape, BF16),
            pltpu.VMEM(gates.shape, F32),
            pltpu.VMEM((count * cap, depth), BF16),
            pltpu.VMEM((count * cap, depth), BF16),
            pltpu.VMEM((count * cap, FF), BF16),
            pltpu.VMEM((count * cap, 2 * FF), BF16),
            pltpu.VMEM(rows.shape, BF16),
            pltpu.VMEM(gates.shape, F32),
            pltpu.VMEM(half_in.shape, BF16),
            pltpu.VMEM(half_down.shape, BF16),
            pltpu.VMEM(half_in.shape, BF16),
            pltpu.VMEM(half_down.shape, BF16),
        ]
        + [dma((count,))] * 8
        + [dma((2,)), dma((2,)), dma((4,))],
        compiler_params=pltpu.CompilerParams(
            collective_id=2, has_side_effects=True, vmem_limit_bytes=60 * 2**20
        ),
        name="experts",
    )(rows, gates, grads, w_in, w_down)


def add_rows(total, part, rows):
    slab = 16

    @pl.loop(0, rows // slab)
    def _(i):
        at = pl.ds(pl.multiple_of(i * slab, slab), slab)
        total[at, :] = (total[at, :].astype(F32) + part[at, :].astype(F32)).astype(BF16)


class Chain:
    def __init__(self, layers, z, above, below, own, rows, up, down, sems, sends):
        self.layers, self.z, self.above, self.below = layers, z, above, below
        self.own, self.rows, self.up, self.down = own, rows, up, down
        self.sems, self.sends = sems, sends
        self.parts = sems.shape[2]
        self.width = up.shape[2] // self.parts

    def columns(self, ref, h):
        return ref.at[:, pl.ds(h * self.width, self.width)]

    def rise(self, d, h):
        return remote(
            self.columns(self.own(d), h),
            self.columns(self.up.at[d], h),
            self.sends.at[0, d, h],
            self.sems.at[0, d, h],
            self.above,
        )

    def fall(self, d, h):
        return remote(
            self.columns(self.own(d), h),
            self.columns(self.down.at[d], h),
            self.sends.at[1, d, h],
            self.sems.at[1, d, h],
            self.below,
        )

    def end(self, step):
        for h in range(self.parts):
            pl.when(self.z == 0)(self.rise(self.layers - 1 - step, h).start)
            pl.when(self.z == self.layers - 1)(self.fall(step, h).start)

    def ends(self):
        for step in range(self.layers - 1):
            self.end(step)

    def add(self, d, h, buffer):
        add_rows(self.columns(self.own(d), h), self.columns(buffer.at[d], h), self.rows)

    def middle(self):
        z, last = self.z, self.layers - 1

        def pass_on(make, d, buffer):
            for h in range(self.parts):
                copy = make(d, h)
                copy.wait_recv()
                self.add(d, h, buffer)
                copy.start()

        def both(first_half):
            for step in range(last):
                high, low = last - step, step

                def upward(high=high):
                    pl.when((z > 0) & (z < high))(lambda: pass_on(self.rise, high, self.up))

                def downward(low=low):
                    pl.when((z < last) & (z > low))(lambda: pass_on(self.fall, low, self.down))

                for turn in (upward, downward) if first_half else (downward, upward):
                    turn()

        pl.when(z <= last // 2)(lambda: both(True))
        pl.when(z > last // 2)(lambda: both(False))

    def finish(self):
        z, last = self.z, self.layers - 1

        def take(make, buffer):
            for h in range(self.parts):
                make(z, h).wait_recv()
                self.add(z, h, buffer)

        pl.when(z > 0)(lambda: take(self.rise, self.up))
        pl.when(z < last)(lambda: take(self.fall, self.down))

    def wait_sends(self):
        for d in range(self.layers):
            for h in range(self.parts):
                pl.when(self.z < d)(self.rise(d, h).wait_send)
                pl.when(self.z > d)(self.fall(d, h).wait_send)


def finish_kernel(
    layers,
    grad_kv_ref,
    grad_q_ref,
    first_ref,
    tokens_ref,
    gain_ref,
    middle_ref,
    w_all_ref,
    attended_ref,
    second_ref,
    logits_ref,
    gain_moe_ref,
    base_ref,
    returned_ref,
    picks_ref,
    gates_ref,
    in_ref,
    down_ref,
    block_ref,
    d_tokens_ref,
    d_qkv_ref,
    d_out_ref,
    d_aux_ref,
    got_in_ref,
    got_down_ref,
    weights,
    projected,
    grad_first,
    kv_own,
    kv_pair,
    kv_up,
    kv_down,
    late_both,
    late_pair,
    late_near,
    late_up,
    late_down,
    q_both,
    q_pair,
    q_near,
    q_up,
    q_down,
    k_both,
    k_pair,
    k_near,
    k_up,
    k_down,
    load_sem,
    kv_pair_sem,
    kv_pair_send,
    kv_sem,
    kv_send,
    half_sem,
    half_send,
    pair_sem,
    pair_send,
    near_sem,
    near_send,
    line_sem,
    line_send,
):
    z, core, exp = lax.axis_index("le"), lax.axis_index("core"), lax.axis_index("exp")
    other = 1 - core
    partner = place(z, other, exp)
    above, below = place(z + 1, core, exp), place(z - 1, core, exp)
    x, y = x_of(exp), y_of(exp)
    mates = (x, y, y_of(x))
    own_layer, mate, farthest, middle = near_to_far(z)
    ctx = z * 2 + core
    rows = d_qkv_ref.shape[0]
    count = tokens_ref.shape[0]
    head_cols = HEADS * HEAD
    qkv_cols = d_qkv_ref.shape[1]
    kv_cols = qkv_cols - head_cols

    loads = []

    def load(src, dst):
        copy = pltpu.make_async_copy(src, dst, load_sem.at[len(loads)])
        copy.start()
        loads.append(copy)
        return copy

    kv_loads = [
        load(grad_kv_ref.at[pl.ds(pl.multiple_of((d * 2 + core) * count, 16), count), :], kv_own.at[d])
        for d in range(layers)
    ]
    depth = w_all_ref.shape[0]

    def weights_part(i):
        part = w_all_ref.at[pl.ds(i * depth // 2, depth // 2), pl.ds(0, qkv_cols)]
        return pltpu.make_async_copy(part, weights, load_sem.at[2 * layers + 2])

    weights_part(0).start()
    meet(
        [
            place((z + s) % layers, (core + p) % 2, exp)
            for s in range(layers)
            for p in range(2)
            if s + p > 0
        ]
        + [place(z, core, mate) for mate in mates]
    )
    started = []

    def go(copy):
        copy.start()
        started.append(copy)

    arrays = ((in_ref, got_in_ref), (down_ref, got_down_ref))

    def mine(a, owner):
        n = arrays[a][1].shape[1]
        return arrays[a][0].at[pl.ds(owner * n, n), :]

    def half(a, expert, p):
        cols = arrays[a][0].shape[1]
        return arrays[a][1].at[expert, :, pl.ds(pl.multiple_of(p * cols, 128), cols)]

    for a in range(2):
        load(mine(a, ctx), half(a, z, core))

    def hand_back(a, early):
        for s, zz in enumerate([mate, farthest, middle, own_layer]):
            across = between(z, zz)
            for p in range(2):
                if s == layers - 1 and p == 0:
                    continue
                pp = (core + p) % 2
                copy = remote(
                    mine(a, zz * 2 + pp),
                    half(a, z, core),
                    half_send.at[a, s * 2 + p],
                    half_sem.at[a, ctx],
                    place(zz, pp, exp),
                )
                if early:
                    pl.when(across)(copy.start)
                else:
                    pl.when(~across)(copy.start)
                    started.append(copy)

    hand_back(0, True)

    for d in range(layers):
        go(
            remote(
                grad_kv_ref.at[pl.ds(pl.multiple_of((d * 2 + other) * count, 16), count), :],
                kv_pair.at[d],
                kv_pair_send.at[d],
                kv_pair_sem.at[d],
                partner,
            )
        )
    kv_line = Chain(
        layers, z, above, below, lambda d: kv_own.at[d], count, kv_up, kv_down, kv_sem, kv_send
    )
    for copy in kv_loads:
        copy.wait()
    for k in range(layers):
        d = jnp.where(z < layers // 2, layers - 1 - k, k)
        remote(kv_pair.at[d], kv_pair.at[d], kv_pair_send.at[d], kv_pair_sem.at[d], partner).wait_recv()
        add_rows(kv_own.at[d], kv_pair.at[d], count)
        if k < layers - 1:
            kv_line.end(k)

    def near_copy(i, near, own, d, m, target):
        return remote(
            own.at[d, pl.ds(pl.multiple_of(target * rows, 16), rows), :],
            near.at[m, d],
            near_send.at[i, m, d],
            near_sem.at[i, m, d],
            place(z, core, mates[m]),
        )

    def pair_sums(i, own, pair, near):
        for d in range(layers):
            remote(pair.at[d], pair.at[d], pair_send.at[i, d], pair_sem.at[i, d], partner).wait_recv()
            add_rows(own.at[d], pair.at[d], 4 * rows)
            for m in range(3):
                go(near_copy(i, near, own, d, m, mates[m]))

    def near_sums(i, own, near):
        for d in range(layers):
            for m in range(3):
                near_copy(i, near, own, d, m, exp).wait_recv()
            mine = own.at[d, pl.ds(pl.multiple_of(exp * rows, 16), rows), :]

            @pl.loop(0, rows // 16)
            def _(r, mine=mine, d=d):
                at = pl.ds(pl.multiple_of(r * 16, 16), 16)
                total = mine[at, :].astype(F32)
                for m in range(3):
                    total = total + near[m, d, at, :].astype(F32)
                mine[at, :] = total.astype(BF16)

    def line_of(i, own, up, down):
        return Chain(
            layers,
            z,
            above,
            below,
            lambda d: own.at[d, pl.ds(pl.multiple_of(exp * rows, 16), rows), :],
            rows,
            up,
            down,
            line_sem.at[i],
            line_send.at[i],
        )

    def outer_product(both, cols, left, right, gains=None):
        for d in range(layers):
            block = left[:, d * 8 * rows : (d + 1) * 8 * rows]
            part = dot(block, right, ((0,), (0,)))
            if gains is not None:
                turned = [
                    jnp.transpose(jnp.broadcast_to(gains[:, at : at + 128], (128, 128)))
                    for at in range(d * 8 * rows, (d + 1) * 8 * rows, 128)
                ]
                lane = lax.broadcasted_iota(jnp.int32, part.shape, 1)
                part = jnp.where(lane == 0, jnp.concatenate(turned, axis=0), part)
            part = part.astype(BF16)
            both[0, d, :, cols] = part[: 4 * rows]
            both[1, d, :, cols] = part[4 * rows :]

    def pair_up(i, both, pair):
        for d in range(layers):
            go(remote(both.at[other, d], pair.at[d], pair_send.at[i, d], pair_sem.at[i, d], partner))

    outer_product(q_both, slice(0, head_cols), first_ref, grad_q_ref[...])
    pair_up(1, q_both, q_pair)
    width = middle_ref.shape[1]
    outer_product(late_both, slice(0, width), attended_ref, middle_ref[...].astype(BF16))
    outer_product(late_both, slice(width, width + AUX), second_ref, logits_ref[...], gain_moe_ref[...])
    pair_up(0, late_both, late_pair)
    late_own = late_both.at[core]
    q_own = q_both.at[core]
    pair_sums(1, q_own, q_pair, q_near)
    pair_sums(0, late_own, late_pair, late_near)
    kv_line.middle()
    hand_back(0, False)
    hand_back(1, True)
    hand_back(1, False)
    kv_line.finish()

    projected[:, :head_cols] = grad_q_ref[...]
    projected[:, head_cols:] = kv_own[z]
    outer_product(k_both, slice(0, kv_cols), first_ref, projected[:, head_cols:])
    tile = 256
    for i in range(2):
        weights_part(i).wait()

        @pl.loop(0, depth // 2 // tile)
        def _(j, i=i):
            at = pl.ds(pl.multiple_of(j * tile, tile), tile)
            to = pl.ds(pl.multiple_of(i * depth // 2 + j * tile, tile), tile)
            grad_first[:, to] = dot(projected[...], weights[at, :], ((1,), (1,)))

        if i == 0:
            weights_part(1).start()

    inputs = tokens_ref[...].astype(F32)
    scale = norm_scale(inputs)
    norm = inputs * scale
    grad = grad_first[...]
    grad_gain = jnp.sum(grad * norm, axis=0, keepdims=True)
    for d in range(layers):
        block = jnp.concatenate(
            [
                jnp.transpose(jnp.broadcast_to(grad_gain[:, at : at + 128], (128, 128)))
                for at in range(d * 8 * rows, (d + 1) * 8 * rows, 128)
            ],
            axis=0,
        ).astype(BF16)
        k_both[0, d, :, kv_cols:] = block[: 4 * rows]
        k_both[1, d, :, kv_cols:] = block[4 * rows :]
    pair_up(2, k_both, k_pair)
    grad = grad * gain_ref[...]
    d_tokens_ref[...] = (
        middle_ref[...] + scale * (grad - norm * jnp.mean(grad * norm, axis=-1, keepdims=True))
    ).astype(BF16)
    k_own = k_both.at[core]
    pair_sums(2, k_own, k_pair, k_near)

    @pl.loop(0, depth // tile)
    def _(i):
        at = pl.ds(pl.multiple_of(i * tile, tile), tile)
        total = base_ref[:, at]
        for k in range(2):
            total = total + gates_ref[:, k : k + 1] * dot(picks_ref[k], returned_ref[:, at])
        block_ref[:, at] = total.astype(BF16)

    late_line = line_of(0, late_own, late_up, late_down)
    q_line = line_of(1, q_own, q_up, q_down)
    k_line = line_of(2, k_own, k_up, k_down)
    near_sums(1, q_own, q_near)
    q_line.ends()
    near_sums(0, late_own, late_near)
    late_line.ends()
    q_line.middle()
    near_sums(2, k_own, k_near)
    k_line.ends()
    late_line.middle()
    k_line.middle()
    mine_rows = pl.ds(pl.multiple_of(exp * rows, 16), rows)
    q_line.finish()
    d_qkv_ref[:, :head_cols] = q_both[core, z, mine_rows, :].astype(F32)
    late_line.finish()
    last = late_both[core, z, mine_rows, :].astype(F32)
    d_out_ref[...] = last[:, :width]
    d_aux_ref[:, AUX:] = last[:, width:]
    k_line.finish()
    last = k_both[core, z, mine_rows, :].astype(F32)
    d_qkv_ref[:, head_cols:] = last[:, :kv_cols]
    d_aux_ref[:, :AUX] = last[:, kv_cols:]

    for source in range(2 * layers):
        for a in range(2):

            @pl.when(source != ctx)
            def _(source=source, a=a):
                remote(
                    half(a, source // 2, source % 2),
                    half(a, source // 2, source % 2),
                    half_send.at[a, 0],
                    half_sem.at[a, source],
                    partner,
                ).wait_recv()

    for copy in loads[-2:]:
        copy.wait()
    for line in (kv_line, late_line, q_line, k_line):
        line.wait_sends()
    for copy in started:
        copy.wait_send()


def finish(
    grad_kv,
    grad_q,
    first,
    tokens,
    gain,
    middle,
    w_all,
    attended,
    second,
    grad_logits,
    gain_moe,
    base,
    returned,
    picks,
    gates,
    grad_in,
    grad_down,
    layers,
):
    depth, count = first.shape[1], first.shape[0]
    rows = depth // (8 * layers)
    qkv_cols = grad_q.shape[1] + grad_kv.shape[1]
    n_in, n_down = grad_in.shape[0] // (2 * layers), grad_down.shape[0] // (2 * layers)
    any_space = pl.BlockSpec(memory_space=pl.ANY)
    vmem = pl.BlockSpec(memory_space=pltpu.VMEM)
    dma = pltpu.SemaphoreType.DMA

    def sums(cols):
        return [
            pltpu.VMEM((2, layers, 4 * rows, cols), BF16),
            pltpu.VMEM((layers, 4 * rows, cols), BF16),
            pltpu.VMEM((3, layers, rows, cols), BF16),
            pltpu.VMEM((layers, rows, cols), BF16),
            pltpu.VMEM((layers, rows, cols), BF16),
        ]

    return pl.pallas_call(
        functools.partial(finish_kernel, layers),
        out_shape=(
            jax.ShapeDtypeStruct((count, depth), BF16),
            jax.ShapeDtypeStruct((count, depth), BF16),
            jax.ShapeDtypeStruct((rows, qkv_cols), F32),
            jax.ShapeDtypeStruct((rows, depth), F32),
            jax.ShapeDtypeStruct((rows, 2 * AUX), F32),
            jax.ShapeDtypeStruct((layers, n_in, 2 * grad_in.shape[1]), BF16),
            jax.ShapeDtypeStruct((layers, n_down, 2 * grad_down.shape[1]), BF16),
        ),
        in_specs=[any_space] + [vmem] * 5 + [any_space] + [vmem] * 8 + [any_space] * 2,
        out_specs=(vmem,) * 5 + (any_space,) * 2,
        scratch_shapes=[
            pltpu.VMEM((depth // 2, qkv_cols), BF16),
            pltpu.VMEM((count, qkv_cols), BF16),
            pltpu.VMEM((count, depth), F32),
        ]
        + [pltpu.VMEM((layers, count, grad_kv.shape[1]), BF16)] * 4
        + sums(depth + AUX)
        + sums(grad_q.shape[1])
        + sums(grad_kv.shape[1] + AUX)
        + [
            dma((2 * layers + 3,)),
            dma((layers,)),
            dma((layers,)),
            dma((2, layers, 2)),
            dma((2, layers, 2)),
            dma((2, 2 * layers)),
            dma((2, 2 * layers)),
            dma((3, layers)),
            dma((3, layers)),
            dma((3, 3, layers)),
            dma((3, 3, layers)),
            dma((3, 2, layers, 1)),
            dma((3, 2, layers, 1)),
        ],
        compiler_params=pltpu.CompilerParams(
            collective_id=1, has_side_effects=True, vmem_limit_bytes=60 * 2**20
        ),
        name="finish",
    )(
        grad_kv,
        grad_q,
        first,
        tokens,
        gain,
        middle,
        w_all,
        attended,
        second,
        grad_logits,
        gain_moe,
        base,
        returned,
        picks,
        gates,
        grad_in,
        grad_down,
    )


def settle_kernel(*refs):
    count = len(refs) // 2
    for src, dst in zip(refs[:count], refs[count:]):
        dst[...] = src[...].astype(dst.dtype)


def settle(arrays, steps):
    def spec(array):
        if array.ndim == 2 and array.shape[0] % (16 * steps) == 0:
            return pl.BlockSpec((array.shape[0] // steps, array.shape[1]), lambda i: (i, 0))
        if array.ndim == 3 and array.shape[1] % (16 * steps) == 0:
            return pl.BlockSpec(
                (array.shape[0], array.shape[1] // steps, array.shape[2]), lambda i: (0, i, 0)
            )
        return pl.BlockSpec(array.shape, lambda i: (0,) * array.ndim)

    specs = [spec(array) for array, _ in arrays]
    return pl.pallas_call(
        settle_kernel,
        grid=(steps,),
        out_shape=[jax.ShapeDtypeStruct(array.shape, dtype) for array, dtype in arrays],
        in_specs=specs,
        out_specs=specs,
        compiler_params=pltpu.CompilerParams(vmem_limit_bytes=60 * 2**20),
        name="settle",
    )(*[array for array, _ in arrays])


CTX = ("le", "rep", "core")
ALL = ("le", "rep", "core", "exp")
OWNERS = ("exp", "le")


def on_device(
    tokens,
    cotangent,
    routes,
    lengths,
    block_order,
    gain_attn,
    qkv_weight,
    out_weight,
    gain_moe,
    router_weight,
    expert_in,
    expert_out,
):
    tok_rows = tokens.shape[1]
    head_width = HEADS * HEAD
    exp_local = expert_in.shape[0]
    n_ctx = D // expert_in.shape[1]
    copies = n_ctx // exp_local
    n_exp = EXPERTS // exp_local
    in_rows, out_rows = expert_in.shape[1], expert_out.shape[1]

    cols = qkv_weight.shape[1]
    aux = jnp.concatenate([gain_attn[:, None], gain_moe[:, None], router_weight], axis=1)
    aux = jnp.pad(aux, ((0, 0), (0, AUX - aux.shape[1])))
    shard = jnp.concatenate([qkv_weight, aux, out_weight], axis=1).astype(BF16)
    special = (copies, exp_local, n_exp) == (2, 4, 4)
    if special:
        w_all, w_in, w_down, first, projected, kv = front(shard, expert_in, expert_out, tokens[0], cols)
    else:
        w_all = lax.all_gather(shard, ALL, axis=0, tiled=True)

        def to_owner(weight):
            rows, width = weight.shape[1:]
            halves = weight.astype(BF16).reshape(exp_local, rows, 2, width // 2).transpose(0, 2, 1, 3)
            halves = jnp.broadcast_to(
                halves[:, None], (exp_local, copies // 2, 2, rows, width // 2)
            ).reshape(n_ctx, rows, width // 2)
            mine = lax.all_to_all(halves, CTX, split_axis=0, concat_axis=0, tiled=True)
            return lax.all_gather(mine.reshape(n_ctx * rows, width // 2), "core", axis=1, tiled=True)

        w_in = to_owner(expert_in)
        w_down = to_owner(expert_out)
    w_qkv = w_all[:, :cols]
    aux_all = w_all[:, cols : cols + AUX]
    w_attn_out = w_all[:, cols + AUX :]
    gain_first = aux_all[:, 0].astype(F32)
    gain_second = aux_all[:, 1].astype(F32)
    w_router = aux_all[:, 2 : 2 + EXPERTS]

    route_hot = (
        routes[0][:, :, None] == jnp.arange(EXPERTS, dtype=jnp.int32)[None, None, :]
    ).astype(F32)
    flat_hot = route_hot.reshape(tok_rows * 2, EXPERTS).astype(BF16)
    order = jnp.arange(tok_rows * 2, dtype=jnp.int32)
    earlier = (order[:, None] > order[None, :]).astype(BF16)
    ranks = dot(earlier, flat_hot)
    slot_index = jnp.sum(ranks * flat_hot.astype(F32), axis=1).astype(jnp.int32)
    target = (routes[0].reshape(tok_rows * 2) * CAP + slot_index).reshape(tok_rows, 2)
    slots = jnp.arange(EXPERTS * CAP, dtype=jnp.int32)
    picks = [(target[:, k : k + 1] == slots[None, :]) for k in range(2)]
    sends = [(target[:, k][None, :] == slots[:, None]) for k in range(2)]
    send_hot = (sends[0] | sends[1]).astype(BF16)

    def to_experts(rows):
        return lax.all_to_all(
            rows.reshape((EXPERTS, CAP) + rows.shape[1:]),
            OWNERS,
            split_axis=0,
            concat_axis=0,
            tiled=True,
        ).reshape(rows.shape)

    inputs = tokens[0].astype(F32)
    scale_first = norm_scale(inputs)
    norm_first = inputs * scale_first
    if not special:
        first = (norm_first * gain_first).astype(BF16)
        projected = dot(first, w_qkv).astype(BF16)
        kv = lax.all_gather(projected[:, head_width:], CTX, axis=0, tiled=True)
    kv, grad_y_send = lax.optimization_barrier((kv, dot(send_hot, cotangent[0]).astype(BF16)))
    grad_y_rows = to_experts(grad_y_send)
    mine = (lax.axis_index(CTX) * (tok_rows // BLK)).astype(jnp.int32).reshape(1)
    exact, attended, lse = attend(lengths, block_order, mine, projected, kv)
    middle = inputs + dot(attended, w_attn_out)
    scale_second = norm_scale(middle)
    norm_second = middle * scale_second
    second = (norm_second * gain_second).astype(BF16)
    logits = dot(second, w_router)
    chosen = jnp.sum(route_hot * logits[:, None, :], axis=-1)
    gates = jax.nn.softmax(chosen, axis=-1)

    gate_rows = jnp.sum(
        jnp.where(sends[0], gates[:, 0][None, :], 0.0) + jnp.where(sends[1], gates[:, 1][None, :], 0.0),
        axis=1,
        keepdims=True,
    )
    if special:
        slot_gates = jnp.broadcast_to(
            jnp.pad(gate_rows.reshape(EXPERTS, 1, CAP), ((0, 0), (0, 0), (0, 128 - CAP))), (EXPERTS, 8, 128)
        )
        expert_rows, grad_returned, gate_grads, grad_in, grad_down = experts(
            dot(send_hot, second).astype(BF16).reshape(EXPERTS, CAP, D),
            slot_gates,
            grad_y_rows.reshape(EXPERTS, CAP, D),
            w_in,
            w_down,
            exp_local,
        )
        returned = to_experts(expert_rows.reshape(EXPERTS * CAP, D))
        grad_returned = grad_returned.reshape(EXPERTS * CAP, D)
        gate_grads = gate_grads[:, 0, :CAP].reshape(1, EXPERTS * CAP)
    else:
        def in_parts(column):
            high = lax.reduce_precision(column, 8, 7)
            rest = column - high
            mid = lax.reduce_precision(rest, 8, 7)
            parts = jnp.concatenate([high, mid, rest - mid], axis=1).astype(BF16)
            return jnp.pad(parts, ((0, 0), (0, AUX - 3)))

        gate_parts = in_parts(gate_rows)
        payload = to_experts(
            jnp.concatenate([dot(send_hot, second).astype(BF16), gate_parts], axis=1)
        )
        received = payload[:, :D]
        gate_got = jnp.sum(payload[:, D : D + 3].astype(F32), axis=1, keepdims=True)

        gate_up = dot(received, w_in)
        gate_part = gate_up[:, :FF]
        up_part = gate_up[:, FF:]
        sigmoid_gate = jax.nn.sigmoid(gate_part)
        silu_gate = gate_part * sigmoid_gate
        hidden = (silu_gate * up_part).astype(BF16)
        expert_rows = dot(hidden, w_down)
        expert_rows = expert_rows.astype(BF16)
        grad_y_rows = grad_y_rows.astype(F32)
        returned = to_experts(expert_rows)

        grad_rows = (gate_got * grad_y_rows).astype(BF16)
        gate_grad_parts = in_parts(
            jnp.sum(grad_y_rows * expert_rows.astype(F32), axis=1, keepdims=True)
        )
        half_d = D // 2
        grad_hidden = dot(grad_rows, w_down, ((1,), (1,)))
        grad_gate = (
            grad_hidden * up_part * sigmoid_gate * (1.0 + gate_part * (1.0 - sigmoid_gate))
        ).astype(BF16)
        grad_up = (grad_hidden * silu_gate).astype(BF16)
        grad_gate_up = jnp.concatenate([grad_gate, grad_up], axis=1)
        grad_back = dot(grad_gate_up, w_in, ((1,), (1,)))
        grad_returned = to_experts(jnp.concatenate([grad_back.astype(BF16), gate_grad_parts], axis=1))

        grad_in = jnp.stack(
            [dot(received, grad_gate, ((0,), (0,))), dot(received, grad_up, ((0,), (0,)))]
        ).astype(BF16)
        grad_down = jnp.stack(
            [
                dot(hidden, grad_rows[:, :half_d], ((0,), (0,))),
                dot(hidden, grad_rows[:, half_d:], ((0,), (0,))),
            ]
        ).astype(BF16)

        grad_in = lax.psum_scatter(grad_in, "core", scatter_dimension=0, tiled=True)[0]
        grad_down = lax.psum_scatter(grad_down, "core", scatter_dimension=0, tiled=True)[0]
        grad_returned, grad_in, grad_down = lax.optimization_barrier((grad_returned, grad_in, grad_down))
        gate_grads = jnp.sum(grad_returned[:, D:].astype(F32), axis=1).reshape(1, EXPERTS * CAP)
        grad_returned = grad_returned[:, :D]

    grad_y = cotangent[0].astype(F32)
    pick_hot = [p.astype(BF16) for p in picks]
    grad_gates = jnp.concatenate(
        [jnp.sum(jnp.where(p, gate_grads, 0.0), axis=1, keepdims=True) for p in picks], axis=1
    )
    grad_chosen = gates * (grad_gates - jnp.sum(gates * grad_gates, axis=-1, keepdims=True))
    grad_logits = jnp.sum(grad_chosen[:, :, None] * route_hot, axis=1).astype(BF16)
    grad_second = dot(pick_hot[0] + pick_hot[1], grad_returned) + dot(
        grad_logits, w_router, ((1,), (1,))
    )
    grad_gain_second = jnp.sum(grad_second * norm_second, axis=0)
    grad_norm_second = grad_second * gain_second
    grad_middle = grad_y + scale_second * (
        grad_norm_second
        - norm_second * jnp.mean(grad_norm_second * norm_second, axis=-1, keepdims=True)
    )
    grad_branch = grad_middle.astype(BF16)
    grad_attended = dot(grad_branch, w_attn_out, ((1,), (1,))).astype(BF16)
    grad_queries, grad_kv = attend_back(
        lengths, block_order, mine, projected, kv, grad_attended, lse, exact
    )
    grad_queries, grad_kv, returned = lax.optimization_barrier((grad_queries, grad_kv, returned))
    if special:
        block_out, grad_inputs, sum_qkv, sum_out, sum_aux, sum_in, sum_down = finish(
            grad_kv,
            grad_queries,
            first,
            tokens[0],
            gain_first[None, :],
            grad_middle,
            w_all,
            attended,
            second,
            jnp.pad(grad_logits, ((0, 0), (1, AUX - 1 - EXPERTS))),
            grad_gain_second[None, :],
            middle,
            returned,
            jnp.stack(pick_hot),
            gates,
            grad_in,
            grad_down,
            exp_local,
        )
        block_out, grad_inputs, sum_qkv, sum_out, sum_in, sum_down = settle(
            (
                (block_out, BF16),
                (grad_inputs, BF16),
                (sum_qkv, F32),
                (sum_out, F32),
                (sum_in, F32),
                (sum_down, F32),
            ),
            4,
        )
    else:
        grad_router = dot(second, grad_logits, ((0,), (0,)))
        grad_attn_out = dot(attended, grad_branch, ((0,), (0,)))
        late = jnp.concatenate([grad_gain_second[:, None], grad_router], axis=1)
        late = jnp.pad(late, ((0, 0), (0, AUX - late.shape[1])))
        late = jnp.concatenate([grad_attn_out.astype(BF16), late.astype(BF16)], axis=1)
        grad_kv = lax.psum_scatter(grad_kv, CTX, scatter_dimension=0, tiled=True)
        grad_projected = jnp.concatenate([grad_queries, grad_kv], axis=1)
        grad_qkv = dot(first, grad_projected, ((0,), (0,)))
        grad_first = dot(grad_projected, w_qkv, ((1,), (1,)))
        grad_gain_first = jnp.sum(grad_first * norm_first, axis=0)
        grad_norm_first = grad_first * gain_first
        grad_inputs = grad_middle + scale_first * (
            grad_norm_first
            - norm_first * jnp.mean(grad_norm_first * norm_first, axis=-1, keepdims=True)
        )
        grad_inputs = grad_inputs.astype(BF16)
        last = jnp.pad(grad_gain_first[:, None], ((0, 0), (0, AUX - 1)))
        part = jnp.concatenate([grad_qkv.astype(BF16), last.astype(BF16), late], axis=1)
        total = lax.psum_scatter(part, ALL, scatter_dimension=0, tiled=True).astype(F32)
        sum_qkv, sum_out = total[:, :cols], total[:, cols + AUX : cols + AUX + D]
        sum_aux = jnp.concatenate([total[:, cols : cols + AUX], total[:, cols + AUX + D :]], axis=1)
        picked = [dot(p, returned) for p in pick_hot]
        block_out = (middle + gates[:, 0:1] * picked[0] + gates[:, 1:2] * picked[1]).astype(BF16)

        def to_rows(half, rows):
            width = half.shape[1]
            got = lax.all_to_all(
                half.reshape(n_ctx, rows, width), CTX, split_axis=0, concat_axis=0, tiled=True
            ).astype(F32)
            got = got.reshape(exp_local, copies // 2, 2, rows, width).sum(axis=1)
            return got.transpose(0, 2, 1, 3).reshape(exp_local, rows, 2 * width)

        sum_in = to_rows(grad_in, in_rows)
        sum_down = to_rows(grad_down, out_rows)
    return (
        block_out[None],
        grad_inputs[None],
        sum_aux[:, 0],
        sum_qkv,
        sum_out,
        sum_aux[:, AUX],
        sum_aux[:, AUX + 1 : AUX + 1 + EXPERTS],
        sum_in.astype(F32),
        sum_down.astype(F32),
    )


def solution(mesh):
    n_ctx, n_exp = mesh.shape["ctx"], mesh.shape["exp"]
    exp_local = EXPERTS // n_exp
    copies = n_ctx // exp_local
    inner = Mesh(mesh.devices.reshape(exp_local, copies // 2, 2, n_exp), ALL)
    by_token = P("exp", CTX, None)
    by_row = P(ALL, None)
    by_expert = P("exp", CTX, None)
    return jax.shard_map(
        on_device,
        mesh=inner,
        in_specs=(
            by_token,
            by_token,
            by_token,
            P("exp", None),
            P("exp", None),
            P(ALL),
            by_row,
            by_row,
            P(ALL),
            by_row,
            by_expert,
            by_expert,
        ),
        out_specs=(
            by_token,
            by_token,
            P(ALL),
            by_row,
            by_row,
            P(ALL),
            by_row,
            by_expert,
            by_expert,
        ),
        check_vma=False,
    )
```

```python
import functools

import jax
import jax.numpy as jnp
from jax import lax
from jax.experimental import pallas as pl
from jax.experimental.pallas import tpu as pltpu
from jax.sharding import Mesh
from jax.sharding import PartitionSpec as P

D = 1536
HEADS = 24
KV_HEADS = 8
HEAD = 64
GROUP = HEADS // KV_HEADS
FF = 1024
EXPERTS = 16
BLK = 128
CAP = 48
AUX = 128

epsilon = 1e-05
far_negative = -1e30
start_max = -1e29
F32 = jnp.float32
BF16 = jnp.bfloat16


def norm_scale(values):
    return lax.rsqrt(jnp.mean(values * values, axis=-1, keepdims=True) + epsilon)


def dot(a, b, dims=((1,), (0,))):
    return lax.dot_general(a, b, (dims, ((), ())), preferred_element_type=F32)


def lane_half(shape, half):
    lane = lax.broadcasted_iota(jnp.int32, shape, 1)
    return (lane >= HEAD) if half else (lane < HEAD)


def head_tiles(ref, rows, pair, scale):
    tiles = []
    for i in range(2 * GROUP):
        head = pair * 2 * GROUP + i
        group = head // GROUP
        tile = ref[rows, (head // 2) * 128 : (head // 2 + 1) * 128].astype(F32)
        if head % 2 != group % 2:
            tile = pltpu.roll(tile, HEAD, 1)
        tile = jnp.where(lane_half(tile.shape, group % 2), tile * scale, 0.0)
        tiles.append(tile.astype(BF16))
    return jnp.concatenate(tiles, axis=0)


def block_visibility(lengths_ref, query_block, key_block, parts):
    lanes = lax.broadcasted_iota(jnp.int32, (1, BLK), 1)
    query_pos = query_block * BLK + lanes
    start = jnp.zeros((1, BLK), jnp.int32)
    bound = jnp.int32(0)
    for s in range(parts - 1):
        bound = bound + lengths_ref[0, s]
        start = jnp.where(query_pos >= bound, bound, start)
    key_pos = key_block * BLK + lax.broadcasted_iota(jnp.int32, (BLK, BLK), 0)
    one = ((key_pos >= start) & (key_pos <= query_pos)).astype(jnp.int32)
    return jnp.concatenate([one] * (2 * GROUP), axis=1) > 0


def first_row_start(lengths_ref, query_block, parts):
    start = jnp.int32(0)
    bound = jnp.int32(0)
    for s in range(parts - 1):
        bound = bound + lengths_ref[0, s]
        start = jnp.where(query_block * BLK >= bound, bound, start)
    return start


def attend_blocks(
    parts,
    skip,
    lengths_ref,
    order_ref,
    mine,
    q_ref,
    kv_ref,
    exact_ref,
    out_ref,
    lse_ref,
    q_s,
    m_s,
    sum_s,
    acc_s,
):
    width = KV_HEADS * HEAD
    wide = 2 * GROUP * BLK
    for qb in range(q_ref.shape[0] // BLK):
        rows = pl.ds(qb * BLK, BLK)
        for pair in range(KV_HEADS // 2):
            q_s[pair] = head_tiles(q_ref, rows, pair, HEAD**-0.5)
            m_s[pair] = jnp.full((8, wide), start_max, F32)
            sum_s[pair] = jnp.zeros((8, wide), F32)
            acc_s[pair] = jnp.zeros((BLK, wide), F32)
        query_block = order_ref[0, mine + qb]
        first = first_row_start(lengths_ref, query_block, parts)

        @pl.loop(0, order_ref.shape[1])
        def _(kb):
            key_block = order_ref[0, kb]

            def fold():
                seen = block_visibility(lengths_ref, query_block, key_block, parts)
                key_rows = pl.ds(kb * BLK, BLK)
                for pair in range(KV_HEADS // 2):
                    keys = kv_ref[key_rows, pl.ds(pair * 128, 128)]
                    values = kv_ref[key_rows, pl.ds(width + pair * 128, 128)]
                    scores = dot(keys, q_s[pair], ((1,), (1,)))
                    scores = jnp.where(seen, scores, far_negative)
                    old = m_s[pair, 0:1, :]
                    new = jnp.maximum(old, jnp.max(scores, axis=0, keepdims=True))
                    weights = jnp.exp(scores - new)
                    factor = jnp.exp(old - new)
                    sum_s[pair, 0:1, :] = sum_s[pair, 0:1, :] * factor + jnp.sum(
                        weights, axis=0, keepdims=True
                    )
                    acc_s[pair] = acc_s[pair] * factor + dot(values, weights.astype(BF16), ((0,), (0,)))
                    m_s[pair, 0:1, :] = new

            if skip:
                pl.when((key_block <= query_block) & (key_block * BLK + BLK > first))(fold)
            else:
                fold()

        tiles = []
        for pair in range(KV_HEADS // 2):
            total = sum_s[pair, 0:1, :]
            lse_ref[qb, pair : pair + 1, :] = m_s[pair, 0:1, :] + jnp.log(total)
            acc = acc_s[pair] / total
            for i in range(2 * GROUP):
                head = pair * 2 * GROUP + i
                tile = jnp.transpose(acc[:, i * BLK : (i + 1) * BLK])
                if head % 2 != (head // GROUP) % 2:
                    tile = pltpu.roll(tile, HEAD, 1)
                tiles.append(tile)
                if head % 2 == 1:
                    both = jnp.where(lane_half(tile.shape, 0), tiles[head - 1], tile)
                    lanes = pl.ds((head // 2) * 128, 128)
                    exact_ref[rows, lanes] = both
                    out_ref[rows, lanes] = both.astype(BF16)


def attend_kernel(parts, lengths_ref, order_ref, mine_ref, *refs):
    attend_blocks(parts, True, lengths_ref, order_ref, mine_ref[0], *refs)


def attend(lengths, order, mine, projected, kv):
    rows = projected.shape[0]
    smem = pl.BlockSpec(memory_space=pltpu.SMEM)
    vmem = pl.BlockSpec(memory_space=pltpu.VMEM)
    wide = 2 * GROUP * BLK
    pairs = KV_HEADS // 2
    return pl.pallas_call(
        functools.partial(attend_kernel, lengths.shape[1]),
        out_shape=(
            jax.ShapeDtypeStruct((rows, HEADS * HEAD), F32),
            jax.ShapeDtypeStruct((rows, HEADS * HEAD), BF16),
            jax.ShapeDtypeStruct((rows // BLK, pairs, wide), F32),
        ),
        in_specs=[smem, smem, smem, vmem, vmem],
        out_specs=(vmem, vmem, vmem),
        scratch_shapes=[
            pltpu.VMEM((pairs, wide, 128), BF16),
            pltpu.VMEM((pairs, 8, wide), F32),
            pltpu.VMEM((pairs, 8, wide), F32),
            pltpu.VMEM((pairs, BLK, wide), F32),
        ],
        compiler_params=pltpu.CompilerParams(vmem_limit_bytes=48 * 2**20),
        cost_estimate=pl.CostEstimate(flops=10**10, bytes_accessed=10**7, transcendentals=10**7),
        name="attend",
    )(lengths, order, mine, projected, kv)


def attend_back_kernel(
    parts,
    lengths_ref,
    order_ref,
    mine_ref,
    q_ref,
    kv_ref,
    grad_ref,
    lse_ref,
    exact_ref,
    dq_ref,
    dkv_ref,
    q_s,
    g_s,
    delta_s,
    dq_s,
    dkv_s,
):
    width = KV_HEADS * HEAD

    @pl.loop(0, order_ref.shape[1])
    def _(kb):
        dkv_s[pl.ds(kb * BLK, BLK), :] = jnp.zeros((BLK, 2 * width), F32)

    for qb in range(q_ref.shape[0] // BLK):
        rows = pl.ds(qb * BLK, BLK)
        for pair in range(KV_HEADS // 2):
            q_s[pair] = head_tiles(q_ref, rows, pair, HEAD**-0.5)
            g_s[pair] = head_tiles(grad_ref, rows, pair, 1.0)
            dq_s[pair] = jnp.zeros((2 * GROUP * BLK, 128), F32)
            for i in range(2 * GROUP):
                head = pair * 2 * GROUP + i
                exact = exact_ref[rows, (head // 2) * 128 : (head // 2 + 1) * 128]
                if head % 2 != (head // GROUP) % 2:
                    exact = pltpu.roll(exact, HEAD, 1)
                product = exact * g_s[pair, i * BLK : (i + 1) * BLK, :].astype(F32)
                delta_s[pair : pair + 1, i * BLK : (i + 1) * BLK] = jnp.sum(
                    jnp.transpose(product), axis=0, keepdims=True
                )
        query_block = order_ref[0, mine_ref[0] + qb]
        first = first_row_start(lengths_ref, query_block, parts)

        @pl.loop(0, order_ref.shape[1])
        def _(kb):
            key_block = order_ref[0, kb]

            @pl.when((key_block <= query_block) & (key_block * BLK + BLK > first))
            def _():
                seen = block_visibility(lengths_ref, query_block, key_block, parts)
                key_rows = pl.ds(kb * BLK, BLK)
                for pair in range(KV_HEADS // 2):
                    key_lanes = pl.ds(pair * 128, 128)
                    value_lanes = pl.ds(width + pair * 128, 128)
                    keys = kv_ref[key_rows, key_lanes]
                    values = kv_ref[key_rows, value_lanes]
                    scores = dot(keys, q_s[pair], ((1,), (1,)))
                    scores = jnp.where(seen, scores, far_negative)
                    probs = jnp.exp(scores - lse_ref[qb, pair : pair + 1, :])
                    grad_probs = dot(values, g_s[pair], ((1,), (1,)))
                    grad_scores = (probs * (grad_probs - delta_s[pair : pair + 1, :])).astype(BF16)
                    dkv_s[key_rows, value_lanes] += dot(probs.astype(BF16), g_s[pair])
                    dkv_s[key_rows, key_lanes] += dot(grad_scores, q_s[pair])
                    dq_s[pair] += dot(grad_scores, keys, ((0,), (0,)))

        tiles = []
        for pair in range(KV_HEADS // 2):
            for i in range(2 * GROUP):
                head = pair * 2 * GROUP + i
                tile = dq_s[pair, i * BLK : (i + 1) * BLK, :] * HEAD**-0.5
                if head % 2 != (head // GROUP) % 2:
                    tile = pltpu.roll(tile, HEAD, 1)
                tiles.append(tile)
                if head % 2 == 1:
                    both = jnp.where(lane_half(tile.shape, 0), tiles[head - 1], tile)
                    dq_ref[rows, (head // 2) * 128 : (head // 2 + 1) * 128] = both.astype(BF16)

    @pl.loop(0, order_ref.shape[1])
    def _(kb):
        key_rows = pl.ds(kb * BLK, BLK)
        dkv_ref[key_rows, :] = dkv_s[key_rows, :].astype(BF16)


def attend_back(lengths, order, mine, projected, kv, grad_attended, lse, exact):
    rows = projected.shape[0]
    smem = pl.BlockSpec(memory_space=pltpu.SMEM)
    vmem = pl.BlockSpec(memory_space=pltpu.VMEM)
    wide = 2 * GROUP * BLK
    pairs = KV_HEADS // 2
    return pl.pallas_call(
        functools.partial(attend_back_kernel, lengths.shape[1]),
        out_shape=(
            jax.ShapeDtypeStruct((rows, HEADS * HEAD), BF16),
            jax.ShapeDtypeStruct(kv.shape, BF16),
        ),
        in_specs=[smem, smem, smem, vmem, vmem, vmem, vmem, vmem],
        out_specs=(vmem, vmem),
        scratch_shapes=[
            pltpu.VMEM((pairs, wide, 128), BF16),
            pltpu.VMEM((pairs, wide, 128), BF16),
            pltpu.VMEM((pairs, wide), F32),
            pltpu.VMEM((pairs, wide, 128), F32),
            pltpu.VMEM(kv.shape, F32),
        ],
        compiler_params=pltpu.CompilerParams(vmem_limit_bytes=56 * 2**20),
        cost_estimate=pl.CostEstimate(flops=10**9, bytes_accessed=10**6, transcendentals=10**5),
        name="attend_back",
    )(lengths, order, mine, projected, kv, grad_attended, lse, exact)


MESH = pl.DeviceIdType.MESH


def place(z, core, exp):
    return {"le": z, "rep": 0, "core": core, "exp": exp}


def x_of(exp):
    return (exp // 2) * 2 + 1 - exp % 2


def y_of(exp):
    return (1 - exp // 2) * 2 + exp % 2


def remote(src, dst, send_sem, recv_sem, device):
    return pltpu.make_async_remote_copy(
        src_ref=src,
        dst_ref=dst,
        send_sem=send_sem,
        recv_sem=recv_sem,
        device_id=device,
        device_id_type=MESH,
    )


def near_to_far(z):
    first_half = z < 2
    return [z, z + 1 - 2 * (z % 2), jnp.where(first_half, 3, 0), jnp.where(first_half, 2, 1)]


def between(z, zz):
    return ((z == 1) & (zz == 2)) | ((z == 2) & (zz == 1))


def meet(devices):
    barrier = pltpu.get_barrier_semaphore()
    for device in devices:
        pl.semaphore_signal(barrier, inc=1, device_id=device, device_id_type=MESH)
    pl.semaphore_wait(barrier, len(devices))


def front_kernel(
    layers,
    shard_ref,
    in_ref,
    down_ref,
    tokens_ref,
    lengths_ref,
    order_ref,
    routes_ref,
    hot_ref,
    grads_ref,
    w_all_ref,
    w_in_ref,
    w_down_ref,
    first_ref,
    projected_ref,
    kv_ref,
    exact_ref,
    attended_ref,
    lse_ref,
    middle_ref,
    second_ref,
    gates_ref,
    rows_ref,
    got_grads_ref,
    weights,
    kv_s,
    q_s,
    m_s,
    sum_s,
    acc_s,
    in_wide,
    down_wide,
    in_half,
    down_half,
    unit_sem,
    line_sem,
    x_sem,
    y_sem,
    far_sem,
    core_sem,
    half_sem,
    half_send,
    over_sem,
    over_send,
    kv_sem,
    kv_send,
    own_sem,
    wide_sem,
    grad_sem,
    grad_send,
):
    z, core, exp = lax.axis_index("le"), lax.axis_index("core"), lax.axis_index("exp")
    other = 1 - core
    x, y = x_of(exp), y_of(exp)
    ctx = z * 2 + core
    rows = shard_ref.shape[0]
    own_layer, mate, farthest, middle = near_to_far(z)
    order = [mate, middle, farthest, own_layer]
    wides = ((in_ref, in_wide), (down_ref, down_wide))
    halves = ((in_half, w_in_ref), (down_half, w_down_ref))

    loads = []
    for k, zz in enumerate(order):
        for a in range(2):
            load = pltpu.make_async_copy(wides[a][0].at[zz], wides[a][1].at[zz], wide_sem.at[a, k])
            load.start()
            loads.append(load)
    peers = [
        (zz, (exp + t) % 4)
        for s, zz in enumerate(order)
        for t in range(4)
        if not (s == layers - 1 and t == 0)
    ]
    meet([place(zz, core, ee) for zz, ee in peers] + [place(zz, other, exp) for zz in order])

    def number(zz, cc, ee):
        return (zz * 2 + cc) * 4 + ee

    def unit(zz, cc, ee):
        return weights.at[pl.ds(pl.multiple_of(number(zz, cc, ee) * rows, 16), rows), :]

    def send(src, who, sem, device):
        return remote(src, unit(*who), sem, unit_sem.at[number(*who)], device)

    def arrive(who):
        send(unit(*who), who, line_sem.at[0], place(z, other, exp)).wait_recv()

    started = []

    def go(copy, condition=None):
        if condition is None:
            copy.start()
        else:
            pl.when(condition)(copy.start)
        started.append((copy, condition))

    me = (z, core, exp)
    keep = pltpu.make_async_copy(shard_ref, unit(*me), own_sem.at[0])
    keep.start()
    go(send(shard_ref, me, line_sem.at[layers], place(z + 1, core, exp)), z < layers - 1)
    go(send(shard_ref, me, line_sem.at[layers + 1], place(z - 1, core, exp)), z > 0)
    go(send(shard_ref, me, x_sem.at[layers], place(z, core, x)))
    go(send(shard_ref, me, y_sem.at[layers], place(z, core, y)))
    go(send(shard_ref, me, core_sem.at[layers], place(z, other, exp)))

    slab = 16
    for k, zz in enumerate(order):
        for a in range(2):
            loads[2 * k + a].wait()
            src, dst = wides[a][1], halves[a][0]

            @pl.loop(0, src.shape[1] // slab)
            def _(i, zz=zz, src=src, dst=dst):
                at = pl.ds(pl.multiple_of(i * slab, slab), slab)
                dst[zz, at, :] = src[zz, at, :].astype(BF16)

    def half(a, source, p):
        src, dst = halves[a]
        n, cols = src.shape[1], src.shape[2] // 2
        return dst.at[pl.ds(source * n, n), pl.ds(pl.multiple_of(p * cols, 128), cols)]

    def mine(a, zz, p):
        src = halves[a][0]
        cols = src.shape[2] // 2
        return src.at[zz, :, pl.ds(pl.multiple_of(p * cols, 128), cols)]

    def layer(k):
        return jnp.where(z < layers // 2, k, layers - 1 - k)

    def ahead(zz):
        return between(z, zz)

    def hand_out(a, early):
        for s, zz in enumerate(order):
            across = ahead(zz)
            for p in range(2):
                if s == layers - 1 and p == 0:
                    continue
                pp = (core + p) % 2
                copy = remote(
                    mine(a, zz, pp),
                    half(a, ctx, pp),
                    half_send.at[a, s * 2 + p],
                    half_sem.at[a, ctx],
                    place(zz, pp, exp),
                )
                if early:
                    pl.when(across)(copy.start)
                else:
                    pl.when(~across)(copy.start)
                    started.append((copy, None))
        if not early:
            go(
                remote(
                    mine(a, z, core),
                    half(a, ctx, core),
                    over_send.at[a, 2 * layers],
                    over_sem.at[a, ctx],
                    place(z, other, exp),
                )
            )

    for k in range(layers):
        zz = layer(k)
        who = (zz, core, exp)

        @pl.when(zz != z)
        def _(who=who):
            arrive(who)

        go(send(unit(*who), who, line_sem.at[k], place(z + 1, core, exp)), (zz < z) & (z < layers - 1))
        go(send(unit(*who), who, line_sem.at[k], place(z - 1, core, exp)), (zz > z) & (z > 0))
        go(send(unit(*who), who, x_sem.at[k], place(z, core, x)), zz != z)
        go(send(unit(*who), who, y_sem.at[k], place(z, core, y)), zz != z)
        go(send(unit(*who), who, core_sem.at[k], place(z, other, exp)), zz != z)
        if k == 0:
            hand_out(0, True)

    for a in range(2):
        pltpu.make_async_copy(mine(a, z, core), half(a, ctx, core), own_sem.at[1 + a]).start()

    hand_out(0, False)

    for k in range(layers):
        zz = layer(k)
        from_x, from_y = (zz, core, x), (zz, core, y)
        arrive(from_x)
        go(send(unit(*from_x), from_x, core_sem.at[layers + 1 + k], place(z, other, exp)))
        if k % 2 == 0:
            go(send(unit(*from_x), from_x, far_sem.at[k], place(z, core, y)))
        arrive(from_y)
        go(send(unit(*from_y), from_y, core_sem.at[2 * layers + 1 + k], place(z, other, exp)))
        if k % 2 == 1:
            go(send(unit(*from_y), from_y, far_sem.at[k], place(z, core, x)))
    for k in range(layers):
        far = (layer(k), core, y_of(x))
        arrive(far)
        go(send(unit(*far), far, core_sem.at[3 * layers + 1 + k], place(z, other, exp)))
    for ee in range(4):
        for zz in range(layers):
            arrive((zz, other, ee))
    keep.wait()
    save = pltpu.make_async_copy(weights, w_all_ref, own_sem.at[3])
    save.start()

    depth, count = tokens_ref.shape[1], tokens_ref.shape[0]
    qkv_cols, head_cols = projected_ref.shape[1], HEADS * HEAD
    inputs = tokens_ref[...].astype(F32)
    gains = jnp.concatenate(
        [
            jnp.transpose(weights[i * 128 : (i + 1) * 128, qkv_cols : qkv_cols + AUX].astype(F32))[0:8, :]
            for i in range(depth // 128)
        ],
        axis=1,
    )
    first_ref[...] = (inputs * norm_scale(inputs) * gains[0:1, :]).astype(BF16)
    tile = 512

    @pl.loop(0, (qkv_cols - head_cols) // tile)
    def _(i):
        at = pl.ds(pl.multiple_of(head_cols + i * tile, tile), tile)
        projected_ref[:, at] = dot(first_ref[...], weights[:, at]).astype(BF16)

    def block(source):
        return kv_s.at[pl.ds(pl.multiple_of(source * count, 16), count), :]

    def share(src, source, sem, device):
        return remote(src, block(source), sem, kv_sem.at[source], device)

    own = projected_ref.at[:, pl.ds(head_cols, qkv_cols - head_cols)]
    keep_kv = pltpu.make_async_copy(own, block(ctx), own_sem.at[0])
    keep_kv.start()
    go(share(own, ctx, kv_send.at[2 * layers], place(z + 1, core, exp)), z < layers - 1)
    go(share(own, ctx, kv_send.at[2 * layers + 1], place(z - 1, core, exp)), z > 0)
    go(share(own, ctx, kv_send.at[2 * layers + 2], place(z, other, exp)))

    @pl.loop(0, head_cols // tile)
    def _(i):
        at = pl.ds(pl.multiple_of(i * tile, tile), tile)
        projected_ref[:, at] = dot(first_ref[...], weights[:, at]).astype(BF16)

    for k in range(layers):
        zz = layer(k)
        source = zz * 2 + core

        @pl.when(zz != z)
        def _(source=source):
            share(block(source), source, kv_send.at[0], place(z, other, exp)).wait_recv()

        go(share(block(source), source, kv_send.at[k], place(z + 1, core, exp)), (zz < z) & (z < layers - 1))
        go(share(block(source), source, kv_send.at[k], place(z - 1, core, exp)), (zz > z) & (z > 0))
        go(share(block(source), source, kv_send.at[layers + k], place(z, other, exp)), zz != z)

    hand_out(1, True)
    hand_out(1, False)

    me_slot = exp * layers + z
    keep_grads = pltpu.make_async_copy(grads_ref.at[me_slot], got_grads_ref.at[me_slot], own_sem.at[4])
    keep_grads.start()
    for k, (zz, ee) in enumerate(peers):
        there = ee * layers + zz
        go(
            remote(
                grads_ref.at[there],
                got_grads_ref.at[me_slot],
                grad_send.at[k],
                grad_sem.at[me_slot],
                place(zz, core, ee),
            )
        )

    def pass_over(a):
        for s, zz in enumerate(order[::-1]):
            for p in range(2):
                if s == 0 and p == 0:
                    continue
                source = zz * 2 + (core + p) % 2
                remote(
                    half(a, source, core),
                    half(a, source, core),
                    half_send.at[a, 0],
                    half_sem.at[a, source],
                    place(z, other, exp),
                ).wait_recv()
                go(
                    remote(
                        half(a, source, core),
                        half(a, source, core),
                        over_send.at[a, s * 2 + p],
                        over_sem.at[a, source],
                        place(z, other, exp),
                    )
                )

    pass_over(0)
    for zz in range(layers):
        source = zz * 2 + other
        share(block(source), source, kv_send.at[0], place(z, other, exp)).wait_recv()
    keep_kv.wait()
    save_kv = pltpu.make_async_copy(kv_s, kv_ref, own_sem.at[0])
    save_kv.start()

    attend_blocks(
        lengths_ref.shape[1],
        False,
        lengths_ref,
        order_ref,
        ctx * (count // BLK),
        projected_ref,
        kv_s,
        exact_ref,
        attended_ref,
        lse_ref,
        q_s,
        m_s,
        sum_s,
        acc_s,
    )
    tile = 256

    @pl.loop(0, depth // tile)
    def _(i):
        at = pl.ds(pl.multiple_of(i * tile, tile), tile)
        w_at = pl.ds(pl.multiple_of(qkv_cols + AUX + i * tile, 128), tile)
        middle_ref[:, at] = tokens_ref[:, at].astype(F32) + dot(attended_ref[...], weights[:, w_at])

    middle = middle_ref[...]
    second_ref[...] = (middle * norm_scale(middle) * gains[1:2, :]).astype(BF16)
    logits = dot(second_ref[...], weights[:, qkv_cols : qkv_cols + AUX])
    lane = lax.broadcasted_iota(jnp.int32, logits.shape, 1)
    chosen = [
        jnp.sum(jnp.where(lane == routes_ref[:, k : k + 1] + 2, logits, 0.0), axis=1, keepdims=True)
        for k in range(2)
    ]
    largest = jnp.maximum(chosen[0], chosen[1])
    exps = [jnp.exp(value - largest) for value in chosen]
    total = exps[0] + exps[1]
    gates_ref[...] = jnp.where(lane == 0, exps[0] / total, jnp.where(lane == 1, exps[1] / total, 0.0))

    @pl.loop(0, depth // tile)
    def _(i):
        at = pl.ds(pl.multiple_of(i * tile, tile), tile)
        rows_out = dot(hot_ref[...], second_ref[:, at]).astype(BF16)
        cap = rows_ref.shape[1]
        for e in range(rows_ref.shape[0]):
            rows_ref[e, :, at] = rows_out[e * cap : (e + 1) * cap]

    pass_over(1)
    for source in range(2 * layers):
        for a in range(2):
            remote(
                half(a, source, other),
                half(a, source, other),
                half_send.at[a, 0],
                over_sem.at[a, source],
                place(z, other, exp),
            ).wait_recv()
    for zz, ee in peers:
        source = ee * layers + zz
        remote(
            got_grads_ref.at[source],
            got_grads_ref.at[source],
            grad_send.at[0],
            grad_sem.at[source],
            place(zz, core, ee),
        ).wait_recv()
    keep_grads.wait()
    save_kv.wait()
    save.wait()
    for a in range(2):
        pltpu.make_async_copy(mine(a, z, core), half(a, ctx, core), own_sem.at[1 + a]).wait()
    for copy, condition in started:
        if condition is None:
            copy.wait_send()
        else:
            pl.when(condition)(copy.wait_send)


def front(shard, expert_in, expert_out, tokens, lengths, block_order, routes, hot, grads, qkv_cols):
    layers = expert_in.shape[0]
    rows_in, rows_out = expert_in.shape[1], expert_out.shape[1]
    depth, cols = shard.shape[0] * 8 * layers, shard.shape[1]
    count = tokens.shape[0]
    kv_shape = (count * 2 * layers, qkv_cols - HEADS * HEAD)
    wide, pairs = 2 * GROUP * BLK, KV_HEADS // 2
    any_space = pl.BlockSpec(memory_space=pl.ANY)
    smem = pl.BlockSpec(memory_space=pltpu.SMEM)
    vmem = pl.BlockSpec(memory_space=pltpu.VMEM)
    dma = pltpu.SemaphoreType.DMA
    return pl.pallas_call(
        functools.partial(front_kernel, layers),
        out_shape=(
            jax.ShapeDtypeStruct((depth, cols), BF16),
            jax.ShapeDtypeStruct((rows_in * 2 * layers, expert_in.shape[2]), BF16),
            jax.ShapeDtypeStruct((rows_out * 2 * layers, expert_out.shape[2]), BF16),
            jax.ShapeDtypeStruct((count, depth), BF16),
            jax.ShapeDtypeStruct((count, qkv_cols), BF16),
            jax.ShapeDtypeStruct(kv_shape, BF16),
            jax.ShapeDtypeStruct((count, HEADS * HEAD), F32),
            jax.ShapeDtypeStruct((count, HEADS * HEAD), BF16),
            jax.ShapeDtypeStruct((count // BLK, pairs, wide), F32),
            jax.ShapeDtypeStruct((count, depth), F32),
            jax.ShapeDtypeStruct((count, depth), BF16),
            jax.ShapeDtypeStruct((count, AUX), F32),
            jax.ShapeDtypeStruct(grads.shape, BF16),
            jax.ShapeDtypeStruct(grads.shape, BF16),
        ),
        in_specs=[any_space] * 3 + [vmem, smem, smem, vmem, vmem, any_space],
        out_specs=(any_space,) * 3 + (vmem, vmem, any_space) + (vmem,) * 7 + (any_space,),
        scratch_shapes=[
            pltpu.VMEM((depth, cols), BF16),
            pltpu.VMEM(kv_shape, BF16),
            pltpu.VMEM((pairs, wide, 128), BF16),
            pltpu.VMEM((pairs, 8, wide), F32),
            pltpu.VMEM((pairs, 8, wide), F32),
            pltpu.VMEM((pairs, BLK, wide), F32),
            pltpu.VMEM(expert_in.shape, F32),
            pltpu.VMEM(expert_out.shape, F32),
            pltpu.VMEM(expert_in.shape, BF16),
            pltpu.VMEM(expert_out.shape, BF16),
            dma((8 * layers,)),
            dma((layers + 2,)),
            dma((layers + 1,)),
            dma((layers + 1,)),
            dma((layers,)),
            dma((4 * layers + 1,)),
            dma((2, 2 * layers)),
            dma((2, 2 * layers)),
            dma((2, 2 * layers)),
            dma((2, 2 * layers + 1)),
            dma((2 * layers,)),
            dma((2 * layers + 3,)),
            dma((5,)),
            dma((2, layers)),
            dma((4 * layers,)),
            dma((4 * layers,)),
        ],
        compiler_params=pltpu.CompilerParams(
            collective_id=0, has_side_effects=True, vmem_limit_bytes=60 * 2**20
        ),
        name="front",
    )(shard, expert_in, expert_out, tokens, lengths, block_order, routes, hot, grads)


def experts_kernel(
    layers,
    rows_ref,
    gates_ref,
    grads_ref,
    w_in_ref,
    w_down_ref,
    out_ref,
    back_ref,
    back_gates_ref,
    d_in_ref,
    d_down_ref,
    w_in,
    w_down,
    got,
    got_gates,
    x_s,
    grad_s,
    hidden_s,
    inner_s,
    back_s,
    back_gates_s,
    other_in,
    other_down,
    pair_in,
    pair_down,
    row_sem,
    row_send,
    gate_sem,
    gate_send,
    back_sem,
    back_send,
    back_gate_sem,
    back_gate_send,
    pair_sem,
    pair_send,
    load_sem,
):
    z, core, exp = lax.axis_index("le"), lax.axis_index("core"), lax.axis_index("exp")
    other = 1 - core
    columns = rows_ref.shape[0] // layers
    me = exp * layers + z
    cap, depth = rows_ref.shape[1], rows_ref.shape[2]
    chunk = columns * cap
    loads = [
        pltpu.make_async_copy(w_in_ref, w_in, load_sem.at[0]),
        pltpu.make_async_copy(w_down_ref, w_down, load_sem.at[1]),
    ]
    for load in loads:
        load.start()
    own_layer, mate, farthest, middle = near_to_far(z)
    peers = [
        (zz, (exp + t) % columns)
        for s, zz in enumerate([mate, farthest, middle, own_layer])
        for t in range(columns)
        if not (s == layers - 1 and t == 0)
    ]
    meet([place(zz, core, ee) for zz, ee in peers] + [place(z, other, exp)])

    started = []

    def go(copy):
        copy.start()
        started.append(copy)

    keeps = [
        pltpu.make_async_copy(rows_ref.at[me], got.at[me], load_sem.at[2]),
        pltpu.make_async_copy(gates_ref.at[me], got_gates.at[me], load_sem.at[3]),
    ]
    for keep in keeps:
        keep.start()
    for k, (zz, ee) in enumerate(peers):
        there = ee * layers + zz
        go(remote(gates_ref.at[there], got_gates.at[me], gate_send.at[k], gate_sem.at[me], place(zz, core, ee)))
        go(remote(rows_ref.at[there], got.at[me], row_send.at[k], row_sem.at[me], place(zz, core, ee)))
    for load in loads + keeps:
        load.wait()

    eye = lax.broadcasted_iota(jnp.int32, (cap, 128), 0) == lax.broadcasted_iota(jnp.int32, (cap, 128), 1)
    tile = 256

    def tiles(i):
        return pl.ds(pl.multiple_of(i * tile, tile), tile)

    for k, zz in enumerate([own_layer, mate, farthest, middle]):
        rows = pl.ds(k * chunk, chunk)
        for ee in range(columns):
            source = ee * layers + zz

            @pl.when(source != me)
            def _(source=source):
                here = place(z, other, exp)
                remote(got.at[source], got.at[source], row_send.at[0], row_sem.at[source], here).wait_recv()
                remote(
                    got_gates.at[source], got_gates.at[source], gate_send.at[0], gate_sem.at[source], here
                ).wait_recv()

            at = pl.ds(k * chunk + ee * cap, cap)
            x_s[at, :] = got[source]
            gate = jnp.sum(jnp.where(eye, got_gates[source, 0:1, :], 0.0), axis=1, keepdims=True)
            grad_s[at, :] = (gate * grads_ref[source].astype(F32)).astype(BF16)

        @pl.loop(0, FF // tile)
        def _(i, rows=rows):
            up_at = pl.ds(pl.multiple_of(FF + i * tile, tile), tile)
            gate = dot(x_s[rows, :], w_in[:, tiles(i)])
            up = dot(x_s[rows, :], w_in[:, up_at])
            grad_hidden = dot(grad_s[rows, :], w_down[tiles(i), :], ((1,), (1,)))
            sigmoid = jax.nn.sigmoid(gate)
            silu = gate * sigmoid
            hidden_s[rows, tiles(i)] = (silu * up).astype(BF16)
            inner_s[rows, tiles(i)] = (grad_hidden * up * sigmoid * (1.0 + gate * (1.0 - sigmoid))).astype(BF16)
            inner_s[rows, up_at] = (grad_hidden * silu).astype(BF16)

        @pl.loop(0, depth // tile)
        def _(i, rows=rows, zz=zz):
            back = dot(inner_s[rows, :], w_in[tiles(i), :], ((1,), (1,))).astype(BF16)
            for ee in range(columns):
                back_s[ee * layers + zz, :, tiles(i)] = back[ee * cap : (ee + 1) * cap]

        @pl.loop(0, depth // tile, init_carry=jnp.zeros((chunk, 128), F32))
        def gate_grads(i, sums, rows=rows, zz=zz):
            result = dot(hidden_s[rows, :], w_down[:, tiles(i)]).astype(BF16)
            parts = []
            for ee in range(columns):
                part = result[ee * cap : (ee + 1) * cap]
                out_ref[ee * layers + zz, :, tiles(i)] = part
                parts.append(part.astype(F32) * grads_ref[ee * layers + zz, :, tiles(i)].astype(F32))
            product = jnp.concatenate(parts, axis=0)
            return sums + product[:, :128] + product[:, 128:]

        gate_grads = jnp.sum(gate_grads, axis=1, keepdims=True)
        for ee in range(columns):
            there = ee * layers + zz
            column = gate_grads[ee * cap : (ee + 1) * cap]
            line = jnp.sum(jnp.where(eye, column, 0.0), axis=0, keepdims=True)
            back_gates_s[there] = jnp.broadcast_to(line, (8, 128))
            row_copy = remote(
                back_s.at[there],
                back_ref.at[me],
                back_send.at[there],
                back_sem.at[me],
                place(zz, core, ee),
            )
            gate_copy = remote(
                back_gates_s.at[there],
                back_gates_ref.at[me],
                back_gate_send.at[there],
                back_gate_sem.at[me],
                place(zz, core, ee),
            )

            @pl.when(there != me)
            def _(row_copy=row_copy, gate_copy=gate_copy):
                row_copy.start()
                gate_copy.start()

    own = [
        pltpu.make_async_copy(back_s.at[me], back_ref.at[me], load_sem.at[2]),
        pltpu.make_async_copy(back_gates_s.at[me], back_gates_ref.at[me], load_sem.at[3]),
    ]
    for copy in own:
        copy.start()

    half_in, half_down = d_in_ref.shape[1], d_down_ref.shape[1]

    def in_part(i, p):
        cols = pl.ds(pl.multiple_of(p * half_in, 128), half_in)
        return dot(x_s[:, tiles(i)], inner_s[:, cols], ((0,), (0,)))

    def down_part(i, p):
        cols = pl.ds(pl.multiple_of(p * half_down, 128), half_down)
        return dot(hidden_s[:, tiles(i)], grad_s[:, cols], ((0,), (0,)))

    @pl.loop(0, depth // tile)
    def _(i):
        other_in[tiles(i), :] = in_part(i, other).astype(BF16)

    go(remote(other_in, pair_in, pair_send.at[0], pair_sem.at[0], place(z, other, exp)))

    @pl.loop(0, FF // tile)
    def _(i):
        other_down[tiles(i), :] = down_part(i, other).astype(BF16)

    go(remote(other_down, pair_down, pair_send.at[1], pair_sem.at[1], place(z, other, exp)))
    remote(other_in, pair_in, pair_send.at[0], pair_sem.at[0], place(z, other, exp)).wait_recv()

    @pl.loop(0, depth // tile)
    def _(i):
        d_in_ref[tiles(i), :] = (in_part(i, core) + pair_in[tiles(i), :].astype(F32)).astype(BF16)

    remote(other_down, pair_down, pair_send.at[1], pair_sem.at[1], place(z, other, exp)).wait_recv()

    @pl.loop(0, FF // tile)
    def _(i):
        d_down_ref[tiles(i), :] = (down_part(i, core) + pair_down[tiles(i), :].astype(F32)).astype(BF16)

    for copy in own:
        copy.wait()
    for k, (zz, ee) in enumerate(peers):
        there = ee * layers + zz
        row_copy = remote(
            back_s.at[there], back_ref.at[there], back_send.at[there], back_sem.at[there], place(zz, core, ee)
        )
        gate_copy = remote(
            back_gates_s.at[there],
            back_gates_ref.at[there],
            back_gate_send.at[there],
            back_gate_sem.at[there],
            place(zz, core, ee),
        )
        row_copy.wait()
        gate_copy.wait()
    for copy in started:
        copy.wait_send()


def experts(rows, gates, grads, w_in, w_down, layers):
    count, cap, depth = rows.shape
    any_space = pl.BlockSpec(memory_space=pl.ANY)
    vmem = pl.BlockSpec(memory_space=pltpu.VMEM)
    dma = pltpu.SemaphoreType.DMA
    half_in = jax.ShapeDtypeStruct((depth, FF), BF16)
    half_down = jax.ShapeDtypeStruct((FF, depth // 2), BF16)
    return pl.pallas_call(
        functools.partial(experts_kernel, layers),
        out_shape=(
            jax.ShapeDtypeStruct(rows.shape, BF16),
            jax.ShapeDtypeStruct(rows.shape, BF16),
            jax.ShapeDtypeStruct(gates.shape, F32),
            half_in,
            half_down,
        ),
        in_specs=[any_space, any_space, vmem, any_space, any_space],
        out_specs=(vmem, any_space, any_space, vmem, vmem),
        scratch_shapes=[
            pltpu.VMEM(w_in.shape, BF16),
            pltpu.VMEM(w_down.shape, BF16),
            pltpu.VMEM(rows.shape, BF16),
            pltpu.VMEM(gates.shape, F32),
            pltpu.VMEM((count * cap, depth), BF16),
            pltpu.VMEM((count * cap, depth), BF16),
            pltpu.VMEM((count * cap, FF), BF16),
            pltpu.VMEM((count * cap, 2 * FF), BF16),
            pltpu.VMEM(rows.shape, BF16),
            pltpu.VMEM(gates.shape, F32),
            pltpu.VMEM(half_in.shape, BF16),
            pltpu.VMEM(half_down.shape, BF16),
            pltpu.VMEM(half_in.shape, BF16),
            pltpu.VMEM(half_down.shape, BF16),
        ]
        + [dma((count,))] * 8
        + [dma((2,)), dma((2,)), dma((4,))],
        compiler_params=pltpu.CompilerParams(
            collective_id=2, has_side_effects=True, vmem_limit_bytes=60 * 2**20
        ),
        name="experts",
    )(rows, gates, grads, w_in, w_down)


def add_rows(total, part, rows):
    slab = 16

    @pl.loop(0, rows // slab)
    def _(i):
        at = pl.ds(pl.multiple_of(i * slab, slab), slab)
        total[at, :] = (total[at, :].astype(F32) + part[at, :].astype(F32)).astype(BF16)


class Chain:
    def __init__(self, layers, z, above, below, own, rows, up, down, sems, sends):
        self.layers, self.z, self.above, self.below = layers, z, above, below
        self.own, self.rows, self.up, self.down = own, rows, up, down
        self.sems, self.sends = sems, sends
        self.parts = sems.shape[2]
        self.width = up.shape[2] // self.parts

    def columns(self, ref, h):
        return ref.at[:, pl.ds(h * self.width, self.width)]

    def rise(self, d, h):
        return remote(
            self.columns(self.own(d), h),
            self.columns(self.up.at[d], h),
            self.sends.at[0, d, h],
            self.sems.at[0, d, h],
            self.above,
        )

    def fall(self, d, h):
        return remote(
            self.columns(self.own(d), h),
            self.columns(self.down.at[d], h),
            self.sends.at[1, d, h],
            self.sems.at[1, d, h],
            self.below,
        )

    def end(self, step):
        for h in range(self.parts):
            pl.when(self.z == 0)(self.rise(self.layers - 1 - step, h).start)
            pl.when(self.z == self.layers - 1)(self.fall(step, h).start)

    def ends(self):
        for step in range(self.layers - 1):
            self.end(step)

    def add(self, d, h, buffer):
        add_rows(self.columns(self.own(d), h), self.columns(buffer.at[d], h), self.rows)

    def middle(self):
        z, last = self.z, self.layers - 1

        def pass_on(make, d, buffer):
            for h in range(self.parts):
                copy = make(d, h)
                copy.wait_recv()
                self.add(d, h, buffer)
                copy.start()

        def both(first_half):
            for step in range(last):
                high, low = last - step, step

                def upward(high=high):
                    pl.when((z > 0) & (z < high))(lambda: pass_on(self.rise, high, self.up))

                def downward(low=low):
                    pl.when((z < last) & (z > low))(lambda: pass_on(self.fall, low, self.down))

                for turn in (upward, downward) if first_half else (downward, upward):
                    turn()

        pl.when(z <= last // 2)(lambda: both(True))
        pl.when(z > last // 2)(lambda: both(False))

    def finish(self):
        z, last = self.z, self.layers - 1

        def take(make, buffer):
            for h in range(self.parts):
                make(z, h).wait_recv()
                self.add(z, h, buffer)

        pl.when(z > 0)(lambda: take(self.rise, self.up))
        pl.when(z < last)(lambda: take(self.fall, self.down))

    def wait_sends(self):
        for d in range(self.layers):
            for h in range(self.parts):
                pl.when(self.z < d)(self.rise(d, h).wait_send)
                pl.when(self.z > d)(self.fall(d, h).wait_send)


def finish_kernel(
    layers,
    grad_kv_ref,
    grad_q_ref,
    first_ref,
    tokens_ref,
    gain_ref,
    middle_ref,
    w_all_ref,
    attended_ref,
    second_ref,
    logits_ref,
    gain_moe_ref,
    base_ref,
    returned_ref,
    picks_ref,
    gates_ref,
    in_ref,
    down_ref,
    block_ref,
    d_tokens_ref,
    d_qkv_ref,
    d_out_ref,
    d_aux_ref,
    got_in_ref,
    got_down_ref,
    weights,
    projected,
    grad_first,
    kv_own,
    kv_pair,
    kv_up,
    kv_down,
    late_both,
    late_pair,
    late_near,
    late_up,
    late_down,
    q_both,
    q_pair,
    q_near,
    q_up,
    q_down,
    k_both,
    k_pair,
    k_near,
    k_up,
    k_down,
    load_sem,
    kv_pair_sem,
    kv_pair_send,
    kv_sem,
    kv_send,
    half_sem,
    half_send,
    pair_sem,
    pair_send,
    near_sem,
    near_send,
    line_sem,
    line_send,
):
    z, core, exp = lax.axis_index("le"), lax.axis_index("core"), lax.axis_index("exp")
    other = 1 - core
    partner = place(z, other, exp)
    above, below = place(z + 1, core, exp), place(z - 1, core, exp)
    x, y = x_of(exp), y_of(exp)
    mates = (x, y, y_of(x))
    own_layer, mate, farthest, middle = near_to_far(z)
    ctx = z * 2 + core
    rows = d_qkv_ref.shape[0]
    count = tokens_ref.shape[0]
    head_cols = HEADS * HEAD
    qkv_cols = d_qkv_ref.shape[1]
    kv_cols = qkv_cols - head_cols

    loads = []

    def load(src, dst):
        copy = pltpu.make_async_copy(src, dst, load_sem.at[len(loads)])
        copy.start()
        loads.append(copy)
        return copy

    kv_loads = [
        load(grad_kv_ref.at[pl.ds(pl.multiple_of((d * 2 + core) * count, 16), count), :], kv_own.at[d])
        for d in range(layers)
    ]
    depth = w_all_ref.shape[0]

    def weights_part(i):
        part = w_all_ref.at[pl.ds(i * depth // 2, depth // 2), pl.ds(0, qkv_cols)]
        return pltpu.make_async_copy(part, weights, load_sem.at[2 * layers + 2])

    weights_part(0).start()
    meet(
        [
            place((z + s) % layers, (core + p) % 2, exp)
            for s in range(layers)
            for p in range(2)
            if s + p > 0
        ]
        + [place(z, core, mate) for mate in mates]
    )
    started = []

    def go(copy):
        copy.start()
        started.append(copy)

    arrays = ((in_ref, got_in_ref), (down_ref, got_down_ref))

    def mine(a, owner):
        n = arrays[a][1].shape[1]
        return arrays[a][0].at[pl.ds(owner * n, n), :]

    def half(a, expert, p):
        cols = arrays[a][0].shape[1]
        return arrays[a][1].at[expert, :, pl.ds(pl.multiple_of(p * cols, 128), cols)]

    for a in range(2):
        load(mine(a, ctx), half(a, z, core))

    def hand_back(a, early):
        for s, zz in enumerate([mate, farthest, middle, own_layer]):
            across = between(z, zz)
            for p in range(2):
                if s == layers - 1 and p == 0:
                    continue
                pp = (core + p) % 2
                copy = remote(
                    mine(a, zz * 2 + pp),
                    half(a, z, core),
                    half_send.at[a, s * 2 + p],
                    half_sem.at[a, ctx],
                    place(zz, pp, exp),
                )
                if early:
                    pl.when(across)(copy.start)
                else:
                    pl.when(~across)(copy.start)
                    started.append(copy)

    hand_back(0, True)

    for d in range(layers):
        go(
            remote(
                grad_kv_ref.at[pl.ds(pl.multiple_of((d * 2 + other) * count, 16), count), :],
                kv_pair.at[d],
                kv_pair_send.at[d],
                kv_pair_sem.at[d],
                partner,
            )
        )
    kv_line = Chain(
        layers, z, above, below, lambda d: kv_own.at[d], count, kv_up, kv_down, kv_sem, kv_send
    )
    for copy in kv_loads:
        copy.wait()
    for k in range(layers):
        d = jnp.where(z < layers // 2, layers - 1 - k, k)
        remote(kv_pair.at[d], kv_pair.at[d], kv_pair_send.at[d], kv_pair_sem.at[d], partner).wait_recv()
        add_rows(kv_own.at[d], kv_pair.at[d], count)
        if k < layers - 1:
            kv_line.end(k)

    def near_copy(i, near, own, d, m, target):
        return remote(
            own.at[d, pl.ds(pl.multiple_of(target * rows, 16), rows), :],
            near.at[m, d],
            near_send.at[i, m, d],
            near_sem.at[i, m, d],
            place(z, core, mates[m]),
        )

    def pair_sums(i, own, pair, near):
        for d in range(layers):
            remote(pair.at[d], pair.at[d], pair_send.at[i, d], pair_sem.at[i, d], partner).wait_recv()
            add_rows(own.at[d], pair.at[d], 4 * rows)
            for m in range(3):
                go(near_copy(i, near, own, d, m, mates[m]))

    def near_sums(i, own, near):
        for d in range(layers):
            for m in range(3):
                near_copy(i, near, own, d, m, exp).wait_recv()
            mine = own.at[d, pl.ds(pl.multiple_of(exp * rows, 16), rows), :]

            @pl.loop(0, rows // 16)
            def _(r, mine=mine, d=d):
                at = pl.ds(pl.multiple_of(r * 16, 16), 16)
                total = mine[at, :].astype(F32)
                for m in range(3):
                    total = total + near[m, d, at, :].astype(F32)
                mine[at, :] = total.astype(BF16)

    def line_of(i, own, up, down):
        return Chain(
            layers,
            z,
            above,
            below,
            lambda d: own.at[d, pl.ds(pl.multiple_of(exp * rows, 16), rows), :],
            rows,
            up,
            down,
            line_sem.at[i],
            line_send.at[i],
        )

    def outer_product(both, cols, left, right, gains=None):
        for d in range(layers):
            block = left[:, d * 8 * rows : (d + 1) * 8 * rows]
            part = dot(block, right, ((0,), (0,)))
            if gains is not None:
                turned = [
                    jnp.transpose(jnp.broadcast_to(gains[:, at : at + 128], (128, 128)))
                    for at in range(d * 8 * rows, (d + 1) * 8 * rows, 128)
                ]
                lane = lax.broadcasted_iota(jnp.int32, part.shape, 1)
                part = jnp.where(lane == 0, jnp.concatenate(turned, axis=0), part)
            part = part.astype(BF16)
            both[0, d, :, cols] = part[: 4 * rows]
            both[1, d, :, cols] = part[4 * rows :]

    def pair_up(i, both, pair):
        for d in range(layers):
            go(remote(both.at[other, d], pair.at[d], pair_send.at[i, d], pair_sem.at[i, d], partner))

    outer_product(q_both, slice(0, head_cols), first_ref, grad_q_ref[...])
    pair_up(1, q_both, q_pair)
    width = middle_ref.shape[1]
    outer_product(late_both, slice(0, width), attended_ref, middle_ref[...].astype(BF16))
    outer_product(late_both, slice(width, width + AUX), second_ref, logits_ref[...], gain_moe_ref[...])
    pair_up(0, late_both, late_pair)
    late_own = late_both.at[core]
    q_own = q_both.at[core]
    pair_sums(1, q_own, q_pair, q_near)
    pair_sums(0, late_own, late_pair, late_near)
    kv_line.middle()
    hand_back(0, False)
    hand_back(1, True)
    hand_back(1, False)
    kv_line.finish()

    projected[:, :head_cols] = grad_q_ref[...]
    projected[:, head_cols:] = kv_own[z]
    outer_product(k_both, slice(0, kv_cols), first_ref, projected[:, head_cols:])
    tile = 256
    for i in range(2):
        weights_part(i).wait()

        @pl.loop(0, depth // 2 // tile)
        def _(j, i=i):
            at = pl.ds(pl.multiple_of(j * tile, tile), tile)
            to = pl.ds(pl.multiple_of(i * depth // 2 + j * tile, tile), tile)
            grad_first[:, to] = dot(projected[...], weights[at, :], ((1,), (1,)))

        if i == 0:
            weights_part(1).start()

    inputs = tokens_ref[...].astype(F32)
    scale = norm_scale(inputs)
    norm = inputs * scale
    grad = grad_first[...]
    grad_gain = jnp.sum(grad * norm, axis=0, keepdims=True)
    for d in range(layers):
        block = jnp.concatenate(
            [
                jnp.transpose(jnp.broadcast_to(grad_gain[:, at : at + 128], (128, 128)))
                for at in range(d * 8 * rows, (d + 1) * 8 * rows, 128)
            ],
            axis=0,
        ).astype(BF16)
        k_both[0, d, :, kv_cols:] = block[: 4 * rows]
        k_both[1, d, :, kv_cols:] = block[4 * rows :]
    pair_up(2, k_both, k_pair)
    grad = grad * gain_ref[...]
    d_tokens_ref[...] = (
        middle_ref[...] + scale * (grad - norm * jnp.mean(grad * norm, axis=-1, keepdims=True))
    ).astype(BF16)
    k_own = k_both.at[core]
    pair_sums(2, k_own, k_pair, k_near)

    @pl.loop(0, depth // tile)
    def _(i):
        at = pl.ds(pl.multiple_of(i * tile, tile), tile)
        total = base_ref[:, at]
        for k in range(2):
            total = total + gates_ref[:, k : k + 1] * dot(picks_ref[k], returned_ref[:, at])
        block_ref[:, at] = total.astype(BF16)

    late_line = line_of(0, late_own, late_up, late_down)
    q_line = line_of(1, q_own, q_up, q_down)
    k_line = line_of(2, k_own, k_up, k_down)
    near_sums(1, q_own, q_near)
    q_line.ends()
    near_sums(0, late_own, late_near)
    late_line.ends()
    q_line.middle()
    near_sums(2, k_own, k_near)
    k_line.ends()
    late_line.middle()
    k_line.middle()
    mine_rows = pl.ds(pl.multiple_of(exp * rows, 16), rows)
    q_line.finish()
    d_qkv_ref[:, :head_cols] = q_both[core, z, mine_rows, :].astype(F32)
    late_line.finish()
    last = late_both[core, z, mine_rows, :].astype(F32)
    d_out_ref[...] = last[:, :width]
    d_aux_ref[:, AUX:] = last[:, width:]
    k_line.finish()
    last = k_both[core, z, mine_rows, :].astype(F32)
    d_qkv_ref[:, head_cols:] = last[:, :kv_cols]
    d_aux_ref[:, :AUX] = last[:, kv_cols:]

    for source in range(2 * layers):
        for a in range(2):

            @pl.when(source != ctx)
            def _(source=source, a=a):
                remote(
                    half(a, source // 2, source % 2),
                    half(a, source // 2, source % 2),
                    half_send.at[a, 0],
                    half_sem.at[a, source],
                    partner,
                ).wait_recv()

    for copy in loads[-2:]:
        copy.wait()
    for line in (kv_line, late_line, q_line, k_line):
        line.wait_sends()
    for copy in started:
        copy.wait_send()


def finish(
    grad_kv,
    grad_q,
    first,
    tokens,
    gain,
    middle,
    w_all,
    attended,
    second,
    grad_logits,
    gain_moe,
    base,
    returned,
    picks,
    gates,
    grad_in,
    grad_down,
    layers,
):
    depth, count = first.shape[1], first.shape[0]
    rows = depth // (8 * layers)
    qkv_cols = grad_q.shape[1] + grad_kv.shape[1]
    n_in, n_down = grad_in.shape[0] // (2 * layers), grad_down.shape[0] // (2 * layers)
    any_space = pl.BlockSpec(memory_space=pl.ANY)
    vmem = pl.BlockSpec(memory_space=pltpu.VMEM)
    dma = pltpu.SemaphoreType.DMA

    def sums(cols):
        return [
            pltpu.VMEM((2, layers, 4 * rows, cols), BF16),
            pltpu.VMEM((layers, 4 * rows, cols), BF16),
            pltpu.VMEM((3, layers, rows, cols), BF16),
            pltpu.VMEM((layers, rows, cols), BF16),
            pltpu.VMEM((layers, rows, cols), BF16),
        ]

    return pl.pallas_call(
        functools.partial(finish_kernel, layers),
        out_shape=(
            jax.ShapeDtypeStruct((count, depth), BF16),
            jax.ShapeDtypeStruct((count, depth), BF16),
            jax.ShapeDtypeStruct((rows, qkv_cols), F32),
            jax.ShapeDtypeStruct((rows, depth), F32),
            jax.ShapeDtypeStruct((rows, 2 * AUX), F32),
            jax.ShapeDtypeStruct((layers, n_in, 2 * grad_in.shape[1]), BF16),
            jax.ShapeDtypeStruct((layers, n_down, 2 * grad_down.shape[1]), BF16),
        ),
        in_specs=[any_space] + [vmem] * 5 + [any_space] + [vmem] * 8 + [any_space] * 2,
        out_specs=(vmem,) * 5 + (any_space,) * 2,
        scratch_shapes=[
            pltpu.VMEM((depth // 2, qkv_cols), BF16),
            pltpu.VMEM((count, qkv_cols), BF16),
            pltpu.VMEM((count, depth), F32),
        ]
        + [pltpu.VMEM((layers, count, grad_kv.shape[1]), BF16)] * 4
        + sums(depth + AUX)
        + sums(grad_q.shape[1])
        + sums(grad_kv.shape[1] + AUX)
        + [
            dma((2 * layers + 3,)),
            dma((layers,)),
            dma((layers,)),
            dma((2, layers, 2)),
            dma((2, layers, 2)),
            dma((2, 2 * layers)),
            dma((2, 2 * layers)),
            dma((3, layers)),
            dma((3, layers)),
            dma((3, 3, layers)),
            dma((3, 3, layers)),
            dma((3, 2, layers, 1)),
            dma((3, 2, layers, 1)),
        ],
        compiler_params=pltpu.CompilerParams(
            collective_id=1, has_side_effects=True, vmem_limit_bytes=60 * 2**20
        ),
        name="finish",
    )(
        grad_kv,
        grad_q,
        first,
        tokens,
        gain,
        middle,
        w_all,
        attended,
        second,
        grad_logits,
        gain_moe,
        base,
        returned,
        picks,
        gates,
        grad_in,
        grad_down,
    )


def settle_kernel(*refs):
    count = len(refs) // 2
    for src, dst in zip(refs[:count], refs[count:]):
        dst[...] = src[...].astype(dst.dtype)


def settle(arrays, steps):
    def spec(array):
        if array.ndim == 2 and array.shape[0] % (16 * steps) == 0:
            return pl.BlockSpec((array.shape[0] // steps, array.shape[1]), lambda i: (i, 0))
        if array.ndim == 3 and array.shape[1] % (16 * steps) == 0:
            return pl.BlockSpec(
                (array.shape[0], array.shape[1] // steps, array.shape[2]), lambda i: (0, i, 0)
            )
        return pl.BlockSpec(array.shape, lambda i: (0,) * array.ndim)

    specs = [spec(array) for array, _ in arrays]
    return pl.pallas_call(
        settle_kernel,
        grid=(steps,),
        out_shape=[jax.ShapeDtypeStruct(array.shape, dtype) for array, dtype in arrays],
        in_specs=specs,
        out_specs=specs,
        compiler_params=pltpu.CompilerParams(vmem_limit_bytes=60 * 2**20),
        name="settle",
    )(*[array for array, _ in arrays])


CTX = ("le", "rep", "core")
ALL = ("le", "rep", "core", "exp")
OWNERS = ("exp", "le")


def on_device(
    tokens,
    cotangent,
    routes,
    lengths,
    block_order,
    gain_attn,
    qkv_weight,
    out_weight,
    gain_moe,
    router_weight,
    expert_in,
    expert_out,
):
    tok_rows = tokens.shape[1]
    head_width = HEADS * HEAD
    exp_local = expert_in.shape[0]
    n_ctx = D // expert_in.shape[1]
    copies = n_ctx // exp_local
    n_exp = EXPERTS // exp_local
    in_rows, out_rows = expert_in.shape[1], expert_out.shape[1]

    route_hot = (
        routes[0][:, :, None] == jnp.arange(EXPERTS, dtype=jnp.int32)[None, None, :]
    ).astype(F32)
    flat_hot = route_hot.reshape(tok_rows * 2, EXPERTS).astype(BF16)
    order = jnp.arange(tok_rows * 2, dtype=jnp.int32)
    earlier = (order[:, None] > order[None, :]).astype(BF16)
    ranks = dot(earlier, flat_hot)
    slot_index = jnp.sum(ranks * flat_hot.astype(F32), axis=1).astype(jnp.int32)
    target = (routes[0].reshape(tok_rows * 2) * CAP + slot_index).reshape(tok_rows, 2)
    slots = jnp.arange(EXPERTS * CAP, dtype=jnp.int32)
    picks = [(target[:, k : k + 1] == slots[None, :]) for k in range(2)]
    sends = [(target[:, k][None, :] == slots[:, None]) for k in range(2)]
    send_hot = (sends[0] | sends[1]).astype(BF16)

    def to_experts(rows):
        return lax.all_to_all(
            rows.reshape((EXPERTS, CAP) + rows.shape[1:]),
            OWNERS,
            split_axis=0,
            concat_axis=0,
            tiled=True,
        ).reshape(rows.shape)

    cols = qkv_weight.shape[1]
    aux = jnp.concatenate([gain_attn[:, None], gain_moe[:, None], router_weight], axis=1)
    aux = jnp.pad(aux, ((0, 0), (0, AUX - aux.shape[1])))
    shard = jnp.concatenate([qkv_weight, aux, out_weight], axis=1).astype(BF16)
    special = (copies, exp_local, n_exp) == (2, 4, 4)
    if special:
        (
            w_all,
            w_in,
            w_down,
            first,
            projected,
            kv,
            exact,
            attended,
            lse,
            middle,
            second,
            gates,
            second_rows,
            grad_y_rows,
        ) = front(
            shard,
            expert_in,
            expert_out,
            tokens[0],
            lengths,
            block_order,
            routes[0],
            send_hot,
            dot(send_hot, cotangent[0]).astype(BF16).reshape(EXPERTS, CAP, D),
            cols,
        )
        gates = gates[:, :2]
    else:
        w_all = lax.all_gather(shard, ALL, axis=0, tiled=True)

        def to_owner(weight):
            rows, width = weight.shape[1:]
            halves = weight.astype(BF16).reshape(exp_local, rows, 2, width // 2).transpose(0, 2, 1, 3)
            halves = jnp.broadcast_to(
                halves[:, None], (exp_local, copies // 2, 2, rows, width // 2)
            ).reshape(n_ctx, rows, width // 2)
            mine = lax.all_to_all(halves, CTX, split_axis=0, concat_axis=0, tiled=True)
            return lax.all_gather(mine.reshape(n_ctx * rows, width // 2), "core", axis=1, tiled=True)

        w_in = to_owner(expert_in)
        w_down = to_owner(expert_out)
    w_qkv = w_all[:, :cols]
    aux_all = w_all[:, cols : cols + AUX]
    w_attn_out = w_all[:, cols + AUX :]
    gain_first = aux_all[:, 0].astype(F32)
    gain_second = aux_all[:, 1].astype(F32)
    w_router = aux_all[:, 2 : 2 + EXPERTS]

    inputs = tokens[0].astype(F32)
    scale_first = norm_scale(inputs)
    norm_first = inputs * scale_first
    mine = (lax.axis_index(CTX) * (tok_rows // BLK)).astype(jnp.int32).reshape(1)
    if not special:
        first = (norm_first * gain_first).astype(BF16)
        projected = dot(first, w_qkv).astype(BF16)
        kv = lax.all_gather(projected[:, head_width:], CTX, axis=0, tiled=True)
        kv, grad_y_send = lax.optimization_barrier((kv, dot(send_hot, cotangent[0]).astype(BF16)))
        grad_y_rows = to_experts(grad_y_send)
        exact, attended, lse = attend(lengths, block_order, mine, projected, kv)
        middle = inputs + dot(attended, w_attn_out)
    scale_second = norm_scale(middle)
    norm_second = middle * scale_second
    if not special:
        second = (norm_second * gain_second).astype(BF16)
        logits = dot(second, w_router)
        chosen = jnp.sum(route_hot * logits[:, None, :], axis=-1)
        gates = jax.nn.softmax(chosen, axis=-1)

    gate_rows = jnp.sum(
        jnp.where(sends[0], gates[:, 0][None, :], 0.0) + jnp.where(sends[1], gates[:, 1][None, :], 0.0),
        axis=1,
        keepdims=True,
    )
    if special:
        slot_gates = jnp.broadcast_to(
            jnp.pad(gate_rows.reshape(EXPERTS, 1, CAP), ((0, 0), (0, 0), (0, 128 - CAP))), (EXPERTS, 8, 128)
        )
        expert_rows, grad_returned, gate_grads, grad_in, grad_down = experts(
            second_rows,
            slot_gates,
            grad_y_rows,
            w_in,
            w_down,
            exp_local,
        )
        returned = to_experts(expert_rows.reshape(EXPERTS * CAP, D))
        grad_returned = grad_returned.reshape(EXPERTS * CAP, D)
        gate_grads = gate_grads[:, 0, :CAP].reshape(1, EXPERTS * CAP)
    else:
        def in_parts(column):
            high = lax.reduce_precision(column, 8, 7)
            rest = column - high
            mid = lax.reduce_precision(rest, 8, 7)
            parts = jnp.concatenate([high, mid, rest - mid], axis=1).astype(BF16)
            return jnp.pad(parts, ((0, 0), (0, AUX - 3)))

        gate_parts = in_parts(gate_rows)
        payload = to_experts(
            jnp.concatenate([dot(send_hot, second).astype(BF16), gate_parts], axis=1)
        )
        received = payload[:, :D]
        gate_got = jnp.sum(payload[:, D : D + 3].astype(F32), axis=1, keepdims=True)

        gate_up = dot(received, w_in)
        gate_part = gate_up[:, :FF]
        up_part = gate_up[:, FF:]
        sigmoid_gate = jax.nn.sigmoid(gate_part)
        silu_gate = gate_part * sigmoid_gate
        hidden = (silu_gate * up_part).astype(BF16)
        expert_rows = dot(hidden, w_down)
        expert_rows = expert_rows.astype(BF16)
        grad_y_rows = grad_y_rows.astype(F32)
        returned = to_experts(expert_rows)

        grad_rows = (gate_got * grad_y_rows).astype(BF16)
        gate_grad_parts = in_parts(
            jnp.sum(grad_y_rows * expert_rows.astype(F32), axis=1, keepdims=True)
        )
        half_d = D // 2
        grad_hidden = dot(grad_rows, w_down, ((1,), (1,)))
        grad_gate = (
            grad_hidden * up_part * sigmoid_gate * (1.0 + gate_part * (1.0 - sigmoid_gate))
        ).astype(BF16)
        grad_up = (grad_hidden * silu_gate).astype(BF16)
        grad_gate_up = jnp.concatenate([grad_gate, grad_up], axis=1)
        grad_back = dot(grad_gate_up, w_in, ((1,), (1,)))
        grad_returned = to_experts(jnp.concatenate([grad_back.astype(BF16), gate_grad_parts], axis=1))

        grad_in = jnp.stack(
            [dot(received, grad_gate, ((0,), (0,))), dot(received, grad_up, ((0,), (0,)))]
        ).astype(BF16)
        grad_down = jnp.stack(
            [
                dot(hidden, grad_rows[:, :half_d], ((0,), (0,))),
                dot(hidden, grad_rows[:, half_d:], ((0,), (0,))),
            ]
        ).astype(BF16)

        grad_in = lax.psum_scatter(grad_in, "core", scatter_dimension=0, tiled=True)[0]
        grad_down = lax.psum_scatter(grad_down, "core", scatter_dimension=0, tiled=True)[0]
        grad_returned, grad_in, grad_down = lax.optimization_barrier((grad_returned, grad_in, grad_down))
        gate_grads = jnp.sum(grad_returned[:, D:].astype(F32), axis=1).reshape(1, EXPERTS * CAP)
        grad_returned = grad_returned[:, :D]

    grad_y = cotangent[0].astype(F32)
    pick_hot = [p.astype(BF16) for p in picks]
    grad_gates = jnp.concatenate(
        [jnp.sum(jnp.where(p, gate_grads, 0.0), axis=1, keepdims=True) for p in picks], axis=1
    )
    grad_chosen = gates * (grad_gates - jnp.sum(gates * grad_gates, axis=-1, keepdims=True))
    grad_logits = jnp.sum(grad_chosen[:, :, None] * route_hot, axis=1).astype(BF16)
    grad_second = dot(pick_hot[0] + pick_hot[1], grad_returned) + dot(
        grad_logits, w_router, ((1,), (1,))
    )
    grad_gain_second = jnp.sum(grad_second * norm_second, axis=0)
    grad_norm_second = grad_second * gain_second
    grad_middle = grad_y + scale_second * (
        grad_norm_second
        - norm_second * jnp.mean(grad_norm_second * norm_second, axis=-1, keepdims=True)
    )
    grad_branch = grad_middle.astype(BF16)
    grad_attended = dot(grad_branch, w_attn_out, ((1,), (1,))).astype(BF16)
    grad_queries, grad_kv = attend_back(
        lengths, block_order, mine, projected, kv, grad_attended, lse, exact
    )
    grad_queries, grad_kv, returned = lax.optimization_barrier((grad_queries, grad_kv, returned))
    if special:
        block_out, grad_inputs, sum_qkv, sum_out, sum_aux, sum_in, sum_down = finish(
            grad_kv,
            grad_queries,
            first,
            tokens[0],
            gain_first[None, :],
            grad_middle,
            w_all,
            attended,
            second,
            jnp.pad(grad_logits, ((0, 0), (1, AUX - 1 - EXPERTS))),
            grad_gain_second[None, :],
            middle,
            returned,
            jnp.stack(pick_hot),
            gates,
            grad_in,
            grad_down,
            exp_local,
        )
        block_out, grad_inputs, sum_qkv, sum_out, sum_in, sum_down = settle(
            (
                (block_out, BF16),
                (grad_inputs, BF16),
                (sum_qkv, F32),
                (sum_out, F32),
                (sum_in, F32),
                (sum_down, F32),
            ),
            4,
        )
    else:
        grad_router = dot(second, grad_logits, ((0,), (0,)))
        grad_attn_out = dot(attended, grad_branch, ((0,), (0,)))
        late = jnp.concatenate([grad_gain_second[:, None], grad_router], axis=1)
        late = jnp.pad(late, ((0, 0), (0, AUX - late.shape[1])))
        late = jnp.concatenate([grad_attn_out.astype(BF16), late.astype(BF16)], axis=1)
        grad_kv = lax.psum_scatter(grad_kv, CTX, scatter_dimension=0, tiled=True)
        grad_projected = jnp.concatenate([grad_queries, grad_kv], axis=1)
        grad_qkv = dot(first, grad_projected, ((0,), (0,)))
        grad_first = dot(grad_projected, w_qkv, ((1,), (1,)))
        grad_gain_first = jnp.sum(grad_first * norm_first, axis=0)
        grad_norm_first = grad_first * gain_first
        grad_inputs = grad_middle + scale_first * (
            grad_norm_first
            - norm_first * jnp.mean(grad_norm_first * norm_first, axis=-1, keepdims=True)
        )
        grad_inputs = grad_inputs.astype(BF16)
        last = jnp.pad(grad_gain_first[:, None], ((0, 0), (0, AUX - 1)))
        part = jnp.concatenate([grad_qkv.astype(BF16), last.astype(BF16), late], axis=1)
        total = lax.psum_scatter(part, ALL, scatter_dimension=0, tiled=True).astype(F32)
        sum_qkv, sum_out = total[:, :cols], total[:, cols + AUX : cols + AUX + D]
        sum_aux = jnp.concatenate([total[:, cols : cols + AUX], total[:, cols + AUX + D :]], axis=1)
        picked = [dot(p, returned) for p in pick_hot]
        block_out = (middle + gates[:, 0:1] * picked[0] + gates[:, 1:2] * picked[1]).astype(BF16)

        def to_rows(half, rows):
            width = half.shape[1]
            got = lax.all_to_all(
                half.reshape(n_ctx, rows, width), CTX, split_axis=0, concat_axis=0, tiled=True
            ).astype(F32)
            got = got.reshape(exp_local, copies // 2, 2, rows, width).sum(axis=1)
            return got.transpose(0, 2, 1, 3).reshape(exp_local, rows, 2 * width)

        sum_in = to_rows(grad_in, in_rows)
        sum_down = to_rows(grad_down, out_rows)
    return (
        block_out[None],
        grad_inputs[None],
        sum_aux[:, 0],
        sum_qkv,
        sum_out,
        sum_aux[:, AUX],
        sum_aux[:, AUX + 1 : AUX + 1 + EXPERTS],
        sum_in.astype(F32),
        sum_down.astype(F32),
    )


def solution(mesh):
    n_ctx, n_exp = mesh.shape["ctx"], mesh.shape["exp"]
    exp_local = EXPERTS // n_exp
    copies = n_ctx // exp_local
    inner = Mesh(mesh.devices.reshape(exp_local, copies // 2, 2, n_exp), ALL)
    by_token = P("exp", CTX, None)
    by_row = P(ALL, None)
    by_expert = P("exp", CTX, None)
    return jax.shard_map(
        on_device,
        mesh=inner,
        in_specs=(
            by_token,
            by_token,
            by_token,
            P("exp", None),
            P("exp", None),
            P(ALL),
            by_row,
            by_row,
            P(ALL),
            by_row,
            by_expert,
            by_expert,
        ),
        out_specs=(
            by_token,
            by_token,
            P(ALL),
            by_row,
            by_row,
            P(ALL),
            by_row,
            by_expert,
            by_expert,
        ),
        check_vma=False,
    )
```

```python
import functools

import jax
import jax.numpy as jnp
from jax import lax
from jax.experimental import pallas as pl
from jax.experimental.pallas import tpu as pltpu
from jax.sharding import Mesh
from jax.sharding import PartitionSpec as P

D = 1536
HEADS = 24
KV_HEADS = 8
HEAD = 64
GROUP = HEADS // KV_HEADS
FF = 1024
EXPERTS = 16
BLK = 128
CAP = 48
AUX = 128

epsilon = 1e-05
far_negative = -1e30
start_max = -1e29
F32 = jnp.float32
BF16 = jnp.bfloat16


def norm_scale(values):
    return lax.rsqrt(jnp.mean(values * values, axis=-1, keepdims=True) + epsilon)


def dot(a, b, dims=((1,), (0,))):
    return lax.dot_general(a, b, (dims, ((), ())), preferred_element_type=F32)


def lane_half(shape, half):
    lane = lax.broadcasted_iota(jnp.int32, shape, 1)
    return (lane >= HEAD) if half else (lane < HEAD)


def head_tiles(ref, rows, pair, scale):
    tiles = []
    for i in range(2 * GROUP):
        head = pair * 2 * GROUP + i
        group = head // GROUP
        tile = ref[rows, (head // 2) * 128 : (head // 2 + 1) * 128].astype(F32)
        if head % 2 != group % 2:
            tile = pltpu.roll(tile, HEAD, 1)
        tile = jnp.where(lane_half(tile.shape, group % 2), tile * scale, 0.0)
        tiles.append(tile.astype(BF16))
    return jnp.concatenate(tiles, axis=0)


def block_visibility(lengths_ref, query_block, key_block, parts):
    lanes = lax.broadcasted_iota(jnp.int32, (1, BLK), 1)
    query_pos = query_block * BLK + lanes
    start = jnp.zeros((1, BLK), jnp.int32)
    bound = jnp.int32(0)
    for s in range(parts - 1):
        bound = bound + lengths_ref[0, s]
        start = jnp.where(query_pos >= bound, bound, start)
    key_pos = key_block * BLK + lax.broadcasted_iota(jnp.int32, (BLK, BLK), 0)
    one = ((key_pos >= start) & (key_pos <= query_pos)).astype(jnp.int32)
    return jnp.concatenate([one] * (2 * GROUP), axis=1) > 0


def first_row_start(lengths_ref, query_block, parts):
    start = jnp.int32(0)
    bound = jnp.int32(0)
    for s in range(parts - 1):
        bound = bound + lengths_ref[0, s]
        start = jnp.where(query_block * BLK >= bound, bound, start)
    return start


def attend_blocks(
    parts,
    skip,
    lengths_ref,
    order_ref,
    mine,
    q_ref,
    kv_ref,
    exact_ref,
    out_ref,
    lse_ref,
    q_s,
    m_s,
    sum_s,
    acc_s,
):
    width = KV_HEADS * HEAD
    wide = 2 * GROUP * BLK
    for qb in range(q_ref.shape[0] // BLK):
        rows = pl.ds(qb * BLK, BLK)
        for pair in range(KV_HEADS // 2):
            q_s[pair] = head_tiles(q_ref, rows, pair, HEAD**-0.5)
            m_s[pair] = jnp.full((8, wide), start_max, F32)
            sum_s[pair] = jnp.zeros((8, wide), F32)
            acc_s[pair] = jnp.zeros((BLK, wide), F32)
        query_block = order_ref[0, mine + qb]
        first = first_row_start(lengths_ref, query_block, parts)

        @pl.loop(0, order_ref.shape[1])
        def _(kb):
            key_block = order_ref[0, kb]

            def fold():
                seen = block_visibility(lengths_ref, query_block, key_block, parts)
                key_rows = pl.ds(kb * BLK, BLK)
                for pair in range(KV_HEADS // 2):
                    keys = kv_ref[key_rows, pl.ds(pair * 128, 128)]
                    values = kv_ref[key_rows, pl.ds(width + pair * 128, 128)]
                    scores = dot(keys, q_s[pair], ((1,), (1,)))
                    scores = jnp.where(seen, scores, far_negative)
                    old = m_s[pair, 0:1, :]
                    new = jnp.maximum(old, jnp.max(scores, axis=0, keepdims=True))
                    weights = jnp.exp(scores - new)
                    factor = jnp.exp(old - new)
                    sum_s[pair, 0:1, :] = sum_s[pair, 0:1, :] * factor + jnp.sum(
                        weights, axis=0, keepdims=True
                    )
                    acc_s[pair] = acc_s[pair] * factor + dot(values, weights.astype(BF16), ((0,), (0,)))
                    m_s[pair, 0:1, :] = new

            if skip:
                pl.when((key_block <= query_block) & (key_block * BLK + BLK > first))(fold)
            else:
                fold()

        tiles = []
        for pair in range(KV_HEADS // 2):
            total = sum_s[pair, 0:1, :]
            lse_ref[qb, pair : pair + 1, :] = m_s[pair, 0:1, :] + jnp.log(total)
            acc = acc_s[pair] / total
            for i in range(2 * GROUP):
                head = pair * 2 * GROUP + i
                tile = jnp.transpose(acc[:, i * BLK : (i + 1) * BLK])
                if head % 2 != (head // GROUP) % 2:
                    tile = pltpu.roll(tile, HEAD, 1)
                tiles.append(tile)
                if head % 2 == 1:
                    both = jnp.where(lane_half(tile.shape, 0), tiles[head - 1], tile)
                    lanes = pl.ds((head // 2) * 128, 128)
                    exact_ref[rows, lanes] = both
                    out_ref[rows, lanes] = both.astype(BF16)


def attend_kernel(parts, lengths_ref, order_ref, mine_ref, *refs):
    attend_blocks(parts, True, lengths_ref, order_ref, mine_ref[0], *refs)


def attend(lengths, order, mine, projected, kv):
    rows = projected.shape[0]
    smem = pl.BlockSpec(memory_space=pltpu.SMEM)
    vmem = pl.BlockSpec(memory_space=pltpu.VMEM)
    wide = 2 * GROUP * BLK
    pairs = KV_HEADS // 2
    return pl.pallas_call(
        functools.partial(attend_kernel, lengths.shape[1]),
        out_shape=(
            jax.ShapeDtypeStruct((rows, HEADS * HEAD), F32),
            jax.ShapeDtypeStruct((rows, HEADS * HEAD), BF16),
            jax.ShapeDtypeStruct((rows // BLK, pairs, wide), F32),
        ),
        in_specs=[smem, smem, smem, vmem, vmem],
        out_specs=(vmem, vmem, vmem),
        scratch_shapes=[
            pltpu.VMEM((pairs, wide, 128), BF16),
            pltpu.VMEM((pairs, 8, wide), F32),
            pltpu.VMEM((pairs, 8, wide), F32),
            pltpu.VMEM((pairs, BLK, wide), F32),
        ],
        compiler_params=pltpu.CompilerParams(vmem_limit_bytes=48 * 2**20),
        cost_estimate=pl.CostEstimate(flops=10**10, bytes_accessed=10**7, transcendentals=10**7),
        name="attend",
    )(lengths, order, mine, projected, kv)


def attend_back_kernel(
    parts,
    lengths_ref,
    order_ref,
    mine_ref,
    q_ref,
    kv_ref,
    grad_ref,
    lse_ref,
    exact_ref,
    dq_ref,
    dkv_ref,
    q_s,
    g_s,
    delta_s,
    dq_s,
    dkv_s,
):
    width = KV_HEADS * HEAD

    @pl.loop(0, order_ref.shape[1])
    def _(kb):
        dkv_s[pl.ds(kb * BLK, BLK), :] = jnp.zeros((BLK, 2 * width), F32)

    for qb in range(q_ref.shape[0] // BLK):
        rows = pl.ds(qb * BLK, BLK)
        for pair in range(KV_HEADS // 2):
            q_s[pair] = head_tiles(q_ref, rows, pair, HEAD**-0.5)
            g_s[pair] = head_tiles(grad_ref, rows, pair, 1.0)
            dq_s[pair] = jnp.zeros((2 * GROUP * BLK, 128), F32)
            for i in range(2 * GROUP):
                head = pair * 2 * GROUP + i
                exact = exact_ref[rows, (head // 2) * 128 : (head // 2 + 1) * 128]
                if head % 2 != (head // GROUP) % 2:
                    exact = pltpu.roll(exact, HEAD, 1)
                product = exact * g_s[pair, i * BLK : (i + 1) * BLK, :].astype(F32)
                delta_s[pair : pair + 1, i * BLK : (i + 1) * BLK] = jnp.sum(
                    jnp.transpose(product), axis=0, keepdims=True
                )
        query_block = order_ref[0, mine_ref[0] + qb]
        first = first_row_start(lengths_ref, query_block, parts)

        @pl.loop(0, order_ref.shape[1])
        def _(kb):
            key_block = order_ref[0, kb]

            @pl.when((key_block <= query_block) & (key_block * BLK + BLK > first))
            def _():
                seen = block_visibility(lengths_ref, query_block, key_block, parts)
                key_rows = pl.ds(kb * BLK, BLK)
                for pair in range(KV_HEADS // 2):
                    key_lanes = pl.ds(pair * 128, 128)
                    value_lanes = pl.ds(width + pair * 128, 128)
                    keys = kv_ref[key_rows, key_lanes]
                    values = kv_ref[key_rows, value_lanes]
                    scores = dot(keys, q_s[pair], ((1,), (1,)))
                    scores = jnp.where(seen, scores, far_negative)
                    probs = jnp.exp(scores - lse_ref[qb, pair : pair + 1, :])
                    grad_probs = dot(values, g_s[pair], ((1,), (1,)))
                    grad_scores = (probs * (grad_probs - delta_s[pair : pair + 1, :])).astype(BF16)
                    dkv_s[key_rows, value_lanes] += dot(probs.astype(BF16), g_s[pair])
                    dkv_s[key_rows, key_lanes] += dot(grad_scores, q_s[pair])
                    dq_s[pair] += dot(grad_scores, keys, ((0,), (0,)))

        tiles = []
        for pair in range(KV_HEADS // 2):
            for i in range(2 * GROUP):
                head = pair * 2 * GROUP + i
                tile = dq_s[pair, i * BLK : (i + 1) * BLK, :] * HEAD**-0.5
                if head % 2 != (head // GROUP) % 2:
                    tile = pltpu.roll(tile, HEAD, 1)
                tiles.append(tile)
                if head % 2 == 1:
                    both = jnp.where(lane_half(tile.shape, 0), tiles[head - 1], tile)
                    dq_ref[rows, (head // 2) * 128 : (head // 2 + 1) * 128] = both.astype(BF16)

    @pl.loop(0, order_ref.shape[1])
    def _(kb):
        key_rows = pl.ds(kb * BLK, BLK)
        dkv_ref[key_rows, :] = dkv_s[key_rows, :].astype(BF16)


def attend_back(lengths, order, mine, projected, kv, grad_attended, lse, exact):
    rows = projected.shape[0]
    smem = pl.BlockSpec(memory_space=pltpu.SMEM)
    vmem = pl.BlockSpec(memory_space=pltpu.VMEM)
    wide = 2 * GROUP * BLK
    pairs = KV_HEADS // 2
    return pl.pallas_call(
        functools.partial(attend_back_kernel, lengths.shape[1]),
        out_shape=(
            jax.ShapeDtypeStruct((rows, HEADS * HEAD), BF16),
            jax.ShapeDtypeStruct(kv.shape, BF16),
        ),
        in_specs=[smem, smem, smem, vmem, vmem, vmem, vmem, vmem],
        out_specs=(vmem, vmem),
        scratch_shapes=[
            pltpu.VMEM((pairs, wide, 128), BF16),
            pltpu.VMEM((pairs, wide, 128), BF16),
            pltpu.VMEM((pairs, wide), F32),
            pltpu.VMEM((pairs, wide, 128), F32),
            pltpu.VMEM(kv.shape, F32),
        ],
        compiler_params=pltpu.CompilerParams(vmem_limit_bytes=56 * 2**20),
        cost_estimate=pl.CostEstimate(flops=10**9, bytes_accessed=10**6, transcendentals=10**5),
        name="attend_back",
    )(lengths, order, mine, projected, kv, grad_attended, lse, exact)


MESH = pl.DeviceIdType.MESH


def place(z, core, exp):
    return {"le": z, "rep": 0, "core": core, "exp": exp}


def x_of(exp):
    return (exp // 2) * 2 + 1 - exp % 2


def y_of(exp):
    return (1 - exp // 2) * 2 + exp % 2


def remote(src, dst, send_sem, recv_sem, device):
    return pltpu.make_async_remote_copy(
        src_ref=src,
        dst_ref=dst,
        send_sem=send_sem,
        recv_sem=recv_sem,
        device_id=device,
        device_id_type=MESH,
    )


def near_to_far(z):
    first_half = z < 2
    return [z, z + 1 - 2 * (z % 2), jnp.where(first_half, 3, 0), jnp.where(first_half, 2, 1)]


def between(z, zz):
    return ((z == 1) & (zz == 2)) | ((z == 2) & (zz == 1))


def meet(devices):
    barrier = pltpu.get_barrier_semaphore()
    for device in devices:
        pl.semaphore_signal(barrier, inc=1, device_id=device, device_id_type=MESH)
    pl.semaphore_wait(barrier, len(devices))


def front_kernel(
    layers,
    shard_ref,
    in_ref,
    down_ref,
    tokens_ref,
    lengths_ref,
    order_ref,
    target_ref,
    cotangent_ref,
    w_all_ref,
    w_in_ref,
    w_down_ref,
    first_ref,
    projected_ref,
    kv_ref,
    exact_ref,
    attended_ref,
    lse_ref,
    middle_ref,
    second_ref,
    gates_ref,
    slot_gates_ref,
    rows_ref,
    got_grads_ref,
    hot_s,
    grads_s,
    weights,
    kv_s,
    q_s,
    m_s,
    sum_s,
    acc_s,
    in_wide,
    down_wide,
    in_half,
    down_half,
    unit_sem,
    line_sem,
    x_sem,
    y_sem,
    far_sem,
    core_sem,
    half_sem,
    half_send,
    over_sem,
    over_send,
    kv_sem,
    kv_send,
    own_sem,
    wide_sem,
    grad_sem,
    grad_send,
):
    z, core, exp = lax.axis_index("le"), lax.axis_index("core"), lax.axis_index("exp")
    other = 1 - core
    x, y = x_of(exp), y_of(exp)
    ctx = z * 2 + core
    rows = shard_ref.shape[0]
    own_layer, mate, farthest, middle = near_to_far(z)
    order = [mate, middle, farthest, own_layer]
    wides = ((in_ref, in_wide), (down_ref, down_wide))
    halves = ((in_half, w_in_ref), (down_half, w_down_ref))

    loads = []
    for k, zz in enumerate(order):
        for a in range(2):
            load = pltpu.make_async_copy(wides[a][0].at[zz], wides[a][1].at[zz], wide_sem.at[a, k])
            load.start()
            loads.append(load)
    peers = [
        (zz, (exp + t) % 4)
        for s, zz in enumerate(order)
        for t in range(4)
        if not (s == layers - 1 and t == 0)
    ]
    meet([place(zz, core, ee) for zz, ee in peers] + [place(zz, other, exp) for zz in order])

    def number(zz, cc, ee):
        return (zz * 2 + cc) * 4 + ee

    def unit(zz, cc, ee):
        return weights.at[pl.ds(pl.multiple_of(number(zz, cc, ee) * rows, 16), rows), :]

    def send(src, who, sem, device):
        return remote(src, unit(*who), sem, unit_sem.at[number(*who)], device)

    def arrive(who):
        send(unit(*who), who, line_sem.at[0], place(z, other, exp)).wait_recv()

    started = []

    def go(copy, condition=None):
        if condition is None:
            copy.start()
        else:
            pl.when(condition)(copy.start)
        started.append((copy, condition))

    me = (z, core, exp)
    keep = pltpu.make_async_copy(shard_ref, unit(*me), own_sem.at[0])
    keep.start()
    go(send(shard_ref, me, line_sem.at[layers], place(z + 1, core, exp)), z < layers - 1)
    go(send(shard_ref, me, line_sem.at[layers + 1], place(z - 1, core, exp)), z > 0)
    go(send(shard_ref, me, x_sem.at[layers], place(z, core, x)))
    go(send(shard_ref, me, y_sem.at[layers], place(z, core, y)))
    go(send(shard_ref, me, core_sem.at[layers], place(z, other, exp)))

    slab = 16
    for k, zz in enumerate(order):
        for a in range(2):
            loads[2 * k + a].wait()
            src, dst = wides[a][1], halves[a][0]

            @pl.loop(0, src.shape[1] // slab)
            def _(i, zz=zz, src=src, dst=dst):
                at = pl.ds(pl.multiple_of(i * slab, slab), slab)
                dst[zz, at, :] = src[zz, at, :].astype(BF16)

    def half(a, source, p):
        src, dst = halves[a]
        n, cols = src.shape[1], src.shape[2] // 2
        return dst.at[pl.ds(source * n, n), pl.ds(pl.multiple_of(p * cols, 128), cols)]

    def mine(a, zz, p):
        src = halves[a][0]
        cols = src.shape[2] // 2
        return src.at[zz, :, pl.ds(pl.multiple_of(p * cols, 128), cols)]

    def layer(k):
        return jnp.where(z < layers // 2, k, layers - 1 - k)

    def ahead(zz):
        return between(z, zz)

    def hand_out(a, early):
        for s, zz in enumerate(order):
            across = ahead(zz)
            for p in range(2):
                if s == layers - 1 and p == 0:
                    continue
                pp = (core + p) % 2
                copy = remote(
                    mine(a, zz, pp),
                    half(a, ctx, pp),
                    half_send.at[a, s * 2 + p],
                    half_sem.at[a, ctx],
                    place(zz, pp, exp),
                )
                if early:
                    pl.when(across)(copy.start)
                else:
                    pl.when(~across)(copy.start)
                    started.append((copy, None))
        if not early:
            go(
                remote(
                    mine(a, z, core),
                    half(a, ctx, core),
                    over_send.at[a, 2 * layers],
                    over_sem.at[a, ctx],
                    place(z, other, exp),
                )
            )

    for k in range(layers):
        zz = layer(k)
        who = (zz, core, exp)

        @pl.when(zz != z)
        def _(who=who):
            arrive(who)

        go(send(unit(*who), who, line_sem.at[k], place(z + 1, core, exp)), (zz < z) & (z < layers - 1))
        go(send(unit(*who), who, line_sem.at[k], place(z - 1, core, exp)), (zz > z) & (z > 0))
        go(send(unit(*who), who, x_sem.at[k], place(z, core, x)), zz != z)
        go(send(unit(*who), who, y_sem.at[k], place(z, core, y)), zz != z)
        go(send(unit(*who), who, core_sem.at[k], place(z, other, exp)), zz != z)
        if k == 0:
            hand_out(0, True)

    def spread_rows(values, out):
        tile, cap = 256, out.shape[1]

        @pl.loop(0, values.shape[1] // tile)
        def _(i):
            at = pl.ds(pl.multiple_of(i * tile, tile), tile)
            spread_out = dot(hot_s[...], values[:, at]).astype(BF16)
            for e in range(out.shape[0]):
                out[e, :, at] = spread_out[e * cap : (e + 1) * cap]

    slot = lax.broadcasted_iota(jnp.int32, hot_s.shape, 0)
    takes = [slot == target_ref[k : k + 1, :] for k in range(2)]
    hot_s[...] = jnp.where(takes[0] | takes[1], 1.0, 0.0).astype(BF16)
    spread_rows(cotangent_ref, grads_s)

    for a in range(2):
        pltpu.make_async_copy(mine(a, z, core), half(a, ctx, core), own_sem.at[1 + a]).start()

    hand_out(0, False)

    for k in range(layers):
        zz = layer(k)
        from_x, from_y = (zz, core, x), (zz, core, y)
        arrive(from_x)
        go(send(unit(*from_x), from_x, core_sem.at[layers + 1 + k], place(z, other, exp)))
        if k % 2 == 0:
            go(send(unit(*from_x), from_x, far_sem.at[k], place(z, core, y)))
        arrive(from_y)
        go(send(unit(*from_y), from_y, core_sem.at[2 * layers + 1 + k], place(z, other, exp)))
        if k % 2 == 1:
            go(send(unit(*from_y), from_y, far_sem.at[k], place(z, core, x)))
    for k in range(layers):
        far = (layer(k), core, y_of(x))
        arrive(far)
        go(send(unit(*far), far, core_sem.at[3 * layers + 1 + k], place(z, other, exp)))
    for ee in range(4):
        for zz in range(layers):
            arrive((zz, other, ee))
    keep.wait()
    save = pltpu.make_async_copy(weights, w_all_ref, own_sem.at[3])
    save.start()

    depth, count = tokens_ref.shape[1], tokens_ref.shape[0]
    qkv_cols, head_cols = projected_ref.shape[1], HEADS * HEAD
    inputs = tokens_ref[...].astype(F32)
    gains = jnp.concatenate(
        [
            jnp.transpose(weights[i * 128 : (i + 1) * 128, qkv_cols : qkv_cols + AUX].astype(F32))[0:8, :]
            for i in range(depth // 128)
        ],
        axis=1,
    )
    first_ref[...] = (inputs * norm_scale(inputs) * gains[0:1, :]).astype(BF16)
    tile = 512

    @pl.loop(0, (qkv_cols - head_cols) // tile)
    def _(i):
        at = pl.ds(pl.multiple_of(head_cols + i * tile, tile), tile)
        projected_ref[:, at] = dot(first_ref[...], weights[:, at]).astype(BF16)

    def block(source):
        return kv_s.at[pl.ds(pl.multiple_of(source * count, 16), count), :]

    def share(src, source, sem, device):
        return remote(src, block(source), sem, kv_sem.at[source], device)

    own = projected_ref.at[:, pl.ds(head_cols, qkv_cols - head_cols)]
    keep_kv = pltpu.make_async_copy(own, block(ctx), own_sem.at[0])
    keep_kv.start()
    go(share(own, ctx, kv_send.at[2 * layers], place(z + 1, core, exp)), z < layers - 1)
    go(share(own, ctx, kv_send.at[2 * layers + 1], place(z - 1, core, exp)), z > 0)
    go(share(own, ctx, kv_send.at[2 * layers + 2], place(z, other, exp)))

    @pl.loop(0, head_cols // tile)
    def _(i):
        at = pl.ds(pl.multiple_of(i * tile, tile), tile)
        projected_ref[:, at] = dot(first_ref[...], weights[:, at]).astype(BF16)

    for k in range(layers):
        zz = layer(k)
        source = zz * 2 + core

        @pl.when(zz != z)
        def _(source=source):
            share(block(source), source, kv_send.at[0], place(z, other, exp)).wait_recv()

        go(share(block(source), source, kv_send.at[k], place(z + 1, core, exp)), (zz < z) & (z < layers - 1))
        go(share(block(source), source, kv_send.at[k], place(z - 1, core, exp)), (zz > z) & (z > 0))
        go(share(block(source), source, kv_send.at[layers + k], place(z, other, exp)), zz != z)

    hand_out(1, True)
    hand_out(1, False)

    me_slot = exp * layers + z
    keep_grads = pltpu.make_async_copy(grads_s.at[me_slot], got_grads_ref.at[me_slot], own_sem.at[4])
    keep_grads.start()
    for k, (zz, ee) in enumerate(peers):
        there = ee * layers + zz
        go(
            remote(
                grads_s.at[there],
                got_grads_ref.at[me_slot],
                grad_send.at[k],
                grad_sem.at[me_slot],
                place(zz, core, ee),
            )
        )

    def pass_over(a):
        for s, zz in enumerate(order[::-1]):
            for p in range(2):
                if s == 0 and p == 0:
                    continue
                source = zz * 2 + (core + p) % 2
                remote(
                    half(a, source, core),
                    half(a, source, core),
                    half_send.at[a, 0],
                    half_sem.at[a, source],
                    place(z, other, exp),
                ).wait_recv()
                go(
                    remote(
                        half(a, source, core),
                        half(a, source, core),
                        over_send.at[a, s * 2 + p],
                        over_sem.at[a, source],
                        place(z, other, exp),
                    )
                )

    pass_over(0)
    for zz in range(layers):
        source = zz * 2 + other
        share(block(source), source, kv_send.at[0], place(z, other, exp)).wait_recv()
    keep_kv.wait()
    save_kv = pltpu.make_async_copy(kv_s, kv_ref, own_sem.at[0])
    save_kv.start()

    attend_blocks(
        lengths_ref.shape[1],
        False,
        lengths_ref,
        order_ref,
        ctx * (count // BLK),
        projected_ref,
        kv_s,
        exact_ref,
        attended_ref,
        lse_ref,
        q_s,
        m_s,
        sum_s,
        acc_s,
    )
    tile = 256

    @pl.loop(0, depth // tile)
    def _(i):
        at = pl.ds(pl.multiple_of(i * tile, tile), tile)
        w_at = pl.ds(pl.multiple_of(qkv_cols + AUX + i * tile, 128), tile)
        middle_ref[:, at] = tokens_ref[:, at].astype(F32) + dot(attended_ref[...], weights[:, w_at])

    middle = middle_ref[...]
    second_ref[...] = (middle * norm_scale(middle) * gains[1:2, :]).astype(BF16)
    logits = dot(second_ref[...], weights[:, qkv_cols : qkv_cols + AUX])
    lane = lax.broadcasted_iota(jnp.int32, logits.shape, 1)
    token = lax.broadcasted_iota(jnp.int32, (count, count), 0)
    eye = token == lax.broadcasted_iota(jnp.int32, (count, count), 1)
    chosen = []
    for k in range(2):
        line = target_ref[2 + k : 3 + k, :].astype(F32)
        expert = jnp.sum(jnp.where(eye, line, 0.0), axis=1, keepdims=True)
        chosen.append(jnp.sum(jnp.where(lane.astype(F32) == expert + 2.0, logits, 0.0), axis=1, keepdims=True))
    largest = jnp.maximum(chosen[0], chosen[1])
    exps = [jnp.exp(value - largest) for value in chosen]
    total = exps[0] + exps[1]
    gates = [value / total for value in exps]
    gates_ref[...] = jnp.where(lane == 0, gates[0], jnp.where(lane == 1, gates[1], 0.0))
    spread_rows(second_ref, rows_ref)
    slot = lax.broadcasted_iota(jnp.int32, hot_s.shape, 0)
    by_slot = jnp.zeros(hot_s.shape, F32)
    for k in range(2):
        line = jnp.sum(jnp.where(eye, gates[k], 0.0), axis=0, keepdims=True)
        by_slot = by_slot + jnp.where(slot == target_ref[k : k + 1, :], line, 0.0)
    by_slot = jnp.sum(by_slot, axis=1, keepdims=True)
    cap = rows_ref.shape[1]
    eye = lax.broadcasted_iota(jnp.int32, (cap, 128), 0) == lax.broadcasted_iota(jnp.int32, (cap, 128), 1)
    for e in range(rows_ref.shape[0]):
        line = jnp.sum(jnp.where(eye, by_slot[e * cap : (e + 1) * cap], 0.0), axis=0, keepdims=True)
        slot_gates_ref[e] = jnp.broadcast_to(line, (8, 128))

    pass_over(1)
    for source in range(2 * layers):
        for a in range(2):
            remote(
                half(a, source, other),
                half(a, source, other),
                half_send.at[a, 0],
                over_sem.at[a, source],
                place(z, other, exp),
            ).wait_recv()
    for zz, ee in peers:
        source = ee * layers + zz
        remote(
            got_grads_ref.at[source],
            got_grads_ref.at[source],
            grad_send.at[0],
            grad_sem.at[source],
            place(zz, core, ee),
        ).wait_recv()
    keep_grads.wait()
    save_kv.wait()
    save.wait()
    for a in range(2):
        pltpu.make_async_copy(mine(a, z, core), half(a, ctx, core), own_sem.at[1 + a]).wait()
    for copy, condition in started:
        if condition is None:
            copy.wait_send()
        else:
            pl.when(condition)(copy.wait_send)


def front(shard, expert_in, expert_out, tokens, lengths, block_order, target, cotangent, qkv_cols):
    layers = expert_in.shape[0]
    rows_in, rows_out = expert_in.shape[1], expert_out.shape[1]
    depth, cols = shard.shape[0] * 8 * layers, shard.shape[1]
    count = tokens.shape[0]
    kv_shape = (count * 2 * layers, qkv_cols - HEADS * HEAD)
    wide, pairs = 2 * GROUP * BLK, KV_HEADS // 2
    slots = (EXPERTS, CAP, depth)
    any_space = pl.BlockSpec(memory_space=pl.ANY)
    smem = pl.BlockSpec(memory_space=pltpu.SMEM)
    vmem = pl.BlockSpec(memory_space=pltpu.VMEM)
    dma = pltpu.SemaphoreType.DMA
    return pl.pallas_call(
        functools.partial(front_kernel, layers),
        out_shape=(
            jax.ShapeDtypeStruct((depth, cols), BF16),
            jax.ShapeDtypeStruct((rows_in * 2 * layers, expert_in.shape[2]), BF16),
            jax.ShapeDtypeStruct((rows_out * 2 * layers, expert_out.shape[2]), BF16),
            jax.ShapeDtypeStruct((count, depth), BF16),
            jax.ShapeDtypeStruct((count, qkv_cols), BF16),
            jax.ShapeDtypeStruct(kv_shape, BF16),
            jax.ShapeDtypeStruct((count, HEADS * HEAD), F32),
            jax.ShapeDtypeStruct((count, HEADS * HEAD), BF16),
            jax.ShapeDtypeStruct((count // BLK, pairs, wide), F32),
            jax.ShapeDtypeStruct((count, depth), F32),
            jax.ShapeDtypeStruct((count, depth), BF16),
            jax.ShapeDtypeStruct((count, AUX), F32),
            jax.ShapeDtypeStruct((EXPERTS, 8, 128), F32),
            jax.ShapeDtypeStruct(slots, BF16),
            jax.ShapeDtypeStruct(slots, BF16),
        ),
        in_specs=[any_space] * 3 + [vmem, smem, smem, vmem, vmem],
        out_specs=(any_space,) * 3 + (vmem, vmem, any_space) + (vmem,) * 8 + (any_space,),
        scratch_shapes=[
            pltpu.VMEM((EXPERTS * CAP, count), BF16),
            pltpu.VMEM(slots, BF16),
            pltpu.VMEM((depth, cols), BF16),
            pltpu.VMEM(kv_shape, BF16),
            pltpu.VMEM((pairs, wide, 128), BF16),
            pltpu.VMEM((pairs, 8, wide), F32),
            pltpu.VMEM((pairs, 8, wide), F32),
            pltpu.VMEM((pairs, BLK, wide), F32),
            pltpu.VMEM(expert_in.shape, F32),
            pltpu.VMEM(expert_out.shape, F32),
            pltpu.VMEM(expert_in.shape, BF16),
            pltpu.VMEM(expert_out.shape, BF16),
            dma((8 * layers,)),
            dma((layers + 2,)),
            dma((layers + 1,)),
            dma((layers + 1,)),
            dma((layers,)),
            dma((4 * layers + 1,)),
            dma((2, 2 * layers)),
            dma((2, 2 * layers)),
            dma((2, 2 * layers)),
            dma((2, 2 * layers + 1)),
            dma((2 * layers,)),
            dma((2 * layers + 3,)),
            dma((5,)),
            dma((2, layers)),
            dma((4 * layers,)),
            dma((4 * layers,)),
        ],
        compiler_params=pltpu.CompilerParams(
            collective_id=0, has_side_effects=True, vmem_limit_bytes=60 * 2**20
        ),
        name="front",
    )(shard, expert_in, expert_out, tokens, lengths, block_order, target, cotangent)


def experts_kernel(
    layers,
    rows_ref,
    gates_ref,
    grads_ref,
    w_in_ref,
    w_down_ref,
    out_ref,
    back_ref,
    back_gates_ref,
    d_in_ref,
    d_down_ref,
    w_in,
    w_down,
    got,
    got_gates,
    x_s,
    grad_s,
    hidden_s,
    inner_s,
    back_s,
    back_gates_s,
    other_in,
    other_down,
    pair_in,
    pair_down,
    row_sem,
    row_send,
    gate_sem,
    gate_send,
    back_sem,
    back_send,
    back_gate_sem,
    back_gate_send,
    pair_sem,
    pair_send,
    load_sem,
):
    z, core, exp = lax.axis_index("le"), lax.axis_index("core"), lax.axis_index("exp")
    other = 1 - core
    columns = rows_ref.shape[0] // layers
    me = exp * layers + z
    cap, depth = rows_ref.shape[1], rows_ref.shape[2]
    chunk = columns * cap
    loads = [
        pltpu.make_async_copy(w_in_ref, w_in, load_sem.at[0]),
        pltpu.make_async_copy(w_down_ref, w_down, load_sem.at[1]),
    ]
    for load in loads:
        load.start()
    own_layer, mate, farthest, middle = near_to_far(z)
    peers = [
        (zz, (exp + t) % columns)
        for s, zz in enumerate([mate, farthest, middle, own_layer])
        for t in range(columns)
        if not (s == layers - 1 and t == 0)
    ]
    meet([place(zz, core, ee) for zz, ee in peers] + [place(z, other, exp)])

    started = []

    def go(copy):
        copy.start()
        started.append(copy)

    keeps = [
        pltpu.make_async_copy(rows_ref.at[me], got.at[me], load_sem.at[2]),
        pltpu.make_async_copy(gates_ref.at[me], got_gates.at[me], load_sem.at[3]),
    ]
    for keep in keeps:
        keep.start()
    for k, (zz, ee) in enumerate(peers):
        there = ee * layers + zz
        go(remote(gates_ref.at[there], got_gates.at[me], gate_send.at[k], gate_sem.at[me], place(zz, core, ee)))
        go(remote(rows_ref.at[there], got.at[me], row_send.at[k], row_sem.at[me], place(zz, core, ee)))
    for load in loads + keeps:
        load.wait()

    eye = lax.broadcasted_iota(jnp.int32, (cap, 128), 0) == lax.broadcasted_iota(jnp.int32, (cap, 128), 1)
    tile = 256

    def tiles(i):
        return pl.ds(pl.multiple_of(i * tile, tile), tile)

    for k, zz in enumerate([own_layer, mate, farthest, middle]):
        rows = pl.ds(k * chunk, chunk)
        for ee in range(columns):
            source = ee * layers + zz

            @pl.when(source != me)
            def _(source=source):
                here = place(z, other, exp)
                remote(got.at[source], got.at[source], row_send.at[0], row_sem.at[source], here).wait_recv()
                remote(
                    got_gates.at[source], got_gates.at[source], gate_send.at[0], gate_sem.at[source], here
                ).wait_recv()

            at = pl.ds(k * chunk + ee * cap, cap)
            x_s[at, :] = got[source]
            gate = jnp.sum(jnp.where(eye, got_gates[source, 0:1, :], 0.0), axis=1, keepdims=True)
            grad_s[at, :] = (gate * grads_ref[source].astype(F32)).astype(BF16)

        @pl.loop(0, FF // tile)
        def _(i, rows=rows):
            up_at = pl.ds(pl.multiple_of(FF + i * tile, tile), tile)
            gate = dot(x_s[rows, :], w_in[:, tiles(i)])
            up = dot(x_s[rows, :], w_in[:, up_at])
            grad_hidden = dot(grad_s[rows, :], w_down[tiles(i), :], ((1,), (1,)))
            sigmoid = jax.nn.sigmoid(gate)
            silu = gate * sigmoid
            hidden_s[rows, tiles(i)] = (silu * up).astype(BF16)
            inner_s[rows, tiles(i)] = (grad_hidden * up * sigmoid * (1.0 + gate * (1.0 - sigmoid))).astype(BF16)
            inner_s[rows, up_at] = (grad_hidden * silu).astype(BF16)

        @pl.loop(0, depth // tile)
        def _(i, rows=rows, zz=zz):
            back = dot(inner_s[rows, :], w_in[tiles(i), :], ((1,), (1,))).astype(BF16)
            for ee in range(columns):
                back_s[ee * layers + zz, :, tiles(i)] = back[ee * cap : (ee + 1) * cap]

        @pl.loop(0, depth // tile, init_carry=jnp.zeros((chunk, 128), F32))
        def gate_grads(i, sums, rows=rows, zz=zz):
            result = dot(hidden_s[rows, :], w_down[:, tiles(i)]).astype(BF16)
            parts = []
            for ee in range(columns):
                part = result[ee * cap : (ee + 1) * cap]
                out_ref[ee * layers + zz, :, tiles(i)] = part
                parts.append(part.astype(F32) * grads_ref[ee * layers + zz, :, tiles(i)].astype(F32))
            product = jnp.concatenate(parts, axis=0)
            return sums + product[:, :128] + product[:, 128:]

        gate_grads = jnp.sum(gate_grads, axis=1, keepdims=True)
        for ee in range(columns):
            there = ee * layers + zz
            column = gate_grads[ee * cap : (ee + 1) * cap]
            line = jnp.sum(jnp.where(eye, column, 0.0), axis=0, keepdims=True)
            back_gates_s[there] = jnp.broadcast_to(line, (8, 128))
            row_copy = remote(
                back_s.at[there],
                back_ref.at[me],
                back_send.at[there],
                back_sem.at[me],
                place(zz, core, ee),
            )
            gate_copy = remote(
                back_gates_s.at[there],
                back_gates_ref.at[me],
                back_gate_send.at[there],
                back_gate_sem.at[me],
                place(zz, core, ee),
            )

            @pl.when(there != me)
            def _(row_copy=row_copy, gate_copy=gate_copy):
                row_copy.start()
                gate_copy.start()

    own = [
        pltpu.make_async_copy(back_s.at[me], back_ref.at[me], load_sem.at[2]),
        pltpu.make_async_copy(back_gates_s.at[me], back_gates_ref.at[me], load_sem.at[3]),
    ]
    for copy in own:
        copy.start()

    half_in, half_down = d_in_ref.shape[1], d_down_ref.shape[1]

    def in_part(i, p):
        cols = pl.ds(pl.multiple_of(p * half_in, 128), half_in)
        return dot(x_s[:, tiles(i)], inner_s[:, cols], ((0,), (0,)))

    def down_part(i, p):
        cols = pl.ds(pl.multiple_of(p * half_down, 128), half_down)
        return dot(hidden_s[:, tiles(i)], grad_s[:, cols], ((0,), (0,)))

    @pl.loop(0, depth // tile)
    def _(i):
        other_in[tiles(i), :] = in_part(i, other).astype(BF16)

    go(remote(other_in, pair_in, pair_send.at[0], pair_sem.at[0], place(z, other, exp)))

    @pl.loop(0, FF // tile)
    def _(i):
        other_down[tiles(i), :] = down_part(i, other).astype(BF16)

    go(remote(other_down, pair_down, pair_send.at[1], pair_sem.at[1], place(z, other, exp)))
    remote(other_in, pair_in, pair_send.at[0], pair_sem.at[0], place(z, other, exp)).wait_recv()

    @pl.loop(0, depth // tile)
    def _(i):
        d_in_ref[tiles(i), :] = (in_part(i, core) + pair_in[tiles(i), :].astype(F32)).astype(BF16)

    remote(other_down, pair_down, pair_send.at[1], pair_sem.at[1], place(z, other, exp)).wait_recv()

    @pl.loop(0, FF // tile)
    def _(i):
        d_down_ref[tiles(i), :] = (down_part(i, core) + pair_down[tiles(i), :].astype(F32)).astype(BF16)

    for copy in own:
        copy.wait()
    for k, (zz, ee) in enumerate(peers):
        there = ee * layers + zz
        row_copy = remote(
            back_s.at[there], back_ref.at[there], back_send.at[there], back_sem.at[there], place(zz, core, ee)
        )
        gate_copy = remote(
            back_gates_s.at[there],
            back_gates_ref.at[there],
            back_gate_send.at[there],
            back_gate_sem.at[there],
            place(zz, core, ee),
        )
        row_copy.wait()
        gate_copy.wait()
    for copy in started:
        copy.wait_send()


def experts(rows, gates, grads, w_in, w_down, layers):
    count, cap, depth = rows.shape
    any_space = pl.BlockSpec(memory_space=pl.ANY)
    vmem = pl.BlockSpec(memory_space=pltpu.VMEM)
    dma = pltpu.SemaphoreType.DMA
    half_in = jax.ShapeDtypeStruct((depth, FF), BF16)
    half_down = jax.ShapeDtypeStruct((FF, depth // 2), BF16)
    return pl.pallas_call(
        functools.partial(experts_kernel, layers),
        out_shape=(
            jax.ShapeDtypeStruct(rows.shape, BF16),
            jax.ShapeDtypeStruct(rows.shape, BF16),
            jax.ShapeDtypeStruct(gates.shape, F32),
            half_in,
            half_down,
        ),
        in_specs=[any_space, any_space, vmem, any_space, any_space],
        out_specs=(vmem, any_space, any_space, vmem, vmem),
        scratch_shapes=[
            pltpu.VMEM(w_in.shape, BF16),
            pltpu.VMEM(w_down.shape, BF16),
            pltpu.VMEM(rows.shape, BF16),
            pltpu.VMEM(gates.shape, F32),
            pltpu.VMEM((count * cap, depth), BF16),
            pltpu.VMEM((count * cap, depth), BF16),
            pltpu.VMEM((count * cap, FF), BF16),
            pltpu.VMEM((count * cap, 2 * FF), BF16),
            pltpu.VMEM(rows.shape, BF16),
            pltpu.VMEM(gates.shape, F32),
            pltpu.VMEM(half_in.shape, BF16),
            pltpu.VMEM(half_down.shape, BF16),
            pltpu.VMEM(half_in.shape, BF16),
            pltpu.VMEM(half_down.shape, BF16),
        ]
        + [dma((count,))] * 8
        + [dma((2,)), dma((2,)), dma((4,))],
        compiler_params=pltpu.CompilerParams(
            collective_id=2, has_side_effects=True, vmem_limit_bytes=60 * 2**20
        ),
        name="experts",
    )(rows, gates, grads, w_in, w_down)


def add_rows(total, part, rows):
    slab = 16

    @pl.loop(0, rows // slab)
    def _(i):
        at = pl.ds(pl.multiple_of(i * slab, slab), slab)
        total[at, :] = (total[at, :].astype(F32) + part[at, :].astype(F32)).astype(BF16)


class Chain:
    def __init__(self, layers, z, above, below, own, rows, up, down, sems, sends):
        self.layers, self.z, self.above, self.below = layers, z, above, below
        self.own, self.rows, self.up, self.down = own, rows, up, down
        self.sems, self.sends = sems, sends
        self.parts = sems.shape[2]
        self.width = up.shape[2] // self.parts

    def columns(self, ref, h):
        return ref.at[:, pl.ds(h * self.width, self.width)]

    def rise(self, d, h):
        return remote(
            self.columns(self.own(d), h),
            self.columns(self.up.at[d], h),
            self.sends.at[0, d, h],
            self.sems.at[0, d, h],
            self.above,
        )

    def fall(self, d, h):
        return remote(
            self.columns(self.own(d), h),
            self.columns(self.down.at[d], h),
            self.sends.at[1, d, h],
            self.sems.at[1, d, h],
            self.below,
        )

    def end(self, step):
        for h in range(self.parts):
            pl.when(self.z == 0)(self.rise(self.layers - 1 - step, h).start)
            pl.when(self.z == self.layers - 1)(self.fall(step, h).start)

    def ends(self):
        for step in range(self.layers - 1):
            self.end(step)

    def add(self, d, h, buffer):
        add_rows(self.columns(self.own(d), h), self.columns(buffer.at[d], h), self.rows)

    def middle(self):
        z, last = self.z, self.layers - 1

        def pass_on(make, d, buffer):
            for h in range(self.parts):
                copy = make(d, h)
                copy.wait_recv()
                self.add(d, h, buffer)
                copy.start()

        def both(first_half):
            for step in range(last):
                high, low = last - step, step

                def upward(high=high):
                    pl.when((z > 0) & (z < high))(lambda: pass_on(self.rise, high, self.up))

                def downward(low=low):
                    pl.when((z < last) & (z > low))(lambda: pass_on(self.fall, low, self.down))

                for turn in (upward, downward) if first_half else (downward, upward):
                    turn()

        pl.when(z <= last // 2)(lambda: both(True))
        pl.when(z > last // 2)(lambda: both(False))

    def finish(self):
        z, last = self.z, self.layers - 1

        def take(make, buffer):
            for h in range(self.parts):
                make(z, h).wait_recv()
                self.add(z, h, buffer)

        pl.when(z > 0)(lambda: take(self.rise, self.up))
        pl.when(z < last)(lambda: take(self.fall, self.down))

    def wait_sends(self):
        for d in range(self.layers):
            for h in range(self.parts):
                pl.when(self.z < d)(self.rise(d, h).wait_send)
                pl.when(self.z > d)(self.fall(d, h).wait_send)


def finish_kernel(
    layers,
    grad_kv_ref,
    grad_q_ref,
    first_ref,
    tokens_ref,
    gain_ref,
    middle_ref,
    w_all_ref,
    attended_ref,
    second_ref,
    logits_ref,
    gain_moe_ref,
    base_ref,
    returned_ref,
    picks_ref,
    gates_ref,
    in_ref,
    down_ref,
    block_ref,
    d_tokens_ref,
    d_qkv_ref,
    d_out_ref,
    d_aux_ref,
    got_in_ref,
    got_down_ref,
    weights,
    projected,
    grad_first,
    kv_own,
    kv_pair,
    kv_up,
    kv_down,
    late_both,
    late_pair,
    late_near,
    late_up,
    late_down,
    q_both,
    q_pair,
    q_near,
    q_up,
    q_down,
    k_both,
    k_pair,
    k_near,
    k_up,
    k_down,
    load_sem,
    kv_pair_sem,
    kv_pair_send,
    kv_sem,
    kv_send,
    half_sem,
    half_send,
    pair_sem,
    pair_send,
    near_sem,
    near_send,
    line_sem,
    line_send,
):
    z, core, exp = lax.axis_index("le"), lax.axis_index("core"), lax.axis_index("exp")
    other = 1 - core
    partner = place(z, other, exp)
    above, below = place(z + 1, core, exp), place(z - 1, core, exp)
    x, y = x_of(exp), y_of(exp)
    mates = (x, y, y_of(x))
    own_layer, mate, farthest, middle = near_to_far(z)
    ctx = z * 2 + core
    rows = d_qkv_ref.shape[0]
    count = tokens_ref.shape[0]
    head_cols = HEADS * HEAD
    qkv_cols = d_qkv_ref.shape[1]
    kv_cols = qkv_cols - head_cols

    loads = []

    def load(src, dst):
        copy = pltpu.make_async_copy(src, dst, load_sem.at[len(loads)])
        copy.start()
        loads.append(copy)
        return copy

    kv_loads = [
        load(grad_kv_ref.at[pl.ds(pl.multiple_of((d * 2 + core) * count, 16), count), :], kv_own.at[d])
        for d in range(layers)
    ]
    depth = w_all_ref.shape[0]

    def weights_part(i):
        part = w_all_ref.at[pl.ds(i * depth // 2, depth // 2), pl.ds(0, qkv_cols)]
        return pltpu.make_async_copy(part, weights, load_sem.at[2 * layers + 2])

    weights_part(0).start()
    meet(
        [
            place((z + s) % layers, (core + p) % 2, exp)
            for s in range(layers)
            for p in range(2)
            if s + p > 0
        ]
        + [place(z, core, mate) for mate in mates]
    )
    started = []

    def go(copy):
        copy.start()
        started.append(copy)

    arrays = ((in_ref, got_in_ref), (down_ref, got_down_ref))

    def mine(a, owner):
        n = arrays[a][1].shape[1]
        return arrays[a][0].at[pl.ds(owner * n, n), :]

    def half(a, expert, p):
        cols = arrays[a][0].shape[1]
        return arrays[a][1].at[expert, :, pl.ds(pl.multiple_of(p * cols, 128), cols)]

    for a in range(2):
        load(mine(a, ctx), half(a, z, core))

    def hand_back(a, early):
        for s, zz in enumerate([mate, farthest, middle, own_layer]):
            across = between(z, zz)
            for p in range(2):
                if s == layers - 1 and p == 0:
                    continue
                pp = (core + p) % 2
                copy = remote(
                    mine(a, zz * 2 + pp),
                    half(a, z, core),
                    half_send.at[a, s * 2 + p],
                    half_sem.at[a, ctx],
                    place(zz, pp, exp),
                )
                if early:
                    pl.when(across)(copy.start)
                else:
                    pl.when(~across)(copy.start)
                    started.append(copy)

    hand_back(0, True)

    for d in range(layers):
        go(
            remote(
                grad_kv_ref.at[pl.ds(pl.multiple_of((d * 2 + other) * count, 16), count), :],
                kv_pair.at[d],
                kv_pair_send.at[d],
                kv_pair_sem.at[d],
                partner,
            )
        )
    kv_line = Chain(
        layers, z, above, below, lambda d: kv_own.at[d], count, kv_up, kv_down, kv_sem, kv_send
    )
    for copy in kv_loads:
        copy.wait()
    for k in range(layers):
        d = jnp.where(z < layers // 2, layers - 1 - k, k)
        remote(kv_pair.at[d], kv_pair.at[d], kv_pair_send.at[d], kv_pair_sem.at[d], partner).wait_recv()
        add_rows(kv_own.at[d], kv_pair.at[d], count)
        if k < layers - 1:
            kv_line.end(k)

    def near_copy(i, near, own, d, m, target):
        return remote(
            own.at[d, pl.ds(pl.multiple_of(target * rows, 16), rows), :],
            near.at[m, d],
            near_send.at[i, m, d],
            near_sem.at[i, m, d],
            place(z, core, mates[m]),
        )

    def pair_sums(i, own, pair, near):
        for d in range(layers):
            remote(pair.at[d], pair.at[d], pair_send.at[i, d], pair_sem.at[i, d], partner).wait_recv()
            add_rows(own.at[d], pair.at[d], 4 * rows)
            for m in range(3):
                go(near_copy(i, near, own, d, m, mates[m]))

    def near_sums(i, own, near):
        for d in range(layers):
            for m in range(3):
                near_copy(i, near, own, d, m, exp).wait_recv()
            mine = own.at[d, pl.ds(pl.multiple_of(exp * rows, 16), rows), :]

            @pl.loop(0, rows // 16)
            def _(r, mine=mine, d=d):
                at = pl.ds(pl.multiple_of(r * 16, 16), 16)
                total = mine[at, :].astype(F32)
                for m in range(3):
                    total = total + near[m, d, at, :].astype(F32)
                mine[at, :] = total.astype(BF16)

    def line_of(i, own, up, down):
        return Chain(
            layers,
            z,
            above,
            below,
            lambda d: own.at[d, pl.ds(pl.multiple_of(exp * rows, 16), rows), :],
            rows,
            up,
            down,
            line_sem.at[i],
            line_send.at[i],
        )

    def outer_product(both, cols, left, right, gains=None):
        for d in range(layers):
            block = left[:, d * 8 * rows : (d + 1) * 8 * rows]
            part = dot(block, right, ((0,), (0,)))
            if gains is not None:
                turned = [
                    jnp.transpose(jnp.broadcast_to(gains[:, at : at + 128], (128, 128)))
                    for at in range(d * 8 * rows, (d + 1) * 8 * rows, 128)
                ]
                lane = lax.broadcasted_iota(jnp.int32, part.shape, 1)
                part = jnp.where(lane == 0, jnp.concatenate(turned, axis=0), part)
            part = part.astype(BF16)
            both[0, d, :, cols] = part[: 4 * rows]
            both[1, d, :, cols] = part[4 * rows :]

    def pair_up(i, both, pair):
        for d in range(layers):
            go(remote(both.at[other, d], pair.at[d], pair_send.at[i, d], pair_sem.at[i, d], partner))

    outer_product(q_both, slice(0, head_cols), first_ref, grad_q_ref[...])
    pair_up(1, q_both, q_pair)
    width = middle_ref.shape[1]
    outer_product(late_both, slice(0, width), attended_ref, middle_ref[...].astype(BF16))
    outer_product(late_both, slice(width, width + AUX), second_ref, logits_ref[...], gain_moe_ref[...])
    pair_up(0, late_both, late_pair)
    late_own = late_both.at[core]
    q_own = q_both.at[core]
    pair_sums(1, q_own, q_pair, q_near)
    pair_sums(0, late_own, late_pair, late_near)
    kv_line.middle()
    hand_back(0, False)
    hand_back(1, True)
    hand_back(1, False)
    kv_line.finish()

    projected[:, :head_cols] = grad_q_ref[...]
    projected[:, head_cols:] = kv_own[z]
    outer_product(k_both, slice(0, kv_cols), first_ref, projected[:, head_cols:])
    tile = 256
    for i in range(2):
        weights_part(i).wait()

        @pl.loop(0, depth // 2 // tile)
        def _(j, i=i):
            at = pl.ds(pl.multiple_of(j * tile, tile), tile)
            to = pl.ds(pl.multiple_of(i * depth // 2 + j * tile, tile), tile)
            grad_first[:, to] = dot(projected[...], weights[at, :], ((1,), (1,)))

        if i == 0:
            weights_part(1).start()

    inputs = tokens_ref[...].astype(F32)
    scale = norm_scale(inputs)
    norm = inputs * scale
    grad = grad_first[...]
    grad_gain = jnp.sum(grad * norm, axis=0, keepdims=True)
    for d in range(layers):
        block = jnp.concatenate(
            [
                jnp.transpose(jnp.broadcast_to(grad_gain[:, at : at + 128], (128, 128)))
                for at in range(d * 8 * rows, (d + 1) * 8 * rows, 128)
            ],
            axis=0,
        ).astype(BF16)
        k_both[0, d, :, kv_cols:] = block[: 4 * rows]
        k_both[1, d, :, kv_cols:] = block[4 * rows :]
    pair_up(2, k_both, k_pair)
    grad = grad * gain_ref[...]
    d_tokens_ref[...] = (
        middle_ref[...] + scale * (grad - norm * jnp.mean(grad * norm, axis=-1, keepdims=True))
    ).astype(BF16)
    k_own = k_both.at[core]
    pair_sums(2, k_own, k_pair, k_near)

    @pl.loop(0, depth // tile)
    def _(i):
        at = pl.ds(pl.multiple_of(i * tile, tile), tile)
        total = base_ref[:, at]
        for k in range(2):
            total = total + gates_ref[:, k : k + 1] * dot(picks_ref[k], returned_ref[:, at])
        block_ref[:, at] = total.astype(BF16)

    late_line = line_of(0, late_own, late_up, late_down)
    q_line = line_of(1, q_own, q_up, q_down)
    k_line = line_of(2, k_own, k_up, k_down)
    near_sums(1, q_own, q_near)
    q_line.ends()
    near_sums(0, late_own, late_near)
    late_line.ends()
    q_line.middle()
    near_sums(2, k_own, k_near)
    k_line.ends()
    late_line.middle()
    k_line.middle()
    mine_rows = pl.ds(pl.multiple_of(exp * rows, 16), rows)
    q_line.finish()
    d_qkv_ref[:, :head_cols] = q_both[core, z, mine_rows, :].astype(F32)
    late_line.finish()
    last = late_both[core, z, mine_rows, :].astype(F32)
    d_out_ref[...] = last[:, :width]
    d_aux_ref[:, AUX:] = last[:, width:]
    k_line.finish()
    last = k_both[core, z, mine_rows, :].astype(F32)
    d_qkv_ref[:, head_cols:] = last[:, :kv_cols]
    d_aux_ref[:, :AUX] = last[:, kv_cols:]

    for source in range(2 * layers):
        for a in range(2):

            @pl.when(source != ctx)
            def _(source=source, a=a):
                remote(
                    half(a, source // 2, source % 2),
                    half(a, source // 2, source % 2),
                    half_send.at[a, 0],
                    half_sem.at[a, source],
                    partner,
                ).wait_recv()

    for copy in loads[-2:]:
        copy.wait()
    for line in (kv_line, late_line, q_line, k_line):
        line.wait_sends()
    for copy in started:
        copy.wait_send()


def finish(
    grad_kv,
    grad_q,
    first,
    tokens,
    gain,
    middle,
    w_all,
    attended,
    second,
    grad_logits,
    gain_moe,
    base,
    returned,
    picks,
    gates,
    grad_in,
    grad_down,
    layers,
):
    depth, count = first.shape[1], first.shape[0]
    rows = depth // (8 * layers)
    qkv_cols = grad_q.shape[1] + grad_kv.shape[1]
    n_in, n_down = grad_in.shape[0] // (2 * layers), grad_down.shape[0] // (2 * layers)
    any_space = pl.BlockSpec(memory_space=pl.ANY)
    vmem = pl.BlockSpec(memory_space=pltpu.VMEM)
    dma = pltpu.SemaphoreType.DMA

    def sums(cols):
        return [
            pltpu.VMEM((2, layers, 4 * rows, cols), BF16),
            pltpu.VMEM((layers, 4 * rows, cols), BF16),
            pltpu.VMEM((3, layers, rows, cols), BF16),
            pltpu.VMEM((layers, rows, cols), BF16),
            pltpu.VMEM((layers, rows, cols), BF16),
        ]

    return pl.pallas_call(
        functools.partial(finish_kernel, layers),
        out_shape=(
            jax.ShapeDtypeStruct((count, depth), BF16),
            jax.ShapeDtypeStruct((count, depth), BF16),
            jax.ShapeDtypeStruct((rows, qkv_cols), F32),
            jax.ShapeDtypeStruct((rows, depth), F32),
            jax.ShapeDtypeStruct((rows, 2 * AUX), F32),
            jax.ShapeDtypeStruct((layers, n_in, 2 * grad_in.shape[1]), BF16),
            jax.ShapeDtypeStruct((layers, n_down, 2 * grad_down.shape[1]), BF16),
        ),
        in_specs=[any_space] + [vmem] * 5 + [any_space] + [vmem] * 8 + [any_space] * 2,
        out_specs=(vmem,) * 5 + (any_space,) * 2,
        scratch_shapes=[
            pltpu.VMEM((depth // 2, qkv_cols), BF16),
            pltpu.VMEM((count, qkv_cols), BF16),
            pltpu.VMEM((count, depth), F32),
        ]
        + [pltpu.VMEM((layers, count, grad_kv.shape[1]), BF16)] * 4
        + sums(depth + AUX)
        + sums(grad_q.shape[1])
        + sums(grad_kv.shape[1] + AUX)
        + [
            dma((2 * layers + 3,)),
            dma((layers,)),
            dma((layers,)),
            dma((2, layers, 2)),
            dma((2, layers, 2)),
            dma((2, 2 * layers)),
            dma((2, 2 * layers)),
            dma((3, layers)),
            dma((3, layers)),
            dma((3, 3, layers)),
            dma((3, 3, layers)),
            dma((3, 2, layers, 1)),
            dma((3, 2, layers, 1)),
        ],
        compiler_params=pltpu.CompilerParams(
            collective_id=1, has_side_effects=True, vmem_limit_bytes=60 * 2**20
        ),
        name="finish",
    )(
        grad_kv,
        grad_q,
        first,
        tokens,
        gain,
        middle,
        w_all,
        attended,
        second,
        grad_logits,
        gain_moe,
        base,
        returned,
        picks,
        gates,
        grad_in,
        grad_down,
    )


def settle_kernel(count, aux_ref, *refs):
    for src, dst in zip(refs[:count], refs[count : 2 * count]):
        dst[...] = src[...].astype(dst.dtype)
    rows = aux_ref.shape[0]
    eye = lax.broadcasted_iota(jnp.int32, (rows, 128), 0) == lax.broadcasted_iota(jnp.int32, (rows, 128), 1)
    for at, dst in zip((0, AUX), refs[2 * count :]):
        line = jnp.sum(jnp.where(eye, aux_ref[:, at : at + 1], 0.0), axis=0, keepdims=True)
        dst[...] = line[:, :rows]
    block = jnp.concatenate([aux_ref[:, AUX:], jnp.zeros((128 - rows, AUX), F32)], axis=0)
    refs[-1][...] = jnp.transpose(block)[1 : 1 + EXPERTS, :rows]


def settle(aux, arrays, steps):
    def spec(array):
        if array.ndim == 2 and array.shape[0] % (16 * steps) == 0:
            return pl.BlockSpec((array.shape[0] // steps, array.shape[1]), lambda i: (i, 0))
        if array.ndim == 3 and array.shape[1] % (16 * steps) == 0:
            return pl.BlockSpec(
                (array.shape[0], array.shape[1] // steps, array.shape[2]), lambda i: (0, i, 0)
            )
        return pl.BlockSpec(array.shape, lambda i: (0,) * array.ndim)

    specs = [spec(array) for array, _ in arrays]
    rows = aux.shape[0]
    small = [jax.ShapeDtypeStruct(shape, F32) for shape in ((1, rows), (1, rows), (EXPERTS, rows))]
    return pl.pallas_call(
        functools.partial(settle_kernel, len(arrays)),
        grid=(steps,),
        out_shape=[jax.ShapeDtypeStruct(array.shape, dtype) for array, dtype in arrays] + small,
        in_specs=[spec(aux)] + specs,
        out_specs=specs + [spec(shape) for shape in small],
        compiler_params=pltpu.CompilerParams(vmem_limit_bytes=60 * 2**20),
        name="settle",
    )(aux, *[array for array, _ in arrays])


CTX = ("le", "rep", "core")
ALL = ("le", "rep", "core", "exp")
OWNERS = ("exp", "le")


def on_device(
    tokens,
    cotangent,
    routes,
    lengths,
    block_order,
    gain_attn,
    qkv_weight,
    out_weight,
    gain_moe,
    router_weight,
    expert_in,
    expert_out,
):
    tok_rows = tokens.shape[1]
    head_width = HEADS * HEAD
    exp_local = expert_in.shape[0]
    n_ctx = D // expert_in.shape[1]
    copies = n_ctx // exp_local
    n_exp = EXPERTS // exp_local
    in_rows, out_rows = expert_in.shape[1], expert_out.shape[1]

    route_hot = (
        routes[0][:, :, None] == jnp.arange(EXPERTS, dtype=jnp.int32)[None, None, :]
    ).astype(F32)
    flat_hot = route_hot.reshape(tok_rows * 2, EXPERTS).astype(BF16)
    order = jnp.arange(tok_rows * 2, dtype=jnp.int32)
    earlier = (order[:, None] > order[None, :]).astype(BF16)
    ranks = dot(earlier, flat_hot)
    slot_index = jnp.sum(ranks * flat_hot.astype(F32), axis=1).astype(jnp.int32)
    target = (routes[0].reshape(tok_rows * 2) * CAP + slot_index).reshape(tok_rows, 2)
    slots = jnp.arange(EXPERTS * CAP, dtype=jnp.int32)
    picks = [(target[:, k : k + 1] == slots[None, :]) for k in range(2)]
    sends = [(target[:, k][None, :] == slots[:, None]) for k in range(2)]
    send_hot = (sends[0] | sends[1]).astype(BF16)

    def to_experts(rows):
        return lax.all_to_all(
            rows.reshape((EXPERTS, CAP) + rows.shape[1:]),
            OWNERS,
            split_axis=0,
            concat_axis=0,
            tiled=True,
        ).reshape(rows.shape)

    cols = qkv_weight.shape[1]
    aux = jnp.concatenate([gain_attn[:, None], gain_moe[:, None], router_weight], axis=1)
    aux = jnp.pad(aux, ((0, 0), (0, AUX - aux.shape[1])))
    shard = jnp.concatenate([qkv_weight, aux, out_weight], axis=1).astype(BF16)
    special = (copies, exp_local, n_exp) == (2, 4, 4)
    if special:
        (
            w_all,
            w_in,
            w_down,
            first,
            projected,
            kv,
            exact,
            attended,
            lse,
            middle,
            second,
            gates,
            slot_gates,
            second_rows,
            grad_y_rows,
        ) = front(
            shard,
            expert_in,
            expert_out,
            tokens[0],
            lengths,
            block_order,
            jnp.concatenate([target, routes[0]], axis=1).T,
            cotangent[0],
            cols,
        )
        gates = gates[:, :2]
    else:
        w_all = lax.all_gather(shard, ALL, axis=0, tiled=True)

        def to_owner(weight):
            rows, width = weight.shape[1:]
            halves = weight.astype(BF16).reshape(exp_local, rows, 2, width // 2).transpose(0, 2, 1, 3)
            halves = jnp.broadcast_to(
                halves[:, None], (exp_local, copies // 2, 2, rows, width // 2)
            ).reshape(n_ctx, rows, width // 2)
            mine = lax.all_to_all(halves, CTX, split_axis=0, concat_axis=0, tiled=True)
            return lax.all_gather(mine.reshape(n_ctx * rows, width // 2), "core", axis=1, tiled=True)

        w_in = to_owner(expert_in)
        w_down = to_owner(expert_out)
    w_qkv = w_all[:, :cols]
    aux_all = w_all[:, cols : cols + AUX]
    w_attn_out = w_all[:, cols + AUX :]
    gain_first = aux_all[:, 0].astype(F32)
    gain_second = aux_all[:, 1].astype(F32)
    w_router = aux_all[:, 2 : 2 + EXPERTS]

    inputs = tokens[0].astype(F32)
    scale_first = norm_scale(inputs)
    norm_first = inputs * scale_first
    mine = (lax.axis_index(CTX) * (tok_rows // BLK)).astype(jnp.int32).reshape(1)
    if not special:
        first = (norm_first * gain_first).astype(BF16)
        projected = dot(first, w_qkv).astype(BF16)
        kv = lax.all_gather(projected[:, head_width:], CTX, axis=0, tiled=True)
        kv, grad_y_send = lax.optimization_barrier((kv, dot(send_hot, cotangent[0]).astype(BF16)))
        grad_y_rows = to_experts(grad_y_send)
        exact, attended, lse = attend(lengths, block_order, mine, projected, kv)
        middle = inputs + dot(attended, w_attn_out)
    scale_second = norm_scale(middle)
    norm_second = middle * scale_second
    if not special:
        second = (norm_second * gain_second).astype(BF16)
        logits = dot(second, w_router)
        chosen = jnp.sum(route_hot * logits[:, None, :], axis=-1)
        gates = jax.nn.softmax(chosen, axis=-1)

    if special:
        expert_rows, grad_returned, gate_grads, grad_in, grad_down = experts(
            second_rows,
            slot_gates,
            grad_y_rows,
            w_in,
            w_down,
            exp_local,
        )
        returned = to_experts(expert_rows.reshape(EXPERTS * CAP, D))
        grad_returned = grad_returned.reshape(EXPERTS * CAP, D)
        gate_grads = gate_grads[:, 0, :CAP].reshape(1, EXPERTS * CAP)
    else:
        gate_rows = jnp.sum(
            jnp.where(sends[0], gates[:, 0][None, :], 0.0) + jnp.where(sends[1], gates[:, 1][None, :], 0.0),
            axis=1,
            keepdims=True,
        )

        def in_parts(column):
            high = lax.reduce_precision(column, 8, 7)
            rest = column - high
            mid = lax.reduce_precision(rest, 8, 7)
            parts = jnp.concatenate([high, mid, rest - mid], axis=1).astype(BF16)
            return jnp.pad(parts, ((0, 0), (0, AUX - 3)))

        gate_parts = in_parts(gate_rows)
        payload = to_experts(
            jnp.concatenate([dot(send_hot, second).astype(BF16), gate_parts], axis=1)
        )
        received = payload[:, :D]
        gate_got = jnp.sum(payload[:, D : D + 3].astype(F32), axis=1, keepdims=True)

        gate_up = dot(received, w_in)
        gate_part = gate_up[:, :FF]
        up_part = gate_up[:, FF:]
        sigmoid_gate = jax.nn.sigmoid(gate_part)
        silu_gate = gate_part * sigmoid_gate
        hidden = (silu_gate * up_part).astype(BF16)
        expert_rows = dot(hidden, w_down)
        expert_rows = expert_rows.astype(BF16)
        grad_y_rows = grad_y_rows.astype(F32)
        returned = to_experts(expert_rows)

        grad_rows = (gate_got * grad_y_rows).astype(BF16)
        gate_grad_parts = in_parts(
            jnp.sum(grad_y_rows * expert_rows.astype(F32), axis=1, keepdims=True)
        )
        half_d = D // 2
        grad_hidden = dot(grad_rows, w_down, ((1,), (1,)))
        grad_gate = (
            grad_hidden * up_part * sigmoid_gate * (1.0 + gate_part * (1.0 - sigmoid_gate))
        ).astype(BF16)
        grad_up = (grad_hidden * silu_gate).astype(BF16)
        grad_gate_up = jnp.concatenate([grad_gate, grad_up], axis=1)
        grad_back = dot(grad_gate_up, w_in, ((1,), (1,)))
        grad_returned = to_experts(jnp.concatenate([grad_back.astype(BF16), gate_grad_parts], axis=1))

        grad_in = jnp.stack(
            [dot(received, grad_gate, ((0,), (0,))), dot(received, grad_up, ((0,), (0,)))]
        ).astype(BF16)
        grad_down = jnp.stack(
            [
                dot(hidden, grad_rows[:, :half_d], ((0,), (0,))),
                dot(hidden, grad_rows[:, half_d:], ((0,), (0,))),
            ]
        ).astype(BF16)

        grad_in = lax.psum_scatter(grad_in, "core", scatter_dimension=0, tiled=True)[0]
        grad_down = lax.psum_scatter(grad_down, "core", scatter_dimension=0, tiled=True)[0]
        grad_returned, grad_in, grad_down = lax.optimization_barrier((grad_returned, grad_in, grad_down))
        gate_grads = jnp.sum(grad_returned[:, D:].astype(F32), axis=1).reshape(1, EXPERTS * CAP)
        grad_returned = grad_returned[:, :D]

    grad_y = cotangent[0].astype(F32)
    pick_hot = [p.astype(BF16) for p in picks]
    grad_gates = jnp.concatenate(
        [jnp.sum(jnp.where(p, gate_grads, 0.0), axis=1, keepdims=True) for p in picks], axis=1
    )
    grad_chosen = gates * (grad_gates - jnp.sum(gates * grad_gates, axis=-1, keepdims=True))
    grad_logits = jnp.sum(grad_chosen[:, :, None] * route_hot, axis=1).astype(BF16)
    grad_second = dot(pick_hot[0] + pick_hot[1], grad_returned) + dot(
        grad_logits, w_router, ((1,), (1,))
    )
    grad_gain_second = jnp.sum(grad_second * norm_second, axis=0)
    grad_norm_second = grad_second * gain_second
    grad_middle = grad_y + scale_second * (
        grad_norm_second
        - norm_second * jnp.mean(grad_norm_second * norm_second, axis=-1, keepdims=True)
    )
    grad_branch = grad_middle.astype(BF16)
    grad_attended = dot(grad_branch, w_attn_out, ((1,), (1,))).astype(BF16)
    grad_queries, grad_kv = attend_back(
        lengths, block_order, mine, projected, kv, grad_attended, lse, exact
    )
    grad_queries, grad_kv, returned = lax.optimization_barrier((grad_queries, grad_kv, returned))
    if special:
        block_out, grad_inputs, sum_qkv, sum_out, sum_aux, sum_in, sum_down = finish(
            grad_kv,
            grad_queries,
            first,
            tokens[0],
            gain_first[None, :],
            grad_middle,
            w_all,
            attended,
            second,
            jnp.pad(grad_logits, ((0, 0), (1, AUX - 1 - EXPERTS))),
            grad_gain_second[None, :],
            middle,
            returned,
            jnp.stack(pick_hot),
            gates,
            grad_in,
            grad_down,
            exp_local,
        )
        block_out, grad_inputs, sum_qkv, sum_out, sum_in, sum_down, gain_a, gain_m, sum_router = settle(
            sum_aux,
            (
                (block_out, BF16),
                (grad_inputs, BF16),
                (sum_qkv, F32),
                (sum_out, F32),
                (sum_in, F32),
                (sum_down, F32),
            ),
            4,
        )
        gain_a, gain_m, sum_router = gain_a[0], gain_m[0], sum_router.T
    else:
        grad_router = dot(second, grad_logits, ((0,), (0,)))
        grad_attn_out = dot(attended, grad_branch, ((0,), (0,)))
        late = jnp.concatenate([grad_gain_second[:, None], grad_router], axis=1)
        late = jnp.pad(late, ((0, 0), (0, AUX - late.shape[1])))
        late = jnp.concatenate([grad_attn_out.astype(BF16), late.astype(BF16)], axis=1)
        grad_kv = lax.psum_scatter(grad_kv, CTX, scatter_dimension=0, tiled=True)
        grad_projected = jnp.concatenate([grad_queries, grad_kv], axis=1)
        grad_qkv = dot(first, grad_projected, ((0,), (0,)))
        grad_first = dot(grad_projected, w_qkv, ((1,), (1,)))
        grad_gain_first = jnp.sum(grad_first * norm_first, axis=0)
        grad_norm_first = grad_first * gain_first
        grad_inputs = grad_middle + scale_first * (
            grad_norm_first
            - norm_first * jnp.mean(grad_norm_first * norm_first, axis=-1, keepdims=True)
        )
        grad_inputs = grad_inputs.astype(BF16)
        last = jnp.pad(grad_gain_first[:, None], ((0, 0), (0, AUX - 1)))
        part = jnp.concatenate([grad_qkv.astype(BF16), last.astype(BF16), late], axis=1)
        total = lax.psum_scatter(part, ALL, scatter_dimension=0, tiled=True).astype(F32)
        sum_qkv, sum_out = total[:, :cols], total[:, cols + AUX : cols + AUX + D]
        gain_a, gain_m = total[:, cols], total[:, cols + AUX + D]
        sum_router = total[:, cols + AUX + D + 1 : cols + AUX + D + 1 + EXPERTS]
        picked = [dot(p, returned) for p in pick_hot]
        block_out = (middle + gates[:, 0:1] * picked[0] + gates[:, 1:2] * picked[1]).astype(BF16)

        def to_rows(half, rows):
            width = half.shape[1]
            got = lax.all_to_all(
                half.reshape(n_ctx, rows, width), CTX, split_axis=0, concat_axis=0, tiled=True
            ).astype(F32)
            got = got.reshape(exp_local, copies // 2, 2, rows, width).sum(axis=1)
            return got.transpose(0, 2, 1, 3).reshape(exp_local, rows, 2 * width)

        sum_in = to_rows(grad_in, in_rows)
        sum_down = to_rows(grad_down, out_rows)
    return (
        block_out[None],
        grad_inputs[None],
        gain_a,
        sum_qkv,
        sum_out,
        gain_m,
        sum_router,
        sum_in.astype(F32),
        sum_down.astype(F32),
    )


def solution(mesh):
    n_ctx, n_exp = mesh.shape["ctx"], mesh.shape["exp"]
    exp_local = EXPERTS // n_exp
    copies = n_ctx // exp_local
    inner = Mesh(mesh.devices.reshape(exp_local, copies // 2, 2, n_exp), ALL)
    by_token = P("exp", CTX, None)
    by_row = P(ALL, None)
    by_expert = P("exp", CTX, None)
    return jax.shard_map(
        on_device,
        mesh=inner,
        in_specs=(
            by_token,
            by_token,
            by_token,
            P("exp", None),
            P("exp", None),
            P(ALL),
            by_row,
            by_row,
            P(ALL),
            by_row,
            by_expert,
            by_expert,
        ),
        out_specs=(
            by_token,
            by_token,
            P(ALL),
            by_row,
            by_row,
            P(ALL),
            by_row,
            by_expert,
            by_expert,
        ),
        check_vma=False,
    )
```

```python
import functools

import jax
import jax.numpy as jnp
from jax import lax
from jax.experimental import pallas as pl
from jax.experimental.pallas import tpu as pltpu
from jax.sharding import Mesh
from jax.sharding import PartitionSpec as P

D = 1536
HEADS = 24
KV_HEADS = 8
HEAD = 64
GROUP = HEADS // KV_HEADS
FF = 1024
EXPERTS = 16
BLK = 128
CAP = 48
AUX = 128

epsilon = 1e-05
far_negative = -1e30
start_max = -1e29
F32 = jnp.float32
BF16 = jnp.bfloat16


def norm_scale(values):
    return lax.rsqrt(jnp.mean(values * values, axis=-1, keepdims=True) + epsilon)


def dot(a, b, dims=((1,), (0,))):
    return lax.dot_general(a, b, (dims, ((), ())), preferred_element_type=F32)


def lane_half(shape, half):
    lane = lax.broadcasted_iota(jnp.int32, shape, 1)
    return (lane >= HEAD) if half else (lane < HEAD)


def head_tiles(ref, rows, pair, scale):
    tiles = []
    for i in range(2 * GROUP):
        head = pair * 2 * GROUP + i
        group = head // GROUP
        tile = ref[rows, (head // 2) * 128 : (head // 2 + 1) * 128].astype(F32)
        if head % 2 != group % 2:
            tile = pltpu.roll(tile, HEAD, 1)
        tile = jnp.where(lane_half(tile.shape, group % 2), tile * scale, 0.0)
        tiles.append(tile.astype(BF16))
    return jnp.concatenate(tiles, axis=0)


def block_visibility(lengths_ref, query_block, key_block, parts):
    lanes = lax.broadcasted_iota(jnp.int32, (1, BLK), 1)
    query_pos = query_block * BLK + lanes
    start = jnp.zeros((1, BLK), jnp.int32)
    bound = jnp.int32(0)
    for s in range(parts - 1):
        bound = bound + lengths_ref[0, s]
        start = jnp.where(query_pos >= bound, bound, start)
    key_pos = key_block * BLK + lax.broadcasted_iota(jnp.int32, (BLK, BLK), 0)
    one = ((key_pos >= start) & (key_pos <= query_pos)).astype(jnp.int32)
    return jnp.concatenate([one] * (2 * GROUP), axis=1) > 0


def first_row_start(lengths_ref, query_block, parts):
    start = jnp.int32(0)
    bound = jnp.int32(0)
    for s in range(parts - 1):
        bound = bound + lengths_ref[0, s]
        start = jnp.where(query_block * BLK >= bound, bound, start)
    return start


def attend_blocks(
    parts,
    skip,
    lengths_ref,
    order_ref,
    mine,
    q_ref,
    kv_ref,
    exact_ref,
    out_ref,
    lse_ref,
    q_s,
    m_s,
    sum_s,
    acc_s,
):
    width = KV_HEADS * HEAD
    wide = 2 * GROUP * BLK
    for qb in range(q_ref.shape[0] // BLK):
        rows = pl.ds(qb * BLK, BLK)
        for pair in range(KV_HEADS // 2):
            q_s[pair] = head_tiles(q_ref, rows, pair, HEAD**-0.5)
            m_s[pair] = jnp.full((8, wide), start_max, F32)
            sum_s[pair] = jnp.zeros((8, wide), F32)
            acc_s[pair] = jnp.zeros((BLK, wide), F32)
        query_block = order_ref[0, mine + qb]
        first = first_row_start(lengths_ref, query_block, parts)

        @pl.loop(0, order_ref.shape[1])
        def _(kb):
            key_block = order_ref[0, kb]

            def fold():
                seen = block_visibility(lengths_ref, query_block, key_block, parts)
                key_rows = pl.ds(kb * BLK, BLK)
                for pair in range(KV_HEADS // 2):
                    keys = kv_ref[key_rows, pl.ds(pair * 128, 128)]
                    values = kv_ref[key_rows, pl.ds(width + pair * 128, 128)]
                    scores = dot(keys, q_s[pair], ((1,), (1,)))
                    scores = jnp.where(seen, scores, far_negative)
                    old = m_s[pair, 0:1, :]
                    new = jnp.maximum(old, jnp.max(scores, axis=0, keepdims=True))
                    weights = jnp.exp(scores - new)
                    factor = jnp.exp(old - new)
                    sum_s[pair, 0:1, :] = sum_s[pair, 0:1, :] * factor + jnp.sum(
                        weights, axis=0, keepdims=True
                    )
                    acc_s[pair] = acc_s[pair] * factor + dot(values, weights.astype(BF16), ((0,), (0,)))
                    m_s[pair, 0:1, :] = new

            if skip:
                pl.when((key_block <= query_block) & (key_block * BLK + BLK > first))(fold)
            else:
                fold()

        tiles = []
        for pair in range(KV_HEADS // 2):
            total = sum_s[pair, 0:1, :]
            lse_ref[qb, pair : pair + 1, :] = m_s[pair, 0:1, :] + jnp.log(total)
            acc = acc_s[pair] / total
            for i in range(2 * GROUP):
                head = pair * 2 * GROUP + i
                tile = jnp.transpose(acc[:, i * BLK : (i + 1) * BLK])
                if head % 2 != (head // GROUP) % 2:
                    tile = pltpu.roll(tile, HEAD, 1)
                tiles.append(tile)
                if head % 2 == 1:
                    both = jnp.where(lane_half(tile.shape, 0), tiles[head - 1], tile)
                    lanes = pl.ds((head // 2) * 128, 128)
                    exact_ref[rows, lanes] = both
                    out_ref[rows, lanes] = both.astype(BF16)


def attend_kernel(parts, lengths_ref, order_ref, mine_ref, *refs):
    attend_blocks(parts, True, lengths_ref, order_ref, mine_ref[0], *refs)


def attend(lengths, order, mine, projected, kv):
    rows = projected.shape[0]
    smem = pl.BlockSpec(memory_space=pltpu.SMEM)
    vmem = pl.BlockSpec(memory_space=pltpu.VMEM)
    wide = 2 * GROUP * BLK
    pairs = KV_HEADS // 2
    return pl.pallas_call(
        functools.partial(attend_kernel, lengths.shape[1]),
        out_shape=(
            jax.ShapeDtypeStruct((rows, HEADS * HEAD), F32),
            jax.ShapeDtypeStruct((rows, HEADS * HEAD), BF16),
            jax.ShapeDtypeStruct((rows // BLK, pairs, wide), F32),
        ),
        in_specs=[smem, smem, smem, vmem, vmem],
        out_specs=(vmem, vmem, vmem),
        scratch_shapes=[
            pltpu.VMEM((pairs, wide, 128), BF16),
            pltpu.VMEM((pairs, 8, wide), F32),
            pltpu.VMEM((pairs, 8, wide), F32),
            pltpu.VMEM((pairs, BLK, wide), F32),
        ],
        compiler_params=pltpu.CompilerParams(vmem_limit_bytes=48 * 2**20),
        cost_estimate=pl.CostEstimate(flops=10**10, bytes_accessed=10**7, transcendentals=10**7),
        name="attend",
    )(lengths, order, mine, projected, kv)


def attend_back_kernel(
    parts,
    lengths_ref,
    order_ref,
    mine_ref,
    q_ref,
    kv_ref,
    grad_ref,
    lse_ref,
    exact_ref,
    dq_ref,
    dkv_ref,
    q_s,
    g_s,
    delta_s,
    dq_s,
    dkv_s,
):
    width = KV_HEADS * HEAD

    @pl.loop(0, order_ref.shape[1])
    def _(kb):
        dkv_s[pl.ds(kb * BLK, BLK), :] = jnp.zeros((BLK, 2 * width), F32)

    for qb in range(q_ref.shape[0] // BLK):
        rows = pl.ds(qb * BLK, BLK)
        for pair in range(KV_HEADS // 2):
            q_s[pair] = head_tiles(q_ref, rows, pair, HEAD**-0.5)
            g_s[pair] = head_tiles(grad_ref, rows, pair, 1.0)
            dq_s[pair] = jnp.zeros((2 * GROUP * BLK, 128), F32)
            for i in range(2 * GROUP):
                head = pair * 2 * GROUP + i
                exact = exact_ref[rows, (head // 2) * 128 : (head // 2 + 1) * 128]
                if head % 2 != (head // GROUP) % 2:
                    exact = pltpu.roll(exact, HEAD, 1)
                product = exact * g_s[pair, i * BLK : (i + 1) * BLK, :].astype(F32)
                delta_s[pair : pair + 1, i * BLK : (i + 1) * BLK] = jnp.sum(
                    jnp.transpose(product), axis=0, keepdims=True
                )
        query_block = order_ref[0, mine_ref[0] + qb]
        first = first_row_start(lengths_ref, query_block, parts)

        @pl.loop(0, order_ref.shape[1])
        def _(kb):
            key_block = order_ref[0, kb]

            @pl.when((key_block <= query_block) & (key_block * BLK + BLK > first))
            def _():
                seen = block_visibility(lengths_ref, query_block, key_block, parts)
                key_rows = pl.ds(kb * BLK, BLK)
                for pair in range(KV_HEADS // 2):
                    key_lanes = pl.ds(pair * 128, 128)
                    value_lanes = pl.ds(width + pair * 128, 128)
                    keys = kv_ref[key_rows, key_lanes]
                    values = kv_ref[key_rows, value_lanes]
                    scores = dot(keys, q_s[pair], ((1,), (1,)))
                    scores = jnp.where(seen, scores, far_negative)
                    probs = jnp.exp(scores - lse_ref[qb, pair : pair + 1, :])
                    grad_probs = dot(values, g_s[pair], ((1,), (1,)))
                    grad_scores = (probs * (grad_probs - delta_s[pair : pair + 1, :])).astype(BF16)
                    dkv_s[key_rows, value_lanes] += dot(probs.astype(BF16), g_s[pair])
                    dkv_s[key_rows, key_lanes] += dot(grad_scores, q_s[pair])
                    dq_s[pair] += dot(grad_scores, keys, ((0,), (0,)))

        tiles = []
        for pair in range(KV_HEADS // 2):
            for i in range(2 * GROUP):
                head = pair * 2 * GROUP + i
                tile = dq_s[pair, i * BLK : (i + 1) * BLK, :] * HEAD**-0.5
                if head % 2 != (head // GROUP) % 2:
                    tile = pltpu.roll(tile, HEAD, 1)
                tiles.append(tile)
                if head % 2 == 1:
                    both = jnp.where(lane_half(tile.shape, 0), tiles[head - 1], tile)
                    dq_ref[rows, (head // 2) * 128 : (head // 2 + 1) * 128] = both.astype(BF16)

    @pl.loop(0, order_ref.shape[1])
    def _(kb):
        key_rows = pl.ds(kb * BLK, BLK)
        dkv_ref[key_rows, :] = dkv_s[key_rows, :].astype(BF16)


def attend_back(lengths, order, mine, projected, kv, grad_attended, lse, exact):
    rows = projected.shape[0]
    smem = pl.BlockSpec(memory_space=pltpu.SMEM)
    vmem = pl.BlockSpec(memory_space=pltpu.VMEM)
    wide = 2 * GROUP * BLK
    pairs = KV_HEADS // 2
    return pl.pallas_call(
        functools.partial(attend_back_kernel, lengths.shape[1]),
        out_shape=(
            jax.ShapeDtypeStruct((rows, HEADS * HEAD), BF16),
            jax.ShapeDtypeStruct(kv.shape, BF16),
        ),
        in_specs=[smem, smem, smem, vmem, vmem, vmem, vmem, vmem],
        out_specs=(vmem, vmem),
        scratch_shapes=[
            pltpu.VMEM((pairs, wide, 128), BF16),
            pltpu.VMEM((pairs, wide, 128), BF16),
            pltpu.VMEM((pairs, wide), F32),
            pltpu.VMEM((pairs, wide, 128), F32),
            pltpu.VMEM(kv.shape, F32),
        ],
        compiler_params=pltpu.CompilerParams(vmem_limit_bytes=56 * 2**20),
        cost_estimate=pl.CostEstimate(flops=10**9, bytes_accessed=10**6, transcendentals=10**5),
        name="attend_back",
    )(lengths, order, mine, projected, kv, grad_attended, lse, exact)


MESH = pl.DeviceIdType.MESH


def place(z, core, exp):
    return {"le": z, "rep": 0, "core": core, "exp": exp}


def x_of(exp):
    return (exp // 2) * 2 + 1 - exp % 2


def y_of(exp):
    return (1 - exp // 2) * 2 + exp % 2


def remote(src, dst, send_sem, recv_sem, device):
    return pltpu.make_async_remote_copy(
        src_ref=src,
        dst_ref=dst,
        send_sem=send_sem,
        recv_sem=recv_sem,
        device_id=device,
        device_id_type=MESH,
    )


def near_to_far(z):
    first_half = z < 2
    return [z, z + 1 - 2 * (z % 2), jnp.where(first_half, 3, 0), jnp.where(first_half, 2, 1)]


def between(z, zz):
    return ((z == 1) & (zz == 2)) | ((z == 2) & (zz == 1))


def meet(devices):
    barrier = pltpu.get_barrier_semaphore()
    for device in devices:
        pl.semaphore_signal(barrier, inc=1, device_id=device, device_id_type=MESH)
    pl.semaphore_wait(barrier, len(devices))


def front_kernel(
    layers,
    shard_ref,
    in_ref,
    down_ref,
    tokens_ref,
    lengths_ref,
    order_ref,
    target_ref,
    cotangent_ref,
    w_all_ref,
    w_in_ref,
    w_down_ref,
    first_ref,
    projected_ref,
    kv_ref,
    exact_ref,
    attended_ref,
    lse_ref,
    middle_ref,
    second_ref,
    gates_ref,
    slot_gates_ref,
    rows_ref,
    got_grads_ref,
    hot_s,
    grads_s,
    weights,
    kv_s,
    q_s,
    m_s,
    sum_s,
    acc_s,
    in_wide,
    down_wide,
    in_half,
    down_half,
    unit_sem,
    line_sem,
    x_sem,
    y_sem,
    far_sem,
    core_sem,
    half_sem,
    half_send,
    over_sem,
    over_send,
    kv_sem,
    kv_send,
    own_sem,
    wide_sem,
    grad_sem,
    grad_send,
):
    z, core, exp = lax.axis_index("le"), lax.axis_index("core"), lax.axis_index("exp")
    other = 1 - core
    x, y = x_of(exp), y_of(exp)
    ctx = z * 2 + core
    rows = shard_ref.shape[0]
    own_layer, mate, farthest, middle = near_to_far(z)
    order = [mate, middle, farthest, own_layer]
    wides = ((in_ref, in_wide), (down_ref, down_wide))
    halves = ((in_half, w_in_ref), (down_half, w_down_ref))

    loads = []
    for k, zz in enumerate(order):
        for a in range(2):
            load = pltpu.make_async_copy(wides[a][0].at[zz], wides[a][1].at[zz], wide_sem.at[a, k])
            load.start()
            loads.append(load)
    peers = [
        (zz, (exp + t) % 4)
        for s, zz in enumerate(order)
        for t in range(4)
        if not (s == layers - 1 and t == 0)
    ]
    meet([place(zz, core, ee) for zz, ee in peers] + [place(zz, other, exp) for zz in order])

    def number(zz, cc, ee):
        return (zz * 2 + cc) * 4 + ee

    def unit(zz, cc, ee):
        return weights.at[pl.ds(pl.multiple_of(number(zz, cc, ee) * rows, 16), rows), :]

    def send(src, who, sem, device):
        return remote(src, unit(*who), sem, unit_sem.at[number(*who)], device)

    def arrive(who):
        send(unit(*who), who, line_sem.at[0], place(z, other, exp)).wait_recv()

    started = []

    def go(copy, condition=None):
        if condition is None:
            copy.start()
        else:
            pl.when(condition)(copy.start)
        started.append((copy, condition))

    me = (z, core, exp)
    keep = pltpu.make_async_copy(shard_ref, unit(*me), own_sem.at[0])
    keep.start()
    go(send(shard_ref, me, line_sem.at[layers], place(z + 1, core, exp)), z < layers - 1)
    go(send(shard_ref, me, line_sem.at[layers + 1], place(z - 1, core, exp)), z > 0)
    go(send(shard_ref, me, x_sem.at[layers], place(z, core, x)))
    go(send(shard_ref, me, y_sem.at[layers], place(z, core, y)))
    go(send(shard_ref, me, core_sem.at[layers], place(z, other, exp)))

    slab = 16
    for k, zz in enumerate(order):
        for a in range(2):
            loads[2 * k + a].wait()
            src, dst = wides[a][1], halves[a][0]

            @pl.loop(0, src.shape[1] // slab)
            def _(i, zz=zz, src=src, dst=dst):
                at = pl.ds(pl.multiple_of(i * slab, slab), slab)
                dst[zz, at, :] = src[zz, at, :].astype(BF16)

    def half(a, source, p):
        src, dst = halves[a]
        n, cols = src.shape[1], src.shape[2] // 2
        return dst.at[pl.ds(source * n, n), pl.ds(pl.multiple_of(p * cols, 128), cols)]

    def mine(a, zz, p):
        src = halves[a][0]
        cols = src.shape[2] // 2
        return src.at[zz, :, pl.ds(pl.multiple_of(p * cols, 128), cols)]

    def layer(k):
        return jnp.where(z < layers // 2, k, layers - 1 - k)

    def ahead(zz):
        return between(z, zz)

    def hand_out(a, early):
        for s, zz in enumerate(order):
            across = ahead(zz)
            for p in range(2):
                if s == layers - 1 and p == 0:
                    continue
                pp = (core + p) % 2
                copy = remote(
                    mine(a, zz, pp),
                    half(a, ctx, pp),
                    half_send.at[a, s * 2 + p],
                    half_sem.at[a, ctx],
                    place(zz, pp, exp),
                )
                if early:
                    pl.when(across)(copy.start)
                else:
                    pl.when(~across)(copy.start)
                    started.append((copy, None))
        if not early:
            go(
                remote(
                    mine(a, z, core),
                    half(a, ctx, core),
                    over_send.at[a, 2 * layers],
                    over_sem.at[a, ctx],
                    place(z, other, exp),
                )
            )

    for k in range(layers):
        zz = layer(k)
        who = (zz, core, exp)

        @pl.when(zz != z)
        def _(who=who):
            arrive(who)

        go(send(unit(*who), who, line_sem.at[k], place(z + 1, core, exp)), (zz < z) & (z < layers - 1))
        go(send(unit(*who), who, line_sem.at[k], place(z - 1, core, exp)), (zz > z) & (z > 0))
        go(send(unit(*who), who, x_sem.at[k], place(z, core, x)), zz != z)
        go(send(unit(*who), who, y_sem.at[k], place(z, core, y)), zz != z)
        go(send(unit(*who), who, core_sem.at[k], place(z, other, exp)), zz != z)
        if k == 0:
            hand_out(0, True)

    def spread_rows(values, out):
        tile, cap = 256, out.shape[1]

        @pl.loop(0, values.shape[1] // tile)
        def _(i):
            at = pl.ds(pl.multiple_of(i * tile, tile), tile)
            spread_out = dot(hot_s[...], values[:, at]).astype(BF16)
            for e in range(out.shape[0]):
                out[e, :, at] = spread_out[e * cap : (e + 1) * cap]

    slot = lax.broadcasted_iota(jnp.int32, hot_s.shape, 0)
    takes = [slot == target_ref[k : k + 1, :] for k in range(2)]
    hot_s[...] = jnp.where(takes[0] | takes[1], 1.0, 0.0).astype(BF16)
    spread_rows(cotangent_ref, grads_s)

    for a in range(2):
        pltpu.make_async_copy(mine(a, z, core), half(a, ctx, core), own_sem.at[1 + a]).start()

    hand_out(0, False)

    for k in range(layers):
        zz = layer(k)
        from_x, from_y = (zz, core, x), (zz, core, y)
        arrive(from_x)
        go(send(unit(*from_x), from_x, core_sem.at[layers + 1 + k], place(z, other, exp)))
        if k % 2 == 0:
            go(send(unit(*from_x), from_x, far_sem.at[k], place(z, core, y)))
        arrive(from_y)
        go(send(unit(*from_y), from_y, core_sem.at[2 * layers + 1 + k], place(z, other, exp)))
        if k % 2 == 1:
            go(send(unit(*from_y), from_y, far_sem.at[k], place(z, core, x)))
    for k in range(layers):
        far = (layer(k), core, y_of(x))
        arrive(far)
        go(send(unit(*far), far, core_sem.at[3 * layers + 1 + k], place(z, other, exp)))
    for ee in range(4):
        for zz in range(layers):
            arrive((zz, other, ee))
    keep.wait()
    save = pltpu.make_async_copy(weights, w_all_ref, own_sem.at[3])
    save.start()

    depth, count = tokens_ref.shape[1], tokens_ref.shape[0]
    qkv_cols, head_cols = projected_ref.shape[1], HEADS * HEAD
    inputs = tokens_ref[...].astype(F32)
    gains = jnp.concatenate(
        [
            jnp.transpose(weights[i * 128 : (i + 1) * 128, qkv_cols : qkv_cols + AUX].astype(F32))[0:8, :]
            for i in range(depth // 128)
        ],
        axis=1,
    )
    first_ref[...] = (inputs * norm_scale(inputs) * gains[0:1, :]).astype(BF16)
    tile = 512

    @pl.loop(0, (qkv_cols - head_cols) // tile)
    def _(i):
        at = pl.ds(pl.multiple_of(head_cols + i * tile, tile), tile)
        projected_ref[:, at] = dot(first_ref[...], weights[:, at]).astype(BF16)

    def block(source):
        return kv_s.at[pl.ds(pl.multiple_of(source * count, 16), count), :]

    def share(src, source, sem, device):
        return remote(src, block(source), sem, kv_sem.at[source], device)

    own = projected_ref.at[:, pl.ds(head_cols, qkv_cols - head_cols)]
    keep_kv = pltpu.make_async_copy(own, block(ctx), own_sem.at[0])
    keep_kv.start()
    go(share(own, ctx, kv_send.at[2 * layers], place(z + 1, core, exp)), z < layers - 1)
    go(share(own, ctx, kv_send.at[2 * layers + 1], place(z - 1, core, exp)), z > 0)
    go(share(own, ctx, kv_send.at[2 * layers + 2], place(z, other, exp)))

    @pl.loop(0, head_cols // tile)
    def _(i):
        at = pl.ds(pl.multiple_of(i * tile, tile), tile)
        projected_ref[:, at] = dot(first_ref[...], weights[:, at]).astype(BF16)

    for k in range(layers):
        zz = layer(k)
        source = zz * 2 + core

        @pl.when(zz != z)
        def _(source=source):
            share(block(source), source, kv_send.at[0], place(z, other, exp)).wait_recv()

        go(share(block(source), source, kv_send.at[k], place(z + 1, core, exp)), (zz < z) & (z < layers - 1))
        go(share(block(source), source, kv_send.at[k], place(z - 1, core, exp)), (zz > z) & (z > 0))
        go(share(block(source), source, kv_send.at[layers + k], place(z, other, exp)), zz != z)

    hand_out(1, True)
    hand_out(1, False)

    me_slot = exp * layers + z
    keep_grads = pltpu.make_async_copy(grads_s.at[me_slot], got_grads_ref.at[me_slot], own_sem.at[4])
    keep_grads.start()
    for k, (zz, ee) in enumerate(peers):
        there = ee * layers + zz
        go(
            remote(
                grads_s.at[there],
                got_grads_ref.at[me_slot],
                grad_send.at[k],
                grad_sem.at[me_slot],
                place(zz, core, ee),
            )
        )

    def pass_over(a):
        for s, zz in enumerate(order[::-1]):
            for p in range(2):
                if s == 0 and p == 0:
                    continue
                source = zz * 2 + (core + p) % 2
                remote(
                    half(a, source, core),
                    half(a, source, core),
                    half_send.at[a, 0],
                    half_sem.at[a, source],
                    place(z, other, exp),
                ).wait_recv()
                go(
                    remote(
                        half(a, source, core),
                        half(a, source, core),
                        over_send.at[a, s * 2 + p],
                        over_sem.at[a, source],
                        place(z, other, exp),
                    )
                )

    pass_over(0)
    for zz in range(layers):
        source = zz * 2 + other
        share(block(source), source, kv_send.at[0], place(z, other, exp)).wait_recv()
    keep_kv.wait()
    save_kv = pltpu.make_async_copy(kv_s, kv_ref, own_sem.at[0])
    save_kv.start()

    attend_blocks(
        lengths_ref.shape[1],
        False,
        lengths_ref,
        order_ref,
        ctx * (count // BLK),
        projected_ref,
        kv_s,
        exact_ref,
        attended_ref,
        lse_ref,
        q_s,
        m_s,
        sum_s,
        acc_s,
    )
    tile = 256

    @pl.loop(0, depth // tile)
    def _(i):
        at = pl.ds(pl.multiple_of(i * tile, tile), tile)
        w_at = pl.ds(pl.multiple_of(qkv_cols + AUX + i * tile, 128), tile)
        middle_ref[:, at] = tokens_ref[:, at].astype(F32) + dot(attended_ref[...], weights[:, w_at])

    middle = middle_ref[...]
    second_ref[...] = (middle * norm_scale(middle) * gains[1:2, :]).astype(BF16)
    logits = dot(second_ref[...], weights[:, qkv_cols : qkv_cols + AUX])
    lane = lax.broadcasted_iota(jnp.int32, logits.shape, 1)
    token = lax.broadcasted_iota(jnp.int32, (count, count), 0)
    eye = token == lax.broadcasted_iota(jnp.int32, (count, count), 1)
    chosen = []
    for k in range(2):
        line = target_ref[2 + k : 3 + k, :].astype(F32)
        expert = jnp.sum(jnp.where(eye, line, 0.0), axis=1, keepdims=True)
        chosen.append(jnp.sum(jnp.where(lane.astype(F32) == expert + 2.0, logits, 0.0), axis=1, keepdims=True))
    largest = jnp.maximum(chosen[0], chosen[1])
    exps = [jnp.exp(value - largest) for value in chosen]
    total = exps[0] + exps[1]
    gates = [value / total for value in exps]
    gates_ref[...] = jnp.where(lane == 0, gates[0], jnp.where(lane == 1, gates[1], 0.0))
    spread_rows(second_ref, rows_ref)
    slot = lax.broadcasted_iota(jnp.int32, hot_s.shape, 0)
    by_slot = jnp.zeros(hot_s.shape, F32)
    for k in range(2):
        line = jnp.sum(jnp.where(eye, gates[k], 0.0), axis=0, keepdims=True)
        by_slot = by_slot + jnp.where(slot == target_ref[k : k + 1, :], line, 0.0)
    by_slot = jnp.sum(by_slot, axis=1, keepdims=True)
    cap = rows_ref.shape[1]
    eye = lax.broadcasted_iota(jnp.int32, (cap, 128), 0) == lax.broadcasted_iota(jnp.int32, (cap, 128), 1)
    for e in range(rows_ref.shape[0]):
        line = jnp.sum(jnp.where(eye, by_slot[e * cap : (e + 1) * cap], 0.0), axis=0, keepdims=True)
        slot_gates_ref[e] = jnp.broadcast_to(line, (8, 128))

    pass_over(1)
    for source in range(2 * layers):
        for a in range(2):
            remote(
                half(a, source, other),
                half(a, source, other),
                half_send.at[a, 0],
                over_sem.at[a, source],
                place(z, other, exp),
            ).wait_recv()
    for zz, ee in peers:
        source = ee * layers + zz
        remote(
            got_grads_ref.at[source],
            got_grads_ref.at[source],
            grad_send.at[0],
            grad_sem.at[source],
            place(zz, core, ee),
        ).wait_recv()
    keep_grads.wait()
    save_kv.wait()
    save.wait()
    for a in range(2):
        pltpu.make_async_copy(mine(a, z, core), half(a, ctx, core), own_sem.at[1 + a]).wait()
    for copy, condition in started:
        if condition is None:
            copy.wait_send()
        else:
            pl.when(condition)(copy.wait_send)


def front(shard, expert_in, expert_out, tokens, lengths, block_order, target, cotangent, qkv_cols):
    layers = expert_in.shape[0]
    rows_in, rows_out = expert_in.shape[1], expert_out.shape[1]
    depth, cols = shard.shape[0] * 8 * layers, shard.shape[1]
    count = tokens.shape[0]
    kv_shape = (count * 2 * layers, qkv_cols - HEADS * HEAD)
    wide, pairs = 2 * GROUP * BLK, KV_HEADS // 2
    slots = (EXPERTS, CAP, depth)
    any_space = pl.BlockSpec(memory_space=pl.ANY)
    smem = pl.BlockSpec(memory_space=pltpu.SMEM)
    vmem = pl.BlockSpec(memory_space=pltpu.VMEM)
    dma = pltpu.SemaphoreType.DMA
    return pl.pallas_call(
        functools.partial(front_kernel, layers),
        out_shape=(
            jax.ShapeDtypeStruct((depth, cols), BF16),
            jax.ShapeDtypeStruct((rows_in * 2 * layers, expert_in.shape[2]), BF16),
            jax.ShapeDtypeStruct((rows_out * 2 * layers, expert_out.shape[2]), BF16),
            jax.ShapeDtypeStruct((count, depth), BF16),
            jax.ShapeDtypeStruct((count, qkv_cols), BF16),
            jax.ShapeDtypeStruct(kv_shape, BF16),
            jax.ShapeDtypeStruct((count, HEADS * HEAD), F32),
            jax.ShapeDtypeStruct((count, HEADS * HEAD), BF16),
            jax.ShapeDtypeStruct((count // BLK, pairs, wide), F32),
            jax.ShapeDtypeStruct((count, depth), F32),
            jax.ShapeDtypeStruct((count, depth), BF16),
            jax.ShapeDtypeStruct((count, AUX), F32),
            jax.ShapeDtypeStruct((EXPERTS, 8, 128), F32),
            jax.ShapeDtypeStruct(slots, BF16),
            jax.ShapeDtypeStruct(slots, BF16),
        ),
        in_specs=[any_space] * 3 + [vmem, smem, smem, vmem, vmem],
        out_specs=(any_space,) * 3 + (vmem, vmem, any_space) + (vmem,) * 8 + (any_space,),
        scratch_shapes=[
            pltpu.VMEM((EXPERTS * CAP, count), BF16),
            pltpu.VMEM(slots, BF16),
            pltpu.VMEM((depth, cols), BF16),
            pltpu.VMEM(kv_shape, BF16),
            pltpu.VMEM((pairs, wide, 128), BF16),
            pltpu.VMEM((pairs, 8, wide), F32),
            pltpu.VMEM((pairs, 8, wide), F32),
            pltpu.VMEM((pairs, BLK, wide), F32),
            pltpu.VMEM(expert_in.shape, F32),
            pltpu.VMEM(expert_out.shape, F32),
            pltpu.VMEM(expert_in.shape, BF16),
            pltpu.VMEM(expert_out.shape, BF16),
            dma((8 * layers,)),
            dma((layers + 2,)),
            dma((layers + 1,)),
            dma((layers + 1,)),
            dma((layers,)),
            dma((4 * layers + 1,)),
            dma((2, 2 * layers)),
            dma((2, 2 * layers)),
            dma((2, 2 * layers)),
            dma((2, 2 * layers + 1)),
            dma((2 * layers,)),
            dma((2 * layers + 3,)),
            dma((5,)),
            dma((2, layers)),
            dma((4 * layers,)),
            dma((4 * layers,)),
        ],
        compiler_params=pltpu.CompilerParams(
            collective_id=0, has_side_effects=True, vmem_limit_bytes=60 * 2**20
        ),
        name="front",
    )(shard, expert_in, expert_out, tokens, lengths, block_order, target, cotangent)


def experts_kernel(
    layers,
    rows_ref,
    gates_ref,
    grads_ref,
    w_in_ref,
    w_down_ref,
    out_ref,
    back_ref,
    back_gates_ref,
    d_in_ref,
    d_down_ref,
    w_in,
    w_down,
    got,
    got_gates,
    x_s,
    grad_s,
    hidden_s,
    inner_s,
    back_s,
    back_gates_s,
    other_in,
    other_down,
    pair_in,
    pair_down,
    row_sem,
    row_send,
    gate_sem,
    gate_send,
    back_sem,
    back_send,
    back_gate_sem,
    back_gate_send,
    pair_sem,
    pair_send,
    load_sem,
):
    z, core, exp = lax.axis_index("le"), lax.axis_index("core"), lax.axis_index("exp")
    other = 1 - core
    columns = rows_ref.shape[0] // layers
    me = exp * layers + z
    cap, depth = rows_ref.shape[1], rows_ref.shape[2]
    chunk = columns * cap
    loads = [
        pltpu.make_async_copy(w_in_ref, w_in, load_sem.at[0]),
        pltpu.make_async_copy(w_down_ref, w_down, load_sem.at[1]),
    ]
    for load in loads:
        load.start()
    own_layer, mate, farthest, middle = near_to_far(z)
    peers = [
        (zz, (exp + t) % columns)
        for s, zz in enumerate([mate, farthest, middle, own_layer])
        for t in range(columns)
        if not (s == layers - 1 and t == 0)
    ]
    meet([place(zz, core, ee) for zz, ee in peers] + [place(z, other, exp)])

    started = []

    def go(copy):
        copy.start()
        started.append(copy)

    keeps = [
        pltpu.make_async_copy(rows_ref.at[me], got.at[me], load_sem.at[2]),
        pltpu.make_async_copy(gates_ref.at[me], got_gates.at[me], load_sem.at[3]),
    ]
    for keep in keeps:
        keep.start()
    for k, (zz, ee) in enumerate(peers):
        there = ee * layers + zz
        go(remote(gates_ref.at[there], got_gates.at[me], gate_send.at[k], gate_sem.at[me], place(zz, core, ee)))
        go(remote(rows_ref.at[there], got.at[me], row_send.at[k], row_sem.at[me], place(zz, core, ee)))
    for load in loads + keeps:
        load.wait()

    eye = lax.broadcasted_iota(jnp.int32, (cap, 128), 0) == lax.broadcasted_iota(jnp.int32, (cap, 128), 1)
    tile = 256

    def tiles(i):
        return pl.ds(pl.multiple_of(i * tile, tile), tile)

    for k, zz in enumerate([own_layer, mate, farthest, middle]):
        rows = pl.ds(k * chunk, chunk)
        for ee in range(columns):
            source = ee * layers + zz

            @pl.when(source != me)
            def _(source=source):
                here = place(z, other, exp)
                remote(got.at[source], got.at[source], row_send.at[0], row_sem.at[source], here).wait_recv()
                remote(
                    got_gates.at[source], got_gates.at[source], gate_send.at[0], gate_sem.at[source], here
                ).wait_recv()

            at = pl.ds(k * chunk + ee * cap, cap)
            x_s[at, :] = got[source]
            gate = jnp.sum(jnp.where(eye, got_gates[source, 0:1, :], 0.0), axis=1, keepdims=True)
            grad_s[at, :] = (gate * grads_ref[source].astype(F32)).astype(BF16)

        @pl.loop(0, FF // tile)
        def _(i, rows=rows):
            up_at = pl.ds(pl.multiple_of(FF + i * tile, tile), tile)
            gate = dot(x_s[rows, :], w_in[:, tiles(i)])
            up = dot(x_s[rows, :], w_in[:, up_at])
            grad_hidden = dot(grad_s[rows, :], w_down[tiles(i), :], ((1,), (1,)))
            sigmoid = jax.nn.sigmoid(gate)
            silu = gate * sigmoid
            hidden_s[rows, tiles(i)] = (silu * up).astype(BF16)
            inner_s[rows, tiles(i)] = (grad_hidden * up * sigmoid * (1.0 + gate * (1.0 - sigmoid))).astype(BF16)
            inner_s[rows, up_at] = (grad_hidden * silu).astype(BF16)

        @pl.loop(0, depth // tile)
        def _(i, rows=rows, zz=zz):
            back = dot(inner_s[rows, :], w_in[tiles(i), :], ((1,), (1,))).astype(BF16)
            for ee in range(columns):
                back_s[ee * layers + zz, :, tiles(i)] = back[ee * cap : (ee + 1) * cap]

        @pl.loop(0, depth // tile, init_carry=jnp.zeros((chunk, 128), F32))
        def gate_grads(i, sums, rows=rows, zz=zz):
            result = dot(hidden_s[rows, :], w_down[:, tiles(i)]).astype(BF16)
            parts = []
            for ee in range(columns):
                part = result[ee * cap : (ee + 1) * cap]
                out_ref[ee * layers + zz, :, tiles(i)] = part
                parts.append(part.astype(F32) * grads_ref[ee * layers + zz, :, tiles(i)].astype(F32))
            product = jnp.concatenate(parts, axis=0)
            return sums + product[:, :128] + product[:, 128:]

        gate_grads = jnp.sum(gate_grads, axis=1, keepdims=True)
        for ee in range(columns):
            there = ee * layers + zz
            column = gate_grads[ee * cap : (ee + 1) * cap]
            line = jnp.sum(jnp.where(eye, column, 0.0), axis=0, keepdims=True)
            back_gates_s[there] = jnp.broadcast_to(line, (8, 128))
            row_copy = remote(
                back_s.at[there],
                back_ref.at[me],
                back_send.at[there],
                back_sem.at[me],
                place(zz, core, ee),
            )
            gate_copy = remote(
                back_gates_s.at[there],
                back_gates_ref.at[me],
                back_gate_send.at[there],
                back_gate_sem.at[me],
                place(zz, core, ee),
            )

            @pl.when(there != me)
            def _(row_copy=row_copy, gate_copy=gate_copy):
                row_copy.start()
                gate_copy.start()

    own = [
        pltpu.make_async_copy(back_s.at[me], back_ref.at[me], load_sem.at[2]),
        pltpu.make_async_copy(back_gates_s.at[me], back_gates_ref.at[me], load_sem.at[3]),
    ]
    for copy in own:
        copy.start()

    half_in, half_down = d_in_ref.shape[1], d_down_ref.shape[1]

    def in_part(i, p):
        cols = pl.ds(pl.multiple_of(p * half_in, 128), half_in)
        return dot(x_s[:, tiles(i)], inner_s[:, cols], ((0,), (0,)))

    def down_part(i, p):
        cols = pl.ds(pl.multiple_of(p * half_down, 128), half_down)
        return dot(hidden_s[:, tiles(i)], grad_s[:, cols], ((0,), (0,)))

    @pl.loop(0, depth // tile)
    def _(i):
        other_in[tiles(i), :] = in_part(i, other).astype(BF16)

    go(remote(other_in, pair_in, pair_send.at[0], pair_sem.at[0], place(z, other, exp)))

    @pl.loop(0, FF // tile)
    def _(i):
        other_down[tiles(i), :] = down_part(i, other).astype(BF16)

    go(remote(other_down, pair_down, pair_send.at[1], pair_sem.at[1], place(z, other, exp)))
    remote(other_in, pair_in, pair_send.at[0], pair_sem.at[0], place(z, other, exp)).wait_recv()

    @pl.loop(0, depth // tile)
    def _(i):
        d_in_ref[tiles(i), :] = (in_part(i, core) + pair_in[tiles(i), :].astype(F32)).astype(BF16)

    remote(other_down, pair_down, pair_send.at[1], pair_sem.at[1], place(z, other, exp)).wait_recv()

    @pl.loop(0, FF // tile)
    def _(i):
        d_down_ref[tiles(i), :] = (down_part(i, core) + pair_down[tiles(i), :].astype(F32)).astype(BF16)

    for copy in own:
        copy.wait()
    for k, (zz, ee) in enumerate(peers):
        there = ee * layers + zz
        row_copy = remote(
            back_s.at[there], back_ref.at[there], back_send.at[there], back_sem.at[there], place(zz, core, ee)
        )
        gate_copy = remote(
            back_gates_s.at[there],
            back_gates_ref.at[there],
            back_gate_send.at[there],
            back_gate_sem.at[there],
            place(zz, core, ee),
        )
        row_copy.wait()
        gate_copy.wait()
    for copy in started:
        copy.wait_send()


def experts(rows, gates, grads, w_in, w_down, layers):
    count, cap, depth = rows.shape
    any_space = pl.BlockSpec(memory_space=pl.ANY)
    vmem = pl.BlockSpec(memory_space=pltpu.VMEM)
    dma = pltpu.SemaphoreType.DMA
    half_in = jax.ShapeDtypeStruct((depth, FF), BF16)
    half_down = jax.ShapeDtypeStruct((FF, depth // 2), BF16)
    return pl.pallas_call(
        functools.partial(experts_kernel, layers),
        out_shape=(
            jax.ShapeDtypeStruct(rows.shape, BF16),
            jax.ShapeDtypeStruct(rows.shape, BF16),
            jax.ShapeDtypeStruct(gates.shape, F32),
            half_in,
            half_down,
        ),
        in_specs=[any_space, any_space, vmem, any_space, any_space],
        out_specs=(vmem, any_space, any_space, vmem, vmem),
        scratch_shapes=[
            pltpu.VMEM(w_in.shape, BF16),
            pltpu.VMEM(w_down.shape, BF16),
            pltpu.VMEM(rows.shape, BF16),
            pltpu.VMEM(gates.shape, F32),
            pltpu.VMEM((count * cap, depth), BF16),
            pltpu.VMEM((count * cap, depth), BF16),
            pltpu.VMEM((count * cap, FF), BF16),
            pltpu.VMEM((count * cap, 2 * FF), BF16),
            pltpu.VMEM(rows.shape, BF16),
            pltpu.VMEM(gates.shape, F32),
            pltpu.VMEM(half_in.shape, BF16),
            pltpu.VMEM(half_down.shape, BF16),
            pltpu.VMEM(half_in.shape, BF16),
            pltpu.VMEM(half_down.shape, BF16),
        ]
        + [dma((count,))] * 8
        + [dma((2,)), dma((2,)), dma((4,))],
        compiler_params=pltpu.CompilerParams(
            collective_id=2, has_side_effects=True, vmem_limit_bytes=60 * 2**20
        ),
        name="experts",
    )(rows, gates, grads, w_in, w_down)


def add_rows(total, part, rows):
    slab = 16

    @pl.loop(0, rows // slab)
    def _(i):
        at = pl.ds(pl.multiple_of(i * slab, slab), slab)
        total[at, :] = (total[at, :].astype(F32) + part[at, :].astype(F32)).astype(BF16)


class Chain:
    def __init__(self, layers, z, above, below, own, rows, up, down, sems, sends):
        self.layers, self.z, self.above, self.below = layers, z, above, below
        self.own, self.rows, self.up, self.down = own, rows, up, down
        self.sems, self.sends = sems, sends
        self.parts = sems.shape[2]
        self.width = up.shape[2] // self.parts

    def columns(self, ref, h):
        return ref.at[:, pl.ds(h * self.width, self.width)]

    def rise(self, d, h):
        return remote(
            self.columns(self.own(d), h),
            self.columns(self.up.at[d], h),
            self.sends.at[0, d, h],
            self.sems.at[0, d, h],
            self.above,
        )

    def fall(self, d, h):
        return remote(
            self.columns(self.own(d), h),
            self.columns(self.down.at[d], h),
            self.sends.at[1, d, h],
            self.sems.at[1, d, h],
            self.below,
        )

    def end(self, step):
        for h in range(self.parts):
            pl.when(self.z == 0)(self.rise(self.layers - 1 - step, h).start)
            pl.when(self.z == self.layers - 1)(self.fall(step, h).start)

    def ends(self):
        for step in range(self.layers - 1):
            self.end(step)

    def add(self, d, h, buffer):
        add_rows(self.columns(self.own(d), h), self.columns(buffer.at[d], h), self.rows)

    def middle(self):
        z, last = self.z, self.layers - 1

        def pass_on(make, d, buffer):
            for h in range(self.parts):
                copy = make(d, h)
                copy.wait_recv()
                self.add(d, h, buffer)
                copy.start()

        def both(first_half):
            for step in range(last):
                high, low = last - step, step

                def upward(high=high):
                    pl.when((z > 0) & (z < high))(lambda: pass_on(self.rise, high, self.up))

                def downward(low=low):
                    pl.when((z < last) & (z > low))(lambda: pass_on(self.fall, low, self.down))

                for turn in (upward, downward) if first_half else (downward, upward):
                    turn()

        pl.when(z <= last // 2)(lambda: both(True))
        pl.when(z > last // 2)(lambda: both(False))

    def finish(self):
        z, last = self.z, self.layers - 1

        def take(make, buffer):
            for h in range(self.parts):
                make(z, h).wait_recv()
                self.add(z, h, buffer)

        pl.when(z > 0)(lambda: take(self.rise, self.up))
        pl.when(z < last)(lambda: take(self.fall, self.down))

    def wait_sends(self):
        for d in range(self.layers):
            for h in range(self.parts):
                pl.when(self.z < d)(self.rise(d, h).wait_send)
                pl.when(self.z > d)(self.fall(d, h).wait_send)


def finish_kernel(
    layers,
    grad_kv_ref,
    grad_q_ref,
    first_ref,
    tokens_ref,
    gain_ref,
    middle_ref,
    w_all_ref,
    attended_ref,
    second_ref,
    logits_ref,
    gain_moe_ref,
    in_ref,
    down_ref,
    d_tokens_ref,
    d_qkv_ref,
    d_out_ref,
    d_aux_ref,
    got_in_ref,
    got_down_ref,
    weights,
    projected,
    grad_first,
    kv_own,
    kv_pair,
    kv_up,
    kv_down,
    late_both,
    late_pair,
    late_near,
    late_up,
    late_down,
    q_both,
    q_pair,
    q_near,
    q_up,
    q_down,
    k_both,
    k_pair,
    k_near,
    k_up,
    k_down,
    load_sem,
    kv_pair_sem,
    kv_pair_send,
    kv_sem,
    kv_send,
    half_sem,
    half_send,
    pair_sem,
    pair_send,
    near_sem,
    near_send,
    line_sem,
    line_send,
):
    z, core, exp = lax.axis_index("le"), lax.axis_index("core"), lax.axis_index("exp")
    other = 1 - core
    partner = place(z, other, exp)
    above, below = place(z + 1, core, exp), place(z - 1, core, exp)
    x, y = x_of(exp), y_of(exp)
    mates = (x, y, y_of(x))
    own_layer, mate, farthest, middle = near_to_far(z)
    ctx = z * 2 + core
    rows = d_qkv_ref.shape[0]
    count = tokens_ref.shape[0]
    head_cols = HEADS * HEAD
    qkv_cols = d_qkv_ref.shape[1]
    kv_cols = qkv_cols - head_cols

    loads = []

    def load(src, dst):
        copy = pltpu.make_async_copy(src, dst, load_sem.at[len(loads)])
        copy.start()
        loads.append(copy)
        return copy

    kv_loads = [
        load(grad_kv_ref.at[pl.ds(pl.multiple_of((d * 2 + core) * count, 16), count), :], kv_own.at[d])
        for d in range(layers)
    ]
    depth = w_all_ref.shape[0]

    def weights_part(i):
        part = w_all_ref.at[pl.ds(i * depth // 2, depth // 2), pl.ds(0, qkv_cols)]
        return pltpu.make_async_copy(part, weights, load_sem.at[2 * layers + 2])

    weights_part(0).start()
    meet(
        [
            place((z + s) % layers, (core + p) % 2, exp)
            for s in range(layers)
            for p in range(2)
            if s + p > 0
        ]
        + [place(z, core, mate) for mate in mates]
    )
    started = []

    def go(copy):
        copy.start()
        started.append(copy)

    arrays = ((in_ref, got_in_ref), (down_ref, got_down_ref))

    def mine(a, owner):
        n = arrays[a][1].shape[1]
        return arrays[a][0].at[pl.ds(owner * n, n), :]

    def half(a, expert, p):
        cols = arrays[a][0].shape[1]
        return arrays[a][1].at[expert, :, pl.ds(pl.multiple_of(p * cols, 128), cols)]

    for a in range(2):
        load(mine(a, ctx), half(a, z, core))

    def hand_back(a, early):
        for s, zz in enumerate([mate, farthest, middle, own_layer]):
            across = between(z, zz)
            for p in range(2):
                if s == layers - 1 and p == 0:
                    continue
                pp = (core + p) % 2
                copy = remote(
                    mine(a, zz * 2 + pp),
                    half(a, z, core),
                    half_send.at[a, s * 2 + p],
                    half_sem.at[a, ctx],
                    place(zz, pp, exp),
                )
                if early:
                    pl.when(across)(copy.start)
                else:
                    pl.when(~across)(copy.start)
                    started.append(copy)

    hand_back(0, True)

    for d in range(layers):
        go(
            remote(
                grad_kv_ref.at[pl.ds(pl.multiple_of((d * 2 + other) * count, 16), count), :],
                kv_pair.at[d],
                kv_pair_send.at[d],
                kv_pair_sem.at[d],
                partner,
            )
        )
    kv_line = Chain(
        layers, z, above, below, lambda d: kv_own.at[d], count, kv_up, kv_down, kv_sem, kv_send
    )
    for copy in kv_loads:
        copy.wait()
    for k in range(layers):
        d = jnp.where(z < layers // 2, layers - 1 - k, k)
        remote(kv_pair.at[d], kv_pair.at[d], kv_pair_send.at[d], kv_pair_sem.at[d], partner).wait_recv()
        add_rows(kv_own.at[d], kv_pair.at[d], count)
        if k < layers - 1:
            kv_line.end(k)

    def near_copy(i, near, own, d, m, target):
        return remote(
            own.at[d, pl.ds(pl.multiple_of(target * rows, 16), rows), :],
            near.at[m, d],
            near_send.at[i, m, d],
            near_sem.at[i, m, d],
            place(z, core, mates[m]),
        )

    def pair_sums(i, own, pair, near):
        for d in range(layers):
            remote(pair.at[d], pair.at[d], pair_send.at[i, d], pair_sem.at[i, d], partner).wait_recv()
            add_rows(own.at[d], pair.at[d], 4 * rows)
            for m in range(3):
                go(near_copy(i, near, own, d, m, mates[m]))

    def near_sums(i, own, near):
        for d in range(layers):
            for m in range(3):
                near_copy(i, near, own, d, m, exp).wait_recv()
            mine = own.at[d, pl.ds(pl.multiple_of(exp * rows, 16), rows), :]

            @pl.loop(0, rows // 16)
            def _(r, mine=mine, d=d):
                at = pl.ds(pl.multiple_of(r * 16, 16), 16)
                total = mine[at, :].astype(F32)
                for m in range(3):
                    total = total + near[m, d, at, :].astype(F32)
                mine[at, :] = total.astype(BF16)

    def line_of(i, own, up, down):
        return Chain(
            layers,
            z,
            above,
            below,
            lambda d: own.at[d, pl.ds(pl.multiple_of(exp * rows, 16), rows), :],
            rows,
            up,
            down,
            line_sem.at[i],
            line_send.at[i],
        )

    def outer_product(both, cols, left, right, gains=None):
        for d in range(layers):
            block = left[:, d * 8 * rows : (d + 1) * 8 * rows]
            part = dot(block, right, ((0,), (0,)))
            if gains is not None:
                turned = [
                    jnp.transpose(jnp.broadcast_to(gains[:, at : at + 128], (128, 128)))
                    for at in range(d * 8 * rows, (d + 1) * 8 * rows, 128)
                ]
                lane = lax.broadcasted_iota(jnp.int32, part.shape, 1)
                part = jnp.where(lane == 0, jnp.concatenate(turned, axis=0), part)
            part = part.astype(BF16)
            both[0, d, :, cols] = part[: 4 * rows]
            both[1, d, :, cols] = part[4 * rows :]

    def pair_up(i, both, pair):
        for d in range(layers):
            go(remote(both.at[other, d], pair.at[d], pair_send.at[i, d], pair_sem.at[i, d], partner))

    outer_product(q_both, slice(0, head_cols), first_ref, grad_q_ref[...])
    pair_up(1, q_both, q_pair)
    width = middle_ref.shape[1]
    outer_product(late_both, slice(0, width), attended_ref, middle_ref[...].astype(BF16))
    outer_product(late_both, slice(width, width + AUX), second_ref, logits_ref[...], gain_moe_ref[...])
    pair_up(0, late_both, late_pair)
    late_own = late_both.at[core]
    q_own = q_both.at[core]
    pair_sums(1, q_own, q_pair, q_near)
    pair_sums(0, late_own, late_pair, late_near)
    kv_line.middle()
    hand_back(0, False)
    hand_back(1, True)
    hand_back(1, False)
    kv_line.finish()

    projected[:, :head_cols] = grad_q_ref[...]
    projected[:, head_cols:] = kv_own[z]
    outer_product(k_both, slice(0, kv_cols), first_ref, projected[:, head_cols:])
    tile = 256
    for i in range(2):
        weights_part(i).wait()

        @pl.loop(0, depth // 2 // tile)
        def _(j, i=i):
            at = pl.ds(pl.multiple_of(j * tile, tile), tile)
            to = pl.ds(pl.multiple_of(i * depth // 2 + j * tile, tile), tile)
            grad_first[:, to] = dot(projected[...], weights[at, :], ((1,), (1,)))

        if i == 0:
            weights_part(1).start()

    inputs = tokens_ref[...].astype(F32)
    scale = norm_scale(inputs)
    norm = inputs * scale
    grad = grad_first[...]
    grad_gain = jnp.sum(grad * norm, axis=0, keepdims=True)
    for d in range(layers):
        block = jnp.concatenate(
            [
                jnp.transpose(jnp.broadcast_to(grad_gain[:, at : at + 128], (128, 128)))
                for at in range(d * 8 * rows, (d + 1) * 8 * rows, 128)
            ],
            axis=0,
        ).astype(BF16)
        k_both[0, d, :, kv_cols:] = block[: 4 * rows]
        k_both[1, d, :, kv_cols:] = block[4 * rows :]
    pair_up(2, k_both, k_pair)
    grad = grad * gain_ref[...]
    d_tokens_ref[...] = (
        middle_ref[...] + scale * (grad - norm * jnp.mean(grad * norm, axis=-1, keepdims=True))
    ).astype(BF16)
    k_own = k_both.at[core]
    pair_sums(2, k_own, k_pair, k_near)

    late_line = line_of(0, late_own, late_up, late_down)
    q_line = line_of(1, q_own, q_up, q_down)
    k_line = line_of(2, k_own, k_up, k_down)
    near_sums(1, q_own, q_near)
    q_line.ends()
    near_sums(0, late_own, late_near)
    late_line.ends()
    q_line.middle()
    near_sums(2, k_own, k_near)
    k_line.ends()
    late_line.middle()
    k_line.middle()
    mine_rows = pl.ds(pl.multiple_of(exp * rows, 16), rows)
    q_line.finish()
    d_qkv_ref[:, :head_cols] = q_both[core, z, mine_rows, :].astype(F32)
    late_line.finish()
    last = late_both[core, z, mine_rows, :].astype(F32)
    d_out_ref[...] = last[:, :width]
    d_aux_ref[:, AUX:] = last[:, width:]
    k_line.finish()
    last = k_both[core, z, mine_rows, :].astype(F32)
    d_qkv_ref[:, head_cols:] = last[:, :kv_cols]
    d_aux_ref[:, :AUX] = last[:, kv_cols:]

    for source in range(2 * layers):
        for a in range(2):

            @pl.when(source != ctx)
            def _(source=source, a=a):
                remote(
                    half(a, source // 2, source % 2),
                    half(a, source // 2, source % 2),
                    half_send.at[a, 0],
                    half_sem.at[a, source],
                    partner,
                ).wait_recv()

    for copy in loads[-2:]:
        copy.wait()
    for line in (kv_line, late_line, q_line, k_line):
        line.wait_sends()
    for copy in started:
        copy.wait_send()


def finish(
    grad_kv,
    grad_q,
    first,
    tokens,
    gain,
    middle,
    w_all,
    attended,
    second,
    grad_logits,
    gain_moe,
    grad_in,
    grad_down,
    layers,
):
    depth, count = first.shape[1], first.shape[0]
    rows = depth // (8 * layers)
    qkv_cols = grad_q.shape[1] + grad_kv.shape[1]
    n_in, n_down = grad_in.shape[0] // (2 * layers), grad_down.shape[0] // (2 * layers)
    any_space = pl.BlockSpec(memory_space=pl.ANY)
    vmem = pl.BlockSpec(memory_space=pltpu.VMEM)
    dma = pltpu.SemaphoreType.DMA

    def sums(cols):
        return [
            pltpu.VMEM((2, layers, 4 * rows, cols), BF16),
            pltpu.VMEM((layers, 4 * rows, cols), BF16),
            pltpu.VMEM((3, layers, rows, cols), BF16),
            pltpu.VMEM((layers, rows, cols), BF16),
            pltpu.VMEM((layers, rows, cols), BF16),
        ]

    return pl.pallas_call(
        functools.partial(finish_kernel, layers),
        out_shape=(
            jax.ShapeDtypeStruct((count, depth), BF16),
            jax.ShapeDtypeStruct((rows, qkv_cols), F32),
            jax.ShapeDtypeStruct((rows, depth), F32),
            jax.ShapeDtypeStruct((rows, 2 * AUX), F32),
            jax.ShapeDtypeStruct((layers, n_in, 2 * grad_in.shape[1]), BF16),
            jax.ShapeDtypeStruct((layers, n_down, 2 * grad_down.shape[1]), BF16),
        ),
        in_specs=[any_space] + [vmem] * 5 + [any_space] + [vmem] * 4 + [any_space] * 2,
        out_specs=(vmem,) * 4 + (any_space,) * 2,
        scratch_shapes=[
            pltpu.VMEM((depth // 2, qkv_cols), BF16),
            pltpu.VMEM((count, qkv_cols), BF16),
            pltpu.VMEM((count, depth), F32),
        ]
        + [pltpu.VMEM((layers, count, grad_kv.shape[1]), BF16)] * 4
        + sums(depth + AUX)
        + sums(grad_q.shape[1])
        + sums(grad_kv.shape[1] + AUX)
        + [
            dma((2 * layers + 3,)),
            dma((layers,)),
            dma((layers,)),
            dma((2, layers, 2)),
            dma((2, layers, 2)),
            dma((2, 2 * layers)),
            dma((2, 2 * layers)),
            dma((3, layers)),
            dma((3, layers)),
            dma((3, 3, layers)),
            dma((3, 3, layers)),
            dma((3, 2, layers, 1)),
            dma((3, 2, layers, 1)),
        ],
        compiler_params=pltpu.CompilerParams(
            collective_id=1, has_side_effects=True, vmem_limit_bytes=60 * 2**20
        ),
        name="finish",
    )(
        grad_kv,
        grad_q,
        first,
        tokens,
        gain,
        middle,
        w_all,
        attended,
        second,
        grad_logits,
        gain_moe,
        grad_in,
        grad_down,
    )


def settle_kernel(count, base_ref, gates_ref, target_ref, returned_ref, aux_ref, *refs):
    block_ref, refs = refs[count], refs[:count] + refs[count + 1 :]
    total = base_ref[...]
    slot = lax.broadcasted_iota(jnp.int32, (total.shape[0], returned_ref.shape[0]), 1)
    for k in range(2):
        pick = jnp.where(target_ref[:, k : k + 1] == slot, 1.0, 0.0).astype(BF16)
        total = total + gates_ref[:, k : k + 1] * dot(pick, returned_ref[...])
    block_ref[...] = total.astype(BF16)
    for src, dst in zip(refs[:count], refs[count : 2 * count]):
        dst[...] = src[...].astype(dst.dtype)
    rows = aux_ref.shape[0]
    eye = lax.broadcasted_iota(jnp.int32, (rows, 128), 0) == lax.broadcasted_iota(jnp.int32, (rows, 128), 1)
    for at, dst in zip((0, AUX), refs[2 * count :]):
        line = jnp.sum(jnp.where(eye, aux_ref[:, at : at + 1], 0.0), axis=0, keepdims=True)
        dst[...] = line[:, :rows]
    block = jnp.concatenate([aux_ref[:, AUX:], jnp.zeros((128 - rows, AUX), F32)], axis=0)
    refs[-1][...] = jnp.transpose(block)[1 : 1 + EXPERTS, :rows]


def settle(base, gates, target, returned, aux, arrays, steps):
    def spec(array):
        if array.ndim == 2 and array.shape[0] % (16 * steps) == 0:
            return pl.BlockSpec((array.shape[0] // steps, array.shape[1]), lambda i: (i, 0))
        if array.ndim == 3 and array.shape[1] % (16 * steps) == 0:
            return pl.BlockSpec(
                (array.shape[0], array.shape[1] // steps, array.shape[2]), lambda i: (0, i, 0)
            )
        return pl.BlockSpec(array.shape, lambda i: (0,) * array.ndim)

    specs = [spec(array) for array, _ in arrays]
    rows = aux.shape[0]
    small = [jax.ShapeDtypeStruct(shape, F32) for shape in ((1, rows), (1, rows), (EXPERTS, rows))]
    return pl.pallas_call(
        functools.partial(settle_kernel, len(arrays)),
        grid=(steps,),
        out_shape=[jax.ShapeDtypeStruct(base.shape, BF16)]
        + [jax.ShapeDtypeStruct(array.shape, dtype) for array, dtype in arrays]
        + small,
        in_specs=[
            spec(base),
            spec(gates),
            spec(target),
            pl.BlockSpec(returned.shape, lambda i: (0, 0)),
            spec(aux),
        ]
        + specs,
        out_specs=[spec(base)] + specs + [spec(shape) for shape in small],
        compiler_params=pltpu.CompilerParams(vmem_limit_bytes=60 * 2**20),
        name="settle",
    )(base, gates, target, returned, aux, *[array for array, _ in arrays])


CTX = ("le", "rep", "core")
ALL = ("le", "rep", "core", "exp")
OWNERS = ("exp", "le")


def on_device(
    tokens,
    cotangent,
    routes,
    lengths,
    block_order,
    gain_attn,
    qkv_weight,
    out_weight,
    gain_moe,
    router_weight,
    expert_in,
    expert_out,
):
    tok_rows = tokens.shape[1]
    head_width = HEADS * HEAD
    exp_local = expert_in.shape[0]
    n_ctx = D // expert_in.shape[1]
    copies = n_ctx // exp_local
    n_exp = EXPERTS // exp_local
    in_rows, out_rows = expert_in.shape[1], expert_out.shape[1]

    route_hot = (
        routes[0][:, :, None] == jnp.arange(EXPERTS, dtype=jnp.int32)[None, None, :]
    ).astype(F32)
    flat_hot = route_hot.reshape(tok_rows * 2, EXPERTS).astype(BF16)
    order = jnp.arange(tok_rows * 2, dtype=jnp.int32)
    earlier = (order[:, None] > order[None, :]).astype(BF16)
    ranks = dot(earlier, flat_hot)
    slot_index = jnp.sum(ranks * flat_hot.astype(F32), axis=1).astype(jnp.int32)
    target = (routes[0].reshape(tok_rows * 2) * CAP + slot_index).reshape(tok_rows, 2)
    slots = jnp.arange(EXPERTS * CAP, dtype=jnp.int32)
    picks = [(target[:, k : k + 1] == slots[None, :]) for k in range(2)]
    sends = [(target[:, k][None, :] == slots[:, None]) for k in range(2)]
    send_hot = (sends[0] | sends[1]).astype(BF16)

    def to_experts(rows):
        return lax.all_to_all(
            rows.reshape((EXPERTS, CAP) + rows.shape[1:]),
            OWNERS,
            split_axis=0,
            concat_axis=0,
            tiled=True,
        ).reshape(rows.shape)

    cols = qkv_weight.shape[1]
    aux = jnp.concatenate([gain_attn[:, None], gain_moe[:, None], router_weight], axis=1)
    aux = jnp.pad(aux, ((0, 0), (0, AUX - aux.shape[1])))
    shard = jnp.concatenate([qkv_weight, aux, out_weight], axis=1).astype(BF16)
    special = (copies, exp_local, n_exp) == (2, 4, 4)
    if special:
        (
            w_all,
            w_in,
            w_down,
            first,
            projected,
            kv,
            exact,
            attended,
            lse,
            middle,
            second,
            gates,
            slot_gates,
            second_rows,
            grad_y_rows,
        ) = front(
            shard,
            expert_in,
            expert_out,
            tokens[0],
            lengths,
            block_order,
            jnp.concatenate([target, routes[0]], axis=1).T,
            cotangent[0],
            cols,
        )
        gates = gates[:, :2]
    else:
        w_all = lax.all_gather(shard, ALL, axis=0, tiled=True)

        def to_owner(weight):
            rows, width = weight.shape[1:]
            halves = weight.astype(BF16).reshape(exp_local, rows, 2, width // 2).transpose(0, 2, 1, 3)
            halves = jnp.broadcast_to(
                halves[:, None], (exp_local, copies // 2, 2, rows, width // 2)
            ).reshape(n_ctx, rows, width // 2)
            mine = lax.all_to_all(halves, CTX, split_axis=0, concat_axis=0, tiled=True)
            return lax.all_gather(mine.reshape(n_ctx * rows, width // 2), "core", axis=1, tiled=True)

        w_in = to_owner(expert_in)
        w_down = to_owner(expert_out)
    w_qkv = w_all[:, :cols]
    aux_all = w_all[:, cols : cols + AUX]
    w_attn_out = w_all[:, cols + AUX :]
    gain_first = aux_all[:, 0].astype(F32)
    gain_second = aux_all[:, 1].astype(F32)
    w_router = aux_all[:, 2 : 2 + EXPERTS]

    inputs = tokens[0].astype(F32)
    scale_first = norm_scale(inputs)
    norm_first = inputs * scale_first
    mine = (lax.axis_index(CTX) * (tok_rows // BLK)).astype(jnp.int32).reshape(1)
    if not special:
        first = (norm_first * gain_first).astype(BF16)
        projected = dot(first, w_qkv).astype(BF16)
        kv = lax.all_gather(projected[:, head_width:], CTX, axis=0, tiled=True)
        kv, grad_y_send = lax.optimization_barrier((kv, dot(send_hot, cotangent[0]).astype(BF16)))
        grad_y_rows = to_experts(grad_y_send)
        exact, attended, lse = attend(lengths, block_order, mine, projected, kv)
        middle = inputs + dot(attended, w_attn_out)
    scale_second = norm_scale(middle)
    norm_second = middle * scale_second
    if not special:
        second = (norm_second * gain_second).astype(BF16)
        logits = dot(second, w_router)
        chosen = jnp.sum(route_hot * logits[:, None, :], axis=-1)
        gates = jax.nn.softmax(chosen, axis=-1)

    if special:
        expert_rows, grad_returned, gate_grads, grad_in, grad_down = experts(
            second_rows,
            slot_gates,
            grad_y_rows,
            w_in,
            w_down,
            exp_local,
        )
        returned = to_experts(expert_rows.reshape(EXPERTS * CAP, D))
        grad_returned = grad_returned.reshape(EXPERTS * CAP, D)
        gate_grads = gate_grads[:, 0, :CAP].reshape(1, EXPERTS * CAP)
    else:
        gate_rows = jnp.sum(
            jnp.where(sends[0], gates[:, 0][None, :], 0.0) + jnp.where(sends[1], gates[:, 1][None, :], 0.0),
            axis=1,
            keepdims=True,
        )

        def in_parts(column):
            high = lax.reduce_precision(column, 8, 7)
            rest = column - high
            mid = lax.reduce_precision(rest, 8, 7)
            parts = jnp.concatenate([high, mid, rest - mid], axis=1).astype(BF16)
            return jnp.pad(parts, ((0, 0), (0, AUX - 3)))

        gate_parts = in_parts(gate_rows)
        payload = to_experts(
            jnp.concatenate([dot(send_hot, second).astype(BF16), gate_parts], axis=1)
        )
        received = payload[:, :D]
        gate_got = jnp.sum(payload[:, D : D + 3].astype(F32), axis=1, keepdims=True)

        gate_up = dot(received, w_in)
        gate_part = gate_up[:, :FF]
        up_part = gate_up[:, FF:]
        sigmoid_gate = jax.nn.sigmoid(gate_part)
        silu_gate = gate_part * sigmoid_gate
        hidden = (silu_gate * up_part).astype(BF16)
        expert_rows = dot(hidden, w_down)
        expert_rows = expert_rows.astype(BF16)
        grad_y_rows = grad_y_rows.astype(F32)
        returned = to_experts(expert_rows)

        grad_rows = (gate_got * grad_y_rows).astype(BF16)
        gate_grad_parts = in_parts(
            jnp.sum(grad_y_rows * expert_rows.astype(F32), axis=1, keepdims=True)
        )
        half_d = D // 2
        grad_hidden = dot(grad_rows, w_down, ((1,), (1,)))
        grad_gate = (
            grad_hidden * up_part * sigmoid_gate * (1.0 + gate_part * (1.0 - sigmoid_gate))
        ).astype(BF16)
        grad_up = (grad_hidden * silu_gate).astype(BF16)
        grad_gate_up = jnp.concatenate([grad_gate, grad_up], axis=1)
        grad_back = dot(grad_gate_up, w_in, ((1,), (1,)))
        grad_returned = to_experts(jnp.concatenate([grad_back.astype(BF16), gate_grad_parts], axis=1))

        grad_in = jnp.stack(
            [dot(received, grad_gate, ((0,), (0,))), dot(received, grad_up, ((0,), (0,)))]
        ).astype(BF16)
        grad_down = jnp.stack(
            [
                dot(hidden, grad_rows[:, :half_d], ((0,), (0,))),
                dot(hidden, grad_rows[:, half_d:], ((0,), (0,))),
            ]
        ).astype(BF16)

        grad_in = lax.psum_scatter(grad_in, "core", scatter_dimension=0, tiled=True)[0]
        grad_down = lax.psum_scatter(grad_down, "core", scatter_dimension=0, tiled=True)[0]
        grad_returned, grad_in, grad_down = lax.optimization_barrier((grad_returned, grad_in, grad_down))
        gate_grads = jnp.sum(grad_returned[:, D:].astype(F32), axis=1).reshape(1, EXPERTS * CAP)
        grad_returned = grad_returned[:, :D]

    grad_y = cotangent[0].astype(F32)
    pick_hot = [p.astype(BF16) for p in picks]
    grad_gates = jnp.concatenate(
        [jnp.sum(jnp.where(p, gate_grads, 0.0), axis=1, keepdims=True) for p in picks], axis=1
    )
    grad_chosen = gates * (grad_gates - jnp.sum(gates * grad_gates, axis=-1, keepdims=True))
    grad_logits = jnp.sum(grad_chosen[:, :, None] * route_hot, axis=1).astype(BF16)
    grad_second = dot(pick_hot[0] + pick_hot[1], grad_returned) + dot(
        grad_logits, w_router, ((1,), (1,))
    )
    grad_gain_second = jnp.sum(grad_second * norm_second, axis=0)
    grad_norm_second = grad_second * gain_second
    grad_middle = grad_y + scale_second * (
        grad_norm_second
        - norm_second * jnp.mean(grad_norm_second * norm_second, axis=-1, keepdims=True)
    )
    grad_branch = grad_middle.astype(BF16)
    grad_attended = dot(grad_branch, w_attn_out, ((1,), (1,))).astype(BF16)
    grad_queries, grad_kv = attend_back(
        lengths, block_order, mine, projected, kv, grad_attended, lse, exact
    )
    if special:
        grad_inputs, sum_qkv, sum_out, sum_aux, sum_in, sum_down = finish(
            grad_kv,
            grad_queries,
            first,
            tokens[0],
            gain_first[None, :],
            grad_middle,
            w_all,
            attended,
            second,
            jnp.pad(grad_logits, ((0, 0), (1, AUX - 1 - EXPERTS))),
            grad_gain_second[None, :],
            grad_in,
            grad_down,
            exp_local,
        )
        block_out, grad_inputs, sum_qkv, sum_out, sum_in, sum_down, gain_a, gain_m, sum_router = settle(
            middle,
            gates,
            target,
            returned,
            sum_aux,
            (
                (grad_inputs, BF16),
                (sum_qkv, F32),
                (sum_out, F32),
                (sum_in, F32),
                (sum_down, F32),
            ),
            4,
        )
        gain_a, gain_m, sum_router = gain_a[0], gain_m[0], sum_router.T
    else:
        grad_router = dot(second, grad_logits, ((0,), (0,)))
        grad_attn_out = dot(attended, grad_branch, ((0,), (0,)))
        late = jnp.concatenate([grad_gain_second[:, None], grad_router], axis=1)
        late = jnp.pad(late, ((0, 0), (0, AUX - late.shape[1])))
        late = jnp.concatenate([grad_attn_out.astype(BF16), late.astype(BF16)], axis=1)
        grad_kv = lax.psum_scatter(grad_kv, CTX, scatter_dimension=0, tiled=True)
        grad_projected = jnp.concatenate([grad_queries, grad_kv], axis=1)
        grad_qkv = dot(first, grad_projected, ((0,), (0,)))
        grad_first = dot(grad_projected, w_qkv, ((1,), (1,)))
        grad_gain_first = jnp.sum(grad_first * norm_first, axis=0)
        grad_norm_first = grad_first * gain_first
        grad_inputs = grad_middle + scale_first * (
            grad_norm_first
            - norm_first * jnp.mean(grad_norm_first * norm_first, axis=-1, keepdims=True)
        )
        grad_inputs = grad_inputs.astype(BF16)
        last = jnp.pad(grad_gain_first[:, None], ((0, 0), (0, AUX - 1)))
        part = jnp.concatenate([grad_qkv.astype(BF16), last.astype(BF16), late], axis=1)
        total = lax.psum_scatter(part, ALL, scatter_dimension=0, tiled=True).astype(F32)
        sum_qkv, sum_out = total[:, :cols], total[:, cols + AUX : cols + AUX + D]
        gain_a, gain_m = total[:, cols], total[:, cols + AUX + D]
        sum_router = total[:, cols + AUX + D + 1 : cols + AUX + D + 1 + EXPERTS]
        picked = [dot(p, returned) for p in pick_hot]
        block_out = (middle + gates[:, 0:1] * picked[0] + gates[:, 1:2] * picked[1]).astype(BF16)

        def to_rows(half, rows):
            width = half.shape[1]
            got = lax.all_to_all(
                half.reshape(n_ctx, rows, width), CTX, split_axis=0, concat_axis=0, tiled=True
            ).astype(F32)
            got = got.reshape(exp_local, copies // 2, 2, rows, width).sum(axis=1)
            return got.transpose(0, 2, 1, 3).reshape(exp_local, rows, 2 * width)

        sum_in = to_rows(grad_in, in_rows)
        sum_down = to_rows(grad_down, out_rows)
    return (
        block_out[None],
        grad_inputs[None],
        gain_a,
        sum_qkv,
        sum_out,
        gain_m,
        sum_router,
        sum_in.astype(F32),
        sum_down.astype(F32),
    )


def solution(mesh):
    n_ctx, n_exp = mesh.shape["ctx"], mesh.shape["exp"]
    exp_local = EXPERTS // n_exp
    copies = n_ctx // exp_local
    inner = Mesh(mesh.devices.reshape(exp_local, copies // 2, 2, n_exp), ALL)
    by_token = P("exp", CTX, None)
    by_row = P(ALL, None)
    by_expert = P("exp", CTX, None)
    return jax.shard_map(
        on_device,
        mesh=inner,
        in_specs=(
            by_token,
            by_token,
            by_token,
            P("exp", None),
            P("exp", None),
            P(ALL),
            by_row,
            by_row,
            P(ALL),
            by_row,
            by_expert,
            by_expert,
        ),
        out_specs=(
            by_token,
            by_token,
            P(ALL),
            by_row,
            by_row,
            P(ALL),
            by_row,
            by_expert,
            by_expert,
        ),
        check_vma=False,
    )
```

```python
import functools

import jax
import jax.numpy as jnp
from jax import lax
from jax.experimental import pallas as pl
from jax.experimental.pallas import tpu as pltpu
from jax.sharding import Mesh
from jax.sharding import PartitionSpec as P

D = 1536
HEADS = 24
KV_HEADS = 8
HEAD = 64
GROUP = HEADS // KV_HEADS
FF = 1024
EXPERTS = 16
BLK = 128
CAP = 48
AUX = 128

epsilon = 1e-05
far_negative = -1e30
start_max = -1e29
F32 = jnp.float32
BF16 = jnp.bfloat16


def norm_scale(values):
    return lax.rsqrt(jnp.mean(values * values, axis=-1, keepdims=True) + epsilon)


def dot(a, b, dims=((1,), (0,))):
    return lax.dot_general(a, b, (dims, ((), ())), preferred_element_type=F32)


def lane_half(shape, half):
    lane = lax.broadcasted_iota(jnp.int32, shape, 1)
    return (lane >= HEAD) if half else (lane < HEAD)


def head_tiles(ref, rows, pair, scale):
    tiles = []
    for i in range(2 * GROUP):
        head = pair * 2 * GROUP + i
        group = head // GROUP
        tile = ref[rows, (head // 2) * 128 : (head // 2 + 1) * 128].astype(F32)
        if head % 2 != group % 2:
            tile = pltpu.roll(tile, HEAD, 1)
        tile = jnp.where(lane_half(tile.shape, group % 2), tile * scale, 0.0)
        tiles.append(tile.astype(BF16))
    return jnp.concatenate(tiles, axis=0)


def block_visibility(lengths_ref, query_block, key_block, parts):
    lanes = lax.broadcasted_iota(jnp.int32, (1, BLK), 1)
    query_pos = query_block * BLK + lanes
    start = jnp.zeros((1, BLK), jnp.int32)
    bound = jnp.int32(0)
    for s in range(parts - 1):
        bound = bound + lengths_ref[0, s]
        start = jnp.where(query_pos >= bound, bound, start)
    key_pos = key_block * BLK + lax.broadcasted_iota(jnp.int32, (BLK, BLK), 0)
    one = ((key_pos >= start) & (key_pos <= query_pos)).astype(jnp.int32)
    return jnp.concatenate([one] * (2 * GROUP), axis=1) > 0


def first_row_start(lengths_ref, query_block, parts):
    start = jnp.int32(0)
    bound = jnp.int32(0)
    for s in range(parts - 1):
        bound = bound + lengths_ref[0, s]
        start = jnp.where(query_block * BLK >= bound, bound, start)
    return start


def attend_blocks(
    parts,
    skip,
    lengths_ref,
    order_ref,
    mine,
    q_ref,
    kv_ref,
    exact_ref,
    out_ref,
    lse_ref,
    q_s,
    m_s,
    sum_s,
    acc_s,
):
    width = KV_HEADS * HEAD
    wide = 2 * GROUP * BLK
    for qb in range(q_ref.shape[0] // BLK):
        rows = pl.ds(qb * BLK, BLK)
        for pair in range(KV_HEADS // 2):
            q_s[pair] = head_tiles(q_ref, rows, pair, HEAD**-0.5)
            m_s[pair] = jnp.full((8, wide), start_max, F32)
            sum_s[pair] = jnp.zeros((8, wide), F32)
            acc_s[pair] = jnp.zeros((BLK, wide), F32)
        query_block = order_ref[0, mine + qb]
        first = first_row_start(lengths_ref, query_block, parts)

        @pl.loop(0, order_ref.shape[1])
        def _(kb):
            key_block = order_ref[0, kb]

            def fold():
                seen = block_visibility(lengths_ref, query_block, key_block, parts)
                key_rows = pl.ds(kb * BLK, BLK)
                for pair in range(KV_HEADS // 2):
                    keys = kv_ref[key_rows, pl.ds(pair * 128, 128)]
                    values = kv_ref[key_rows, pl.ds(width + pair * 128, 128)]
                    scores = dot(keys, q_s[pair], ((1,), (1,)))
                    scores = jnp.where(seen, scores, far_negative)
                    old = m_s[pair, 0:1, :]
                    new = jnp.maximum(old, jnp.max(scores, axis=0, keepdims=True))
                    weights = jnp.exp(scores - new)
                    factor = jnp.exp(old - new)
                    sum_s[pair, 0:1, :] = sum_s[pair, 0:1, :] * factor + jnp.sum(
                        weights, axis=0, keepdims=True
                    )
                    acc_s[pair] = acc_s[pair] * factor + dot(values, weights.astype(BF16), ((0,), (0,)))
                    m_s[pair, 0:1, :] = new

            if skip:
                pl.when((key_block <= query_block) & (key_block * BLK + BLK > first))(fold)
            else:
                fold()

        tiles = []
        for pair in range(KV_HEADS // 2):
            total = sum_s[pair, 0:1, :]
            lse_ref[qb, pair : pair + 1, :] = m_s[pair, 0:1, :] + jnp.log(total)
            acc = acc_s[pair] / total
            for i in range(2 * GROUP):
                head = pair * 2 * GROUP + i
                tile = jnp.transpose(acc[:, i * BLK : (i + 1) * BLK])
                if head % 2 != (head // GROUP) % 2:
                    tile = pltpu.roll(tile, HEAD, 1)
                tiles.append(tile)
                if head % 2 == 1:
                    both = jnp.where(lane_half(tile.shape, 0), tiles[head - 1], tile)
                    lanes = pl.ds((head // 2) * 128, 128)
                    exact_ref[rows, lanes] = both
                    out_ref[rows, lanes] = both.astype(BF16)


def attend_kernel(parts, lengths_ref, order_ref, mine_ref, *refs):
    attend_blocks(parts, True, lengths_ref, order_ref, mine_ref[0], *refs)


def attend(lengths, order, mine, projected, kv):
    rows = projected.shape[0]
    smem = pl.BlockSpec(memory_space=pltpu.SMEM)
    vmem = pl.BlockSpec(memory_space=pltpu.VMEM)
    wide = 2 * GROUP * BLK
    pairs = KV_HEADS // 2
    return pl.pallas_call(
        functools.partial(attend_kernel, lengths.shape[1]),
        out_shape=(
            jax.ShapeDtypeStruct((rows, HEADS * HEAD), F32),
            jax.ShapeDtypeStruct((rows, HEADS * HEAD), BF16),
            jax.ShapeDtypeStruct((rows // BLK, pairs, wide), F32),
        ),
        in_specs=[smem, smem, smem, vmem, vmem],
        out_specs=(vmem, vmem, vmem),
        scratch_shapes=[
            pltpu.VMEM((pairs, wide, 128), BF16),
            pltpu.VMEM((pairs, 8, wide), F32),
            pltpu.VMEM((pairs, 8, wide), F32),
            pltpu.VMEM((pairs, BLK, wide), F32),
        ],
        compiler_params=pltpu.CompilerParams(vmem_limit_bytes=48 * 2**20),
        cost_estimate=pl.CostEstimate(flops=10**10, bytes_accessed=10**7, transcendentals=10**7),
        name="attend",
    )(lengths, order, mine, projected, kv)


def attend_back_kernel(
    parts,
    lengths_ref,
    order_ref,
    mine_ref,
    q_ref,
    kv_ref,
    grad_ref,
    lse_ref,
    exact_ref,
    dq_ref,
    dkv_ref,
    q_s,
    g_s,
    delta_s,
    dq_s,
    dkv_s,
):
    width = KV_HEADS * HEAD

    @pl.loop(0, order_ref.shape[1])
    def _(kb):
        dkv_s[pl.ds(kb * BLK, BLK), :] = jnp.zeros((BLK, 2 * width), F32)

    for qb in range(q_ref.shape[0] // BLK):
        rows = pl.ds(qb * BLK, BLK)
        for pair in range(KV_HEADS // 2):
            q_s[pair] = head_tiles(q_ref, rows, pair, HEAD**-0.5)
            g_s[pair] = head_tiles(grad_ref, rows, pair, 1.0)
            dq_s[pair] = jnp.zeros((2 * GROUP * BLK, 128), F32)
            for i in range(2 * GROUP):
                head = pair * 2 * GROUP + i
                exact = exact_ref[rows, (head // 2) * 128 : (head // 2 + 1) * 128]
                if head % 2 != (head // GROUP) % 2:
                    exact = pltpu.roll(exact, HEAD, 1)
                product = exact * g_s[pair, i * BLK : (i + 1) * BLK, :].astype(F32)
                delta_s[pair : pair + 1, i * BLK : (i + 1) * BLK] = jnp.sum(
                    jnp.transpose(product), axis=0, keepdims=True
                )
        query_block = order_ref[0, mine_ref[0] + qb]
        first = first_row_start(lengths_ref, query_block, parts)

        @pl.loop(0, order_ref.shape[1])
        def _(kb):
            key_block = order_ref[0, kb]

            @pl.when((key_block <= query_block) & (key_block * BLK + BLK > first))
            def _():
                seen = block_visibility(lengths_ref, query_block, key_block, parts)
                key_rows = pl.ds(kb * BLK, BLK)
                for pair in range(KV_HEADS // 2):
                    key_lanes = pl.ds(pair * 128, 128)
                    value_lanes = pl.ds(width + pair * 128, 128)
                    keys = kv_ref[key_rows, key_lanes]
                    values = kv_ref[key_rows, value_lanes]
                    scores = dot(keys, q_s[pair], ((1,), (1,)))
                    scores = jnp.where(seen, scores, far_negative)
                    probs = jnp.exp(scores - lse_ref[qb, pair : pair + 1, :])
                    grad_probs = dot(values, g_s[pair], ((1,), (1,)))
                    grad_scores = (probs * (grad_probs - delta_s[pair : pair + 1, :])).astype(BF16)
                    dkv_s[key_rows, value_lanes] += dot(probs.astype(BF16), g_s[pair])
                    dkv_s[key_rows, key_lanes] += dot(grad_scores, q_s[pair])
                    dq_s[pair] += dot(grad_scores, keys, ((0,), (0,)))

        tiles = []
        for pair in range(KV_HEADS // 2):
            for i in range(2 * GROUP):
                head = pair * 2 * GROUP + i
                tile = dq_s[pair, i * BLK : (i + 1) * BLK, :] * HEAD**-0.5
                if head % 2 != (head // GROUP) % 2:
                    tile = pltpu.roll(tile, HEAD, 1)
                tiles.append(tile)
                if head % 2 == 1:
                    both = jnp.where(lane_half(tile.shape, 0), tiles[head - 1], tile)
                    dq_ref[rows, (head // 2) * 128 : (head // 2 + 1) * 128] = both.astype(BF16)

    @pl.loop(0, order_ref.shape[1])
    def _(kb):
        key_rows = pl.ds(kb * BLK, BLK)
        dkv_ref[key_rows, :] = dkv_s[key_rows, :].astype(BF16)


def attend_back(lengths, order, mine, projected, kv, grad_attended, lse, exact):
    rows = projected.shape[0]
    smem = pl.BlockSpec(memory_space=pltpu.SMEM)
    vmem = pl.BlockSpec(memory_space=pltpu.VMEM)
    wide = 2 * GROUP * BLK
    pairs = KV_HEADS // 2
    return pl.pallas_call(
        functools.partial(attend_back_kernel, lengths.shape[1]),
        out_shape=(
            jax.ShapeDtypeStruct((rows, HEADS * HEAD), BF16),
            jax.ShapeDtypeStruct(kv.shape, BF16),
        ),
        in_specs=[smem, smem, smem, vmem, vmem, vmem, vmem, vmem],
        out_specs=(vmem, vmem),
        scratch_shapes=[
            pltpu.VMEM((pairs, wide, 128), BF16),
            pltpu.VMEM((pairs, wide, 128), BF16),
            pltpu.VMEM((pairs, wide), F32),
            pltpu.VMEM((pairs, wide, 128), F32),
            pltpu.VMEM(kv.shape, F32),
        ],
        compiler_params=pltpu.CompilerParams(vmem_limit_bytes=56 * 2**20),
        cost_estimate=pl.CostEstimate(flops=10**9, bytes_accessed=10**6, transcendentals=10**5),
        name="attend_back",
    )(lengths, order, mine, projected, kv, grad_attended, lse, exact)


MESH = pl.DeviceIdType.MESH


def place(z, core, exp):
    return {"le": z, "rep": 0, "core": core, "exp": exp}


def x_of(exp):
    return (exp // 2) * 2 + 1 - exp % 2


def y_of(exp):
    return (1 - exp // 2) * 2 + exp % 2


def remote(src, dst, send_sem, recv_sem, device):
    return pltpu.make_async_remote_copy(
        src_ref=src,
        dst_ref=dst,
        send_sem=send_sem,
        recv_sem=recv_sem,
        device_id=device,
        device_id_type=MESH,
    )


def near_to_far(z):
    first_half = z < 2
    return [z, z + 1 - 2 * (z % 2), jnp.where(first_half, 3, 0), jnp.where(first_half, 2, 1)]


def between(z, zz):
    return ((z == 1) & (zz == 2)) | ((z == 2) & (zz == 1))


def meet(devices):
    barrier = pltpu.get_barrier_semaphore()
    for device in devices:
        pl.semaphore_signal(barrier, inc=1, device_id=device, device_id_type=MESH)
    pl.semaphore_wait(barrier, len(devices))


def front_kernel(
    layers,
    shard_ref,
    in_ref,
    down_ref,
    tokens_ref,
    lengths_ref,
    order_ref,
    target_ref,
    cotangent_ref,
    w_all_ref,
    w_in_ref,
    w_down_ref,
    first_ref,
    projected_ref,
    kv_ref,
    exact_ref,
    attended_ref,
    lse_ref,
    middle_ref,
    second_ref,
    gates_ref,
    slot_gates_ref,
    gains_ref,
    rows_ref,
    got_grads_ref,
    hot_s,
    grads_s,
    weights,
    kv_s,
    q_s,
    m_s,
    sum_s,
    acc_s,
    in_wide,
    down_wide,
    in_half,
    down_half,
    unit_sem,
    line_sem,
    x_sem,
    y_sem,
    far_sem,
    core_sem,
    half_sem,
    half_send,
    over_sem,
    over_send,
    kv_sem,
    kv_send,
    own_sem,
    wide_sem,
    grad_sem,
    grad_send,
):
    z, core, exp = lax.axis_index("le"), lax.axis_index("core"), lax.axis_index("exp")
    other = 1 - core
    x, y = x_of(exp), y_of(exp)
    ctx = z * 2 + core
    rows = shard_ref.shape[0]
    own_layer, mate, farthest, middle = near_to_far(z)
    order = [mate, middle, farthest, own_layer]
    wides = ((in_ref, in_wide), (down_ref, down_wide))
    halves = ((in_half, w_in_ref), (down_half, w_down_ref))

    loads = []
    for k, zz in enumerate(order):
        for a in range(2):
            load = pltpu.make_async_copy(wides[a][0].at[zz], wides[a][1].at[zz], wide_sem.at[a, k])
            load.start()
            loads.append(load)
    peers = [
        (zz, (exp + t) % 4)
        for s, zz in enumerate(order)
        for t in range(4)
        if not (s == layers - 1 and t == 0)
    ]
    meet([place(zz, core, ee) for zz, ee in peers] + [place(zz, other, exp) for zz in order])

    def number(zz, cc, ee):
        return (zz * 2 + cc) * 4 + ee

    def unit(zz, cc, ee):
        return weights.at[pl.ds(pl.multiple_of(number(zz, cc, ee) * rows, 16), rows), :]

    def send(src, who, sem, device):
        return remote(src, unit(*who), sem, unit_sem.at[number(*who)], device)

    def arrive(who):
        send(unit(*who), who, line_sem.at[0], place(z, other, exp)).wait_recv()

    started = []

    def go(copy, condition=None):
        if condition is None:
            copy.start()
        else:
            pl.when(condition)(copy.start)
        started.append((copy, condition))

    me = (z, core, exp)
    keep = pltpu.make_async_copy(shard_ref, unit(*me), own_sem.at[0])
    keep.start()
    go(send(shard_ref, me, line_sem.at[layers], place(z + 1, core, exp)), z < layers - 1)
    go(send(shard_ref, me, line_sem.at[layers + 1], place(z - 1, core, exp)), z > 0)
    go(send(shard_ref, me, x_sem.at[layers], place(z, core, x)))
    go(send(shard_ref, me, y_sem.at[layers], place(z, core, y)))
    go(send(shard_ref, me, core_sem.at[layers], place(z, other, exp)))

    slab = 16
    for k, zz in enumerate(order):
        for a in range(2):
            loads[2 * k + a].wait()
            src, dst = wides[a][1], halves[a][0]

            @pl.loop(0, src.shape[1] // slab)
            def _(i, zz=zz, src=src, dst=dst):
                at = pl.ds(pl.multiple_of(i * slab, slab), slab)
                dst[zz, at, :] = src[zz, at, :].astype(BF16)

    def half(a, source, p):
        src, dst = halves[a]
        n, cols = src.shape[1], src.shape[2] // 2
        return dst.at[pl.ds(source * n, n), pl.ds(pl.multiple_of(p * cols, 128), cols)]

    def mine(a, zz, p):
        src = halves[a][0]
        cols = src.shape[2] // 2
        return src.at[zz, :, pl.ds(pl.multiple_of(p * cols, 128), cols)]

    def layer(k):
        return jnp.where(z < layers // 2, k, layers - 1 - k)

    def ahead(zz):
        return between(z, zz)

    def hand_out(a, early):
        for s, zz in enumerate(order):
            across = ahead(zz)
            for p in range(2):
                if s == layers - 1 and p == 0:
                    continue
                pp = (core + p) % 2
                copy = remote(
                    mine(a, zz, pp),
                    half(a, ctx, pp),
                    half_send.at[a, s * 2 + p],
                    half_sem.at[a, ctx],
                    place(zz, pp, exp),
                )
                if early:
                    pl.when(across)(copy.start)
                else:
                    pl.when(~across)(copy.start)
                    started.append((copy, None))
        if not early:
            go(
                remote(
                    mine(a, z, core),
                    half(a, ctx, core),
                    over_send.at[a, 2 * layers],
                    over_sem.at[a, ctx],
                    place(z, other, exp),
                )
            )

    for k in range(layers):
        zz = layer(k)
        who = (zz, core, exp)

        @pl.when(zz != z)
        def _(who=who):
            arrive(who)

        go(send(unit(*who), who, line_sem.at[k], place(z + 1, core, exp)), (zz < z) & (z < layers - 1))
        go(send(unit(*who), who, line_sem.at[k], place(z - 1, core, exp)), (zz > z) & (z > 0))
        go(send(unit(*who), who, x_sem.at[k], place(z, core, x)), zz != z)
        go(send(unit(*who), who, y_sem.at[k], place(z, core, y)), zz != z)
        go(send(unit(*who), who, core_sem.at[k], place(z, other, exp)), zz != z)
        if k == 0:
            hand_out(0, True)

    def spread_rows(values, out):
        tile, cap = 256, out.shape[1]

        @pl.loop(0, values.shape[1] // tile)
        def _(i):
            at = pl.ds(pl.multiple_of(i * tile, tile), tile)
            spread_out = dot(hot_s[...], values[:, at]).astype(BF16)
            for e in range(out.shape[0]):
                out[e, :, at] = spread_out[e * cap : (e + 1) * cap]

    slot = lax.broadcasted_iota(jnp.int32, hot_s.shape, 0)
    takes = [slot == target_ref[k : k + 1, :] for k in range(2)]
    hot_s[...] = jnp.where(takes[0] | takes[1], 1.0, 0.0).astype(BF16)
    spread_rows(cotangent_ref, grads_s)

    for a in range(2):
        pltpu.make_async_copy(mine(a, z, core), half(a, ctx, core), own_sem.at[1 + a]).start()

    hand_out(0, False)

    for k in range(layers):
        zz = layer(k)
        from_x, from_y = (zz, core, x), (zz, core, y)
        arrive(from_x)
        go(send(unit(*from_x), from_x, core_sem.at[layers + 1 + k], place(z, other, exp)))
        if k % 2 == 0:
            go(send(unit(*from_x), from_x, far_sem.at[k], place(z, core, y)))
        arrive(from_y)
        go(send(unit(*from_y), from_y, core_sem.at[2 * layers + 1 + k], place(z, other, exp)))
        if k % 2 == 1:
            go(send(unit(*from_y), from_y, far_sem.at[k], place(z, core, x)))
    for k in range(layers):
        far = (layer(k), core, y_of(x))
        arrive(far)
        go(send(unit(*far), far, core_sem.at[3 * layers + 1 + k], place(z, other, exp)))
    for ee in range(4):
        for zz in range(layers):
            arrive((zz, other, ee))
    keep.wait()
    save = pltpu.make_async_copy(weights, w_all_ref, own_sem.at[3])
    save.start()

    depth, count = tokens_ref.shape[1], tokens_ref.shape[0]
    qkv_cols, head_cols = projected_ref.shape[1], HEADS * HEAD
    inputs = tokens_ref[...].astype(F32)
    gains = jnp.concatenate(
        [
            jnp.transpose(weights[i * 128 : (i + 1) * 128, qkv_cols : qkv_cols + AUX].astype(F32))[0:8, :]
            for i in range(depth // 128)
        ],
        axis=1,
    )
    gains_ref[...] = gains
    first_ref[...] = (inputs * norm_scale(inputs) * gains[0:1, :]).astype(BF16)
    tile = 512

    @pl.loop(0, (qkv_cols - head_cols) // tile)
    def _(i):
        at = pl.ds(pl.multiple_of(head_cols + i * tile, tile), tile)
        projected_ref[:, at] = dot(first_ref[...], weights[:, at]).astype(BF16)

    def block(source):
        return kv_s.at[pl.ds(pl.multiple_of(source * count, 16), count), :]

    def share(src, source, sem, device):
        return remote(src, block(source), sem, kv_sem.at[source], device)

    own = projected_ref.at[:, pl.ds(head_cols, qkv_cols - head_cols)]
    keep_kv = pltpu.make_async_copy(own, block(ctx), own_sem.at[0])
    keep_kv.start()
    go(share(own, ctx, kv_send.at[2 * layers], place(z + 1, core, exp)), z < layers - 1)
    go(share(own, ctx, kv_send.at[2 * layers + 1], place(z - 1, core, exp)), z > 0)
    go(share(own, ctx, kv_send.at[2 * layers + 2], place(z, other, exp)))

    @pl.loop(0, head_cols // tile)
    def _(i):
        at = pl.ds(pl.multiple_of(i * tile, tile), tile)
        projected_ref[:, at] = dot(first_ref[...], weights[:, at]).astype(BF16)

    for k in range(layers):
        zz = layer(k)
        source = zz * 2 + core

        @pl.when(zz != z)
        def _(source=source):
            share(block(source), source, kv_send.at[0], place(z, other, exp)).wait_recv()

        go(share(block(source), source, kv_send.at[k], place(z + 1, core, exp)), (zz < z) & (z < layers - 1))
        go(share(block(source), source, kv_send.at[k], place(z - 1, core, exp)), (zz > z) & (z > 0))
        go(share(block(source), source, kv_send.at[layers + k], place(z, other, exp)), zz != z)

    hand_out(1, True)
    hand_out(1, False)

    me_slot = exp * layers + z
    keep_grads = pltpu.make_async_copy(grads_s.at[me_slot], got_grads_ref.at[me_slot], own_sem.at[4])
    keep_grads.start()
    for k, (zz, ee) in enumerate(peers):
        there = ee * layers + zz
        go(
            remote(
                grads_s.at[there],
                got_grads_ref.at[me_slot],
                grad_send.at[k],
                grad_sem.at[me_slot],
                place(zz, core, ee),
            )
        )

    def pass_over(a):
        for s, zz in enumerate(order[::-1]):
            for p in range(2):
                if s == 0 and p == 0:
                    continue
                source = zz * 2 + (core + p) % 2
                remote(
                    half(a, source, core),
                    half(a, source, core),
                    half_send.at[a, 0],
                    half_sem.at[a, source],
                    place(z, other, exp),
                ).wait_recv()
                go(
                    remote(
                        half(a, source, core),
                        half(a, source, core),
                        over_send.at[a, s * 2 + p],
                        over_sem.at[a, source],
                        place(z, other, exp),
                    )
                )

    pass_over(0)
    for zz in range(layers):
        source = zz * 2 + other
        share(block(source), source, kv_send.at[0], place(z, other, exp)).wait_recv()
    keep_kv.wait()
    save_kv = pltpu.make_async_copy(kv_s, kv_ref, own_sem.at[0])
    save_kv.start()

    attend_blocks(
        lengths_ref.shape[1],
        False,
        lengths_ref,
        order_ref,
        ctx * (count // BLK),
        projected_ref,
        kv_s,
        exact_ref,
        attended_ref,
        lse_ref,
        q_s,
        m_s,
        sum_s,
        acc_s,
    )
    tile = 256

    @pl.loop(0, depth // tile)
    def _(i):
        at = pl.ds(pl.multiple_of(i * tile, tile), tile)
        w_at = pl.ds(pl.multiple_of(qkv_cols + AUX + i * tile, 128), tile)
        middle_ref[:, at] = tokens_ref[:, at].astype(F32) + dot(attended_ref[...], weights[:, w_at])

    middle = middle_ref[...]
    second_ref[...] = (middle * norm_scale(middle) * gains[1:2, :]).astype(BF16)
    logits = dot(second_ref[...], weights[:, qkv_cols : qkv_cols + AUX])
    lane = lax.broadcasted_iota(jnp.int32, logits.shape, 1)
    token = lax.broadcasted_iota(jnp.int32, (count, count), 0)
    eye = token == lax.broadcasted_iota(jnp.int32, (count, count), 1)
    chosen = []
    for k in range(2):
        line = target_ref[2 + k : 3 + k, :].astype(F32)
        expert = jnp.sum(jnp.where(eye, line, 0.0), axis=1, keepdims=True)
        chosen.append(jnp.sum(jnp.where(lane.astype(F32) == expert + 2.0, logits, 0.0), axis=1, keepdims=True))
    largest = jnp.maximum(chosen[0], chosen[1])
    exps = [jnp.exp(value - largest) for value in chosen]
    total = exps[0] + exps[1]
    gates = [value / total for value in exps]
    gates_ref[...] = jnp.where(lane == 0, gates[0], jnp.where(lane == 1, gates[1], 0.0))
    spread_rows(second_ref, rows_ref)
    slot = lax.broadcasted_iota(jnp.int32, hot_s.shape, 0)
    by_slot = jnp.zeros(hot_s.shape, F32)
    for k in range(2):
        line = jnp.sum(jnp.where(eye, gates[k], 0.0), axis=0, keepdims=True)
        by_slot = by_slot + jnp.where(slot == target_ref[k : k + 1, :], line, 0.0)
    by_slot = jnp.sum(by_slot, axis=1, keepdims=True)
    cap = rows_ref.shape[1]
    eye = lax.broadcasted_iota(jnp.int32, (cap, 128), 0) == lax.broadcasted_iota(jnp.int32, (cap, 128), 1)
    for e in range(rows_ref.shape[0]):
        line = jnp.sum(jnp.where(eye, by_slot[e * cap : (e + 1) * cap], 0.0), axis=0, keepdims=True)
        slot_gates_ref[e] = jnp.broadcast_to(line, (8, 128))

    pass_over(1)
    for source in range(2 * layers):
        for a in range(2):
            remote(
                half(a, source, other),
                half(a, source, other),
                half_send.at[a, 0],
                over_sem.at[a, source],
                place(z, other, exp),
            ).wait_recv()
    for zz, ee in peers:
        source = ee * layers + zz
        remote(
            got_grads_ref.at[source],
            got_grads_ref.at[source],
            grad_send.at[0],
            grad_sem.at[source],
            place(zz, core, ee),
        ).wait_recv()
    keep_grads.wait()
    save_kv.wait()
    save.wait()
    for a in range(2):
        pltpu.make_async_copy(mine(a, z, core), half(a, ctx, core), own_sem.at[1 + a]).wait()
    for copy, condition in started:
        if condition is None:
            copy.wait_send()
        else:
            pl.when(condition)(copy.wait_send)


def front(shard, expert_in, expert_out, tokens, lengths, block_order, target, cotangent, qkv_cols):
    layers = expert_in.shape[0]
    rows_in, rows_out = expert_in.shape[1], expert_out.shape[1]
    depth, cols = shard.shape[0] * 8 * layers, shard.shape[1]
    count = tokens.shape[0]
    kv_shape = (count * 2 * layers, qkv_cols - HEADS * HEAD)
    wide, pairs = 2 * GROUP * BLK, KV_HEADS // 2
    slots = (EXPERTS, CAP, depth)
    any_space = pl.BlockSpec(memory_space=pl.ANY)
    smem = pl.BlockSpec(memory_space=pltpu.SMEM)
    vmem = pl.BlockSpec(memory_space=pltpu.VMEM)
    dma = pltpu.SemaphoreType.DMA
    return pl.pallas_call(
        functools.partial(front_kernel, layers),
        out_shape=(
            jax.ShapeDtypeStruct((depth, cols), BF16),
            jax.ShapeDtypeStruct((rows_in * 2 * layers, expert_in.shape[2]), BF16),
            jax.ShapeDtypeStruct((rows_out * 2 * layers, expert_out.shape[2]), BF16),
            jax.ShapeDtypeStruct((count, depth), BF16),
            jax.ShapeDtypeStruct((count, qkv_cols), BF16),
            jax.ShapeDtypeStruct(kv_shape, BF16),
            jax.ShapeDtypeStruct((count, HEADS * HEAD), F32),
            jax.ShapeDtypeStruct((count, HEADS * HEAD), BF16),
            jax.ShapeDtypeStruct((count // BLK, pairs, wide), F32),
            jax.ShapeDtypeStruct((count, depth), F32),
            jax.ShapeDtypeStruct((count, depth), BF16),
            jax.ShapeDtypeStruct((count, AUX), F32),
            jax.ShapeDtypeStruct((EXPERTS, 8, 128), F32),
            jax.ShapeDtypeStruct((8, depth), F32),
            jax.ShapeDtypeStruct(slots, BF16),
            jax.ShapeDtypeStruct(slots, BF16),
        ),
        in_specs=[any_space] * 3 + [vmem, smem, smem, vmem, vmem],
        out_specs=(any_space,) * 3 + (vmem, vmem, any_space) + (vmem,) * 9 + (any_space,),
        scratch_shapes=[
            pltpu.VMEM((EXPERTS * CAP, count), BF16),
            pltpu.VMEM(slots, BF16),
            pltpu.VMEM((depth, cols), BF16),
            pltpu.VMEM(kv_shape, BF16),
            pltpu.VMEM((pairs, wide, 128), BF16),
            pltpu.VMEM((pairs, 8, wide), F32),
            pltpu.VMEM((pairs, 8, wide), F32),
            pltpu.VMEM((pairs, BLK, wide), F32),
            pltpu.VMEM(expert_in.shape, F32),
            pltpu.VMEM(expert_out.shape, F32),
            pltpu.VMEM(expert_in.shape, BF16),
            pltpu.VMEM(expert_out.shape, BF16),
            dma((8 * layers,)),
            dma((layers + 2,)),
            dma((layers + 1,)),
            dma((layers + 1,)),
            dma((layers,)),
            dma((4 * layers + 1,)),
            dma((2, 2 * layers)),
            dma((2, 2 * layers)),
            dma((2, 2 * layers)),
            dma((2, 2 * layers + 1)),
            dma((2 * layers,)),
            dma((2 * layers + 3,)),
            dma((5,)),
            dma((2, layers)),
            dma((4 * layers,)),
            dma((4 * layers,)),
        ],
        compiler_params=pltpu.CompilerParams(
            collective_id=0, has_side_effects=True, vmem_limit_bytes=60 * 2**20
        ),
        name="front",
    )(shard, expert_in, expert_out, tokens, lengths, block_order, target, cotangent)


def experts_kernel(
    layers,
    rows_ref,
    gates_ref,
    grads_ref,
    w_in_ref,
    w_down_ref,
    out_ref,
    back_ref,
    back_gates_ref,
    d_in_ref,
    d_down_ref,
    w_in,
    w_down,
    got,
    got_gates,
    x_s,
    grad_s,
    hidden_s,
    inner_s,
    back_s,
    back_gates_s,
    other_in,
    other_down,
    pair_in,
    pair_down,
    row_sem,
    row_send,
    gate_sem,
    gate_send,
    back_sem,
    back_send,
    back_gate_sem,
    back_gate_send,
    pair_sem,
    pair_send,
    load_sem,
):
    z, core, exp = lax.axis_index("le"), lax.axis_index("core"), lax.axis_index("exp")
    other = 1 - core
    columns = rows_ref.shape[0] // layers
    me = exp * layers + z
    cap, depth = rows_ref.shape[1], rows_ref.shape[2]
    chunk = columns * cap
    loads = [
        pltpu.make_async_copy(w_in_ref, w_in, load_sem.at[0]),
        pltpu.make_async_copy(w_down_ref, w_down, load_sem.at[1]),
    ]
    for load in loads:
        load.start()
    own_layer, mate, farthest, middle = near_to_far(z)
    peers = [
        (zz, (exp + t) % columns)
        for s, zz in enumerate([mate, farthest, middle, own_layer])
        for t in range(columns)
        if not (s == layers - 1 and t == 0)
    ]
    meet([place(zz, core, ee) for zz, ee in peers] + [place(z, other, exp)])

    started = []

    def go(copy):
        copy.start()
        started.append(copy)

    keeps = [
        pltpu.make_async_copy(rows_ref.at[me], got.at[me], load_sem.at[2]),
        pltpu.make_async_copy(gates_ref.at[me], got_gates.at[me], load_sem.at[3]),
    ]
    for keep in keeps:
        keep.start()
    for k, (zz, ee) in enumerate(peers):
        there = ee * layers + zz
        go(remote(gates_ref.at[there], got_gates.at[me], gate_send.at[k], gate_sem.at[me], place(zz, core, ee)))
        go(remote(rows_ref.at[there], got.at[me], row_send.at[k], row_sem.at[me], place(zz, core, ee)))
    for load in loads + keeps:
        load.wait()

    eye = lax.broadcasted_iota(jnp.int32, (cap, 128), 0) == lax.broadcasted_iota(jnp.int32, (cap, 128), 1)
    tile = 256

    def tiles(i):
        return pl.ds(pl.multiple_of(i * tile, tile), tile)

    for k, zz in enumerate([own_layer, mate, farthest, middle]):
        rows = pl.ds(k * chunk, chunk)
        for ee in range(columns):
            source = ee * layers + zz

            @pl.when(source != me)
            def _(source=source):
                here = place(z, other, exp)
                remote(got.at[source], got.at[source], row_send.at[0], row_sem.at[source], here).wait_recv()
                remote(
                    got_gates.at[source], got_gates.at[source], gate_send.at[0], gate_sem.at[source], here
                ).wait_recv()

            at = pl.ds(k * chunk + ee * cap, cap)
            x_s[at, :] = got[source]
            gate = jnp.sum(jnp.where(eye, got_gates[source, 0:1, :], 0.0), axis=1, keepdims=True)
            grad_s[at, :] = (gate * grads_ref[source].astype(F32)).astype(BF16)

        @pl.loop(0, FF // tile)
        def _(i, rows=rows):
            up_at = pl.ds(pl.multiple_of(FF + i * tile, tile), tile)
            gate = dot(x_s[rows, :], w_in[:, tiles(i)])
            up = dot(x_s[rows, :], w_in[:, up_at])
            grad_hidden = dot(grad_s[rows, :], w_down[tiles(i), :], ((1,), (1,)))
            sigmoid = jax.nn.sigmoid(gate)
            silu = gate * sigmoid
            hidden_s[rows, tiles(i)] = (silu * up).astype(BF16)
            inner_s[rows, tiles(i)] = (grad_hidden * up * sigmoid * (1.0 + gate * (1.0 - sigmoid))).astype(BF16)
            inner_s[rows, up_at] = (grad_hidden * silu).astype(BF16)

        @pl.loop(0, depth // tile)
        def _(i, rows=rows, zz=zz):
            back = dot(inner_s[rows, :], w_in[tiles(i), :], ((1,), (1,))).astype(BF16)
            for ee in range(columns):
                back_s[ee * layers + zz, :, tiles(i)] = back[ee * cap : (ee + 1) * cap]

        @pl.loop(0, depth // tile, init_carry=jnp.zeros((chunk, 128), F32))
        def gate_grads(i, sums, rows=rows, zz=zz):
            result = dot(hidden_s[rows, :], w_down[:, tiles(i)]).astype(BF16)
            parts = []
            for ee in range(columns):
                part = result[ee * cap : (ee + 1) * cap]
                out_ref[ee * layers + zz, :, tiles(i)] = part
                parts.append(part.astype(F32) * grads_ref[ee * layers + zz, :, tiles(i)].astype(F32))
            product = jnp.concatenate(parts, axis=0)
            return sums + product[:, :128] + product[:, 128:]

        gate_grads = jnp.sum(gate_grads, axis=1, keepdims=True)
        for ee in range(columns):
            there = ee * layers + zz
            column = gate_grads[ee * cap : (ee + 1) * cap]
            line = jnp.sum(jnp.where(eye, column, 0.0), axis=0, keepdims=True)
            back_gates_s[there] = jnp.broadcast_to(line, (8, 128))
            row_copy = remote(
                back_s.at[there],
                back_ref.at[me],
                back_send.at[there],
                back_sem.at[me],
                place(zz, core, ee),
            )
            gate_copy = remote(
                back_gates_s.at[there],
                back_gates_ref.at[me],
                back_gate_send.at[there],
                back_gate_sem.at[me],
                place(zz, core, ee),
            )

            @pl.when(there != me)
            def _(row_copy=row_copy, gate_copy=gate_copy):
                row_copy.start()
                gate_copy.start()

    own = [
        pltpu.make_async_copy(back_s.at[me], back_ref.at[me], load_sem.at[2]),
        pltpu.make_async_copy(back_gates_s.at[me], back_gates_ref.at[me], load_sem.at[3]),
    ]
    for copy in own:
        copy.start()

    half_in, half_down = d_in_ref.shape[1], d_down_ref.shape[1]

    def in_part(i, p):
        cols = pl.ds(pl.multiple_of(p * half_in, 128), half_in)
        return dot(x_s[:, tiles(i)], inner_s[:, cols], ((0,), (0,)))

    def down_part(i, p):
        cols = pl.ds(pl.multiple_of(p * half_down, 128), half_down)
        return dot(hidden_s[:, tiles(i)], grad_s[:, cols], ((0,), (0,)))

    @pl.loop(0, depth // tile)
    def _(i):
        other_in[tiles(i), :] = in_part(i, other).astype(BF16)

    go(remote(other_in, pair_in, pair_send.at[0], pair_sem.at[0], place(z, other, exp)))

    @pl.loop(0, FF // tile)
    def _(i):
        other_down[tiles(i), :] = down_part(i, other).astype(BF16)

    go(remote(other_down, pair_down, pair_send.at[1], pair_sem.at[1], place(z, other, exp)))
    remote(other_in, pair_in, pair_send.at[0], pair_sem.at[0], place(z, other, exp)).wait_recv()

    @pl.loop(0, depth // tile)
    def _(i):
        d_in_ref[tiles(i), :] = (in_part(i, core) + pair_in[tiles(i), :].astype(F32)).astype(BF16)

    remote(other_down, pair_down, pair_send.at[1], pair_sem.at[1], place(z, other, exp)).wait_recv()

    @pl.loop(0, FF // tile)
    def _(i):
        d_down_ref[tiles(i), :] = (down_part(i, core) + pair_down[tiles(i), :].astype(F32)).astype(BF16)

    for copy in own:
        copy.wait()
    for k, (zz, ee) in enumerate(peers):
        there = ee * layers + zz
        row_copy = remote(
            back_s.at[there], back_ref.at[there], back_send.at[there], back_sem.at[there], place(zz, core, ee)
        )
        gate_copy = remote(
            back_gates_s.at[there],
            back_gates_ref.at[there],
            back_gate_send.at[there],
            back_gate_sem.at[there],
            place(zz, core, ee),
        )
        row_copy.wait()
        gate_copy.wait()
    for copy in started:
        copy.wait_send()


def experts(rows, gates, grads, w_in, w_down, layers):
    count, cap, depth = rows.shape
    any_space = pl.BlockSpec(memory_space=pl.ANY)
    vmem = pl.BlockSpec(memory_space=pltpu.VMEM)
    dma = pltpu.SemaphoreType.DMA
    half_in = jax.ShapeDtypeStruct((depth, FF), BF16)
    half_down = jax.ShapeDtypeStruct((FF, depth // 2), BF16)
    return pl.pallas_call(
        functools.partial(experts_kernel, layers),
        out_shape=(
            jax.ShapeDtypeStruct(rows.shape, BF16),
            jax.ShapeDtypeStruct(rows.shape, BF16),
            jax.ShapeDtypeStruct(gates.shape, F32),
            half_in,
            half_down,
        ),
        in_specs=[any_space, any_space, vmem, any_space, any_space],
        out_specs=(vmem, any_space, any_space, vmem, vmem),
        scratch_shapes=[
            pltpu.VMEM(w_in.shape, BF16),
            pltpu.VMEM(w_down.shape, BF16),
            pltpu.VMEM(rows.shape, BF16),
            pltpu.VMEM(gates.shape, F32),
            pltpu.VMEM((count * cap, depth), BF16),
            pltpu.VMEM((count * cap, depth), BF16),
            pltpu.VMEM((count * cap, FF), BF16),
            pltpu.VMEM((count * cap, 2 * FF), BF16),
            pltpu.VMEM(rows.shape, BF16),
            pltpu.VMEM(gates.shape, F32),
            pltpu.VMEM(half_in.shape, BF16),
            pltpu.VMEM(half_down.shape, BF16),
            pltpu.VMEM(half_in.shape, BF16),
            pltpu.VMEM(half_down.shape, BF16),
        ]
        + [dma((count,))] * 8
        + [dma((2,)), dma((2,)), dma((4,))],
        compiler_params=pltpu.CompilerParams(
            collective_id=2, has_side_effects=True, vmem_limit_bytes=60 * 2**20
        ),
        name="experts",
    )(rows, gates, grads, w_in, w_down)


def add_rows(total, part, rows):
    slab = 16

    @pl.loop(0, rows // slab)
    def _(i):
        at = pl.ds(pl.multiple_of(i * slab, slab), slab)
        total[at, :] = (total[at, :].astype(F32) + part[at, :].astype(F32)).astype(BF16)


class Chain:
    def __init__(self, layers, z, above, below, own, rows, up, down, sems, sends):
        self.layers, self.z, self.above, self.below = layers, z, above, below
        self.own, self.rows, self.up, self.down = own, rows, up, down
        self.sems, self.sends = sems, sends
        self.parts = sems.shape[2]
        self.width = up.shape[2] // self.parts

    def columns(self, ref, h):
        return ref.at[:, pl.ds(h * self.width, self.width)]

    def rise(self, d, h):
        return remote(
            self.columns(self.own(d), h),
            self.columns(self.up.at[d], h),
            self.sends.at[0, d, h],
            self.sems.at[0, d, h],
            self.above,
        )

    def fall(self, d, h):
        return remote(
            self.columns(self.own(d), h),
            self.columns(self.down.at[d], h),
            self.sends.at[1, d, h],
            self.sems.at[1, d, h],
            self.below,
        )

    def end(self, step):
        for h in range(self.parts):
            pl.when(self.z == 0)(self.rise(self.layers - 1 - step, h).start)
            pl.when(self.z == self.layers - 1)(self.fall(step, h).start)

    def ends(self):
        for step in range(self.layers - 1):
            self.end(step)

    def add(self, d, h, buffer):
        add_rows(self.columns(self.own(d), h), self.columns(buffer.at[d], h), self.rows)

    def middle(self):
        z, last = self.z, self.layers - 1

        def pass_on(make, d, buffer):
            for h in range(self.parts):
                copy = make(d, h)
                copy.wait_recv()
                self.add(d, h, buffer)
                copy.start()

        def both(first_half):
            for step in range(last):
                high, low = last - step, step

                def upward(high=high):
                    pl.when((z > 0) & (z < high))(lambda: pass_on(self.rise, high, self.up))

                def downward(low=low):
                    pl.when((z < last) & (z > low))(lambda: pass_on(self.fall, low, self.down))

                for turn in (upward, downward) if first_half else (downward, upward):
                    turn()

        pl.when(z <= last // 2)(lambda: both(True))
        pl.when(z > last // 2)(lambda: both(False))

    def finish(self):
        z, last = self.z, self.layers - 1

        def take(make, buffer):
            for h in range(self.parts):
                make(z, h).wait_recv()
                self.add(z, h, buffer)

        pl.when(z > 0)(lambda: take(self.rise, self.up))
        pl.when(z < last)(lambda: take(self.fall, self.down))

    def wait_sends(self):
        for d in range(self.layers):
            for h in range(self.parts):
                pl.when(self.z < d)(self.rise(d, h).wait_send)
                pl.when(self.z > d)(self.fall(d, h).wait_send)


def finish_kernel(
    layers,
    grad_kv_ref,
    grad_q_ref,
    first_ref,
    tokens_ref,
    gain_ref,
    middle_ref,
    w_all_ref,
    attended_ref,
    second_ref,
    logits_ref,
    gain_moe_ref,
    in_ref,
    down_ref,
    d_tokens_ref,
    d_qkv_ref,
    d_out_ref,
    d_aux_ref,
    got_in_ref,
    got_down_ref,
    weights,
    projected,
    grad_first,
    kv_own,
    kv_pair,
    kv_up,
    kv_down,
    late_both,
    late_pair,
    late_near,
    late_up,
    late_down,
    q_both,
    q_pair,
    q_near,
    q_up,
    q_down,
    k_both,
    k_pair,
    k_near,
    k_up,
    k_down,
    load_sem,
    kv_pair_sem,
    kv_pair_send,
    kv_sem,
    kv_send,
    half_sem,
    half_send,
    pair_sem,
    pair_send,
    near_sem,
    near_send,
    line_sem,
    line_send,
):
    z, core, exp = lax.axis_index("le"), lax.axis_index("core"), lax.axis_index("exp")
    other = 1 - core
    partner = place(z, other, exp)
    above, below = place(z + 1, core, exp), place(z - 1, core, exp)
    x, y = x_of(exp), y_of(exp)
    mates = (x, y, y_of(x))
    own_layer, mate, farthest, middle = near_to_far(z)
    ctx = z * 2 + core
    rows = d_qkv_ref.shape[0]
    count = tokens_ref.shape[0]
    head_cols = HEADS * HEAD
    qkv_cols = d_qkv_ref.shape[1]
    kv_cols = qkv_cols - head_cols

    loads = []

    def load(src, dst):
        copy = pltpu.make_async_copy(src, dst, load_sem.at[len(loads)])
        copy.start()
        loads.append(copy)
        return copy

    kv_loads = [
        load(grad_kv_ref.at[pl.ds(pl.multiple_of((d * 2 + core) * count, 16), count), :], kv_own.at[d])
        for d in range(layers)
    ]
    depth = w_all_ref.shape[0]

    def weights_part(i):
        part = w_all_ref.at[pl.ds(i * depth // 2, depth // 2), pl.ds(0, qkv_cols)]
        return pltpu.make_async_copy(part, weights, load_sem.at[2 * layers + 2])

    weights_part(0).start()
    meet(
        [
            place((z + s) % layers, (core + p) % 2, exp)
            for s in range(layers)
            for p in range(2)
            if s + p > 0
        ]
        + [place(z, core, mate) for mate in mates]
    )
    started = []

    def go(copy):
        copy.start()
        started.append(copy)

    arrays = ((in_ref, got_in_ref), (down_ref, got_down_ref))

    def mine(a, owner):
        n = arrays[a][1].shape[1]
        return arrays[a][0].at[pl.ds(owner * n, n), :]

    def half(a, expert, p):
        cols = arrays[a][0].shape[1]
        return arrays[a][1].at[expert, :, pl.ds(pl.multiple_of(p * cols, 128), cols)]

    for a in range(2):
        load(mine(a, ctx), half(a, z, core))

    def hand_back(a, early):
        for s, zz in enumerate([mate, farthest, middle, own_layer]):
            across = between(z, zz)
            for p in range(2):
                if s == layers - 1 and p == 0:
                    continue
                pp = (core + p) % 2
                copy = remote(
                    mine(a, zz * 2 + pp),
                    half(a, z, core),
                    half_send.at[a, s * 2 + p],
                    half_sem.at[a, ctx],
                    place(zz, pp, exp),
                )
                if early:
                    pl.when(across)(copy.start)
                else:
                    pl.when(~across)(copy.start)
                    started.append(copy)

    hand_back(0, True)

    for d in range(layers):
        go(
            remote(
                grad_kv_ref.at[pl.ds(pl.multiple_of((d * 2 + other) * count, 16), count), :],
                kv_pair.at[d],
                kv_pair_send.at[d],
                kv_pair_sem.at[d],
                partner,
            )
        )
    kv_line = Chain(
        layers, z, above, below, lambda d: kv_own.at[d], count, kv_up, kv_down, kv_sem, kv_send
    )
    for copy in kv_loads:
        copy.wait()
    for k in range(layers):
        d = jnp.where(z < layers // 2, layers - 1 - k, k)
        remote(kv_pair.at[d], kv_pair.at[d], kv_pair_send.at[d], kv_pair_sem.at[d], partner).wait_recv()
        add_rows(kv_own.at[d], kv_pair.at[d], count)
        if k < layers - 1:
            kv_line.end(k)

    def near_copy(i, near, own, d, m, target):
        return remote(
            own.at[d, pl.ds(pl.multiple_of(target * rows, 16), rows), :],
            near.at[m, d],
            near_send.at[i, m, d],
            near_sem.at[i, m, d],
            place(z, core, mates[m]),
        )

    def pair_sums(i, own, pair, near):
        for d in range(layers):
            remote(pair.at[d], pair.at[d], pair_send.at[i, d], pair_sem.at[i, d], partner).wait_recv()
            add_rows(own.at[d], pair.at[d], 4 * rows)
            for m in range(3):
                go(near_copy(i, near, own, d, m, mates[m]))

    def near_sums(i, own, near):
        for d in range(layers):
            for m in range(3):
                near_copy(i, near, own, d, m, exp).wait_recv()
            mine = own.at[d, pl.ds(pl.multiple_of(exp * rows, 16), rows), :]

            @pl.loop(0, rows // 16)
            def _(r, mine=mine, d=d):
                at = pl.ds(pl.multiple_of(r * 16, 16), 16)
                total = mine[at, :].astype(F32)
                for m in range(3):
                    total = total + near[m, d, at, :].astype(F32)
                mine[at, :] = total.astype(BF16)

    def line_of(i, own, up, down):
        return Chain(
            layers,
            z,
            above,
            below,
            lambda d: own.at[d, pl.ds(pl.multiple_of(exp * rows, 16), rows), :],
            rows,
            up,
            down,
            line_sem.at[i],
            line_send.at[i],
        )

    def outer_product(both, cols, left, right, gains=None):
        for d in range(layers):
            block = left[:, d * 8 * rows : (d + 1) * 8 * rows]
            part = dot(block, right, ((0,), (0,)))
            if gains is not None:
                turned = [
                    jnp.transpose(jnp.broadcast_to(gains[:, at : at + 128], (128, 128)))
                    for at in range(d * 8 * rows, (d + 1) * 8 * rows, 128)
                ]
                lane = lax.broadcasted_iota(jnp.int32, part.shape, 1)
                part = jnp.where(lane == 0, jnp.concatenate(turned, axis=0), part)
            part = part.astype(BF16)
            both[0, d, :, cols] = part[: 4 * rows]
            both[1, d, :, cols] = part[4 * rows :]

    def pair_up(i, both, pair):
        for d in range(layers):
            go(remote(both.at[other, d], pair.at[d], pair_send.at[i, d], pair_sem.at[i, d], partner))

    outer_product(q_both, slice(0, head_cols), first_ref, grad_q_ref[...])
    pair_up(1, q_both, q_pair)
    width = middle_ref.shape[1]
    outer_product(late_both, slice(0, width), attended_ref, middle_ref[...].astype(BF16))
    outer_product(late_both, slice(width, width + AUX), second_ref, logits_ref[...], gain_moe_ref[...])
    pair_up(0, late_both, late_pair)
    late_own = late_both.at[core]
    q_own = q_both.at[core]
    pair_sums(1, q_own, q_pair, q_near)
    pair_sums(0, late_own, late_pair, late_near)
    kv_line.middle()
    hand_back(0, False)
    hand_back(1, True)
    hand_back(1, False)
    kv_line.finish()

    projected[:, :head_cols] = grad_q_ref[...]
    projected[:, head_cols:] = kv_own[z]
    outer_product(k_both, slice(0, kv_cols), first_ref, projected[:, head_cols:])
    tile = 256
    for i in range(2):
        weights_part(i).wait()

        @pl.loop(0, depth // 2 // tile)
        def _(j, i=i):
            at = pl.ds(pl.multiple_of(j * tile, tile), tile)
            to = pl.ds(pl.multiple_of(i * depth // 2 + j * tile, tile), tile)
            grad_first[:, to] = dot(projected[...], weights[at, :], ((1,), (1,)))

        if i == 0:
            weights_part(1).start()

    inputs = tokens_ref[...].astype(F32)
    scale = norm_scale(inputs)
    norm = inputs * scale
    grad = grad_first[...]
    grad_gain = jnp.sum(grad * norm, axis=0, keepdims=True)
    for d in range(layers):
        block = jnp.concatenate(
            [
                jnp.transpose(jnp.broadcast_to(grad_gain[:, at : at + 128], (128, 128)))
                for at in range(d * 8 * rows, (d + 1) * 8 * rows, 128)
            ],
            axis=0,
        ).astype(BF16)
        k_both[0, d, :, kv_cols:] = block[: 4 * rows]
        k_both[1, d, :, kv_cols:] = block[4 * rows :]
    pair_up(2, k_both, k_pair)
    grad = grad * gain_ref[0:1, :]
    d_tokens_ref[...] = (
        middle_ref[...] + scale * (grad - norm * jnp.mean(grad * norm, axis=-1, keepdims=True))
    ).astype(BF16)
    k_own = k_both.at[core]
    pair_sums(2, k_own, k_pair, k_near)

    late_line = line_of(0, late_own, late_up, late_down)
    q_line = line_of(1, q_own, q_up, q_down)
    k_line = line_of(2, k_own, k_up, k_down)
    near_sums(1, q_own, q_near)
    q_line.ends()
    near_sums(0, late_own, late_near)
    late_line.ends()
    q_line.middle()
    near_sums(2, k_own, k_near)
    k_line.ends()
    late_line.middle()
    k_line.middle()
    mine_rows = pl.ds(pl.multiple_of(exp * rows, 16), rows)
    q_line.finish()
    d_qkv_ref[:, :head_cols] = q_both[core, z, mine_rows, :].astype(F32)
    late_line.finish()
    last = late_both[core, z, mine_rows, :].astype(F32)
    d_out_ref[...] = last[:, :width]
    d_aux_ref[:, AUX:] = last[:, width:]
    k_line.finish()
    last = k_both[core, z, mine_rows, :].astype(F32)
    d_qkv_ref[:, head_cols:] = last[:, :kv_cols]
    d_aux_ref[:, :AUX] = last[:, kv_cols:]

    for source in range(2 * layers):
        for a in range(2):

            @pl.when(source != ctx)
            def _(source=source, a=a):
                remote(
                    half(a, source // 2, source % 2),
                    half(a, source // 2, source % 2),
                    half_send.at[a, 0],
                    half_sem.at[a, source],
                    partner,
                ).wait_recv()

    for copy in loads[-2:]:
        copy.wait()
    for line in (kv_line, late_line, q_line, k_line):
        line.wait_sends()
    for copy in started:
        copy.wait_send()


def finish(
    grad_kv,
    grad_q,
    first,
    tokens,
    gain,
    middle,
    w_all,
    attended,
    second,
    grad_logits,
    gain_moe,
    grad_in,
    grad_down,
    layers,
):
    depth, count = first.shape[1], first.shape[0]
    rows = depth // (8 * layers)
    qkv_cols = grad_q.shape[1] + grad_kv.shape[1]
    n_in, n_down = grad_in.shape[0] // (2 * layers), grad_down.shape[0] // (2 * layers)
    any_space = pl.BlockSpec(memory_space=pl.ANY)
    vmem = pl.BlockSpec(memory_space=pltpu.VMEM)
    dma = pltpu.SemaphoreType.DMA

    def sums(cols):
        return [
            pltpu.VMEM((2, layers, 4 * rows, cols), BF16),
            pltpu.VMEM((layers, 4 * rows, cols), BF16),
            pltpu.VMEM((3, layers, rows, cols), BF16),
            pltpu.VMEM((layers, rows, cols), BF16),
            pltpu.VMEM((layers, rows, cols), BF16),
        ]

    return pl.pallas_call(
        functools.partial(finish_kernel, layers),
        out_shape=(
            jax.ShapeDtypeStruct((count, depth), BF16),
            jax.ShapeDtypeStruct((rows, qkv_cols), F32),
            jax.ShapeDtypeStruct((rows, depth), F32),
            jax.ShapeDtypeStruct((rows, 2 * AUX), F32),
            jax.ShapeDtypeStruct((layers, n_in, 2 * grad_in.shape[1]), BF16),
            jax.ShapeDtypeStruct((layers, n_down, 2 * grad_down.shape[1]), BF16),
        ),
        in_specs=[any_space] + [vmem] * 5 + [any_space] + [vmem] * 4 + [any_space] * 2,
        out_specs=(vmem,) * 4 + (any_space,) * 2,
        scratch_shapes=[
            pltpu.VMEM((depth // 2, qkv_cols), BF16),
            pltpu.VMEM((count, qkv_cols), BF16),
            pltpu.VMEM((count, depth), F32),
        ]
        + [pltpu.VMEM((layers, count, grad_kv.shape[1]), BF16)] * 4
        + sums(depth + AUX)
        + sums(grad_q.shape[1])
        + sums(grad_kv.shape[1] + AUX)
        + [
            dma((2 * layers + 3,)),
            dma((layers,)),
            dma((layers,)),
            dma((2, layers, 4)),
            dma((2, layers, 4)),
            dma((2, 2 * layers)),
            dma((2, 2 * layers)),
            dma((3, layers)),
            dma((3, layers)),
            dma((3, 3, layers)),
            dma((3, 3, layers)),
            dma((3, 2, layers, 1)),
            dma((3, 2, layers, 1)),
        ],
        compiler_params=pltpu.CompilerParams(
            collective_id=1, has_side_effects=True, vmem_limit_bytes=60 * 2**20
        ),
        name="finish",
    )(
        grad_kv,
        grad_q,
        first,
        tokens,
        gain,
        middle,
        w_all,
        attended,
        second,
        grad_logits,
        gain_moe,
        grad_in,
        grad_down,
    )


def settle_kernel(count, base_ref, gates_ref, target_ref, returned_ref, aux_ref, *refs):
    block_ref, refs = refs[count], refs[:count] + refs[count + 1 :]
    total = base_ref[...]
    slot = lax.broadcasted_iota(jnp.int32, (total.shape[0], returned_ref.shape[0]), 1)
    for k in range(2):
        pick = jnp.where(target_ref[:, k : k + 1] == slot, 1.0, 0.0).astype(BF16)
        total = total + gates_ref[:, k : k + 1] * dot(pick, returned_ref[...])
    block_ref[...] = total.astype(BF16)
    for src, dst in zip(refs[:count], refs[count : 2 * count]):
        dst[...] = src[...].astype(dst.dtype)
    rows = aux_ref.shape[0]
    eye = lax.broadcasted_iota(jnp.int32, (rows, 128), 0) == lax.broadcasted_iota(jnp.int32, (rows, 128), 1)
    for at, dst in zip((0, AUX), refs[2 * count :]):
        line = jnp.sum(jnp.where(eye, aux_ref[:, at : at + 1], 0.0), axis=0, keepdims=True)
        dst[...] = line[:, :rows]
    block = jnp.concatenate([aux_ref[:, AUX:], jnp.zeros((128 - rows, AUX), F32)], axis=0)
    refs[-1][...] = jnp.transpose(block)[2 : 2 + EXPERTS, :rows]


def settle(base, gates, target, returned, aux, arrays, steps):
    def spec(array):
        if array.ndim == 2 and array.shape[0] % (16 * steps) == 0:
            return pl.BlockSpec((array.shape[0] // steps, array.shape[1]), lambda i: (i, 0))
        if array.ndim == 3 and array.shape[1] % (16 * steps) == 0:
            return pl.BlockSpec(
                (array.shape[0], array.shape[1] // steps, array.shape[2]), lambda i: (0, i, 0)
            )
        return pl.BlockSpec(array.shape, lambda i: (0,) * array.ndim)

    specs = [spec(array) for array, _ in arrays]
    rows = aux.shape[0]
    small = [jax.ShapeDtypeStruct(shape, F32) for shape in ((1, rows), (1, rows), (EXPERTS, rows))]
    return pl.pallas_call(
        functools.partial(settle_kernel, len(arrays)),
        grid=(steps,),
        out_shape=[jax.ShapeDtypeStruct(base.shape, BF16)]
        + [jax.ShapeDtypeStruct(array.shape, dtype) for array, dtype in arrays]
        + small,
        in_specs=[
            spec(base),
            spec(gates),
            spec(target),
            pl.BlockSpec(returned.shape, lambda i: (0, 0)),
            spec(aux),
        ]
        + specs,
        out_specs=[spec(base)] + specs + [spec(shape) for shape in small],
        compiler_params=pltpu.CompilerParams(vmem_limit_bytes=60 * 2**20),
        name="settle",
    )(base, gates, target, returned, aux, *[array for array, _ in arrays])


CTX = ("le", "rep", "core")
ALL = ("le", "rep", "core", "exp")
OWNERS = ("exp", "le")


def on_device(
    tokens,
    cotangent,
    routes,
    lengths,
    block_order,
    gain_attn,
    qkv_weight,
    out_weight,
    gain_moe,
    router_weight,
    expert_in,
    expert_out,
):
    tok_rows = tokens.shape[1]
    head_width = HEADS * HEAD
    exp_local = expert_in.shape[0]
    n_ctx = D // expert_in.shape[1]
    copies = n_ctx // exp_local
    n_exp = EXPERTS // exp_local
    in_rows, out_rows = expert_in.shape[1], expert_out.shape[1]

    route_hot = (
        routes[0][:, :, None] == jnp.arange(EXPERTS, dtype=jnp.int32)[None, None, :]
    ).astype(F32)
    flat_hot = route_hot.reshape(tok_rows * 2, EXPERTS).astype(BF16)
    order = jnp.arange(tok_rows * 2, dtype=jnp.int32)
    earlier = (order[:, None] > order[None, :]).astype(BF16)
    ranks = dot(earlier, flat_hot)
    slot_index = jnp.sum(ranks * flat_hot.astype(F32), axis=1).astype(jnp.int32)
    target = (routes[0].reshape(tok_rows * 2) * CAP + slot_index).reshape(tok_rows, 2)
    slots = jnp.arange(EXPERTS * CAP, dtype=jnp.int32)
    picks = [(target[:, k : k + 1] == slots[None, :]) for k in range(2)]
    sends = [(target[:, k][None, :] == slots[:, None]) for k in range(2)]
    send_hot = (sends[0] | sends[1]).astype(BF16)

    def to_experts(rows):
        return lax.all_to_all(
            rows.reshape((EXPERTS, CAP) + rows.shape[1:]),
            OWNERS,
            split_axis=0,
            concat_axis=0,
            tiled=True,
        ).reshape(rows.shape)

    cols = qkv_weight.shape[1]
    aux = jnp.concatenate([gain_attn[:, None], gain_moe[:, None], router_weight], axis=1)
    aux = jnp.pad(aux, ((0, 0), (0, AUX - aux.shape[1])))
    shard = jnp.concatenate([qkv_weight, aux, out_weight], axis=1).astype(BF16)
    special = (copies, exp_local, n_exp) == (2, 4, 4)
    if special:
        (
            w_all,
            w_in,
            w_down,
            first,
            projected,
            kv,
            exact,
            attended,
            lse,
            middle,
            second,
            gates,
            slot_gates,
            gain_rows,
            second_rows,
            grad_y_rows,
        ) = front(
            shard,
            expert_in,
            expert_out,
            tokens[0],
            lengths,
            block_order,
            jnp.concatenate([target, routes[0]], axis=1).T,
            cotangent[0],
            cols,
        )
        gates = gates[:, :2]
    else:
        w_all = lax.all_gather(shard, ALL, axis=0, tiled=True)

        def to_owner(weight):
            rows, width = weight.shape[1:]
            halves = weight.astype(BF16).reshape(exp_local, rows, 2, width // 2).transpose(0, 2, 1, 3)
            halves = jnp.broadcast_to(
                halves[:, None], (exp_local, copies // 2, 2, rows, width // 2)
            ).reshape(n_ctx, rows, width // 2)
            mine = lax.all_to_all(halves, CTX, split_axis=0, concat_axis=0, tiled=True)
            return lax.all_gather(mine.reshape(n_ctx * rows, width // 2), "core", axis=1, tiled=True)

        w_in = to_owner(expert_in)
        w_down = to_owner(expert_out)
    w_qkv = w_all[:, :cols]
    aux_all = w_all[:, cols : cols + AUX]
    w_attn_out = w_all[:, cols + AUX :]
    gain_first = aux_all[:, 0].astype(F32)
    gain_second = gain_rows[1] if special else aux_all[:, 1].astype(F32)
    w_router = aux_all[:, 2 : 2 + EXPERTS]

    inputs = tokens[0].astype(F32)
    scale_first = norm_scale(inputs)
    norm_first = inputs * scale_first
    mine = (lax.axis_index(CTX) * (tok_rows // BLK)).astype(jnp.int32).reshape(1)
    if not special:
        first = (norm_first * gain_first).astype(BF16)
        projected = dot(first, w_qkv).astype(BF16)
        kv = lax.all_gather(projected[:, head_width:], CTX, axis=0, tiled=True)
        kv, grad_y_send = lax.optimization_barrier((kv, dot(send_hot, cotangent[0]).astype(BF16)))
        grad_y_rows = to_experts(grad_y_send)
        exact, attended, lse = attend(lengths, block_order, mine, projected, kv)
        middle = inputs + dot(attended, w_attn_out)
    scale_second = norm_scale(middle)
    norm_second = middle * scale_second
    if not special:
        second = (norm_second * gain_second).astype(BF16)
        logits = dot(second, w_router)
        chosen = jnp.sum(route_hot * logits[:, None, :], axis=-1)
        gates = jax.nn.softmax(chosen, axis=-1)

    if special:
        expert_rows, grad_returned, gate_grads, grad_in, grad_down = experts(
            second_rows,
            slot_gates,
            grad_y_rows,
            w_in,
            w_down,
            exp_local,
        )
        returned = to_experts(expert_rows.reshape(EXPERTS * CAP, D))
        grad_returned = grad_returned.reshape(EXPERTS * CAP, D)
        gate_grads = gate_grads[:, 0, :CAP].reshape(1, EXPERTS * CAP)
    else:
        gate_rows = jnp.sum(
            jnp.where(sends[0], gates[:, 0][None, :], 0.0) + jnp.where(sends[1], gates[:, 1][None, :], 0.0),
            axis=1,
            keepdims=True,
        )

        def in_parts(column):
            high = lax.reduce_precision(column, 8, 7)
            rest = column - high
            mid = lax.reduce_precision(rest, 8, 7)
            parts = jnp.concatenate([high, mid, rest - mid], axis=1).astype(BF16)
            return jnp.pad(parts, ((0, 0), (0, AUX - 3)))

        gate_parts = in_parts(gate_rows)
        payload = to_experts(
            jnp.concatenate([dot(send_hot, second).astype(BF16), gate_parts], axis=1)
        )
        received = payload[:, :D]
        gate_got = jnp.sum(payload[:, D : D + 3].astype(F32), axis=1, keepdims=True)

        gate_up = dot(received, w_in)
        gate_part = gate_up[:, :FF]
        up_part = gate_up[:, FF:]
        sigmoid_gate = jax.nn.sigmoid(gate_part)
        silu_gate = gate_part * sigmoid_gate
        hidden = (silu_gate * up_part).astype(BF16)
        expert_rows = dot(hidden, w_down)
        expert_rows = expert_rows.astype(BF16)
        grad_y_rows = grad_y_rows.astype(F32)
        returned = to_experts(expert_rows)

        grad_rows = (gate_got * grad_y_rows).astype(BF16)
        gate_grad_parts = in_parts(
            jnp.sum(grad_y_rows * expert_rows.astype(F32), axis=1, keepdims=True)
        )
        half_d = D // 2
        grad_hidden = dot(grad_rows, w_down, ((1,), (1,)))
        grad_gate = (
            grad_hidden * up_part * sigmoid_gate * (1.0 + gate_part * (1.0 - sigmoid_gate))
        ).astype(BF16)
        grad_up = (grad_hidden * silu_gate).astype(BF16)
        grad_gate_up = jnp.concatenate([grad_gate, grad_up], axis=1)
        grad_back = dot(grad_gate_up, w_in, ((1,), (1,)))
        grad_returned = to_experts(jnp.concatenate([grad_back.astype(BF16), gate_grad_parts], axis=1))

        grad_in = jnp.stack(
            [dot(received, grad_gate, ((0,), (0,))), dot(received, grad_up, ((0,), (0,)))]
        ).astype(BF16)
        grad_down = jnp.stack(
            [
                dot(hidden, grad_rows[:, :half_d], ((0,), (0,))),
                dot(hidden, grad_rows[:, half_d:], ((0,), (0,))),
            ]
        ).astype(BF16)

        grad_in = lax.psum_scatter(grad_in, "core", scatter_dimension=0, tiled=True)[0]
        grad_down = lax.psum_scatter(grad_down, "core", scatter_dimension=0, tiled=True)[0]
        grad_returned, grad_in, grad_down = lax.optimization_barrier((grad_returned, grad_in, grad_down))
        gate_grads = jnp.sum(grad_returned[:, D:].astype(F32), axis=1).reshape(1, EXPERTS * CAP)
        grad_returned = grad_returned[:, :D]

    grad_y = cotangent[0].astype(F32)
    pick_hot = [p.astype(BF16) for p in picks]
    grad_gates = jnp.concatenate(
        [jnp.sum(jnp.where(p, gate_grads, 0.0), axis=1, keepdims=True) for p in picks], axis=1
    )
    grad_chosen = gates * (grad_gates - jnp.sum(gates * grad_gates, axis=-1, keepdims=True))
    lanes = jnp.arange(AUX, dtype=jnp.int32) - 2
    wide_hot = (routes[0][:, :, None] == lanes[None, None, :]).astype(F32)
    grad_logits = jnp.sum(grad_chosen[:, :, None] * wide_hot, axis=1).astype(BF16)
    grad_second = dot(pick_hot[0] + pick_hot[1], grad_returned) + dot(
        grad_logits, aux_all, ((1,), (1,))
    )
    grad_gain_second = jnp.sum(grad_second * norm_second, axis=0, keepdims=True)
    grad_norm_second = grad_second * gain_second
    grad_middle = grad_y + scale_second * (
        grad_norm_second
        - norm_second * jnp.mean(grad_norm_second * norm_second, axis=-1, keepdims=True)
    )
    grad_branch = grad_middle.astype(BF16)
    grad_attended = dot(grad_branch, w_attn_out, ((1,), (1,))).astype(BF16)
    grad_queries, grad_kv = attend_back(
        lengths, block_order, mine, projected, kv, grad_attended, lse, exact
    )
    if special:
        grad_inputs, sum_qkv, sum_out, sum_aux, sum_in, sum_down = finish(
            grad_kv,
            grad_queries,
            first,
            tokens[0],
            gain_rows,
            grad_middle,
            w_all,
            attended,
            second,
            grad_logits,
            grad_gain_second,
            grad_in,
            grad_down,
            exp_local,
        )
        block_out, grad_inputs, sum_qkv, sum_out, sum_in, sum_down, gain_a, gain_m, sum_router = settle(
            middle,
            gates,
            target,
            returned,
            sum_aux,
            (
                (grad_inputs, BF16),
                (sum_qkv, F32),
                (sum_out, F32),
                (sum_in, F32),
                (sum_down, F32),
            ),
            4,
        )
        gain_a, gain_m, sum_router = gain_a[0], gain_m[0], sum_router.T
    else:
        grad_router = dot(second, grad_logits[:, 2 : 2 + EXPERTS], ((0,), (0,)))
        grad_attn_out = dot(attended, grad_branch, ((0,), (0,)))
        late = jnp.concatenate([grad_gain_second.T, grad_router], axis=1)
        late = jnp.pad(late, ((0, 0), (0, AUX - late.shape[1])))
        late = jnp.concatenate([grad_attn_out.astype(BF16), late.astype(BF16)], axis=1)
        grad_kv = lax.psum_scatter(grad_kv, CTX, scatter_dimension=0, tiled=True)
        grad_projected = jnp.concatenate([grad_queries, grad_kv], axis=1)
        grad_qkv = dot(first, grad_projected, ((0,), (0,)))
        grad_first = dot(grad_projected, w_qkv, ((1,), (1,)))
        grad_gain_first = jnp.sum(grad_first * norm_first, axis=0)
        grad_norm_first = grad_first * gain_first
        grad_inputs = grad_middle + scale_first * (
            grad_norm_first
            - norm_first * jnp.mean(grad_norm_first * norm_first, axis=-1, keepdims=True)
        )
        grad_inputs = grad_inputs.astype(BF16)
        last = jnp.pad(grad_gain_first[:, None], ((0, 0), (0, AUX - 1)))
        part = jnp.concatenate([grad_qkv.astype(BF16), last.astype(BF16), late], axis=1)
        total = lax.psum_scatter(part, ALL, scatter_dimension=0, tiled=True).astype(F32)
        sum_qkv, sum_out = total[:, :cols], total[:, cols + AUX : cols + AUX + D]
        gain_a, gain_m = total[:, cols], total[:, cols + AUX + D]
        sum_router = total[:, cols + AUX + D + 1 : cols + AUX + D + 1 + EXPERTS]
        picked = [dot(p, returned) for p in pick_hot]
        block_out = (middle + gates[:, 0:1] * picked[0] + gates[:, 1:2] * picked[1]).astype(BF16)

        def to_rows(half, rows):
            width = half.shape[1]
            got = lax.all_to_all(
                half.reshape(n_ctx, rows, width), CTX, split_axis=0, concat_axis=0, tiled=True
            ).astype(F32)
            got = got.reshape(exp_local, copies // 2, 2, rows, width).sum(axis=1)
            return got.transpose(0, 2, 1, 3).reshape(exp_local, rows, 2 * width)

        sum_in = to_rows(grad_in, in_rows)
        sum_down = to_rows(grad_down, out_rows)
    return (
        block_out[None],
        grad_inputs[None],
        gain_a,
        sum_qkv,
        sum_out,
        gain_m,
        sum_router,
        sum_in.astype(F32),
        sum_down.astype(F32),
    )


def solution(mesh):
    n_ctx, n_exp = mesh.shape["ctx"], mesh.shape["exp"]
    exp_local = EXPERTS // n_exp
    copies = n_ctx // exp_local
    inner = Mesh(mesh.devices.reshape(exp_local, copies // 2, 2, n_exp), ALL)
    by_token = P("exp", CTX, None)
    by_row = P(ALL, None)
    by_expert = P("exp", CTX, None)
    return jax.shard_map(
        on_device,
        mesh=inner,
        in_specs=(
            by_token,
            by_token,
            by_token,
            P("exp", None),
            P("exp", None),
            P(ALL),
            by_row,
            by_row,
            P(ALL),
            by_row,
            by_expert,
            by_expert,
        ),
        out_specs=(
            by_token,
            by_token,
            P(ALL),
            by_row,
            by_row,
            P(ALL),
            by_row,
            by_expert,
            by_expert,
        ),
        check_vma=False,
    )
```
